32 devices in a mesh: gx: 2 (over y), gy: 4 (over z), gz: 4 (over x, core).
Axes of the slice: x: 2, y: 2, z: 4, core: 2. Of those that a mesh axis runs over, the one named last changes fastest.
Arguments:
- velocity: float32 [3, 16, 128, 512], P(None, 'gx', 'gz', 'gy'), may hold values from -4 to 4
- pressure: float32 [16, 128, 512], P('gx', 'gz', 'gy'), may hold values from -4 to 4
- viscosity: float32 [16, 128, 512], P('gx', 'gz', 'gy'), may hold values from 0.1 to 10
- body_force: float32 [3, 16, 128, 512], P(None, 'gx', 'gz', 'gy'), may hold values from -6 to 6
Outputs:
- velocity_out: float32 [3, 16, 128, 512], P(None, 'gx', 'gz', 'gy')
- pressure_out: float32 [16, 128, 512], P('gx', 'gz', 'gy')
The draws below stay inside these ranges and needn't reach their ends.
All inputs are finite; a program needn't handle non-finite values.
Results may differ from the reference program's by a relative error of at most 0.00002.
Values sent between devices are 32-bit elements; how exact they have to be, the bound alone decides.
No kernel may reach another device: no remote copies, remote signals or barrier semaphores. Data moves between devices by JAX's collectives and lax.ppermute only.
A program may use at most 128 MiB of HBM per device.

```python
import math
import jax
import jax.numpy as jnp

PRE = 2
COARSE = 4
POST = 2
NX = 16
NY = 512
NZ = 128


def shard_levels(own_key, shape, split, least, largest):
    level, own = 1.0, jax.random.fold_in(own_key, 6)
    for dim, shards_of in split:
        steps = jnp.exp(jax.random.uniform(jax.random.fold_in(own, dim), (shards_of,), jnp.float32, least / len(split), largest / len(split)))
        level = level * jnp.repeat(steps, shape[dim] // shards_of).reshape([-1 if axis == dim else 1 for axis in range(len(shape))])
    return level


def bell_draw(key, shape, width, bound, cuts=(), held_as=jnp.bfloat16):
    factor_of = shard_levels(key, shape, cuts, -0.22, 0.18) if cuts else 1.0
    array = jax.random.normal(key, shape, jnp.float32) * width * factor_of
    return jnp.minimum(jnp.maximum(array, -bound), bound).astype(held_as)


def setup_inputs(seed: int = 0) -> dict:
    seeds = jax.random.split(jax.random.key(seed), 5)
    velocity = bell_draw(seeds[0], (3, NX, NZ, NY), 0.5, 4.0, ((1, 2), (2, 4), (3, 4)), jnp.float32)
    pressure = bell_draw(seeds[1], (NX, NZ, NY), 0.5, 4.0, ((0, 2), (1, 4), (2, 4)), jnp.float32)
    viscosity = jnp.clip(jnp.exp(math.log(10.0) - 4.6051702 * jax.random.uniform(seeds[2], (NX, NZ, NY), jnp.float32) ** shard_levels(seeds[2], (NX, NZ, NY), ((0, 2), (1, 4), (2, 4)), -0.2, 0.2)), 0.1, 10.0)
    body_force = bell_draw(seeds[3], (3, NX, NZ, NY), 1.0, 6.0, ((1, 2), (2, 4), (3, 4)), jnp.float32)
    return dict(velocity=velocity, pressure=pressure, viscosity=viscosity, body_force=body_force)


relax_weight = 0.6
uzawa_step = 0.5


def window(padded, spatial, offset):
    leading = padded.ndim - 3
    selection = [slice(None)] * leading
    for axis_id in range(3):
        extent = padded.shape[leading + axis_id]
        if axis_id == spatial:
            selection.append(slice(1 + offset, extent - 1 + offset))
        else:
            selection.append(slice(1, extent - 1))
    return padded[tuple(selection)]


def operator_terms(padded_fields, padded_visc, right_side, source, spacing):
    visc_cell = window(padded_visc, 0, 0)
    velocity = window(padded_fields[:3], 0, 0)
    inverse_sq = 1.0 / (spacing * spacing)
    half_inverse = 0.5 / spacing
    diagonal = jnp.zeros_like(visc_cell)
    viscous = jnp.zeros_like(velocity)
    divergence = jnp.zeros_like(visc_cell)
    gradients = []
    for spatial in range(3):
        for offset in (1, -1):
            face_visc = 0.5 * (visc_cell + window(padded_visc, spatial, offset))
            diagonal = diagonal + face_visc
            viscous = viscous + face_visc * (velocity - window(padded_fields[:3], spatial, offset))
        gradients.append((window(padded_fields[3], spatial, 1) - window(padded_fields[3], spatial, -1)) * half_inverse)
        divergence = divergence + (window(padded_fields[spatial], spatial, 1) - window(padded_fields[spatial], spatial, -1)) * half_inverse
    momentum = right_side - viscous * inverse_sq - jnp.stack(gradients)
    continuity = source - divergence
    return momentum, continuity, diagonal * inverse_sq, visc_cell


def relax_sweep(padded_fields, padded_visc, right_side, source, spacing):
    momentum, continuity, diagonal, visc_cell = operator_terms(padded_fields, padded_visc, right_side, source, spacing)
    velocity = window(padded_fields[:3], 0, 0)
    pressure = window(padded_fields[3], 0, 0)
    new_velocity = velocity + relax_weight * momentum / diagonal
    new_pressure = pressure + uzawa_step * visc_cell * continuity
    return jnp.concatenate([new_velocity, new_pressure[None]], axis=0)


def restrict(stacked):
    extents = stacked.shape
    blocks = stacked.reshape(extents[0], extents[1] // 2, 2, extents[2] // 2, 2, extents[3] // 2, 2)
    return blocks.mean(axis=(2, 4, 6))


def prolong(coarse_fields):
    return jnp.repeat(jnp.repeat(jnp.repeat(coarse_fields, 2, axis=1), 2, axis=2), 2, axis=3)


def pad_fields(fields):
    return jnp.pad(fields, ((0, 0), (1, 1), (1, 1), (1, 1)))


def reference(velocity, pressure, viscosity, body_force):
    padded_visc = jnp.pad(viscosity, 1)
    fields = jnp.concatenate([velocity, pressure[None]], axis=0)
    for repeat_index in range(PRE):
        fields = relax_sweep(pad_fields(fields), padded_visc, body_force, 0.0, 1.0)
    momentum, continuity, diagonal, visc_cell = operator_terms(pad_fields(fields), padded_visc, body_force, 0.0, 1.0)
    coarse = restrict(jnp.concatenate([momentum, continuity[None], viscosity[None]], axis=0))
    coarse_visc = jnp.pad(coarse[4], 1)
    correction = relax_sweep(pad_fields(jnp.zeros_like(coarse[:4])), coarse_visc, coarse[:3], coarse[3], 2.0)
    for repeat_index in range(COARSE - 1):
        correction = relax_sweep(pad_fields(correction), coarse_visc, coarse[:3], coarse[3], 2.0)
    fields = fields + prolong(correction)
    for repeat_index in range(POST):
        fields = relax_sweep(pad_fields(fields), padded_visc, body_force, 0.0, 1.0)
    return fields[:3], fields[3]
```

```python
import jax
import jax.numpy as jnp
from jax import lax
from jax.experimental import pallas as pl
from jax.experimental.pallas import tpu as pltpu
from jax.sharding import PartitionSpec as P

LANES = 128
SLOT = 8
F32 = jnp.float32
relax_weight = 0.6


def call(body, outs, args, scratch=(), cost=1):
    return pl.pallas_call(
        body,
        out_shape=[jax.ShapeDtypeStruct(shape, F32) for shape in outs],
        in_specs=[pl.BlockSpec(memory_space=pltpu.VMEM)] * len(args),
        out_specs=[pl.BlockSpec(memory_space=pltpu.VMEM)] * len(outs),
        scratch_shapes=[pltpu.VMEM(shape, F32) for shape in scratch],
        compiler_params=pltpu.CompilerParams(vmem_limit_bytes=40 * 2**20),
        cost_estimate=pl.CostEstimate(
            flops=cost * 10**6, bytes_accessed=cost * 10**6, transcendentals=0
        ),
    )(*args)


def swap(array, axis, which):
    count = lax.axis_size(axis)
    if axis == "gy" and which == 1:
        other = lax.axis_size("gz")
        pairs = []
        for i in range(count):
            j = i + 1 if i % 2 else i - 1
            for k in range(other):
                to = j * other + k if 0 <= j < count else i * other + (k ^ 1)
                pairs.append((i * other + k, to))
        return lax.ppermute(array, ("gy", "gz"), pairs)
    pairs = []
    for i in range(which, count, 2):
        j = (i + 1) % count
        pairs += [(i, j), (j, i)]
    return lax.ppermute(array, axis, pairs)


def place(axis):
    i = lax.axis_index(axis)
    last = lax.axis_size(axis) - 1
    return i, jnp.where(i > 0, 1, 0), jnp.where(i < last, 1, 0)


def iota(shape, dim):
    return lax.broadcasted_iota(jnp.int32, shape, dim)


def truth(flag, shape):
    return jnp.full(shape, flag, jnp.int32) > 0


def roll(x, shift, dim):
    if isinstance(shift, int):
        shift %= x.shape[dim]
        return x if shift == 0 else pltpu.roll(x, shift, dim)
    return pltpu.roll(x, lax.rem(shift + 2 * x.shape[dim], x.shape[dim]), dim)


def high_side(axis, message):
    return jnp.where(lax.axis_index(axis) % 2 == message, 1, 0)


def left_right(axis, a, b):
    odd = truth(lax.axis_index(axis) % 2, a.shape)
    return jnp.where(odd, a, b), jnp.where(odd, b, a)


def x_messages():
    return 1 if lax.axis_size("gx") == 2 else 2


def pair_edges(planes, fields, rows):
    lane = iota((rows, LANES), 1) // SLOT
    half = fields // 2
    out = []
    for j in range(half):
        total = jnp.zeros((rows, LANES), F32)
        for part in range(2):
            for q, x in enumerate(planes(j + part * half)):
                slot = q + part * (LANES // SLOT // 2)
                total = jnp.where(lane == slot, roll(x, slot * SLOT + 4, 1), total)
        out.append(total)
    return out


def merge_y(a, b):
    _, has_left, has_right = place("gy")
    left, right = left_right("gy", a, b)
    spot = iota(a.shape, 1) % SLOT
    kept = (spot < 4 * has_left) | (spot >= SLOT - 4 * has_right)
    return jnp.where(kept, jnp.where(spot < 4, left, right), 0.0)


def first_pack(v, p, e, f, x_main, y_main):
    nx, nz, _ = p.shape

    def plane(i, q):
        return v[i, q] if i < 3 else p[q] if i == 3 else e[q] if i == 4 else f[i - 5, q]

    for m in range(x_main.shape[0]):
        high = high_side("gx", m)
        n = 0
        for i in range(8):
            width = 3 if i < 5 else 2
            for j in range(width):
                x_main[m, n] = plane(i, high * (nx - width) + j)
                n += 1
    edges = pair_edges(lambda i: [plane(i, q) for q in range(nx)], 8, nz)
    for j in range(4):
        y_main[j] = edges[j]


def z_strip(low, high, toward_right, shift):
    row = iota((8, LANES), 0)
    right = truth(toward_right, (8, LANES))
    first = jnp.where(right, roll(high[0], 4, 0), low[0])
    second = jnp.where(right, high[1], roll(low[1], 4, 0))
    return jnp.where(row < 4, first, second)


def second_pack(v, p, e, f, y_a, y_b, halo, z_a, z_b):
    nx, nz, _ = p.shape

    def tile(i, q, top):
        at = pl.ds(nz - 8, 8) if top else pl.ds(0, 8)
        if i < 3:
            return v[i, q, at]
        return p[q, at] if i == 3 else e[q, at] if i == 4 else f[i - 5, q, at]

    merged = [merge_y(y_a[j], y_b[j]) for j in range(4)]
    for j in range(4):
        halo[j] = merged[j]
    for m, out in enumerate((z_a, z_b)):
        right = high_side("gz", m)
        for j in range(4):
            for q in range(nx):
                low = tile(j, q, False), tile(j + 4, q, False)
                high = tile(j, q, True), tile(j + 4, q, True)
                out[j * nx + q] = z_strip(low, high, right, 4)
        for j in range(2):
            low = merged[j][:8], merged[j + 2][:8]
            high = merged[j][nz - 8 :], merged[j + 2][nz - 8 :]
            out[4 * nx + j] = z_strip(low, high, right, 4)


def z_tiles(a, b):
    _, has_left, has_right = place("gz")
    left, right = left_right("gz", a, b)
    row = iota(a.shape, 0)
    kept = (row < 4 * has_right) | (row >= 8 - 4 * has_left)
    first = jnp.where(row < 4, right, roll(left, 4, 0))
    second = jnp.where(row < 4, roll(right, 4, 0), left)
    return jnp.where(kept, first, 0.0), jnp.where(kept, second, 0.0)


def third_pack(z_a, z_b, halo, z_halo, halo_full, x_rim):
    nx = z_halo.shape[1]
    nz = halo.shape[1]
    for j in range(4):
        for q in range(nx):
            z_halo[j, q], z_halo[j + 4, q] = z_tiles(z_a[j * nx + q], z_b[j * nx + q])
    for j in range(4):
        halo_full[j, pl.ds(0, nz)] = halo[j]
    for j in range(2):
        first, second = z_tiles(z_a[4 * nx + j], z_b[4 * nx + j])
        halo_full[j, pl.ds(nz, 8)] = first
        halo_full[j + 2, pl.ds(nz, 8)] = second
    pack_rim(x_rim, z_halo, lambda j: halo_full[j], 8, (2,) * 5 + (1,) * 3, 3, 32)


def pack_rim(x_rim, z_halo, halo_pair, fields, widths, planes, stride):
    nx = z_halo.shape[1]
    half = fields // 2
    per_column = LANES // stride
    for m in range(x_rim.shape[0]):
        high = high_side("gx", m)
        n = 0
        for i in range(fields):
            for j in range(widths[i]):
                x_rim[m, n] = z_halo[i, high * (nx - widths[i]) + j]
                n += 1
        pairs = [halo_pair(j) for j in range(half)]
        rows = pairs[0].shape[0]
        column = iota((rows, LANES), 1) // stride
        first = high * (nx - planes) * SLOT
        for c in range(-(-fields // per_column)):
            total = jnp.zeros((rows, LANES), F32)
            for t in range(min(per_column, fields - c * per_column)):
                i = c * per_column + t
                at = t * stride - first - (i // half) * (LANES // 2)
                total = jnp.where(column == t, roll(pairs[i % half], at + LANES, 1), total)
            for r in range(rows // 8):
                x_rim[m, n] = total[8 * r : 8 * r + 8]
                n += 1


def main_shifts(x, halo, p):
    lane = iota(x.shape, 1)
    beside = roll(halo, LANES - SLOT * p - 4, 1)
    rows = x.shape[0]
    return (
        roll(jnp.where(lane == 0, beside, x), LANES - 1, 1),
        roll(jnp.where(lane == LANES - 1, beside, x), 1, 1),
        roll(x, rows - 1, 0),
        roll(x, 1, 0),
    )


def halo_shifts(x, edge):
    spot = iota(x.shape, 1) % SLOT
    rows = x.shape[0]
    return (
        roll(x, LANES - SLOT, 1),
        roll(x, SLOT, 1),
        roll(jnp.where(spot == 4, edge, x), LANES - 1, 1),
        roll(jnp.where(spot == 3, edge, x), 1, 1),
        roll(x, rows - 1, 0),
        roll(x, 1, 0),
    )


def main_weights(e, halo_e, w, lo, hi):
    def face(p, carry):
        w[0][p] = e[p] + e[p + 1]
        return carry

    lax.fori_loop(lo - 1, hi, face, 0)

    def body(p, carry):
        x = e[p]
        total = w[0][p] + w[0][p - 1]
        for n, y in enumerate(main_shifts(x, halo_e[...], p)):
            total += x + y
            w[1 + n][p] = x + y
        w[5][p] = relax_weight / total
        return carry

    lax.fori_loop(lo, hi, body, 0)


def halo_weights(e, edge_e, w):
    x = e[...]
    total = jnp.zeros_like(x)
    for n, y in enumerate(halo_shifts(x, edge_e[...])):
        total += x + y
        w[n] = x + y
    w[6] = relax_weight / total


def terms(k, up, down, yp, ym, zp, zm):
    return (up - down, zp - zm, yp - ym)[k]


def main_operator(src, halo, w, force, p, fields=(0, 1, 2)):
    wxp, wxm, wyp, wym, wzp, wzm = w[0][p], w[0][p - 1], w[1][p], w[2][p], w[3][p], w[4][p]
    x = src[3, p]
    around = main_shifts(x, halo[3], p)
    up, down = src[3, p + 1], src[3, p - 1]
    olds, sums, spread = [], [], 0.0
    for k in range(3):
        u = src[k, p]
        yp, ym, zp, zm = main_shifts(u, halo[k], p)
        xp, xm = src[k, p + 1], src[k, p - 1]
        total = force[k, p] - terms(k, up, down, *around)
        total += wxp * xp + wxm * xm
        total += wyp * yp + wym * ym
        total += wzp * zp + wzm * zm
        spread += terms(k, xp, xm, yp, ym, zp, zm)
        olds.append(u)
        sums.append(total)
    olds.append(x)
    return olds, sums, spread


def halo_operator(halo, edge, w, force):
    x = halo[3]
    px = halo_shifts(x, edge[3])
    olds, sums, spread = [], [], 0.0
    for k in range(3):
        u = halo[k]
        around = halo_shifts(u, edge[k])
        total = force[k] - terms(k, *px)
        for n in range(6):
            total += w[n] * around[n]
        spread += terms(k, *around)
        olds.append(u)
        sums.append(total)
    olds.append(x)
    return olds, sums, spread


def relaxed(olds, sums, spread, factor, e):
    new = [0.4 * olds[k] + factor * sums[k] for k in range(3)]
    return new + [olds[3] - 0.25 * e * spread]


def add_edge(edge, k, p, x):
    slot = iota(x.shape, 1) // SLOT
    edge[k] = jnp.where(slot == p, roll(x, p * SLOT + 4, 1), edge[k])


def fill_edges(edge, src, fields, lo, hi):
    for k in range(fields):
        edge[k] = jnp.zeros(edge.shape[1:], F32)

    def body(p, carry):
        for k in range(fields):
            add_edge(edge, k, p, src[k, p])
        return carry

    lax.fori_loop(lo, hi, body, 0)


def fine_masks(rows, slots):
    nz = rows - 8
    _, zl, zr = place("gz")
    _, yl, yr = place("gy")
    _, xl, xr = place("gx")
    r = iota((8, LANES), 0)
    tile = (r < 4 * zr) | (r >= 8 - 4 * zl)
    r = iota((rows, LANES), 0)
    lane = iota((rows, LANES), 1)
    spot, slot = lane % SLOT, lane // SLOT
    column = (r < nz + 4 * zr) | (r >= rows - 4 * zl)
    column &= (spot < 4 * yl) | (spot >= SLOT - 4 * yr)
    column &= (slot >= 3 - 3 * xl) & (slot < slots - 3 + 3 * xr)
    return tile, column


def fine_sweep(src, halo, edge, dst, halo_dst, edge_dst, w, hw, e, halo_e, force, halo_f, lo, hi, masks):
    tile, column = masks
    nz = src.shape[2] - 8
    if edge_dst is not None:
        for k in range(4):
            edge_dst[k] = jnp.zeros(edge_dst.shape[1:], F32)

    def body(p, carry):
        new = relaxed(*main_operator(src, halo, w, force, p), w[5][p], e[p])
        for k in range(4):
            x = new[k]
            dst[k, p, pl.ds(0, nz)] = x[:nz]
            x8 = jnp.where(tile, x[nz:], 0.0)
            dst[k, p, pl.ds(nz, 8)] = x8
            if edge_dst is not None:
                add_edge(edge_dst, k, p, jnp.concatenate([x[:nz], x8], axis=0))
        return carry

    lax.fori_loop(lo, hi, body, 0)
    new = relaxed(*halo_operator(halo, edge, hw, halo_f), hw[6], halo_e[...])
    for k in range(4):
        halo_dst[k] = jnp.where(column, new[k], 0.0)


def spans(slots, width):
    _, xl, xr = place("gx")
    return 3 - width * xl, slots - 3 + width * xr


def own_slots(x, nx, part):
    lane = iota(x.shape, 1)
    x = roll(x, 3 * SLOT - part * (LANES // 2), 1)
    return jnp.where((lane >= 3 * SLOT) & (lane < (3 + nx) * SLOT), x, 0.0)


def x_side(m):
    right = high_side("gx", m)
    _, has_left, has_right = place("gx")
    return right, jnp.where(right > 0, has_right, has_left)


def rim_halo(x, t, stride, planes, right, valid, nx):
    base = right * (nx + 3) + (1 - right) * (3 - planes)
    lane = iota(x.shape, 1)
    x = roll(x, base * SLOT - t * stride + LANES, 1)
    kept = (lane >= base * SLOT) & (lane < (base + planes * valid) * SLOT)
    return jnp.where(kept, x, 0.0), kept


def viscosity_force(e_in, f_in, z_halo, halo_full, x_main, x_rim, e, halo_e, force, halo_f):
    nx, nz, _ = e_in.shape
    slots = nx + 6
    zero = jnp.zeros((nz + 8, LANES), F32)
    for p in list(range(3)) + list(range(nx + 3, slots)):
        e[p] = zero
        for k in range(3):
            force[k, p] = zero
    for q in range(nx):
        e[q + 3, pl.ds(0, nz)] = e_in[q]
        e[q + 3, pl.ds(nz, 8)] = z_halo[4, q]
        for k in range(3):
            force[k, q + 3, pl.ds(0, nz)] = 2.0 * f_in[k, q]
            force[k, q + 3, pl.ds(nz, 8)] = 2.0 * z_halo[5 + k, q]
    halo_e[...] = own_slots(halo_full[0], nx, 1)
    for k in range(3):
        halo_f[k] = 2.0 * own_slots(halo_full[k + 1], nx, 1)
    for m in range(x_main.shape[0]):
        right, valid = x_side(m)
        there = truth(valid, (nz, LANES))
        there8 = truth(valid, (8, LANES))
        for j in range(3):
            e[right * (nx + 3) + j, pl.ds(0, nz)] = jnp.where(there, x_main[m, 12 + j], 0.0)
        for j in range(2):
            at = right * (nx + 2) + 1 + j
            e[at, pl.ds(nz, 8)] = jnp.where(there8, x_rim[m, 8 + j], 0.0)
            for k in range(3):
                force[k, at, pl.ds(0, nz)] = jnp.where(there, 2.0 * x_main[m, 15 + 2 * k + j], 0.0)
        for k in range(3):
            at = right * (nx + 1) + 2
            force[k, at, pl.ds(nz, 8)] = jnp.where(there8, 2.0 * x_rim[m, 10 + k], 0.0)
        tiles = (nz + 8) // 8
        column = jnp.concatenate([x_rim[m, 13 + tiles + r] for r in range(tiles)], axis=0)
        x, kept = rim_halo(column, 0, 32, 3, right, valid, nx)
        halo_e[...] = jnp.where(kept, x, halo_e[...])
        for k in range(3):
            x, kept = rim_halo(column, 1 + k, 32, 3, right, valid, nx)
            halo_f[k] = jnp.where(kept, 2.0 * x, halo_f[k])


def first_fields(v, p_in, z_halo, halo_full, x_main, x_rim, u, other, halo):
    nx, nz, _ = p_in.shape
    slots = nx + 6
    zero = jnp.zeros((nz + 8, LANES), F32)
    for k in range(4):
        for p in list(range(3)) + list(range(nx + 3, slots)):
            u[k, p] = zero
            other[k, p] = zero
        for q in range(nx):
            u[k, q + 3, pl.ds(0, nz)] = v[k, q] if k < 3 else p_in[q]
            u[k, q + 3, pl.ds(nz, 8)] = z_halo[k, q]
        halo[k] = own_slots(halo_full[k], nx, 0)
    for m in range(x_main.shape[0]):
        right, valid = x_side(m)
        there = truth(valid, (nz, LANES))
        there8 = truth(valid, (8, LANES))
        tiles = (nz + 8) // 8
        column = jnp.concatenate([x_rim[m, 13 + r] for r in range(tiles)], axis=0)
        for k in range(4):
            for j in range(3):
                x = jnp.where(there, x_main[m, 3 * k + j], 0.0)
                u[k, right * (nx + 3) + j, pl.ds(0, nz)] = x
            for j in range(2):
                x = jnp.where(there8, x_rim[m, 2 * k + j], 0.0)
                u[k, right * (nx + 2) + 1 + j, pl.ds(nz, 8)] = x
            x, kept = rim_halo(column, k, 32, 3, right, valid, nx)
            halo[k] = jnp.where(kept, x, halo[k])


def pre_smooth(
    v, p_in, e_in, f_in, z_halo, halo_full, x_main, x_rim,
    fields, coarse, edges, x_fine,
    ua, ub, ha, hb, ca, cb, e, halo_e, edge_e, force, halo_f, w0, w1, w2, w3, w4, w5, hw, summed,
):
    nx, nz, _ = p_in.shape
    slots = nx + 6
    w = (w0, w1, w2, w3, w4, w5)
    viscosity_force(e_in, f_in, z_halo, halo_full, x_main, x_rim, e, halo_e, force, halo_f)
    first_fields(v, p_in, z_halo, halo_full, x_main, x_rim, ua, ub, ha)
    masks = fine_masks(nz + 8, slots)
    fill_edges(ca, ua, 4, 0, slots)
    edge_e[...] = jnp.zeros(edge_e.shape, F32)

    def body(p, carry):
        slot = iota(edge_e.shape, 1) // SLOT
        edge_e[...] = jnp.where(slot == p, roll(e[p], p * SLOT + 4, 1), edge_e[...])
        return carry

    lax.fori_loop(0, slots, body, 0)
    lo, hi = spans(slots, 2)
    main_weights(e, halo_e, w, lo, hi)
    halo_weights(halo_e, edge_e, hw)
    rest = (w, hw, e, halo_e, force, halo_f)
    fine_sweep(ua, ha, ca, ub, hb, cb, *rest, lo, hi, masks)
    lo, hi = spans(slots, 1)
    fine_sweep(ub, hb, cb, ua, ha, ca, *rest, lo, hi, masks)
    for k in range(4):
        for q in range(nx):
            fields[k, q] = ua[k, q + 3, pl.ds(0, nz)]
    for m in range(x_fine.shape[0]):
        high = high_side("gx", m)
        for k in range(4):
            for j in range(2):
                x_fine[m, 2 * k + j] = ua[k, 3 + high * (nx - 2) + j, pl.ds(0, nz)]
    lane = iota((nz, LANES), 1)
    for j in range(2):
        first = roll(ca[j][:nz], -3 * SLOT, 1)
        second = roll(ca[j + 2][:nz], LANES // 2 - 3 * SLOT, 1)
        edges[j] = jnp.where(lane < LANES // 2, first, second)

    def block(q, carry):
        totals = [0.0] * 5
        for j in range(2):
            p = 2 * q + 3 + j
            olds, sums, spread = main_operator(ua, ha, w, force, p)
            diagonal = w0[p] + w0[p - 1] + w1[p] + w2[p] + w3[p] + w4[p]
            for k in range(3):
                totals[k] += sums[k] - diagonal * olds[k]
            totals[3] += spread
            totals[4] += e[p]
        for k in range(5):
            summed[k, q] = totals[k][:nz]
        return carry

    lax.fori_loop(0, nx // 2, block, 0)
    scale = (0.5, 0.5, 0.5, -1.0 / 32.0, 0.125)
    cz = nz // 2
    left = []
    for k in range(5):
        for r in range(nx // 4):
            halves = []
            for s in range(2):
                q = 2 * r + s
                even = summed[k, q, pl.ds(0, cz, stride=2)]
                halves.append((even + summed[k, q, pl.ds(1, cz, stride=2)]) * scale[k])
            left.append(jnp.concatenate(halves, axis=1))
    left = jnp.concatenate(left, axis=0)
    pick = iota((2 * LANES, LANES), 0) // 2 == iota((2 * LANES, LANES), 1)
    out = jnp.dot(
        left, pick.astype(F32), precision=lax.Precision.HIGHEST, preferred_element_type=F32
    )
    for k in range(5):
        for r in range(nx // 4):
            at = (k * (nx // 4) + r) * cz
            coarse[k, r] = out[at : at + cz]


def fourth_pack(own, other, fields, whole, z_a, z_b):
    nx, nz = fields.shape[1:3]
    pairs = whole.shape[1]
    cz = whole.shape[2]
    gx = lax.axis_index("gx")
    for k in range(5):
        for r in range(pairs):
            if other is None:
                whole[k, r] = own[k, r]
            else:
                mine = truth(jnp.where(gx == r // (pairs // 2), 1, 0), (cz, LANES))
                n = r % (pairs // 2)
                whole[k, r] = jnp.where(mine, own[k, n], other[k, n])
    row = iota((8, LANES), 0) // 2
    for m, out in enumerate((z_a, z_b)):
        right = high_side("gz", m)
        start = pl.multiple_of(right * (cz - 8), 8)
        for k in range(5):
            for r in range(pairs):
                out[k * pairs + r] = whole[k, r, pl.ds(start, 8)]
        toward = truth(right, (8, LANES))
        for q in range(nx):
            total = jnp.zeros((8, LANES), F32)
            for k in range(4):
                low = roll(fields[k, q, pl.ds(0, 8)], 2 * k, 0)
                high = roll(fields[k, q, pl.ds(nz - 8, 8)], 2 * k - 6, 0)
                total = jnp.where(row == k, jnp.where(toward, high, low), total)
            out[5 * pairs + q] = total


def fifth_pack(whole, z_a, z_b, edges, full, z_halo, y_a, y_b):
    pairs, cz = whole.shape[1:3]
    nx = z_halo.shape[1]
    nz = edges.shape[1]
    _, has_left, has_right = place("gz")
    to_left = truth(has_left, (8, LANES))
    to_right = truth(has_right, (8, LANES))
    for k in range(5):
        for r in range(pairs):
            n = k * pairs + r
            left, right = left_right("gz", z_a[n], z_b[n])
            full[k, r, pl.ds(0, cz)] = whole[k, r]
            full[k, r, pl.ds(cz, 8)] = jnp.where(to_right, right, 0.0)
            full[k, r, pl.ds(cz + 8, 8)] = jnp.where(to_left, left, 0.0)
    row = iota((8, LANES), 0)
    for q in range(nx):
        left, right = left_right("gz", z_a[5 * pairs + q], z_b[5 * pairs + q])
        for k in range(4):
            x = jnp.where(row < 2 * has_right, roll(right, -2 * k, 0), 0.0)
            z_halo[k, q] = jnp.where(row >= 8 - 2 * has_left, roll(left, 6 - 2 * k, 0), x)
    rows = cz + 16
    tiles = rows // 8
    slot = iota((rows, LANES), 1) // SLOT
    per = LANES // SLOT
    count = 5 * pairs * 2
    columns = -(-count // per)
    behind = pair_edges(lambda i: [z_halo[i, q] for q in range(nx)], 4, 8)
    for m, out in enumerate((y_a, y_b)):
        high = high_side("gy", m) * (LANES // 2 - SLOT)
        for c in range(columns):
            total = jnp.zeros((rows, LANES), F32)
            for t in range(min(per, count - c * per)):
                n = c * per + t
                k, r, s = n // (2 * pairs), n // 2 % pairs, n % 2
                at = SLOT * t - s * (LANES // 2) - high
                total = jnp.where(slot == t, roll(full[k, r], at + LANES, 1), total)
            for i in range(tiles):
                out[c * tiles + i] = total[8 * i : 8 * i + 8]
        n = columns * tiles
        for j in range(2):
            for i in range(nz // 8):
                out[n] = edges[j, pl.ds(8 * i, 8)]
                n += 1
            out[n] = behind[j]
            n += 1


def sixth_pack(y_a, y_b, z_halo, halo_full, x_rim):
    tiles = halo_full.shape[1] // 8
    first = y_a.shape[0] - 2 * tiles
    for j in range(2):
        for i in range(tiles):
            n = first + j * tiles + i
            halo_full[j, pl.ds(8 * i, 8)] = merge_y(y_a[n], y_b[n])
    pack_rim(x_rim, z_halo, lambda j: halo_full[j], 4, (1,) * 4, 1, SLOT)


def coarse_solve(full, y_a, y_b, main, halo, ca, cb, force, e, w0, w1, w2, w3, w4, w5, grown):
    pairs, rows = full.shape[1:3]
    planes = 2 * pairs
    own = main.shape[1] - 2
    tiles = rows // 8
    per = LANES // SLOT
    lane = iota((rows, LANES), 1)
    row = iota((rows, LANES), 0)
    _, zl, zr = place("gz")
    _, yl, yr = place("gy")
    half = LANES // 2
    inside = (row < rows - 16 + 8 * zr) | (row >= rows - 8 * zl)
    inside &= (lane < half + SLOT * yr) | (lane >= LANES - SLOT * yl)
    zero = jnp.zeros((rows, LANES), F32)
    w = (w0, w1, w2, w3, w4, w5)
    for k in range(4):
        for p in (0, planes + 1):
            ca[k, p] = zero
            cb[k, p] = zero
    e[0] = zero
    e[planes + 1] = zero
    for n in range(10 * pairs):
        k, r, s = n // (2 * pairs), n // 2 % pairs, n % 2
        c, t = n // per, n % per
        a = jnp.concatenate([y_a[c * tiles + i] for i in range(tiles)], axis=0)
        b = jnp.concatenate([y_b[c * tiles + i] for i in range(tiles)], axis=0)
        left, right = left_right("gy", a, b)
        x = roll(full[k, r], -s * half, 1)
        x = jnp.where(lane < half, x, roll(right, half - SLOT * t, 1))
        x = jnp.where(lane < LANES - SLOT, x, roll(left, LANES - SLOT - SLOT * t, 1))
        x = jnp.where(inside, x, 0.0)
        if k < 4:
            force[k, 2 * r + s] = x
        else:
            e[2 * r + s + 1] = x

    def shifts(x):
        return (
            roll(x, LANES - 1, 1),
            roll(x, 1, 1),
            roll(x, rows - 1, 0),
            roll(x, 1, 0),
        )

    for p in range(planes + 1):
        w0[p] = e[p] + e[p + 1]

    def start(p, carry):
        x = e[p]
        total = w0[p] + w0[p - 1]
        for n, y in enumerate(shifts(x)):
            total += x + y
            w[1 + n][p] = x + y
        factor = jnp.where(inside, relax_weight / total, 0.0)
        w5[p] = factor
        for k in range(3):
            ca[k, p] = factor * force[k, p - 1]
        ca[3, p] = x * force[3, p - 1]
        return carry

    lax.fori_loop(1, planes + 1, start, 0)

    def sweep(src, dst):
        def body(p, carry):
            wxp, wxm = w0[p], w0[p - 1]
            wyp, wym, wzp, wzm = w1[p], w2[p], w3[p], w4[p]
            x = src[3, p]
            around = shifts(x)
            up, down = src[3, p + 1], src[3, p - 1]
            spread = 0.0
            for k in range(3):
                u = src[k, p]
                yp, ym, zp, zm = shifts(u)
                xp, xm = src[k, p + 1], src[k, p - 1]
                total = force[k, p - 1] - 2.0 * terms(k, up, down, *around)
                total += wxp * xp + wxm * xm
                total += wyp * yp + wym * ym
                total += wzp * zp + wzm * zm
                spread += terms(k, xp, xm, yp, ym, zp, zm)
                dst[k, p] = jnp.where(inside, 0.4 * u + w5[p] * total, 0.0)
            dst[3, p] = jnp.where(inside, x + e[p] * (force[3, p - 1] - 0.125 * spread), 0.0)
            return carry

        lax.fori_loop(1, planes + 1, body, 0)

    sweep(ca, cb)
    sweep(cb, ca)
    sweep(ca, cb)

    cz = rows - 16
    spread_lanes = (iota((LANES, LANES), 1) // 2 == iota((LANES, LANES), 0)).astype(F32)
    lane = iota((LANES, LANES), 1)
    cell = iota((LANES, LANES), 0)
    spot = lane % SLOT
    wanted = jnp.where(spot < 4, LANES - 2, half - 2) + spot // 2
    column = jnp.zeros((4 * rows, LANES), F32)
    first = lax.axis_index("gx") * own

    def grow(ref, index, x):
        ref[index + (pl.ds(0, cz, stride=2),)] = x[:cz]
        ref[index + (pl.ds(1, cz, stride=2),)] = x[:cz]
        edge = jnp.concatenate([x[cz : cz + 8], x[rows - 8 :]], axis=0)
        grown[pl.ds(0, 16, stride=2)] = edge
        grown[pl.ds(1, 16, stride=2)] = edge
        r = iota((8, LANES), 0)
        tail = jnp.where(r < 4, grown[pl.ds(0, 8)], grown[pl.ds(24, 8)])
        ref[index + (pl.ds(2 * cz, 8),)] = tail

    for i in range(own + 2):
        x = jnp.concatenate([cb[k, first + i] for k in range(4)], axis=0)
        wide = jnp.dot(
            x, spread_lanes, precision=lax.Precision.HIGHEST, preferred_element_type=F32
        )
        for k in range(4):
            grow(main, (k, i), wide[k * rows : (k + 1) * rows])
        here = (lane // SLOT + 1) // 2 - 1 == i
        chosen = (here & (cell == wanted)).astype(F32)
        column += jnp.dot(
            x, chosen, precision=lax.Precision.HIGHEST, preferred_element_type=F32
        )
    for k in range(4):
        grow(halo, (k,), column[k * rows : (k + 1) * rows])


def post_smooth(
    e_in, f_in, z_first, halo_first, x_main, x_first, fields, z_halo, halo_full, x_fine, x_rim,
    main, column, v_out, p_out,
    ua, ub, ha, hb, ca, cb, e, halo_e, edge_e, force, halo_f, w0, w1, w2, w3, w4, w5, hw,
):
    nx, nz, _ = e_in.shape
    slots = nx + 6
    w = (w0, w1, w2, w3, w4, w5)
    viscosity_force(e_in, f_in, z_first, halo_first, x_main, x_first, e, halo_e, force, halo_f)
    zero = jnp.zeros((nz + 8, LANES), F32)
    for k in range(4):
        for p in (1, 2, nx + 3, nx + 4):
            ua[k, p] = zero
            ub[k, p] = zero
        for q in range(nx):
            i = q // 2 + 1
            ua[k, q + 3, pl.ds(0, nz)] = fields[k, q] + main[k, i, pl.ds(0, nz)]
            ua[k, q + 3, pl.ds(nz, 8)] = z_halo[k, q] + main[k, i, pl.ds(nz, 8)]
        ha[k] = own_slots(halo_full[k % 2], nx, k // 2)
    for m in range(x_fine.shape[0]):
        right, valid = x_side(m)
        there = truth(valid, (nz, LANES))
        there8 = truth(valid, (8, LANES))
        tiles = (nz + 8) // 8
        side = jnp.concatenate([x_rim[m, 4 + r] for r in range(tiles)], axis=0)
        i = right * (nx // 2 + 1)
        for k in range(4):
            for j in range(2):
                at = 1 + right * (nx + 2) + j
                x = x_fine[m, 2 * k + j] + main[k, i, pl.ds(0, nz)]
                ua[k, at, pl.ds(0, nz)] = jnp.where(there, x, 0.0)
            x = x_rim[m, k] + main[k, i, pl.ds(nz, 8)]
            ua[k, 2 + right * (nx + 1), pl.ds(nz, 8)] = jnp.where(there8, x, 0.0)
            x, kept = rim_halo(side, k, SLOT, 1, right, valid, nx)
            ha[k] = jnp.where(kept, x, ha[k])
    masks = fine_masks(nz + 8, slots)
    for k in range(4):
        ha[k] = jnp.where(masks[1], ha[k] + column[k], 0.0)
    fill_edges(ca, ua, 4, 1, slots - 1)
    edge_e[...] = jnp.zeros(edge_e.shape, F32)

    def body(p, carry):
        slot = iota(edge_e.shape, 1) // SLOT
        edge_e[...] = jnp.where(slot == p, roll(e[p], p * SLOT + 4, 1), edge_e[...])
        return carry

    lax.fori_loop(1, slots - 1, body, 0)
    lo, hi = spans(slots, 1)
    main_weights(e, halo_e, w, lo, hi)
    halo_weights(halo_e, edge_e, hw)
    rest = (w, hw, e, halo_e, force, halo_f)
    fine_sweep(ua, ha, ca, ub, hb, cb, *rest, lo, hi, masks)

    def last(p, carry):
        new = relaxed(*main_operator(ub, hb, w, force, p), w5[p], e[p])
        for k in range(3):
            v_out[k, p - 3] = new[k][:nz]
        p_out[p - 3] = new[3][:nz]
        return carry

    lax.fori_loop(3, nx + 3, last, 0)


def local(velocity, pressure, viscosity, body_force):
    nx, nz, ny = pressure.shape
    if ny != LANES or nx * SLOT * 2 != LANES or nz % 16:
        raise ValueError("unsupported block")
    sides = x_messages()
    rows, slots = nz + 8, nx + 6
    inputs = [velocity, pressure, viscosity, body_force]
    block = (nz, LANES)

    x_main, y_main = call(first_pack, [(sides, 21) + block, (4,) + block], inputs)
    x_main = swap_x(x_main)
    y_a, y_b = swap(y_main, "gy", 0), swap(y_main, "gy", 1)
    z_shape = (4 * nx + 2, 8, LANES)
    halo, z_a, z_b = call(
        second_pack, [(4,) + block, z_shape, z_shape], inputs + [y_a, y_b]
    )
    z_a, z_b = swap(z_a, "gz", 0), swap(z_b, "gz", 1)
    tiles = rows // 8
    z_first, halo_first, x_first = call(
        third_pack,
        [(8, nx, 8, LANES), (4, rows, LANES), (sides, 13 + 2 * tiles, 8, LANES)],
        [z_a, z_b, halo],
    )
    x_first = swap_x(x_first)

    state = [(4, slots, rows, LANES)] * 2 + [(4, rows, LANES)] * 4
    state += [(slots, rows, LANES), (rows, LANES), (rows, LANES)]
    state += [(3, slots, rows, LANES), (3, rows, LANES)]
    state += [(slots, rows, LANES)] * 6 + [(7, rows, LANES)]
    fields, own, edges, x_fine = call(
        pre_smooth,
        [(4, nx) + block, (5, nx // 4, nz // 2, LANES), (2,) + block, (sides, 8) + block],
        inputs + [z_first, halo_first, x_main, x_first],
        state + [(5, nx // 2, nz, LANES)],
        cost=8,
    )
    if lax.axis_size("gx") == 2:
        parts = [own, swap(own, "gx", 0)]
        gather = fourth_pack
    else:
        parts = [lax.all_gather(own, "gx", axis=1, tiled=True)]

        def gather(a, *refs):
            fourth_pack(a, None, *refs)

    x_fine = swap_x(x_fine)
    pairs = lax.axis_size("gx") * (nx // 4)
    z_shape = (5 * pairs + nx, 8, LANES)
    whole, z_a, z_b = call(
        gather, [(5, pairs, nz // 2, LANES), z_shape, z_shape], parts + [fields]
    )
    z_a, z_b = swap(z_a, "gz", 0), swap(z_b, "gz", 1)
    deep = nz // 2 + 16
    y_shape = (-(-10 * pairs * SLOT // LANES) * (deep // 8) + 2 * tiles, 8, LANES)
    full, z_halo, y_a, y_b = call(
        fifth_pack,
        [(5, pairs, deep, LANES), (4, nx, 8, LANES), y_shape, y_shape],
        [whole, z_a, z_b, edges],
    )
    y_a, y_b = swap(y_a, "gy", 0), swap(y_b, "gy", 1)
    halo_full, x_rim = call(
        sixth_pack,
        [(2, rows, LANES), (sides, 4 + tiles, 8, LANES)],
        [y_a, y_b, z_halo],
    )
    x_rim = swap_x(x_rim)
    planes = 2 * pairs
    deep_plane = (deep, LANES)
    main, column = call(
        coarse_solve,
        [(4, nx // 2 + 2, rows, LANES), (4, rows, LANES)],
        [full, y_a, y_b],
        [(4, planes + 2) + deep_plane] * 2
        + [(4, planes) + deep_plane]
        + [(planes + 2,) + deep_plane] * 7
        + [(32, LANES)],
        cost=4,
    )
    v_out, p_out = call(
        post_smooth,
        [(3, nx) + block, (nx,) + block],
        [viscosity, body_force, z_first, halo_first, x_main, x_first]
        + [fields, z_halo, halo_full, x_fine, x_rim, main, column],
        state,
        cost=8,
    )
    return v_out, p_out


def swap_x(array):
    if array.shape[0] == 1:
        return swap(array, "gx", 0)
    parts = [swap(array[m], "gx", m) for m in range(2)]
    return jnp.stack(parts)


def solution(mesh):
    return jax.shard_map(
        local,
        mesh=mesh,
        in_specs=(
            P(None, "gx", "gz", "gy"),
            P("gx", "gz", "gy"),
            P("gx", "gz", "gy"),
            P(None, "gx", "gz", "gy"),
        ),
        out_specs=(P(None, "gx", "gz", "gy"), P("gx", "gz", "gy")),
        check_vma=False,
    )
```

```python
import jax
import jax.numpy as jnp
from jax import lax
from jax.experimental import pallas as pl
from jax.experimental.pallas import tpu as pltpu
from jax.sharding import PartitionSpec as P

LANES = 128
SLOT = 8
F32 = jnp.float32
relax_weight = 0.6
HELD = 429 * 2**17


def call(body, outs, args, scratch=(), cost=1, outside=0, copies=0):
    return pl.pallas_call(
        body,
        out_shape=[jax.ShapeDtypeStruct(shape, F32) for shape in outs],
        in_specs=[pl.BlockSpec(memory_space=pltpu.HBM)] * outside
        + [pl.BlockSpec(memory_space=pltpu.VMEM)] * (len(args) - outside),
        out_specs=[pl.BlockSpec(memory_space=pltpu.HBM)] * (outside > 0)
        + [pl.BlockSpec(memory_space=pltpu.VMEM)] * (len(outs) - (outside > 0)),
        scratch_shapes=[pltpu.VMEM(shape, F32) for shape in scratch]
        + [pltpu.SemaphoreType.DMA((copies,))] * (copies > 0),
        compiler_params=pltpu.CompilerParams(vmem_limit_bytes=HELD if outside else 40 * 2**20),
        cost_estimate=pl.CostEstimate(
            flops=cost * 10**6, bytes_accessed=cost * 10**6, transcendentals=0
        ),
    )(*args)


def swap(array, axis, which):
    count = lax.axis_size(axis)
    if axis != "gx" and which == 1:
        ys, zs = lax.axis_size("gy"), lax.axis_size("gz")
        pairs = []
        for y in range(ys):
            for z in range(zs):
                i = y if axis == "gy" else z
                j = i + 1 if i % 2 else i - 1
                if axis == "gy":
                    to = (j, z) if 0 <= j < count else (y, z ^ 1)
                else:
                    to = (y, j) if 0 <= j < count else (y ^ 1, z)
                pairs.append((y * zs + z, to[0] * zs + to[1]))
        return lax.ppermute(array, ("gy", "gz"), pairs)
    pairs = []
    for i in range(which, count, 2):
        j = (i + 1) % count
        pairs += [(i, j), (j, i)]
    return lax.ppermute(array, axis, pairs)


def place(axis):
    i = lax.axis_index(axis)
    last = lax.axis_size(axis) - 1
    return i, jnp.where(i > 0, 1, 0), jnp.where(i < last, 1, 0)


def iota(shape, dim):
    return lax.broadcasted_iota(jnp.int32, shape, dim)


def truth(flag, shape):
    return jnp.full(shape, flag, jnp.int32) > 0


def roll(x, shift, dim):
    if isinstance(shift, int):
        shift %= x.shape[dim]
        return x if shift == 0 else pltpu.roll(x, shift, dim)
    return pltpu.roll(x, lax.rem(shift + 2 * x.shape[dim], x.shape[dim]), dim)


def high_side(axis, message):
    return jnp.where(lax.axis_index(axis) % 2 == message, 1, 0)


def left_right(axis, a, b):
    odd = truth(lax.axis_index(axis) % 2, a.shape)
    return jnp.where(odd, a, b), jnp.where(odd, b, a)


def x_messages():
    return 1 if lax.axis_size("gx") == 2 else 2


def pair_edges(planes, fields, rows):
    lane = iota((rows, LANES), 1) // SLOT
    half = fields // 2
    out = []
    for j in range(half):
        total = jnp.zeros((rows, LANES), F32)
        for part in range(2):
            for q, x in enumerate(planes(j + part * half)):
                slot = q + part * (LANES // SLOT // 2)
                total = jnp.where(lane == slot, roll(x, slot * SLOT + 4, 1), total)
        out.append(total)
    return out


def merge_y(a, b):
    _, has_left, has_right = place("gy")
    left, right = left_right("gy", a, b)
    spot = iota(a.shape, 1) % SLOT
    kept = (spot < 4 * has_left) | (spot >= SLOT - 4 * has_right)
    first = jnp.where(spot < 4, left, roll(right, 4, 1))
    second = jnp.where(spot < 4, roll(left, -4, 1), right)
    return jnp.where(kept, first, 0.0), jnp.where(kept, second, 0.0)


def first_pack(v_in, p_in, e_in, f_in, x_main, y_a, y_b, z_a, z_b, v, p, e, f, arrived):
    nx, nz, _ = p.shape
    loads = [
        pltpu.make_async_copy(a, b, arrived.at[i])
        for i, (a, b) in enumerate(((v_in, v), (p_in, p), (e_in, e), (f_in, f)))
    ]
    for load in loads:
        load.start()
    sends = []
    for m in range(x_main.shape[0]):
        high = high_side("gx", m)
        n = 0
        for i in range(8):
            width = 3 if i < 5 else 2
            at = pl.ds(high * (nx - width), width)
            if i < 3:
                planes = v.at[i, at]
            elif i < 5:
                planes = (p, e)[i - 3].at[at]
            else:
                planes = f.at[i - 5, at]
            sends.append(
                pltpu.make_async_copy(
                    planes, x_main.at[m, pl.ds(n, width)], arrived.at[4 + 8 * m + i]
                )
            )
            n += width
    for load in loads:
        load.wait()
    for send in sends:
        send.start()

    def plane(i, q):
        return v[i, q] if i < 3 else p[q] if i == 3 else e[q] if i == 4 else f[i - 5, q]

    edges = pair_edges(lambda i: [plane(i, q) for q in range(nx)], 8, nz)
    for m, out in enumerate((y_a, y_b)):
        for j in range(2):
            out[j] = y_strip(edges[j], edges[j + 2], high_side("gy", m))

    def tile(i, q, top):
        at = pl.ds(nz - 8, 8) if top else pl.ds(0, 8)
        if i < 3:
            return v[i, q, at]
        return p[q, at] if i == 3 else e[q, at] if i == 4 else f[i - 5, q, at]

    for m, out in enumerate((z_a, z_b)):
        for j in range(4):
            for q in range(nx):
                low = tile(j, q, False), tile(j + 4, q, False)
                high = tile(j, q, True), tile(j + 4, q, True)
                out[j * nx + q] = z_strip(low, high, high_side("gz", m))
    for send in sends:
        send.wait()


def y_strip(first, second, toward_right):
    right = truth(toward_right, first.shape)
    spot = iota(first.shape, 1) % SLOT
    first = jnp.where(right, first, roll(first, -4, 1))
    second = jnp.where(right, roll(second, 4, 1), second)
    return jnp.where(spot < 4, first, second)


def z_strip(low, high, toward_right):
    row = iota((8, LANES), 0)
    right = truth(toward_right, (8, LANES))
    first = jnp.where(right, roll(high[0], 4, 0), low[0])
    second = jnp.where(right, high[1], roll(low[1], 4, 0))
    return jnp.where(row < 4, first, second)


def second_pack(z_first_a, z_first_b, y_a, y_b, halo, z_a, z_b):
    nz = y_a.shape[1]
    count = z_first_a.shape[0]
    both = [merge_y(y_a[j], y_b[j]) for j in range(2)]
    merged = [both[j % 2][j // 2] for j in range(4)]
    for j in range(4):
        halo[j] = merged[j]
    for m, (first, out) in enumerate(((z_first_a, z_a), (z_first_b, z_b))):
        for n in range(count):
            out[n] = first[n]
        for j in range(2):
            low = merged[j][:8], merged[j + 2][:8]
            high = merged[j][nz - 8 :], merged[j + 2][nz - 8 :]
            out[count + j] = z_strip(low, high, high_side("gz", m))


def z_tiles(a, b):
    _, has_left, has_right = place("gz")
    left, right = left_right("gz", a, b)
    row = iota(a.shape, 0)
    kept = (row < 4 * has_right) | (row >= 8 - 4 * has_left)
    first = jnp.where(row < 4, right, roll(left, 4, 0))
    second = jnp.where(row < 4, roll(right, 4, 0), left)
    return jnp.where(kept, first, 0.0), jnp.where(kept, second, 0.0)


def third_pack(z_a, z_b, halo, z_halo, halo_full, x_rim):
    nx = z_halo.shape[1]
    nz = halo.shape[1]
    for j in range(4):
        for q in range(nx):
            z_halo[j, q], z_halo[j + 4, q] = z_tiles(z_a[j * nx + q], z_b[j * nx + q])
    for j in range(4):
        halo_full[j, pl.ds(0, nz)] = halo[j]
    for j in range(2):
        first, second = z_tiles(z_a[4 * nx + j], z_b[4 * nx + j])
        halo_full[j, pl.ds(nz, 8)] = first
        halo_full[j + 2, pl.ds(nz, 8)] = second
    pack_rim(x_rim, z_halo, lambda j: halo_full[j], 8, (2,) * 5 + (1,) * 3, 3, 32)


def pack_rim(x_rim, z_halo, halo_pair, fields, widths, planes, stride):
    nx = z_halo.shape[1]
    half = fields // 2
    per_column = LANES // stride
    for m in range(x_rim.shape[0]):
        high = high_side("gx", m)
        n = 0
        for i in range(fields):
            for j in range(widths[i]):
                x_rim[m, n] = z_halo[i, high * (nx - widths[i]) + j]
                n += 1
        pairs = [halo_pair(j) for j in range(half)]
        rows = pairs[0].shape[0]
        column = iota((rows, LANES), 1) // stride
        first = high * (nx - planes) * SLOT
        for c in range(-(-fields // per_column)):
            total = jnp.zeros((rows, LANES), F32)
            for t in range(min(per_column, fields - c * per_column)):
                i = c * per_column + t
                at = t * stride - first - (i // half) * (LANES // 2)
                total = jnp.where(column == t, roll(pairs[i % half], at + LANES, 1), total)
            for r in range(rows // 8):
                x_rim[m, n] = total[8 * r : 8 * r + 8]
                n += 1


def main_shifts(x, halo, p):
    lane = iota(x.shape, 1)
    beside = halo
    rows = x.shape[0]
    return (
        roll(jnp.where(lane == 0, beside, x), LANES - 1, 1),
        roll(jnp.where(lane == LANES - 1, beside, x), 1, 1),
        roll(x, rows - 1, 0),
        roll(x, 1, 0),
    )


def halo_shifts(x, edge):
    spot = iota(x.shape, 1) % SLOT
    rows = x.shape[0]
    return (
        roll(x, LANES - SLOT, 1),
        roll(x, SLOT, 1),
        roll(jnp.where(spot == 4, edge, x), LANES - 1, 1),
        roll(jnp.where(spot == 3, edge, x), 1, 1),
        roll(x, rows - 1, 0),
        roll(x, 1, 0),
    )


def main_weights(e, halo_e, w, width):
    slots = e.shape[0]
    for p in range(2 - width, slots - 3 + width):
        w[0][p] = e[p] + e[p + 1]

    def body(p):
        x = e[p]
        total = w[0][p] + w[0][p - 1]
        for n, y in enumerate(main_shifts(x, roll(halo_e[...], LANES - SLOT * p - 4, 1), p)):
            total += x + y
            w[1 + n][p] = x + y
        w[5][p] = relax_weight / total

    over_planes(slots, width, body)


def halo_weights(e, edge_e, w):
    x = e[...]
    total = jnp.zeros_like(x)
    for n, y in enumerate(halo_shifts(x, edge_e[...])):
        total += x + y
        w[n] = x + y
    w[6] = relax_weight / total


def terms(k, up, down, yp, ym, zp, zm):
    return (up - down, zp - zm, yp - ym)[k]


def spread_halo(halo, beside, slots, width):
    def body(p):
        for k in range(4):
            beside[k, p] = roll(halo[k], LANES - SLOT * p - 4, 1)

    over_planes(slots, width, body)


class Beside:
    def __init__(self, ref, p):
        self.ref, self.p = ref, p

    def __getitem__(self, k):
        return self.ref[k, self.p]


def main_operator(src, halo, w, force, p, fields=(0, 1, 2)):
    halo = Beside(halo, p)
    wxp, wxm, wyp, wym, wzp, wzm = w[0][p], w[0][p - 1], w[1][p], w[2][p], w[3][p], w[4][p]
    x = src[3, p]
    around = main_shifts(x, halo[3], p)
    up, down = src[3, p + 1], src[3, p - 1]
    olds, sums, spread = [], [], 0.0
    for k in range(3):
        u = src[k, p]
        yp, ym, zp, zm = main_shifts(u, halo[k], p)
        xp, xm = src[k, p + 1], src[k, p - 1]
        total = force[k, p] - terms(k, up, down, *around)
        total += wxp * xp + wxm * xm
        total += wyp * yp + wym * ym
        total += wzp * zp + wzm * zm
        spread += terms(k, xp, xm, yp, ym, zp, zm)
        olds.append(u)
        sums.append(total)
    olds.append(x)
    return olds, sums, spread


def halo_operator(halo, edge, w, force):
    x = halo[3]
    px = halo_shifts(x, edge[3])
    olds, sums, spread = [], [], 0.0
    for k in range(3):
        u = halo[k]
        around = halo_shifts(u, edge[k])
        total = force[k] - terms(k, *px)
        for n in range(6):
            total += w[n] * around[n]
        spread += terms(k, *around)
        olds.append(u)
        sums.append(total)
    olds.append(x)
    return olds, sums, spread


def relaxed(olds, sums, spread, factor, e):
    new = [0.4 * olds[k] + factor * sums[k] for k in range(3)]
    return new + [olds[3] - 0.25 * e * spread]


def edges_of(plane, lo, hi):
    first = plane(lo)
    slot = iota(first.shape, 1) // SLOT
    total = jnp.zeros(first.shape, F32)
    for p in range(lo, hi):
        total = jnp.where(slot == p, roll(plane(p), p * SLOT + 4, 1), total)
    return total


def fill_edges(edge, src, fields, lo, hi):
    for k in range(fields):
        edge[k] = edges_of(lambda p: src[k, p], lo, hi)


def fine_masks(rows, slots):
    nz = rows - 8
    _, zl, zr = place("gz")
    _, yl, yr = place("gy")
    _, xl, xr = place("gx")
    r = iota((8, LANES), 0)
    tile = (r < 4 * zr) | (r >= 8 - 4 * zl)
    r = iota((rows, LANES), 0)
    lane = iota((rows, LANES), 1)
    spot, slot = lane % SLOT, lane // SLOT
    column = (r < nz + 4 * zr) | (r >= rows - 4 * zl)
    column &= (spot < 4 * yl) | (spot >= SLOT - 4 * yr)
    column &= (slot >= 3 - 3 * xl) & (slot < slots - 3 + 3 * xr)
    return tile, column


def fine_sweep(src, halo, edge, dst, halo_dst, edge_dst, w, hw, e, halo_e, force, halo_f, width, masks, beside):
    tile, column = masks
    nz = src.shape[2] - 8

    def body(p):
        new = relaxed(*main_operator(src, beside, w, force, p), w[5][p], e[p])
        for k in range(4):
            x = new[k]
            dst[k, p, pl.ds(0, nz)] = x[:nz]
            dst[k, p, pl.ds(nz, 8)] = jnp.where(tile, x[nz:], 0.0)

    spread_halo(halo, beside, src.shape[1], width)
    over_planes(src.shape[1], width, body)
    new = relaxed(*halo_operator(halo, edge, hw, halo_f), hw[6], halo_e[...])
    for k in range(4):
        halo_dst[k] = jnp.where(column, new[k], 0.0)
    if edge_dst is not None:
        fill_edges(edge_dst, dst, 4, 3 - width, dst.shape[1] - 3 + width)


def over_planes(slots, width, body):
    _, xl, xr = place("gx")
    for p in range(3 - width, slots - 3 + width):
        if p < 3:
            pl.when(xl > 0)(lambda p=p: body(p))
        elif p >= slots - 3:
            pl.when(xr > 0)(lambda p=p: body(p))
        else:
            body(p)


def own_slots(x, nx, part):
    lane = iota(x.shape, 1)
    x = roll(x, 3 * SLOT - part * (LANES // 2), 1)
    return jnp.where((lane >= 3 * SLOT) & (lane < (3 + nx) * SLOT), x, 0.0)


def x_side(m):
    right = high_side("gx", m)
    _, has_left, has_right = place("gx")
    return right, jnp.where(right > 0, has_right, has_left)


def rim_halo(x, t, stride, planes, right, valid, nx):
    base = right * (nx + 3) + (1 - right) * (3 - planes)
    lane = iota(x.shape, 1)
    x = roll(x, base * SLOT - t * stride + LANES, 1)
    kept = (lane >= base * SLOT) & (lane < (base + planes * valid) * SLOT)
    return jnp.where(kept, x, 0.0), kept


def viscosity_force(e_in, f_in, z_halo, halo_full, x_main, x_rim, e, halo_e, force, halo_f):
    nx, nz, _ = e_in.shape
    slots = nx + 6
    zero = jnp.zeros((nz + 8, LANES), F32)
    for p in list(range(3)) + list(range(nx + 3, slots)):
        e[p] = zero
        for k in range(3):
            force[k, p] = zero
    for q in range(nx):
        e[q + 3, pl.ds(0, nz)] = e_in[q]
        e[q + 3, pl.ds(nz, 8)] = z_halo[4, q]
        for k in range(3):
            force[k, q + 3, pl.ds(0, nz)] = 2.0 * f_in[k, q]
            force[k, q + 3, pl.ds(nz, 8)] = 2.0 * z_halo[5 + k, q]
    halo_e[...] = own_slots(halo_full[0], nx, 1)
    for k in range(3):
        halo_f[k] = 2.0 * own_slots(halo_full[k + 1], nx, 1)
    for m in range(x_main.shape[0]):
        right, valid = x_side(m)
        there = truth(valid, (nz, LANES))
        there8 = truth(valid, (8, LANES))
        for j in range(3):
            e[right * (nx + 3) + j, pl.ds(0, nz)] = jnp.where(there, x_main[m, 12 + j], 0.0)
        for j in range(2):
            at = right * (nx + 2) + 1 + j
            e[at, pl.ds(nz, 8)] = jnp.where(there8, x_rim[m, 8 + j], 0.0)
            for k in range(3):
                force[k, at, pl.ds(0, nz)] = jnp.where(there, 2.0 * x_main[m, 15 + 2 * k + j], 0.0)
        for k in range(3):
            at = right * (nx + 1) + 2
            force[k, at, pl.ds(nz, 8)] = jnp.where(there8, 2.0 * x_rim[m, 10 + k], 0.0)
        tiles = (nz + 8) // 8
        column = jnp.concatenate([x_rim[m, 13 + tiles + r] for r in range(tiles)], axis=0)
        x, kept = rim_halo(column, 0, 32, 3, right, valid, nx)
        halo_e[...] = jnp.where(kept, x, halo_e[...])
        for k in range(3):
            x, kept = rim_halo(column, 1 + k, 32, 3, right, valid, nx)
            halo_f[k] = jnp.where(kept, 2.0 * x, halo_f[k])


def first_fields(v, p_in, z_halo, halo_full, x_main, x_rim, u, other, halo):
    nx, nz, _ = p_in.shape
    slots = nx + 6
    zero = jnp.zeros((nz + 8, LANES), F32)
    for k in range(4):
        for p in list(range(3)) + list(range(nx + 3, slots)):
            u[k, p] = zero
            other[k, p] = zero
        for q in range(nx):
            u[k, q + 3, pl.ds(0, nz)] = v[k, q] if k < 3 else p_in[q]
            u[k, q + 3, pl.ds(nz, 8)] = z_halo[k, q]
        halo[k] = own_slots(halo_full[k], nx, 0)
    for m in range(x_main.shape[0]):
        right, valid = x_side(m)
        there = truth(valid, (nz, LANES))
        there8 = truth(valid, (8, LANES))
        tiles = (nz + 8) // 8
        column = jnp.concatenate([x_rim[m, 13 + r] for r in range(tiles)], axis=0)
        for k in range(4):
            for j in range(3):
                x = jnp.where(there, x_main[m, 3 * k + j], 0.0)
                u[k, right * (nx + 3) + j, pl.ds(0, nz)] = x
            for j in range(2):
                x = jnp.where(there8, x_rim[m, 2 * k + j], 0.0)
                u[k, right * (nx + 2) + 1 + j, pl.ds(nz, 8)] = x
            x, kept = rim_halo(column, k, 32, 3, right, valid, nx)
            halo[k] = jnp.where(kept, x, halo[k])


def pre_smooth(
    v, p_in, e_in, f_in, z_halo, halo_full, x_main, x_rim,
    fields, coarse, edges, x_fine,
    ua, ub, ha, hb, ca, cb, e, halo_e, edge_e, force, halo_f, w0, w1, w2, w3, w4, w5, hw, beside, summed,
):
    nx, nz, _ = p_in.shape
    slots = nx + 6
    w = (w0, w1, w2, w3, w4, w5)
    viscosity_force(e_in, f_in, z_halo, halo_full, x_main, x_rim, e, halo_e, force, halo_f)
    first_fields(v, p_in, z_halo, halo_full, x_main, x_rim, ua, ub, ha)
    masks = fine_masks(nz + 8, slots)
    fill_edges(ca, ua, 4, 0, slots)
    edge_e[...] = edges_of(lambda p: e[p], 0, slots)
    main_weights(e, halo_e, w, 2)
    halo_weights(halo_e, edge_e, hw)
    rest = (w, hw, e, halo_e, force, halo_f)
    fine_sweep(ua, ha, ca, ub, hb, cb, *rest, 2, masks, beside)
    fine_sweep(ub, hb, cb, ua, ha, ca, *rest, 1, masks, beside)
    for k in range(4):
        for q in range(nx):
            fields[k, q] = ua[k, q + 3, pl.ds(0, nz)]
    for m in range(x_fine.shape[0]):
        high = high_side("gx", m)
        for k in range(4):
            for j in range(2):
                x_fine[m, 2 * k + j] = ua[k, 3 + high * (nx - 2) + j, pl.ds(0, nz)]
    lane = iota((nz, LANES), 1)
    for j in range(2):
        first = roll(ca[j][:nz], -3 * SLOT, 1)
        second = roll(ca[j + 2][:nz], LANES // 2 - 3 * SLOT, 1)
        edges[j] = jnp.where(lane < LANES // 2, first, second)

    spread_halo(ha, beside, slots, 0)
    for q in range(nx // 2):
        totals = [0.0] * 5
        for j in range(2):
            p = 2 * q + 3 + j
            olds, sums, spread = main_operator(ua, beside, w, force, p)
            diagonal = w0[p] + w0[p - 1] + w1[p] + w2[p] + w3[p] + w4[p]
            for k in range(3):
                totals[k] += sums[k] - diagonal * olds[k]
            totals[3] += spread
            totals[4] += e[p]
        for k in range(5):
            summed[k, q] = totals[k][:nz]
    scale = (0.5, 0.5, 0.5, -1.0 / 32.0, 0.125)
    cz = nz // 2
    left = []
    for k in range(5):
        for r in range(nx // 4):
            halves = []
            for s in range(2):
                q = 2 * r + s
                even = summed[k, q, pl.ds(0, cz, stride=2)]
                halves.append((even + summed[k, q, pl.ds(1, cz, stride=2)]) * scale[k])
            left.append(jnp.concatenate(halves, axis=1))
    left = jnp.concatenate(left, axis=0)
    pick = iota((2 * LANES, LANES), 0) // 2 == iota((2 * LANES, LANES), 1)
    out = jnp.dot(
        left, pick.astype(F32), precision=lax.Precision.HIGHEST, preferred_element_type=F32
    )
    for k in range(5):
        for r in range(nx // 4):
            at = (k * (nx // 4) + r) * cz
            coarse[k, r] = out[at : at + cz]


def fourth_pack(own, other, fields, whole, z_a, z_b):
    nx, nz = fields.shape[1:3]
    pairs = whole.shape[1]
    cz = whole.shape[2]
    gx = lax.axis_index("gx")
    for k in range(5):
        for r in range(pairs):
            if other is None:
                whole[k, r] = own[k, r]
            else:
                mine = truth(jnp.where(gx == r // (pairs // 2), 1, 0), (cz, LANES))
                n = r % (pairs // 2)
                whole[k, r] = jnp.where(mine, own[k, n], other[k, n])
    row = iota((8, LANES), 0) // 2
    for m, out in enumerate((z_a, z_b)):
        right = high_side("gz", m)
        start = pl.multiple_of(right * (cz - 8), 8)
        for k in range(5):
            for r in range(pairs):
                out[k * pairs + r] = whole[k, r, pl.ds(start, 8)]
        toward = truth(right, (8, LANES))
        for q in range(nx):
            total = jnp.zeros((8, LANES), F32)
            for k in range(4):
                low = roll(fields[k, q, pl.ds(0, 8)], 2 * k, 0)
                high = roll(fields[k, q, pl.ds(nz - 8, 8)], 2 * k - 6, 0)
                total = jnp.where(row == k, jnp.where(toward, high, low), total)
            out[5 * pairs + q] = total


def fifth_pack(whole, z_a, z_b, edges, full, z_halo, y_a, y_b):
    pairs, cz = whole.shape[1:3]
    nx = z_halo.shape[1]
    nz = edges.shape[1]
    _, has_left, has_right = place("gz")
    to_left = truth(has_left, (8, LANES))
    to_right = truth(has_right, (8, LANES))
    for k in range(5):
        for r in range(pairs):
            n = k * pairs + r
            left, right = left_right("gz", z_a[n], z_b[n])
            full[k, r, pl.ds(0, cz)] = whole[k, r]
            full[k, r, pl.ds(cz, 8)] = jnp.where(to_right, right, 0.0)
            full[k, r, pl.ds(cz + 8, 8)] = jnp.where(to_left, left, 0.0)
    row = iota((8, LANES), 0)
    for q in range(nx):
        left, right = left_right("gz", z_a[5 * pairs + q], z_b[5 * pairs + q])
        for k in range(4):
            x = jnp.where(row < 2 * has_right, roll(right, -2 * k, 0), 0.0)
            z_halo[k, q] = jnp.where(row >= 8 - 2 * has_left, roll(left, 6 - 2 * k, 0), x)
    rows = cz + 16
    tiles = rows // 8
    slot = iota((rows, LANES), 1) // SLOT
    per = LANES // SLOT
    count = 5 * pairs * 2
    columns = -(-count // per)
    behind = pair_edges(lambda i: [z_halo[i, q] for q in range(nx)], 4, 8)
    for m, out in enumerate((y_a, y_b)):
        high = high_side("gy", m) * (LANES // 2 - SLOT)
        for c in range(columns):
            total = jnp.zeros((rows, LANES), F32)
            for t in range(min(per, count - c * per)):
                n = c * per + t
                k, r, s = n // (2 * pairs), n // 2 % pairs, n % 2
                at = SLOT * t - s * (LANES // 2) - high
                total = jnp.where(slot == t, roll(full[k, r], at + LANES, 1), total)
            for i in range(tiles):
                out[c * tiles + i] = total[8 * i : 8 * i + 8]
        n = columns * tiles
        toward = high_side("gy", m)
        for i in range(nz // 8):
            out[n] = y_strip(edges[0, pl.ds(8 * i, 8)], edges[1, pl.ds(8 * i, 8)], toward)
            n += 1
        out[n] = y_strip(behind[0], behind[1], toward)


def sixth_pack(y_a, y_b, z_halo, halo_full, x_rim):
    tiles = halo_full.shape[1] // 8
    first = y_a.shape[0] - tiles
    for i in range(tiles):
        for j, x in enumerate(merge_y(y_a[first + i], y_b[first + i])):
            halo_full[j, pl.ds(8 * i, 8)] = x
    pack_rim(x_rim, z_halo, lambda j: halo_full[j], 4, (1,) * 4, 1, SLOT)


def coarse_solve(full, y_a, y_b, main, halo, ca, cb, force, e, w0, w1, w2, w3, w4, w5, grown):
    pairs, rows = full.shape[1:3]
    planes = 2 * pairs
    own = main.shape[1] - 2
    tiles = rows // 8
    per = LANES // SLOT
    lane = iota((rows, LANES), 1)
    row = iota((rows, LANES), 0)
    _, zl, zr = place("gz")
    _, yl, yr = place("gy")
    half = LANES // 2
    inside = (row < rows - 16 + 8 * zr) | (row >= rows - 8 * zl)
    inside &= (lane < half + SLOT * yr) | (lane >= LANES - SLOT * yl)
    zero = jnp.zeros((rows, LANES), F32)
    w = (w0, w1, w2, w3, w4, w5)
    for k in range(4):
        for p in (0, planes + 1):
            ca[k, p] = zero
            cb[k, p] = zero
    e[0] = zero
    e[planes + 1] = zero
    for n in range(10 * pairs):
        k, r, s = n // (2 * pairs), n // 2 % pairs, n % 2
        c, t = n // per, n % per
        a = jnp.concatenate([y_a[c * tiles + i] for i in range(tiles)], axis=0)
        b = jnp.concatenate([y_b[c * tiles + i] for i in range(tiles)], axis=0)
        left, right = left_right("gy", a, b)
        x = roll(full[k, r], -s * half, 1)
        x = jnp.where(lane < half, x, roll(right, half - SLOT * t, 1))
        x = jnp.where(lane < LANES - SLOT, x, roll(left, LANES - SLOT - SLOT * t, 1))
        x = jnp.where(inside, x, 0.0)
        if k < 4:
            force[k, 2 * r + s] = x
        else:
            e[2 * r + s + 1] = x

    def shifts(x):
        return (
            roll(x, LANES - 1, 1),
            roll(x, 1, 1),
            roll(x, rows - 1, 0),
            roll(x, 1, 0),
        )

    for p in range(planes + 1):
        w0[p] = e[p] + e[p + 1]

    def start(p, carry):
        x = e[p]
        total = w0[p] + w0[p - 1]
        for n, y in enumerate(shifts(x)):
            total += x + y
            w[1 + n][p] = x + y
        factor = jnp.where(inside, relax_weight / total, 0.0)
        w5[p] = factor
        for k in range(3):
            ca[k, p] = factor * force[k, p - 1]
        ca[3, p] = x * force[3, p - 1]
        return carry

    lax.fori_loop(1, planes + 1, start, 0)

    def sweep(src, dst):
        def body(p, carry):
            wxp, wxm = w0[p], w0[p - 1]
            wyp, wym, wzp, wzm = w1[p], w2[p], w3[p], w4[p]
            x = src[3, p]
            around = shifts(x)
            up, down = src[3, p + 1], src[3, p - 1]
            spread = 0.0
            for k in range(3):
                u = src[k, p]
                yp, ym, zp, zm = shifts(u)
                xp, xm = src[k, p + 1], src[k, p - 1]
                total = force[k, p - 1] - 2.0 * terms(k, up, down, *around)
                total += wxp * xp + wxm * xm
                total += wyp * yp + wym * ym
                total += wzp * zp + wzm * zm
                spread += terms(k, xp, xm, yp, ym, zp, zm)
                dst[k, p] = jnp.where(inside, 0.4 * u + w5[p] * total, 0.0)
            dst[3, p] = jnp.where(inside, x + e[p] * (force[3, p - 1] - 0.125 * spread), 0.0)
            return carry

        lax.fori_loop(1, planes + 1, body, 0)

    sweep(ca, cb)
    sweep(cb, ca)
    sweep(ca, cb)

    cz = rows - 16
    spread_lanes = (iota((LANES, LANES), 1) // 2 == iota((LANES, LANES), 0)).astype(F32)
    lane = iota((LANES, LANES), 1)
    cell = iota((LANES, LANES), 0)
    spot = lane % SLOT
    wanted = jnp.where(spot < 4, LANES - 2, half - 2) + spot // 2
    column = jnp.zeros((4 * rows, LANES), F32)
    first = lax.axis_index("gx") * own

    def grow(ref, index, x):
        ref[index + (pl.ds(0, cz, stride=2),)] = x[:cz]
        ref[index + (pl.ds(1, cz, stride=2),)] = x[:cz]
        edge = jnp.concatenate([x[cz : cz + 8], x[rows - 8 :]], axis=0)
        grown[pl.ds(0, 16, stride=2)] = edge
        grown[pl.ds(1, 16, stride=2)] = edge
        r = iota((8, LANES), 0)
        tail = jnp.where(r < 4, grown[pl.ds(0, 8)], grown[pl.ds(24, 8)])
        ref[index + (pl.ds(2 * cz, 8),)] = tail

    for i in range(own + 2):
        x = jnp.concatenate([cb[k, first + i] for k in range(4)], axis=0)
        wide = jnp.dot(
            x, spread_lanes, precision=lax.Precision.HIGHEST, preferred_element_type=F32
        )
        for k in range(4):
            grow(main, (k, i), wide[k * rows : (k + 1) * rows])
        here = (lane // SLOT + 1) // 2 - 1 == i
        chosen = (here & (cell == wanted)).astype(F32)
        column += jnp.dot(
            x, chosen, precision=lax.Precision.HIGHEST, preferred_element_type=F32
        )
    for k in range(4):
        grow(halo, (k,), column[k * rows : (k + 1) * rows])


def post_smooth(
    e_in, f_in, z_first, halo_first, x_main, x_first, fields, z_halo, halo_full, x_fine, x_rim,
    main, column, v_out, p_out,
    ua, ub, ha, hb, ca, cb, e, halo_e, edge_e, force, halo_f, w0, w1, w2, w3, w4, w5, hw, beside,
):
    nx, nz, _ = e_in.shape
    slots = nx + 6
    w = (w0, w1, w2, w3, w4, w5)
    viscosity_force(e_in, f_in, z_first, halo_first, x_main, x_first, e, halo_e, force, halo_f)
    zero = jnp.zeros((nz + 8, LANES), F32)
    for k in range(4):
        for p in (1, 2, nx + 3, nx + 4):
            ua[k, p] = zero
            ub[k, p] = zero
        for q in range(nx):
            i = q // 2 + 1
            ua[k, q + 3, pl.ds(0, nz)] = fields[k, q] + main[k, i, pl.ds(0, nz)]
            ua[k, q + 3, pl.ds(nz, 8)] = z_halo[k, q] + main[k, i, pl.ds(nz, 8)]
        ha[k] = own_slots(halo_full[k % 2], nx, k // 2)
    for m in range(x_fine.shape[0]):
        right, valid = x_side(m)
        there = truth(valid, (nz, LANES))
        there8 = truth(valid, (8, LANES))
        tiles = (nz + 8) // 8
        side = jnp.concatenate([x_rim[m, 4 + r] for r in range(tiles)], axis=0)
        i = right * (nx // 2 + 1)
        for k in range(4):
            for j in range(2):
                at = 1 + right * (nx + 2) + j
                x = x_fine[m, 2 * k + j] + main[k, i, pl.ds(0, nz)]
                ua[k, at, pl.ds(0, nz)] = jnp.where(there, x, 0.0)
            x = x_rim[m, k] + main[k, i, pl.ds(nz, 8)]
            ua[k, 2 + right * (nx + 1), pl.ds(nz, 8)] = jnp.where(there8, x, 0.0)
            x, kept = rim_halo(side, k, SLOT, 1, right, valid, nx)
            ha[k] = jnp.where(kept, x, ha[k])
    masks = fine_masks(nz + 8, slots)
    for k in range(4):
        ha[k] = jnp.where(masks[1], ha[k] + column[k], 0.0)
    fill_edges(ca, ua, 4, 1, slots - 1)
    edge_e[...] = edges_of(lambda p: e[p], 1, slots - 1)
    main_weights(e, halo_e, w, 1)
    halo_weights(halo_e, edge_e, hw)
    rest = (w, hw, e, halo_e, force, halo_f)
    fine_sweep(ua, ha, ca, ub, hb, None, *rest, 1, masks, beside)

    spread_halo(hb, beside, slots, 0)

    def last(p):
        new = relaxed(*main_operator(ub, beside, w, force, p), w5[p], e[p])
        for k in range(3):
            v_out[k, p - 3] = new[k][:nz]
        p_out[p - 3] = new[3][:nz]

    over_planes(slots, 0, last)


def local(velocity, pressure, viscosity, body_force):
    nx, nz, ny = pressure.shape
    if ny != LANES or nx * SLOT * 2 != LANES or nz % 16:
        raise ValueError("unsupported block")
    sides = x_messages()
    rows, slots = nz + 8, nx + 6
    inputs = [velocity, pressure, viscosity, body_force]
    block = (nz, LANES)

    z_shape = (4 * nx, 8, LANES)
    x_main, y_a, y_b, z_a, z_b = call(
        first_pack,
        [(sides, 21) + block, (2,) + block, (2,) + block, z_shape, z_shape],
        inputs,
        [a.shape for a in inputs],
        outside=4,
        copies=4 + 8 * sides,
    )
    x_main = swap_x(x_main)
    y_a, y_b = swap(y_a, "gy", 0), swap(y_b, "gy", 1)
    z_shape = (4 * nx + 2, 8, LANES)
    halo, z_a, z_b = call(
        second_pack, [(4,) + block, z_shape, z_shape], [z_a, z_b, y_a, y_b]
    )
    z_a, z_b = swap(z_a, "gz", 0), swap(z_b, "gz", 1)
    tiles = rows // 8
    z_first, halo_first, x_first = call(
        third_pack,
        [(8, nx, 8, LANES), (4, rows, LANES), (sides, 13 + 2 * tiles, 8, LANES)],
        [z_a, z_b, halo],
    )
    x_first = swap_x(x_first)

    state = [(4, slots, rows, LANES)] * 2 + [(4, rows, LANES)] * 4
    state += [(slots, rows, LANES), (rows, LANES), (rows, LANES)]
    state += [(3, slots, rows, LANES), (3, rows, LANES)]
    state += [(slots, rows, LANES)] * 6 + [(7, rows, LANES), (4, slots, rows, LANES)]
    fields, own, edges, x_fine = call(
        pre_smooth,
        [(4, nx) + block, (5, nx // 4, nz // 2, LANES), (2,) + block, (sides, 8) + block],
        inputs + [z_first, halo_first, x_main, x_first],
        state + [(5, nx // 2, nz, LANES)],
        cost=8,
    )
    if lax.axis_size("gx") == 2:
        parts = [own, swap(own, "gx", 0)]
        gather = fourth_pack
    else:
        parts = [lax.all_gather(own, "gx", axis=1, tiled=True)]

        def gather(a, *refs):
            fourth_pack(a, None, *refs)

    x_fine = swap_x(x_fine)
    pairs = lax.axis_size("gx") * (nx // 4)
    z_shape = (5 * pairs + nx, 8, LANES)
    whole, z_a, z_b = call(
        gather, [(5, pairs, nz // 2, LANES), z_shape, z_shape], parts + [fields]
    )
    z_a, z_b = swap(z_a, "gz", 0), swap(z_b, "gz", 1)
    deep = nz // 2 + 16
    y_shape = (-(-10 * pairs * SLOT // LANES) * (deep // 8) + tiles, 8, LANES)
    full, z_halo, y_a, y_b = call(
        fifth_pack,
        [(5, pairs, deep, LANES), (4, nx, 8, LANES), y_shape, y_shape],
        [whole, z_a, z_b, edges],
    )
    y_a, y_b = swap(y_a, "gy", 0), swap(y_b, "gy", 1)
    halo_full, x_rim = call(
        sixth_pack,
        [(2, rows, LANES), (sides, 4 + tiles, 8, LANES)],
        [y_a, y_b, z_halo],
    )
    x_rim = swap_x(x_rim)
    planes = 2 * pairs
    deep_plane = (deep, LANES)
    main, column = call(
        coarse_solve,
        [(4, nx // 2 + 2, rows, LANES), (4, rows, LANES)],
        [full, y_a, y_b],
        [(4, planes + 2) + deep_plane] * 2
        + [(4, planes) + deep_plane]
        + [(planes + 2,) + deep_plane] * 7
        + [(32, LANES)],
        cost=4,
    )
    v_out, p_out = call(
        post_smooth,
        [(3, nx) + block, (nx,) + block],
        inputs[2:] + [z_first, halo_first, x_main, x_first]
        + [fields, z_halo, halo_full, x_fine, x_rim, main, column],
        state,
        cost=8,
    )
    return v_out, p_out


def swap_x(array):
    if array.shape[0] == 1:
        return swap(array, "gx", 0)
    parts = [swap(array[m], "gx", m) for m in range(2)]
    return jnp.stack(parts)


def solution(mesh):
    return jax.shard_map(
        local,
        mesh=mesh,
        in_specs=(
            P(None, "gx", "gz", "gy"),
            P("gx", "gz", "gy"),
            P("gx", "gz", "gy"),
            P(None, "gx", "gz", "gy"),
        ),
        out_specs=(P(None, "gx", "gz", "gy"), P("gx", "gz", "gy")),
        check_vma=False,
    )
```

```python
import jax
import jax.numpy as jnp
from jax import lax
from jax.experimental import pallas as pl
from jax.experimental.pallas import tpu as pltpu
from jax.sharding import PartitionSpec as P

LANES = 128
SLOT = 8
F32 = jnp.float32
relax_weight = 0.6
HELD = 429 * 2**17
Z_PLACES = (
    ((0, 0, 3), (1, 3, 3), (5, 6, 2)),
    ((2, 0, 3), (3, 3, 3), (6, 6, 2)),
    ((4, 0, 3), (7, 3, 2)),
)


def call(body, outs, args, scratch=(), cost=1, outside=0, copies=0):
    return pl.pallas_call(
        body,
        out_shape=[jax.ShapeDtypeStruct(shape, F32) for shape in outs],
        in_specs=[pl.BlockSpec(memory_space=pltpu.HBM)] * outside
        + [pl.BlockSpec(memory_space=pltpu.VMEM)] * (len(args) - outside),
        out_specs=[pl.BlockSpec(memory_space=pltpu.HBM)] * (outside > 0)
        + [pl.BlockSpec(memory_space=pltpu.VMEM)] * (len(outs) - (outside > 0)),
        scratch_shapes=[pltpu.VMEM(shape, F32) for shape in scratch]
        + [pltpu.SemaphoreType.DMA((copies,))] * (copies > 0),
        compiler_params=pltpu.CompilerParams(vmem_limit_bytes=HELD if outside else 40 * 2**20),
        cost_estimate=pl.CostEstimate(
            flops=cost * 10**6, bytes_accessed=cost * 10**6, transcendentals=0
        ),
    )(*args)


def swap(array, axis, which):
    count = lax.axis_size(axis)
    if axis != "gx" and which == 1:
        ys, zs = lax.axis_size("gy"), lax.axis_size("gz")
        pairs = []
        for y in range(ys):
            for z in range(zs):
                i = y if axis == "gy" else z
                j = i + 1 if i % 2 else i - 1
                if axis == "gy":
                    to = (j, z) if 0 <= j < count else (y, z ^ 1)
                else:
                    to = (y, j) if 0 <= j < count else (y ^ 1, z)
                pairs.append((y * zs + z, to[0] * zs + to[1]))
        return lax.ppermute(array, ("gy", "gz"), pairs)
    pairs = []
    for i in range(which, count, 2):
        j = (i + 1) % count
        pairs += [(i, j), (j, i)]
    return lax.ppermute(array, axis, pairs)


def place(axis):
    i = lax.axis_index(axis)
    last = lax.axis_size(axis) - 1
    return i, jnp.where(i > 0, 1, 0), jnp.where(i < last, 1, 0)


def iota(shape, dim):
    return lax.broadcasted_iota(jnp.int32, shape, dim)


def truth(flag, shape):
    return jnp.full(shape, flag, jnp.int32) > 0


def roll(x, shift, dim):
    if isinstance(shift, int):
        shift %= x.shape[dim]
        return x if shift == 0 else pltpu.roll(x, shift, dim)
    return pltpu.roll(x, lax.rem(shift + 2 * x.shape[dim], x.shape[dim]), dim)


def high_side(axis, message):
    return jnp.where(lax.axis_index(axis) % 2 == message, 1, 0)


def left_right(axis, a, b):
    odd = truth(lax.axis_index(axis) % 2, a.shape)
    return jnp.where(odd, a, b), jnp.where(odd, b, a)


def x_messages():
    return 1 if lax.axis_size("gx") == 2 else 2


def pair_edges(planes, fields, rows):
    lane = iota((rows, LANES), 1) // SLOT
    half = fields // 2
    out = []
    for j in range(half):
        total = jnp.zeros((rows, LANES), F32)
        for part in range(2):
            for q, x in enumerate(planes(j + part * half)):
                slot = q + part * (LANES // SLOT // 2)
                total = jnp.where(lane == slot, roll(x, slot * SLOT + 4, 1), total)
        out.append(total)
    return out


def merge_y(a, b):
    _, has_left, has_right = place("gy")
    left, right = left_right("gy", a, b)
    spot = iota(a.shape, 1) % SLOT
    kept = (spot < 4 * has_left) | (spot >= SLOT - 4 * has_right)
    first = jnp.where(spot < 4, left, roll(right, 4, 1))
    second = jnp.where(spot < 4, roll(left, -4, 1), right)
    return jnp.where(kept, first, 0.0), jnp.where(kept, second, 0.0)


def first_pack(v_in, p_in, e_in, f_in, x_main, y_a, y_b, z_a, z_b, v, p, e, f, arrived):
    nx, nz, _ = p.shape
    loads = [
        pltpu.make_async_copy(a, b, arrived.at[i])
        for i, (a, b) in enumerate(((v_in, v), (p_in, p), (e_in, e), (f_in, f)))
    ]
    for load in loads:
        load.start()
    sends = []
    for m in range(x_main.shape[0]):
        high = high_side("gx", m)
        n = 0
        for i in range(8):
            width = 3 if i < 5 else 2
            at = pl.ds(high * (nx - width), width)
            if i < 3:
                planes = v.at[i, at]
            elif i < 5:
                planes = (p, e)[i - 3].at[at]
            else:
                planes = f.at[i - 5, at]
            sends.append(
                pltpu.make_async_copy(
                    planes, x_main.at[m, pl.ds(n, width)], arrived.at[4 + 8 * m + i]
                )
            )
            n += width
    for load in loads:
        load.wait()
    for send in sends:
        send.start()

    def plane(i, q):
        return v[i, q] if i < 3 else p[q] if i == 3 else e[q] if i == 4 else f[i - 5, q]

    edges = pair_edges(lambda i: [plane(i, q) for q in range(nx)], 8, nz)
    for m, out in enumerate((y_a, y_b)):
        for j in range(2):
            out[j] = y_strip(edges[j], edges[j + 2], high_side("gy", m))

    def tile(i, q, top):
        at = pl.ds(nz - 8, 8) if top else pl.ds(0, 8)
        if i < 3:
            return v[i, q, at]
        return p[q, at] if i == 3 else e[q, at] if i == 4 else f[i - 5, q, at]

    for q in range(nx):
        for n, fields in enumerate(Z_PLACES):
            for m, out in enumerate((z_a, z_b)):
                out[3 * q + n] = z_strip(
                    [(tile(i, q, False), tile(i, q, True), at, rows) for i, at, rows in fields],
                    high_side("gz", m),
                )
    for send in sends:
        send.wait()


def strip(first, second, toward_right, width):
    right = truth(toward_right, first.shape)
    spot = iota(first.shape, 1) % (2 * width)
    first = jnp.where(right, first, roll(first, -width, 1))
    second = jnp.where(right, roll(second, width, 1), second)
    return jnp.where(spot < width, first, second)


def y_strip(first, second, toward_right):
    return strip(first, second, toward_right, SLOT // 2)


def z_strip(parts, toward_right):
    right = truth(toward_right, (8, LANES))
    return rows_of(
        [
            (jnp.where(right, roll(high, at + rows, 0), roll(low, at, 0)), 0, at, rows)
            for low, high, at, rows in parts
        ]
    )


def z_tail(halo, first, out, message):
    nz = halo.shape[1]
    row = iota((8, LANES), 0)
    for n in range(first.shape[0]):
        out[n] = first[n]
    for j in range(4):
        tiles = halo[j, pl.ds(0, 8)], halo[j, pl.ds(nz - 8, 8)]
        x = z_strip([tiles + (5, 3)], high_side("gz", message))
        out[3 * j + 2] = jnp.where(row < 5, first[3 * j + 2], x)


def second_pack(z_first, y_a, y_b, halo, z_b):
    for j in range(2):
        halo[j], halo[j + 2] = merge_y(y_a[j], y_b[j])
    z_tail(halo, z_first, z_b, 1)


def second_pack_near(z_first, halo, z_a):
    z_tail(halo, z_first, z_a, 0)


def z_tile(a, b, at, rows):
    _, has_left, has_right = place("gz")
    left, right = left_right("gz", a, b)
    row = iota(a.shape, 0)
    x = jnp.where(row < rows * has_right, roll(right, -at, 0), 0.0)
    return jnp.where(row >= 8 - rows * has_left, roll(left, 8 - at - rows, 0), x)


def third_pack(z_a, z_b, halo, z_halo, halo_full, x_rim):
    nx = z_halo.shape[1]
    nz = halo.shape[1]
    for q in range(nx):
        for n, fields in enumerate(Z_PLACES):
            for i, at, rows in fields:
                z_halo[i, q] = z_tile(z_a[3 * q + n], z_b[3 * q + n], at, rows)
    for j in range(4):
        halo_full[j, pl.ds(0, nz)] = halo[j]
        halo_full[j, pl.ds(nz, 8)] = z_tile(z_a[3 * j + 2], z_b[3 * j + 2], 5, 3)

    def tiles(plane):
        out = [
            rows_of([(z_halo[i, plane(1)], 0, 6, 4), (z_halo[i, plane(2)], 3, 2, 2)])
            for i in range(5)
        ]
        force = zip((0, 3, 5), (7, 2, 4))
        out.append(
            rows_of([(z_halo[5 + k, plane(1)], at, row, 2) for k, (at, row) in enumerate(force)])
        )
        return out

    pack_rim(x_rim, tiles, lambda j: halo_full[j], 8, 2, nx)


def rows_of(parts):
    row = iota((8, LANES), 0)
    total = jnp.zeros((8, LANES), F32)
    for x, shift, first, count in parts:
        total = jnp.where((row - first) % 8 < count, roll(x, shift, 0), total)
    return total


def pack_rim(x_rim, tiles, halo_pair, fields, planes, nx):
    half = fields // 2
    stride = LANES // 8 if fields == 8 else SLOT
    for m in range(x_rim.shape[0]):
        high = high_side("gx", m)
        done = tiles(lambda d, high=high: high * (nx - 2 * d + 1) + d - 1)
        for n, x in enumerate(done):
            x_rim[m, n] = x
        pairs = [halo_pair(j) for j in range(half)]
        rows = pairs[0].shape[0]
        column = iota((rows, LANES), 1) // stride
        first = high * (nx - planes) * SLOT
        total = jnp.zeros((rows, LANES), F32)
        for i in range(fields):
            at = i * stride - first - (i // half) * (LANES // 2)
            total = jnp.where(column == i, roll(pairs[i % half], at + LANES, 1), total)
        for r in range(rows // 8):
            x_rim[m, len(done) + r] = total[8 * r : 8 * r + 8]


def main_shifts(x, beside, kept):
    rows = x.shape[0]
    y, beside = x[:kept], beside[:kept]
    lane = iota(y.shape, 1)
    return (
        roll(jnp.where(lane == 0, beside, y), LANES - 1, 1),
        roll(jnp.where(lane == LANES - 1, beside, y), 1, 1),
        roll(x, rows - 1, 0)[:kept],
        roll(x, 1, 0)[:kept],
    )


def halo_shifts(x, edge):
    spot = iota(x.shape, 1) % SLOT
    rows = x.shape[0]
    return (
        roll(x, LANES - SLOT, 1),
        roll(x, SLOT, 1),
        roll(jnp.where(spot == 4, edge, x), LANES - 1, 1),
        roll(jnp.where(spot == 3, edge, x), 1, 1),
        roll(x, rows - 1, 0),
        roll(x, 1, 0),
    )


def main_weights(e, halo_e, w, width):
    slots = e.shape[0]
    for p in range(2 - width, slots - 3 + width):
        w[0][p] = e[p] + e[p + 1]

    def body(p):
        x = e[p]
        total = w[0][p] + w[0][p - 1]
        for n, y in enumerate(main_shifts(x, roll(halo_e[...], LANES - SLOT * p - 4, 1), x.shape[0])):
            total += x + y
            w[1 + n][p] = x + y
        w[5][p] = relax_weight / total

    over_planes(slots, width, body)


def halo_weights(e, edge_e, w):
    x = e[...]
    total = jnp.zeros_like(x)
    for n, y in enumerate(halo_shifts(x, edge_e[...])):
        total += x + y
        w[n] = x + y
    w[6] = relax_weight / total


def terms(k, up, down, yp, ym, zp, zm):
    return (up - down, zp - zm, yp - ym)[k]


def spread_halo(halo, beside, slots, width):
    kept = beside.shape[2] - (0 if width else 8)

    def body(p):
        for k in range(4):
            beside[k, p, pl.ds(0, kept)] = roll(halo[k][:kept], LANES - SLOT * p - 4, 1)

    over_planes(slots, width, body)


def main_operator(src, beside, w, force, p, kept):
    def at(ref, *index):
        return ref[index + (pl.ds(0, kept),)]

    wxp, wxm, wyp, wym, wzp, wzm = (
        at(ref, q) for ref, q in zip((w[0],) + w[:5], (p, p - 1, p, p, p, p))
    )
    around = main_shifts(src[3, p], at(beside, 3, p), kept)
    up, down = at(src, 3, p + 1), at(src, 3, p - 1)
    olds, sums, spread = [], [], 0.0
    for k in range(3):
        yp, ym, zp, zm = main_shifts(src[k, p], at(beside, k, p), kept)
        xp, xm = at(src, k, p + 1), at(src, k, p - 1)
        total = at(force, k, p) - terms(k, up, down, *around)
        total += wxp * xp + wxm * xm
        total += wyp * yp + wym * ym
        total += wzp * zp + wzm * zm
        spread += terms(k, xp, xm, yp, ym, zp, zm)
        olds.append(at(src, k, p))
        sums.append(total)
    olds.append(at(src, 3, p))
    return olds, sums, spread


def halo_operator(halo, edge, w, force):
    x = halo[3]
    px = halo_shifts(x, edge[3])
    olds, sums, spread = [], [], 0.0
    for k in range(3):
        u = halo[k]
        around = halo_shifts(u, edge[k])
        total = force[k] - terms(k, *px)
        for n in range(6):
            total += w[n] * around[n]
        spread += terms(k, *around)
        olds.append(u)
        sums.append(total)
    olds.append(x)
    return olds, sums, spread


def relaxed(olds, sums, spread, factor, e):
    new = [0.4 * olds[k] + factor * sums[k] for k in range(3)]
    return new + [olds[3] - 0.25 * e * spread]


def edges_of(plane, lo, hi):
    first = plane(lo)
    slot = iota(first.shape, 1) // SLOT
    total = jnp.zeros(first.shape, F32)
    for p in range(lo, hi):
        total = jnp.where(slot == p, roll(plane(p), p * SLOT + 4, 1), total)
    return total


def fill_edges(edge, src, fields, lo, hi):
    for k in range(fields):
        edge[k] = edges_of(lambda p: src[k, p], lo, hi)


def fine_masks(rows, slots):
    nz = rows - 8
    _, zl, zr = place("gz")
    _, yl, yr = place("gy")
    _, xl, xr = place("gx")
    r = iota((8, LANES), 0)
    tile = (r < 4 * zr) | (r >= 8 - 4 * zl)
    r = iota((rows, LANES), 0)
    lane = iota((rows, LANES), 1)
    spot, slot = lane % SLOT, lane // SLOT
    column = (r < nz + 4 * zr) | (r >= rows - 4 * zl)
    column &= (spot < 4 * yl) | (spot >= SLOT - 4 * yr)
    column &= (slot >= 3 - 3 * xl) & (slot < slots - 3 + 3 * xr)
    return tile, column


def fine_sweep(src, halo, edge, dst, halo_dst, edge_dst, w, hw, e, halo_e, force, halo_f, width, masks, beside):
    tile, column = masks
    nz = src.shape[2] - 8

    def body(p):
        new = relaxed(*main_operator(src, beside, w, force, p, nz + 8), w[5][p], e[p])
        for k in range(4):
            x = new[k]
            dst[k, p, pl.ds(0, nz)] = x[:nz]
            dst[k, p, pl.ds(nz, 8)] = jnp.where(tile, x[nz:], 0.0)

    spread_halo(halo, beside, src.shape[1], width)
    over_planes(src.shape[1], width, body)
    new = relaxed(*halo_operator(halo, edge, hw, halo_f), hw[6], halo_e[...])
    for k in range(4):
        halo_dst[k] = jnp.where(column, new[k], 0.0)
    if edge_dst is not None:
        fill_edges(edge_dst, dst, 4, 3 - width, dst.shape[1] - 3 + width)


def over_planes(slots, width, body):
    _, xl, xr = place("gx")
    for p in range(3 - width, slots - 3 + width):
        if p < 3:
            pl.when(xl > 0)(lambda p=p: body(p))
        elif p >= slots - 3:
            pl.when(xr > 0)(lambda p=p: body(p))
        else:
            body(p)


def own_slots(x, nx, part):
    lane = iota(x.shape, 1)
    x = roll(x, 3 * SLOT - part * (LANES // 2), 1)
    return jnp.where((lane >= 3 * SLOT) & (lane < (3 + nx) * SLOT), x, 0.0)


def x_side(m):
    right = high_side("gx", m)
    _, has_left, has_right = place("gx")
    return right, jnp.where(right > 0, has_right, has_left)


def rim_halo(x, t, stride, planes, right, valid, nx):
    base = right * (nx + 3) + (1 - right) * (3 - planes)
    lane = iota(x.shape, 1)
    x = roll(x, base * SLOT - t * stride + LANES, 1)
    kept = (lane >= base * SLOT) & (lane < (base + planes * valid) * SLOT)
    return jnp.where(kept, x, 0.0), kept


def viscosity_force(e_in, f_in, z_halo, halo_full, x_main, x_rim, e, halo_e, force, halo_f):
    nx, nz, _ = e_in.shape
    slots = nx + 6
    zero = jnp.zeros((nz + 8, LANES), F32)
    for p in list(range(3)) + list(range(nx + 3, slots)):
        e[p] = zero
        for k in range(3):
            force[k, p] = zero
    for q in range(nx):
        e[q + 3, pl.ds(0, nz)] = e_in[q]
        e[q + 3, pl.ds(nz, 8)] = z_halo[4, q]
        for k in range(3):
            force[k, q + 3, pl.ds(0, nz)] = 2.0 * f_in[k, q]
            force[k, q + 3, pl.ds(nz, 8)] = 2.0 * z_halo[5 + k, q]
    halo_e[...] = own_slots(halo_full[0], nx, 1)
    for k in range(3):
        halo_f[k] = 2.0 * own_slots(halo_full[k + 1], nx, 1)
    for m in range(x_main.shape[0]):
        right, valid = x_side(m)
        there = truth(valid, (nz, LANES))
        there8 = truth(valid, (8, LANES))
        for j in range(3):
            e[right * (nx + 3) + j, pl.ds(0, nz)] = jnp.where(there, x_main[m, 12 + j], 0.0)
        for j in range(2):
            at = right * (nx + 2) + 1 + j
            for k in range(3):
                force[k, at, pl.ds(0, nz)] = jnp.where(there, 2.0 * x_main[m, 15 + 2 * k + j], 0.0)
        near = right * (nx + 1) + 2
        x = jnp.where(there8, x_rim[m, 4], 0.0)
        e[near, pl.ds(nz, 8)] = x
        e[near + 2 * right - 1, pl.ds(nz, 8)] = roll(x, -3, 0)
        x = jnp.where(there8, 2.0 * x_rim[m, 5], 0.0)
        for k, at in enumerate((0, 3, 5)):
            force[k, near, pl.ds(nz, 8)] = roll(x, -at, 0)
        tiles = (nz + 8) // 8
        column = jnp.concatenate([x_rim[m, 6 + r] for r in range(tiles)], axis=0)
        x, kept = rim_halo(column, 4, LANES // 8, 2, right, valid, nx)
        halo_e[...] = jnp.where(kept, x, halo_e[...])
        for k in range(3):
            x, kept = rim_halo(column, 5 + k, LANES // 8, 2, right, valid, nx)
            halo_f[k] = jnp.where(kept, 2.0 * x, halo_f[k])


def first_fields(v, p_in, z_halo, halo_full, x_main, x_rim, u, other, halo):
    nx, nz, _ = p_in.shape
    slots = nx + 6
    zero = jnp.zeros((nz + 8, LANES), F32)
    for k in range(4):
        for p in list(range(3)) + list(range(nx + 3, slots)):
            u[k, p] = zero
            other[k, p] = zero
        for q in range(nx):
            u[k, q + 3, pl.ds(0, nz)] = v[k, q] if k < 3 else p_in[q]
            u[k, q + 3, pl.ds(nz, 8)] = z_halo[k, q]
        halo[k] = own_slots(halo_full[k], nx, 0)
    for m in range(x_main.shape[0]):
        right, valid = x_side(m)
        there = truth(valid, (nz, LANES))
        there8 = truth(valid, (8, LANES))
        tiles = (nz + 8) // 8
        column = jnp.concatenate([x_rim[m, 6 + r] for r in range(tiles)], axis=0)
        near = right * (nx + 1) + 2
        for k in range(4):
            for j in range(3):
                x = jnp.where(there, x_main[m, 3 * k + j], 0.0)
                u[k, right * (nx + 3) + j, pl.ds(0, nz)] = x
            x = jnp.where(there8, x_rim[m, k], 0.0)
            u[k, near, pl.ds(nz, 8)] = x
            u[k, near + 2 * right - 1, pl.ds(nz, 8)] = roll(x, -3, 0)
            x, kept = rim_halo(column, k, LANES // 8, 2, right, valid, nx)
            halo[k] = jnp.where(kept, x, halo[k])


def pre_smooth(
    v, p_in, e_in, f_in, z_halo, halo_full, x_main, x_rim,
    fields, coarse, edges, x_fine, e, halo_e, force, halo_f, w0, w1, w2, w3, w4, w5, hw,
    ua, ub, ha, hb, ca, cb, edge_e, beside, summed,
):
    nx, nz, _ = p_in.shape
    slots = nx + 6
    w = (w0, w1, w2, w3, w4, w5)
    viscosity_force(e_in, f_in, z_halo, halo_full, x_main, x_rim, e, halo_e, force, halo_f)
    first_fields(v, p_in, z_halo, halo_full, x_main, x_rim, ua, ub, ha)
    masks = fine_masks(nz + 8, slots)
    fill_edges(ca, ua, 4, 0, slots)
    edge_e[...] = edges_of(lambda p: e[p], 0, slots)
    main_weights(e, halo_e, w, 2)
    halo_weights(halo_e, edge_e, hw)
    rest = (w, hw, e, halo_e, force, halo_f)
    fine_sweep(ua, ha, ca, ub, hb, cb, *rest, 2, masks, beside)
    fine_sweep(ub, hb, cb, ua, ha, ca, *rest, 1, masks, beside)
    for k in range(4):
        for q in range(nx):
            fields[k, q] = ua[k, q + 3, pl.ds(0, nz)]
    for m in range(x_fine.shape[0]):
        high = high_side("gx", m)
        for k in range(4):
            for j in range(2):
                x_fine[m, 2 * k + j] = ua[k, 3 + high * (nx - 2) + j, pl.ds(0, nz)]
    lane = iota((nz, LANES), 1)
    for j in range(2):
        first = roll(ca[j][:nz], -3 * SLOT, 1)
        second = roll(ca[j + 2][:nz], LANES // 2 - 3 * SLOT, 1)
        edges[j] = jnp.where(lane < LANES // 2, first, second)

    spread_halo(ha, beside, slots, 0)
    for q in range(nx // 2):
        totals = [0.0] * 5
        for j in range(2):
            p = 2 * q + 3 + j
            olds, sums, spread = main_operator(ua, beside, w, force, p, nz)
            diagonal = (w0[p] + w0[p - 1] + w1[p] + w2[p] + w3[p] + w4[p])[:nz]
            for k in range(3):
                totals[k] += sums[k] - diagonal * olds[k]
            totals[3] += spread
            totals[4] += e[p, pl.ds(0, nz)]
        for k in range(5):
            summed[k, q] = totals[k]
    scale = (0.5, 0.5, 0.5, -1.0 / 32.0, 0.125)
    cz = nz // 2
    left = []
    for k in range(5):
        for r in range(nx // 4):
            halves = []
            for s in range(2):
                q = 2 * r + s
                even = summed[k, q, pl.ds(0, cz, stride=2)]
                halves.append((even + summed[k, q, pl.ds(1, cz, stride=2)]) * scale[k])
            left.append(jnp.concatenate(halves, axis=1))
    left = jnp.concatenate(left, axis=0)
    pick = iota((2 * LANES, LANES), 0) // 2 == iota((2 * LANES, LANES), 1)
    out = jnp.dot(
        left, pick.astype(F32), precision=lax.Precision.HIGHEST, preferred_element_type=F32
    )
    for k in range(5):
        for r in range(nx // 4):
            at = (k * (nx // 4) + r) * cz
            coarse[k, r] = out[at : at + cz]


def fourth_pack(own, other, fields, whole, z_a, z_b):
    nx, nz = fields.shape[1:3]
    pairs = whole.shape[1]
    cz = whole.shape[2]
    gx = lax.axis_index("gx")
    for k in range(5):
        for r in range(pairs):
            if other is None:
                whole[k, r] = own[k, r]
            else:
                mine = truth(jnp.where(gx == r // (pairs // 2), 1, 0), (cz, LANES))
                n = r % (pairs // 2)
                whole[k, r] = jnp.where(mine, own[k, n], other[k, n])
    row = iota((8, LANES), 0) // 2
    for m, out in enumerate((z_a, z_b)):
        right = high_side("gz", m)
        start = pl.multiple_of(right * (cz - 8), 8)
        for r in range(pairs):
            for k in range(2):
                parts = [
                    (whole[k + 2 * h, r, pl.ds(0, 8)], whole[k + 2 * h, r, pl.ds(cz - 8, 8)])
                    + (4 * h, 4)
                    for h in range(2)
                ]
                out[k * pairs + r] = z_strip(parts, right)
            out[2 * pairs + r] = whole[4, r, pl.ds(start, 8)]
        toward = truth(right, (8, LANES))
        for q in range(nx):
            total = jnp.zeros((8, LANES), F32)
            for k in range(4):
                low = roll(fields[k, q, pl.ds(0, 8)], 2 * k, 0)
                high = roll(fields[k, q, pl.ds(nz - 8, 8)], 2 * k - 6, 0)
                total = jnp.where(row == k, jnp.where(toward, high, low), total)
            out[3 * pairs + q] = total


def fold_rows(x):
    own = x.shape[0] - 16
    row = iota((8, LANES), 0)
    halo = jnp.where(row < 4, x[own : own + 8], x[own + 8 :])
    return jnp.concatenate([x[:own], halo], axis=0)


def deep_edges(pairs):
    per = LANES // 16
    columns = []
    for n, x in enumerate(pairs):
        for g in range(2):
            t = (2 * n + g) % per
            x_t = roll(x, 16 * t + 8 - 64 * g, 1)
            if t == 0:
                columns.append(x_t)
            else:
                slot = iota(x.shape, 1) // 16
                columns[-1] = jnp.where(slot == t, x_t, columns[-1])
    return columns


def fifth_pack(whole, z_a, z_b, edges, full, full_e, z_halo, y_a, y_b):
    pairs, cz = whole.shape[1:3]
    nx = z_halo.shape[1]
    nz = edges.shape[1]
    _, has_left, has_right = place("gz")
    to_left = truth(has_left, (8, LANES))
    to_right = truth(has_right, (8, LANES))
    deep = []
    for k in range(5):
        for r in range(pairs):
            if k < 4:
                n = k % 2 * pairs + r
                tile = z_tile(z_a[n], z_b[n], k // 2 * 4, 4)
                x = jnp.concatenate([whole[k, r], tile], axis=0)
                full[k, r] = x
            else:
                left, right = left_right("gz", z_a[2 * pairs + r], z_b[2 * pairs + r])
                right = jnp.where(to_right, right, 0.0)
                left = jnp.where(to_left, left, 0.0)
                x = jnp.concatenate([whole[k, r], right, left], axis=0)
                full_e[r] = x
            deep.append(x)
    row = iota((8, LANES), 0)
    for q in range(nx):
        left, right = left_right("gz", z_a[3 * pairs + q], z_b[3 * pairs + q])
        for k in range(4):
            x = jnp.where(row < 2 * has_right, roll(right, -2 * k, 0), 0.0)
            z_halo[k, q] = jnp.where(row >= 8 - 2 * has_left, roll(left, 6 - 2 * k, 0), x)
    columns = deep_edges(deep[: 4 * pairs])
    half = len(columns) // 2
    columns_e = deep_edges(deep[4 * pairs :])
    behind = pair_edges(lambda i: [z_halo[i, q] for q in range(nx)], 4, 8)
    for m, out in enumerate((y_a, y_b)):
        toward = high_side("gy", m)
        parts = [
            strip(columns[j], columns[j + half], toward, 8) for j in range(half)
        ] + columns_e
        for i in range(nz // 8):
            parts.append(y_strip(edges[0, pl.ds(8 * i, 8)], edges[1, pl.ds(8 * i, 8)], toward))
        parts.append(y_strip(behind[0], behind[1], toward))
        n = 0
        for x in parts:
            for i in range(x.shape[0] // 8):
                out[n] = x[8 * i : 8 * i + 8]
                n += 1


def sixth_pack(y_a, y_b, z_halo, halo_full, x_rim):
    tiles = halo_full.shape[1] // 8
    first = y_a.shape[0] - tiles
    for i in range(tiles):
        for j, x in enumerate(merge_y(y_a[first + i], y_b[first + i])):
            halo_full[j, pl.ds(8 * i, 8)] = x
    nx = z_halo.shape[1]

    def rim(plane):
        return [rows_of([(z_halo[k, plane(1)], 2 * k, 2 * k - 1, 2) for k in range(4)])]

    pack_rim(x_rim, rim, lambda j: halo_full[j], 4, 1, nx)


def coarse_solve(full, full_e, y_a, y_b, main, halo, ca, cb, force, e, w0, w1, w2, w3, w4, w5, deep_e, grown):
    pairs, rows = full.shape[1:3]
    deep = full_e.shape[1]
    planes = 2 * pairs
    own = main.shape[1] - 2
    cz = rows - 8
    half = LANES // 2
    _, zl, zr = place("gz")
    _, yl, yr = place("gy")
    gx = lax.axis_index("gx")

    def inside(rows, width):
        lane = iota((rows, LANES), 1)
        row = iota((rows, LANES), 0)
        kept = (row < cz + width * zr) | (row >= rows - width * zl)
        return kept & ((lane < half + SLOT * yr) | (lane >= LANES - SLOT * yl))

    zero = jnp.zeros((rows, LANES), F32)
    w = (w0, w1, w2, w3, w4, w5)
    for k in range(4):
        for p in (0, planes + 1):
            ca[k, p] = zero
            cb[k, p] = zero
    e[0] = zero
    e[planes + 1] = zero
    deep_e[0] = jnp.zeros((deep, LANES), F32)
    deep_e[planes + 1] = jnp.zeros((deep, LANES), F32)

    tiles, deep_tiles = rows // 8, deep // 8
    count = pairs // 2
    columns = []

    def taken(ref, n, tiles):
        return jnp.concatenate([ref[n + i] for i in range(tiles)], axis=0)

    seconds = []
    for j in range(count):
        left, right = left_right("gy", taken(y_a, j * tiles, tiles), taken(y_b, j * tiles, tiles))
        spot = iota(left.shape, 1) % 16
        columns.append(jnp.where(spot < 8, left, roll(right, 8, 1)))
        seconds.append(jnp.where(spot < 8, roll(left, -8, 1), right))
    columns += seconds
    columns_e = []
    for j in range(-(-pairs // 4)):
        n = count * tiles + j * deep_tiles
        left, right = left_right("gy", taken(y_a, n, deep_tiles), taken(y_b, n, deep_tiles))
        spot = iota(left.shape, 1) % 16
        columns_e.append(jnp.where(spot < 8, left, right))

    def whole_plane(pair, columns, n, s):
        lane = iota(pair.shape, 1)
        last, first = 2 * n + 1 - s, 2 * n + s
        low = roll(columns[first // 8], half - 16 * (first % 8) - 8, 1)
        high = roll(columns[last // 8], LANES - 8 - 16 * (last % 8), 1)
        x = jnp.where(lane < half, roll(pair, -s * half, 1), low)
        return jnp.where(lane < LANES - 8, x, high)

    near, far = inside(rows, 4), inside(deep, 8)
    for r in range(pairs):
        for s in range(2):
            p = 2 * r + s
            x = jnp.where(far, whole_plane(full_e[r], columns_e, r, s), 0.0)
            deep_e[p + 1] = x
            e[p + 1] = fold_rows(x)
            for k in range(4):
                x = whole_plane(full[k, r], columns, k * pairs + r, s)
                force[k, p] = jnp.where(near, x, 0.0)

    def shifts(x):
        return (
            roll(x, LANES - 1, 1),
            roll(x, 1, 1),
            roll(x, x.shape[0] - 1, 0),
            roll(x, 1, 0),
        )

    def two_by_two(width, body):
        lo = jnp.maximum(gx * own - width, 0)
        hi = jnp.minimum(gx * own + own + width, planes)
        steps = (hi - lo + 1) // 2
        lo = jnp.minimum(lo, planes - 2 * steps)

        def step(i, carry):
            body(lo + 2 * i + 1)
            body(lo + 2 * i + 2)
            return carry

        lax.fori_loop(0, steps, step, 0)

    def start(p):
        x = deep_e[p]
        up, down = x + deep_e[p + 1], x + deep_e[p - 1]
        w0[p] = fold_rows(up)
        total = up + down
        for n, y in enumerate(shifts(x)):
            total += x + y
            w[1 + n][p] = fold_rows(x + y)
        factor = jnp.where(near, fold_rows(relax_weight / total), 0.0)
        w5[p] = factor
        for k in range(3):
            ca[k, p] = factor * force[k, p - 1]
        ca[3, p] = e[p] * force[3, p - 1]

    w0[0] = e[0] + e[1]
    two_by_two(planes, start)

    def sweep(src, dst, width):
        def body(p):
            wxp, wxm = w0[p], w0[p - 1]
            wyp, wym, wzp, wzm = w1[p], w2[p], w3[p], w4[p]
            x = src[3, p]
            around = shifts(x)
            up, down = src[3, p + 1], src[3, p - 1]
            spread = 0.0
            for k in range(3):
                u = src[k, p]
                yp, ym, zp, zm = shifts(u)
                xp, xm = src[k, p + 1], src[k, p - 1]
                total = force[k, p - 1] - 2.0 * terms(k, up, down, *around)
                total += wxp * xp + wxm * xm
                total += wyp * yp + wym * ym
                total += wzp * zp + wzm * zm
                spread += terms(k, xp, xm, yp, ym, zp, zm)
                dst[k, p] = jnp.where(near, 0.4 * u + w5[p] * total, 0.0)
            dst[3, p] = jnp.where(near, x + e[p] * (force[3, p - 1] - 0.125 * spread), 0.0)

        two_by_two(width, body)

    sweep(ca, cb, 3)
    sweep(cb, ca, 2)
    sweep(ca, cb, 1)

    lane = iota((LANES, 2 * LANES), 1)
    cell = iota((LANES, 2 * LANES), 0)
    spot = lane % SLOT
    wanted = jnp.where(spot < 4, LANES - 2, half - 2) + spot // 2
    slot = (lane - LANES) // SLOT
    column = jnp.zeros((4 * rows, LANES), F32)
    first = gx * own

    def grow(ref, index, x):
        ref[index + (pl.ds(0, cz, stride=2),)] = x[:cz]
        ref[index + (pl.ds(1, cz, stride=2),)] = x[:cz]
        grown[pl.ds(0, 8, stride=2)] = x[cz:]
        grown[pl.ds(1, 8, stride=2)] = x[cz:]
        r = iota((8, LANES), 0)
        tail = jnp.where(r < 4, grown[pl.ds(0, 8)], grown[pl.ds(8, 8)])
        ref[index + (pl.ds(2 * cz, 8),)] = tail

    for i in range(own + 2):
        x = jnp.concatenate([cb[k, first + i] for k in range(4)], axis=0)
        here = (lane >= LANES) & ((slot + 1) // 2 - 1 == i) & (cell == wanted)
        chosen = (here | ((lane < LANES) & (lane // 2 == cell))).astype(F32)
        wide = jnp.dot(x, chosen, precision=lax.Precision.HIGHEST, preferred_element_type=F32)
        for k in range(4):
            grow(main, (k, i), wide[k * rows : (k + 1) * rows, :LANES])
        column += wide[:, LANES:]
    for k in range(4):
        grow(halo, (k,), column[k * rows : (k + 1) * rows])


def post_smooth(
    e, halo_e, force, halo_f, w0, w1, w2, w3, w4, w5, hw,
    fields, z_halo, halo_full, x_fine, x_rim, main, column, v_out, p_out,
    ua, ub, ha, hb, ca, cb, beside,
):
    nx, nz, _ = p_out.shape
    slots = nx + 6
    w = (w0, w1, w2, w3, w4, w5)
    zero = jnp.zeros((nz + 8, LANES), F32)
    for k in range(4):
        for p in (1, 2, nx + 3, nx + 4):
            ua[k, p] = zero
            ub[k, p] = zero
        for q in range(nx):
            i = q // 2 + 1
            ua[k, q + 3, pl.ds(0, nz)] = fields[k, q] + main[k, i, pl.ds(0, nz)]
            ua[k, q + 3, pl.ds(nz, 8)] = z_halo[k, q] + main[k, i, pl.ds(nz, 8)]
        ha[k] = own_slots(halo_full[k % 2], nx, k // 2)
    for m in range(x_fine.shape[0]):
        right, valid = x_side(m)
        there = truth(valid, (nz, LANES))
        there8 = truth(valid, (8, LANES))
        tiles = (nz + 8) // 8
        side = jnp.concatenate([x_rim[m, 1 + r] for r in range(tiles)], axis=0)
        i = right * (nx // 2 + 1)
        for k in range(4):
            for j in range(2):
                at = 1 + right * (nx + 2) + j
                x = x_fine[m, 2 * k + j] + main[k, i, pl.ds(0, nz)]
                ua[k, at, pl.ds(0, nz)] = jnp.where(there, x, 0.0)
            x = roll(x_rim[m, 0], -2 * k, 0) + main[k, i, pl.ds(nz, 8)]
            ua[k, 2 + right * (nx + 1), pl.ds(nz, 8)] = jnp.where(there8, x, 0.0)
            x, kept = rim_halo(side, k, SLOT, 1, right, valid, nx)
            ha[k] = jnp.where(kept, x, ha[k])
    masks = fine_masks(nz + 8, slots)
    for k in range(4):
        ha[k] = jnp.where(masks[1], ha[k] + column[k], 0.0)
    fill_edges(ca, ua, 4, 1, slots - 1)
    rest = (w, hw, e, halo_e, force, halo_f)
    fine_sweep(ua, ha, ca, ub, hb, None, *rest, 1, masks, beside)

    spread_halo(hb, beside, slots, 0)

    def last(p):
        new = main_operator(ub, beside, w, force, p, nz)
        new = relaxed(*new, w5[p, pl.ds(0, nz)], e[p, pl.ds(0, nz)])
        for k in range(3):
            v_out[k, p - 3] = new[k]
        p_out[p - 3] = new[3]

    over_planes(slots, 0, last)


def local(velocity, pressure, viscosity, body_force):
    nx, nz, ny = pressure.shape
    if ny != LANES or nx * SLOT * 2 != LANES or nz % 16:
        raise ValueError("unsupported block")
    sides = x_messages()
    rows, slots = nz + 8, nx + 6
    inputs = [velocity, pressure, viscosity, body_force]
    block = (nz, LANES)

    z_shape = (3 * nx, 8, LANES)
    x_main, y_a, y_b, z_a, z_b = call(
        first_pack,
        [(sides, 21) + block, (2,) + block, (2,) + block, z_shape, z_shape],
        inputs,
        [a.shape for a in inputs],
        outside=4,
        copies=4 + 8 * sides,
    )
    x_main = swap_x(x_main)
    y_a, y_b = swap(y_a, "gy", 0), swap(y_b, "gy", 1)
    halo, z_b = call(second_pack, [(4,) + block, z_shape], [z_b, y_a, y_b])
    (z_a,) = call(second_pack_near, [z_shape], [z_a, halo])
    z_a, z_b = swap(z_a, "gz", 0), swap(z_b, "gz", 1)
    tiles = rows // 8
    z_first, halo_first, x_first = call(
        third_pack,
        [(8, nx, 8, LANES), (4, rows, LANES), (sides, 6 + tiles, 8, LANES)],
        [z_a, z_b, halo],
    )
    x_first = swap_x(x_first)

    state = [(4, slots, rows, LANES)] * 2 + [(4, rows, LANES)] * 4
    spread = (4, slots, rows, LANES)
    operator = [(slots, rows, LANES), (rows, LANES), (3, slots, rows, LANES), (3, rows, LANES)]
    operator += [(slots, rows, LANES)] * 6 + [(7, rows, LANES)]
    fields, own, edges, x_fine, *operator = call(
        pre_smooth,
        [(4, nx) + block, (5, nx // 4, nz // 2, LANES), (2,) + block, (sides, 8) + block]
        + operator,
        inputs + [z_first, halo_first, x_main, x_first],
        state + [(rows, LANES), spread, (5, nx // 2, nz, LANES)],
        cost=8,
    )
    if lax.axis_size("gx") == 2:
        parts = [own, swap(own, "gx", 0)]
        gather = fourth_pack
    else:
        parts = [lax.all_gather(own, "gx", axis=1, tiled=True)]

        def gather(a, *refs):
            fourth_pack(a, None, *refs)

    x_fine = swap_x(x_fine)
    pairs = lax.axis_size("gx") * (nx // 4)
    z_shape = (3 * pairs + nx, 8, LANES)
    whole, z_a, z_b = call(
        gather, [(5, pairs, nz // 2, LANES), z_shape, z_shape], parts + [fields]
    )
    z_a, z_b = swap(z_a, "gz", 0), swap(z_b, "gz", 1)
    deep = nz // 2 + 16
    shallow = deep - 8
    y_shape = (pairs // 2 * (shallow // 8) + -(-pairs // 4) * (deep // 8) + tiles, 8, LANES)
    full, full_e, z_halo, y_a, y_b = call(
        fifth_pack,
        [(4, pairs, shallow, LANES), (pairs, deep, LANES), (4, nx, 8, LANES), y_shape, y_shape],
        [whole, z_a, z_b, edges],
    )
    y_a, y_b = swap(y_a, "gy", 0), swap(y_b, "gy", 1)
    halo_full, x_rim = call(
        sixth_pack,
        [(2, rows, LANES), (sides, 1 + tiles, 8, LANES)],
        [y_a, y_b, z_halo],
    )
    x_rim = swap_x(x_rim)
    planes = 2 * pairs
    plane = (shallow, LANES)
    main, column = call(
        coarse_solve,
        [(4, nx // 2 + 2, rows, LANES), (4, rows, LANES)],
        [full, full_e, y_a, y_b],
        [(4, planes + 2) + plane] * 2
        + [(4, planes) + plane]
        + [(planes + 2,) + plane] * 7
        + [(planes + 2, deep, LANES), (16, LANES)],
        cost=4,
    )
    v_out, p_out = call(
        post_smooth,
        [(3, nx) + block, (nx,) + block],
        operator + [fields, z_halo, halo_full, x_fine, x_rim, main, column],
        state + [spread],
        cost=8,
    )
    return v_out, p_out


def swap_x(array):
    if array.shape[0] == 1:
        return swap(array, "gx", 0)
    parts = [swap(array[m], "gx", m) for m in range(2)]
    return jnp.stack(parts)


def solution(mesh):
    return jax.shard_map(
        local,
        mesh=mesh,
        in_specs=(
            P(None, "gx", "gz", "gy"),
            P("gx", "gz", "gy"),
            P("gx", "gz", "gy"),
            P(None, "gx", "gz", "gy"),
        ),
        out_specs=(P(None, "gx", "gz", "gy"), P("gx", "gz", "gy")),
        check_vma=False,
    )
```

```python
import jax
import jax.numpy as jnp
from jax import lax
from jax.experimental import pallas as pl
from jax.experimental.pallas import tpu as pltpu
from jax.sharding import PartitionSpec as P

LANES = 128
SLOT = 8
F32 = jnp.float32
relax_weight = 0.6
HELD = 846 * 2**16
Z_PLACES = (
    ((0, 0, 3), (1, 3, 3), (5, 6, 2)),
    ((2, 0, 3), (3, 3, 3), (6, 6, 2)),
    ((4, 0, 3), (7, 3, 2)),
)


def call(body, outs, args, scratch=(), cost=1, outside=0, copies=0, aliases=None):
    return pl.pallas_call(
        body,
        out_shape=[jax.ShapeDtypeStruct(shape, F32) for shape in outs],
        in_specs=[pl.BlockSpec(memory_space=pltpu.HBM)] * outside
        + [pl.BlockSpec(memory_space=pltpu.VMEM)] * (len(args) - outside),
        out_specs=[pl.BlockSpec(memory_space=pltpu.VMEM)] * len(outs),
        scratch_shapes=[pltpu.VMEM(shape, F32) for shape in scratch]
        + [pltpu.SemaphoreType.DMA((copies,))] * (copies > 0),
        input_output_aliases=aliases or {},
        compiler_params=pltpu.CompilerParams(vmem_limit_bytes=HELD if outside else 40 * 2**20),
        cost_estimate=pl.CostEstimate(
            flops=cost * 10**6, bytes_accessed=cost * 10**6, transcendentals=0
        ),
    )(*args)


def swap(array, axis, which):
    count = lax.axis_size(axis)
    if axis != "gx" and which == 1:
        ys, zs = lax.axis_size("gy"), lax.axis_size("gz")
        pairs = []
        for y in range(ys):
            for z in range(zs):
                i = y if axis == "gy" else z
                j = i + 1 if i % 2 else i - 1
                if axis == "gy":
                    to = (j, z) if 0 <= j < count else (y, z ^ 1)
                else:
                    to = (y, j) if 0 <= j < count else (y ^ 1, z)
                pairs.append((y * zs + z, to[0] * zs + to[1]))
        return lax.ppermute(array, ("gy", "gz"), pairs)
    pairs = []
    for i in range(which, count, 2):
        j = (i + 1) % count
        pairs += [(i, j), (j, i)]
    return lax.ppermute(array, axis, pairs)


def place(axis):
    i = lax.axis_index(axis)
    last = lax.axis_size(axis) - 1
    return i, jnp.where(i > 0, 1, 0), jnp.where(i < last, 1, 0)


def iota(shape, dim):
    return lax.broadcasted_iota(jnp.int32, shape, dim)


def truth(flag, shape):
    return jnp.full(shape, flag, jnp.int32) > 0


def roll(x, shift, dim):
    if isinstance(shift, int):
        shift %= x.shape[dim]
        return x if shift == 0 else pltpu.roll(x, shift, dim)
    return pltpu.roll(x, lax.rem(shift + 2 * x.shape[dim], x.shape[dim]), dim)


def high_side(axis, message):
    return jnp.where(lax.axis_index(axis) % 2 == message, 1, 0)


def left_right(axis, a, b):
    odd = truth(lax.axis_index(axis) % 2, a.shape)
    return jnp.where(odd, a, b), jnp.where(odd, b, a)


def x_messages():
    return 1 if lax.axis_size("gx") == 2 else 2


def pair_edges(planes, fields, rows):
    lane = iota((rows, LANES), 1) // SLOT
    half = fields // 2
    out = []
    for j in range(half):
        total = jnp.zeros((rows, LANES), F32)
        for part in range(2):
            for q, x in enumerate(planes(j + part * half)):
                slot = q + part * (LANES // SLOT // 2)
                total = jnp.where(lane == slot, roll(x, slot * SLOT + 4, 1), total)
        out.append(total)
    return out


def merge_y(a, b):
    _, has_left, has_right = place("gy")
    left, right = left_right("gy", a, b)
    spot = iota(a.shape, 1) % SLOT
    kept = (spot < 4 * has_left) | (spot >= SLOT - 4 * has_right)
    first = jnp.where(spot < 4, left, roll(right, 4, 1))
    second = jnp.where(spot < 4, roll(left, -4, 1), right)
    return jnp.where(kept, first, 0.0), jnp.where(kept, second, 0.0)


class Staged:
    def __init__(self, refs):
        self.refs = refs
        self.half, self.nz = refs[0].shape[:2]
        self.nx = 2 * self.half

    def __getitem__(self, index):
        i, q = index[:2]
        return self.refs[2 * i + q // self.half][(q % self.half,) + index[2:]]


def first_pack(v_in, p_in, e_in, f_in, *refs):
    staged = Staged(refs[:16])
    y_a, y_b, arrived = refs[16:]
    nx, nz = staged.nx, staged.nz
    loads = []
    for n in range(16):
        i, planes = n // 2, pl.ds(n % 2 * staged.half, staged.half)
        if i < 3:
            part = v_in.at[i, planes]
        elif i < 5:
            part = (p_in, e_in)[i - 3].at[planes]
        else:
            part = f_in.at[i - 5, planes]
        loads.append(pltpu.make_async_copy(part, refs[n], arrived.at[n]))
    for load in loads:
        load.start()
    for load in loads:
        load.wait()
    edges = pair_edges(lambda i: [staged[i, q] for q in range(nx)], 8, nz)
    for m, out in enumerate((y_a, y_b)):
        for j in range(2):
            out[j] = y_strip(edges[j], edges[j + 2], high_side("gy", m))


def side_pack(*refs):
    staged = Staged(refs[:16])
    x_main, z_a, z_b = refs[16:]
    nx, nz = staged.nx, staged.nz
    for m in range(x_main.shape[0]):
        top = truth(high_side("gx", m), (nz, LANES))
        n = 0
        for i in range(8):
            width = 3 if i < 5 else 2
            for j in range(width):
                x_main[m, n] = jnp.where(top, staged[i, nx - width + j], staged[i, j])
                n += 1
    low, high = pl.ds(0, 8), pl.ds(nz - 8, 8)
    for q in range(nx):
        for n, fields in enumerate(Z_PLACES):
            for m, out in enumerate((z_a, z_b)):
                out[3 * q + n] = z_strip(
                    [(staged[i, q, low], staged[i, q, high], at, rows) for i, at, rows in fields],
                    high_side("gz", m),
                )


def strip(first, second, toward_right, width):
    right = truth(toward_right, first.shape)
    spot = iota(first.shape, 1) % (2 * width)
    first = jnp.where(right, first, roll(first, -width, 1))
    second = jnp.where(right, roll(second, width, 1), second)
    return jnp.where(spot < width, first, second)


def y_strip(first, second, toward_right):
    return strip(first, second, toward_right, SLOT // 2)


def z_strip(parts, toward_right):
    right = truth(toward_right, (8, LANES))
    return rows_of(
        [
            (jnp.where(right, roll(high, at + rows, 0), roll(low, at, 0)), 0, at, rows)
            for low, high, at, rows in parts
        ]
    )


def z_tail(halo, first, out, message):
    nz = halo.shape[1]
    row = iota((8, LANES), 0)
    for n in range(first.shape[0]):
        out[n] = first[n]
    for j in range(4):
        tiles = halo[j, pl.ds(0, 8)], halo[j, pl.ds(nz - 8, 8)]
        x = z_strip([tiles + (5, 3)], high_side("gz", message))
        out[3 * j + 2] = jnp.where(row < 5, first[3 * j + 2], x)


def second_pack(z_first, y_a, y_b, halo, z_b):
    for j in range(2):
        halo[j], halo[j + 2] = merge_y(y_a[j], y_b[j])
    z_tail(halo, z_first, z_b, 1)


def second_pack_near(z_first, halo, z_a):
    z_tail(halo, z_first, z_a, 0)


def z_tile(a, b, at, rows):
    _, has_left, has_right = place("gz")
    left, right = left_right("gz", a, b)
    row = iota(a.shape, 0)
    x = jnp.where(row < rows * has_right, roll(right, -at, 0), 0.0)
    return jnp.where(row >= 8 - rows * has_left, roll(left, 8 - at - rows, 0), x)


def third_pack(z_a, z_b, halo, z_halo, halo_full, x_rim):
    nx = z_halo.shape[1]
    nz = halo.shape[1]
    for q in range(nx):
        for n, fields in enumerate(Z_PLACES):
            for i, at, rows in fields:
                z_halo[i, q] = z_tile(z_a[3 * q + n], z_b[3 * q + n], at, rows)
    for j in range(4):
        halo_full[j, pl.ds(0, nz)] = halo[j]
        halo_full[j, pl.ds(nz, 8)] = z_tile(z_a[3 * j + 2], z_b[3 * j + 2], 5, 3)

    def tiles(plane):
        out = [
            rows_of([(z_halo[i, plane(1)], 0, 6, 4), (z_halo[i, plane(2)], 3, 2, 2)])
            for i in range(5)
        ]
        force = zip((0, 3, 5), (7, 2, 4))
        out.append(
            rows_of([(z_halo[5 + k, plane(1)], at, row, 2) for k, (at, row) in enumerate(force)])
        )
        return out

    pack_rim(x_rim, tiles, lambda j: halo_full[j], 8, 2, nx)


def rows_of(parts):
    row = iota((8, LANES), 0)
    total = jnp.zeros((8, LANES), F32)
    for x, shift, first, count in parts:
        total = jnp.where((row - first) % 8 < count, roll(x, shift, 0), total)
    return total


def pack_rim(x_rim, tiles, halo_pair, fields, planes, nx):
    half = fields // 2
    stride = LANES // 8 if fields == 8 else SLOT
    for m in range(x_rim.shape[0]):
        high = high_side("gx", m)
        done = tiles(lambda d, high=high: high * (nx - 2 * d + 1) + d - 1)
        for n, x in enumerate(done):
            x_rim[m, n] = x
        pairs = [halo_pair(j) for j in range(half)]
        rows = pairs[0].shape[0]
        column = iota((rows, LANES), 1) // stride
        first = high * (nx - planes) * SLOT
        total = jnp.zeros((rows, LANES), F32)
        for i in range(fields):
            at = i * stride - first - (i // half) * (LANES // 2)
            total = jnp.where(column == i, roll(pairs[i % half], at + LANES, 1), total)
        for r in range(rows // 8):
            x_rim[m, len(done) + r] = total[8 * r : 8 * r + 8]


def main_shifts(x, beside, kept):
    rows = x.shape[0]
    y, beside = x[:kept], beside[:kept]
    lane = iota(y.shape, 1)
    return (
        roll(jnp.where(lane == 0, beside, y), LANES - 1, 1),
        roll(jnp.where(lane == LANES - 1, beside, y), 1, 1),
        roll(x, rows - 1, 0)[:kept],
        roll(x, 1, 0)[:kept],
    )


def halo_shifts(x, edge):
    spot = iota(x.shape, 1) % SLOT
    rows = x.shape[0]
    return (
        roll(x, LANES - SLOT, 1),
        roll(x, SLOT, 1),
        roll(jnp.where(spot == 4, edge, x), LANES - 1, 1),
        roll(jnp.where(spot == 3, edge, x), 1, 1),
        roll(x, rows - 1, 0),
        roll(x, 1, 0),
    )


def main_weights(e, halo_e, w, width, chosen, faces):
    slots = e.shape[0]
    for p in faces:
        w[0][p] = e[p] + e[p + 1]

    def body(p):
        x = e[p]
        total = w[0][p] + w[0][p - 1]
        for n, y in enumerate(main_shifts(x, roll(halo_e[...], LANES - SLOT * p - 4, 1), x.shape[0])):
            total += x + y
            w[1 + n][p] = x + y
        w[5][p] = relax_weight / total

    over_planes(slots, width, body, chosen)


def halo_weights(e, edge_e, w):
    x = e[...]
    total = jnp.zeros_like(x)
    for n, y in enumerate(halo_shifts(x, edge_e[...])):
        total += x + y
        w[n] = x + y
    w[6] = relax_weight / total


def terms(k, up, down, yp, ym, zp, zm):
    return (up - down, zp - zm, yp - ym)[k]


def spread_halo(halo, beside, slots, width, chosen=None, full=True):
    kept = beside.shape[2] - (0 if full else 8)

    def body(p):
        for k in range(4):
            beside[k, p, pl.ds(0, kept)] = roll(halo[k][:kept], LANES - SLOT * p - 4, 1)

    over_planes(slots, width, body, chosen)


def main_operator(src, beside, w, force, p, kept):
    def at(ref, *index):
        return ref[index + (pl.ds(0, kept),)]

    wxp, wxm, wyp, wym, wzp, wzm = (
        at(ref, q) for ref, q in zip((w[0],) + w[:5], (p, p - 1, p, p, p, p))
    )
    around = main_shifts(src[3, p], at(beside, 3, p), kept)
    up, down = at(src, 3, p + 1), at(src, 3, p - 1)
    olds, sums, spread = [], [], 0.0
    for k in range(3):
        yp, ym, zp, zm = main_shifts(src[k, p], at(beside, k, p), kept)
        xp, xm = at(src, k, p + 1), at(src, k, p - 1)
        total = at(force, k, p) - terms(k, up, down, *around)
        total += wxp * xp + wxm * xm
        total += wyp * yp + wym * ym
        total += wzp * zp + wzm * zm
        spread += terms(k, xp, xm, yp, ym, zp, zm)
        olds.append(at(src, k, p))
        sums.append(total)
    olds.append(at(src, 3, p))
    return olds, sums, spread


def halo_operator(halo, edge, w, force):
    x = halo[3]
    px = halo_shifts(x, edge[3])
    olds, sums, spread = [], [], 0.0
    for k in range(3):
        u = halo[k]
        around = halo_shifts(u, edge[k])
        total = force[k] - terms(k, *px)
        for n in range(6):
            total += w[n] * around[n]
        spread += terms(k, *around)
        olds.append(u)
        sums.append(total)
    olds.append(x)
    return olds, sums, spread


def relaxed(olds, sums, spread, factor, e):
    new = [0.4 * olds[k] + factor * sums[k] for k in range(3)]
    return new + [olds[3] - 0.25 * e * spread]


def edges_of(plane, slots, total=None):
    shape = plane(slots[0]).shape
    slot = iota(shape, 1) // SLOT
    total = jnp.zeros(shape, F32) if total is None else total
    for p in slots:
        total = jnp.where(slot == p, roll(plane(p), p * SLOT + 4, 1), total)
    return total


def fill_edges(edge, src, slots, fresh=True):
    for k in range(4):
        edge[k] = edges_of(lambda p: src[k, p], slots, None if fresh else edge[k])


def fine_masks(rows, slots):
    nz = rows - 8
    _, zl, zr = place("gz")
    _, yl, yr = place("gy")
    _, xl, xr = place("gx")
    r = iota((8, LANES), 0)
    tile = (r < 4 * zr) | (r >= 8 - 4 * zl)
    r = iota((rows, LANES), 0)
    lane = iota((rows, LANES), 1)
    spot, slot = lane % SLOT, lane // SLOT
    column = (r < nz + 4 * zr) | (r >= rows - 4 * zl)
    column &= (spot < 4 * yl) | (spot >= SLOT - 4 * yr)
    column &= (slot >= 3 - 3 * xl) & (slot < slots - 3 + 3 * xr)
    return tile, column


def main_sweep(src, halo, dst, w, e, force, width, tile, beside, chosen=None):
    nz = src.shape[2] - 8
    slots = src.shape[1]

    def body(p):
        new = relaxed(*main_operator(src, beside, w, force, p, nz + 8), w[5][p], e[p])
        for k in range(4):
            x = new[k]
            dst[k, p, pl.ds(0, nz)] = x[:nz]
            dst[k, p, pl.ds(nz, 8)] = jnp.where(tile, x[nz:], 0.0)

    spread_halo(halo, beside, slots, width, chosen)
    over_planes(slots, width, body, chosen)


def halo_sweep(halo, edge, halo_dst, hw, halo_e, halo_f, column):
    new = relaxed(*halo_operator(halo, edge, hw, halo_f), hw[6], halo_e[...])
    for k in range(4):
        halo_dst[k] = jnp.where(column, new[k], 0.0)


def over_planes(slots, width, body, chosen=None):
    _, xl, xr = place("gx")
    for p in range(3 - width, slots - 3 + width):
        wanted = True if chosen is None else chosen(p)
        if wanted is False:
            continue
        if p < 3:
            wanted = xl > 0
        elif p >= slots - 3:
            wanted = xr > 0
        if wanted is True:
            body(p)
        else:
            pl.when(wanted)(lambda p=p: body(p))


def own_slots(x, nx, part):
    lane = iota(x.shape, 1)
    x = roll(x, 3 * SLOT - part * (LANES // 2), 1)
    return jnp.where((lane >= 3 * SLOT) & (lane < (3 + nx) * SLOT), x, 0.0)


def x_side(m):
    right = high_side("gx", m)
    _, has_left, has_right = place("gx")
    return right, jnp.where(right > 0, has_right, has_left)


def rim_halo(x, t, stride, planes, right, valid, nx):
    base = right * (nx + 3) + (1 - right) * (3 - planes)
    lane = iota(x.shape, 1)
    x = roll(x, base * SLOT - t * stride + LANES, 1)
    kept = (lane >= base * SLOT) & (lane < (base + planes * valid) * SLOT)
    return jnp.where(kept, x, 0.0), kept


def viscosity_force(staged, z_halo, halo_full, x_main, e, halo_e, force, halo_f):
    nx, nz = staged.nx, staged.nz
    slots = nx + 6
    zero = jnp.zeros((nz + 8, LANES), F32)
    for p in list(range(3)) + list(range(nx + 3, slots)):
        e[p] = zero
        for k in range(3):
            force[k, p] = zero
    for q in range(nx):
        e[q + 3, pl.ds(0, nz)] = staged[4, q]
        e[q + 3, pl.ds(nz, 8)] = z_halo[4, q]
        for k in range(3):
            force[k, q + 3, pl.ds(0, nz)] = 2.0 * staged[5 + k, q]
            force[k, q + 3, pl.ds(nz, 8)] = 2.0 * z_halo[5 + k, q]
    halo_e[...] = own_slots(halo_full[0], nx, 1)
    for k in range(3):
        halo_f[k] = 2.0 * own_slots(halo_full[k + 1], nx, 1)
    for m in range(x_main.shape[0]):
        right, valid = x_side(m)
        there = truth(valid, (nz, LANES))
        for j in range(3):
            e[right * (nx + 3) + j, pl.ds(0, nz)] = jnp.where(there, x_main[m, 12 + j], 0.0)
        for j in range(2):
            at = right * (nx + 2) + 1 + j
            for k in range(3):
                force[k, at, pl.ds(0, nz)] = jnp.where(there, 2.0 * x_main[m, 15 + 2 * k + j], 0.0)


def first_fields(staged, z_halo, halo_full, x_main, u, other, halo):
    nx, nz = staged.nx, staged.nz
    slots = nx + 6
    zero = jnp.zeros((nz + 8, LANES), F32)
    for k in range(4):
        for p in list(range(3)) + list(range(nx + 3, slots)):
            u[k, p] = zero
            other[k, p] = zero
        for q in range(nx):
            u[k, q + 3, pl.ds(0, nz)] = staged[k, q]
            u[k, q + 3, pl.ds(nz, 8)] = z_halo[k, q]
        halo[k] = own_slots(halo_full[k], nx, 0)
    for m in range(x_main.shape[0]):
        right, valid = x_side(m)
        there = truth(valid, (nz, LANES))
        for k in range(4):
            for j in range(3):
                x = jnp.where(there, x_main[m, 3 * k + j], 0.0)
                u[k, right * (nx + 3) + j, pl.ds(0, nz)] = x


def add_rims(x_rim, nx, u, halo, e, halo_e, force, halo_f, edge, edge_e):
    nz = e.shape[1] - 8
    tiles = (nz + 8) // 8
    tail = pl.ds(nz, 8)
    slot = iota((8, LANES), 1) // SLOT
    for m in range(x_rim.shape[0]):
        right, valid = x_side(m)
        there = truth(valid, (8, LANES))
        column = jnp.concatenate([x_rim[m, 6 + r] for r in range(tiles)], axis=0)
        near = right * (nx + 1) + 2
        far = near + 2 * right - 1
        for k in range(5):
            x = jnp.where(there, x_rim[m, k], 0.0)
            for p, y in ((near, x), (far, roll(x, -3, 0))):
                moved = roll(y, p * SLOT + 4, 1)
                if k < 4:
                    u[k, p, tail] = y
                    edge[k, tail] = jnp.where(slot == p, moved, edge[k, tail])
                else:
                    e[p, tail] = y
                    edge_e[tail] = jnp.where(slot == p, moved, edge_e[tail])
            x, kept = rim_halo(column, k, LANES // 8, 2, right, valid, nx)
            if k < 4:
                halo[k] = jnp.where(kept, x, halo[k])
            else:
                halo_e[...] = jnp.where(kept, x, halo_e[...])
        x = jnp.where(there, 2.0 * x_rim[m, 5], 0.0)
        for k, at in enumerate((0, 3, 5)):
            force[k, near, tail] = roll(x, -at, 0)
            x_k, kept = rim_halo(column, 5 + k, LANES // 8, 2, right, valid, nx)
            halo_f[k] = jnp.where(kept, 2.0 * x_k, halo_f[k])


def early(nx, sweep):
    _, xl, xr = place("gx")

    def chosen(p):
        if 3 + sweep <= p < nx + 3 - sweep:
            return True
        if 3 <= p < nx + 3:
            return xl == 0 if p < 3 + sweep else xr == 0
        return False

    return chosen


def early_block(nx):
    _, xl, xr = place("gx")
    return lambda q: xl == 0 if 2 * q + 5 <= nx else xr == 0 if 2 * q + 2 >= 5 else False


def late(chosen):
    def rest(p):
        flag = chosen(p)
        return not flag if isinstance(flag, bool) else jnp.logical_not(flag)

    return rest


def residuals(u, halo, beside, w, force, e, summed, chosen):
    _, blocks, nz, _ = summed.shape
    slots = u.shape[1]
    spread_halo(halo, beside, slots, 0, lambda p: chosen((p - 3) // 2), False)

    def body(q):
        totals = [0.0] * 5
        for j in range(2):
            p = 2 * q + 3 + j
            olds, sums, spread = main_operator(u, beside, w, force, p, nz)
            diagonal = (w[0][p] + w[0][p - 1] + w[1][p] + w[2][p] + w[3][p] + w[4][p])[:nz]
            for k in range(3):
                totals[k] += sums[k] - diagonal * olds[k]
            totals[3] += spread
            totals[4] += e[p, pl.ds(0, nz)]
        for k in range(5):
            summed[k, q] = totals[k]

    for q in range(blocks):
        wanted = chosen(q)
        if wanted is True:
            body(q)
        elif wanted is not False:
            pl.when(wanted)(lambda q=q: body(q))


def pre_start(*refs):
    pre_start_on(Staged(refs[:16]), *refs[16:])


def pre_start_on(
    staged, z_halo, halo_full, x_main,
    e, halo_e, force, halo_f, w0, w1, w2, w3, w4, w5, ua, ub, ha, ca, cb, edge_e, summed,
    hw, hb, hc, beside,
):
    nx, nz = staged.nx, staged.nz
    slots = nx + 6
    w = (w0, w1, w2, w3, w4, w5)
    viscosity_force(staged, z_halo, halo_full, x_main, e, halo_e, force, halo_f)
    first_fields(staged, z_halo, halo_full, x_main, ua, ub, ha)
    tile, column = fine_masks(nz + 8, slots)
    fill_edges(ca, ua, range(slots))
    edge_e[...] = edges_of(lambda p: e[p], range(slots))
    main_weights(e, halo_e, w, 0, early(nx, 1), range(2, nx + 3))
    main_sweep(ua, ha, ub, w, e, force, 0, tile, beside, early(nx, 1))
    halo_weights(halo_e, edge_e, hw)
    halo_sweep(ha, ca, hb, hw, halo_e, halo_f, column)
    fill_edges(cb, ub, range(3, nx + 3))
    main_sweep(ub, hb, ua, w, e, force, 0, tile, beside, early(nx, 2))
    halo_sweep(hb, cb, hc, hw, halo_e, halo_f, column)
    residuals(ua, hc, beside, w, force, e, summed, early_block(nx))


def pre_smooth(
    x_rim, _e, _halo_e, _force, _halo_f, _w0, _w1, _w2, _w3, _w4, _w5, _ua, _ub, _ha, _ca, _cb,
    _edge_e, _summed, e, halo_e, force, halo_f, w0, w1, w2, w3, w4, w5, ua, ub, ha, ca, cb, edge_e,
    summed, hw, coarse, hb, beside,
):
    slots = e.shape[0]
    nx, nz = slots - 6, e.shape[1] - 8
    w = (w0, w1, w2, w3, w4, w5)
    add_rims(x_rim, nx, ua, ha, e, halo_e, force, halo_f, ca, edge_e)
    tile, column = fine_masks(nz + 8, slots)
    faces = [p for p in range(slots - 1) if not 3 <= p < nx + 2]
    main_weights(e, halo_e, w, 2, late(early(nx, 1)), faces)
    halo_weights(halo_e, edge_e, hw)
    main_sweep(ua, ha, ub, w, e, force, 2, tile, beside, late(early(nx, 1)))
    halo_sweep(ha, ca, hb, hw, halo_e, halo_f, column)
    fill_edges(cb, ub, [p for p in range(1, slots - 1) if not 4 <= p < nx + 2], False)
    main_sweep(ub, hb, ua, w, e, force, 1, tile, beside, late(early(nx, 2)))
    halo_sweep(hb, cb, ha, hw, halo_e, halo_f, column)
    residuals(ua, ha, beside, w, force, e, summed, late(early_block(nx)))
    scale = (0.5, 0.5, 0.5, -1.0 / 32.0, 0.125)
    cz = nz // 2
    left = []
    for k in range(5):
        for r in range(nx // 4):
            halves = []
            for s in range(2):
                q = 2 * r + s
                even = summed[k, q, pl.ds(0, cz, stride=2)]
                halves.append((even + summed[k, q, pl.ds(1, cz, stride=2)]) * scale[k])
            left.append(jnp.concatenate(halves, axis=1))
    left = jnp.concatenate(left, axis=0)
    pick = iota((2 * LANES, LANES), 0) // 2 == iota((2 * LANES, LANES), 1)
    out = jnp.dot(
        left, pick.astype(F32), precision=lax.Precision.HIGHEST, preferred_element_type=F32
    )
    for k in range(5):
        for r in range(nx // 4):
            at = (k * (nx // 4) + r) * cz
            coarse[k, r] = out[at : at + cz]


def smooth_pack(fields, edges, x_fine):
    nx, nz = fields.shape[1] - 6, fields.shape[2] - 8
    for m in range(x_fine.shape[0]):
        high = high_side("gx", m)
        for k in range(4):
            for j in range(2):
                x_fine[m, 2 * k + j] = fields[k, 3 + high * (nx - 2) + j, pl.ds(0, nz)]

    def planes(k):
        return [fields[k, q + 3, pl.ds(0, nz)] for q in range(nx)]

    for j, x in enumerate(pair_edges(planes, 4, nz)):
        edges[j] = x


def fourth_pack(own, other, fields, whole, z_a, z_b):
    nx, nz = fields.shape[1] - 6, fields.shape[2] - 8
    pairs = whole.shape[1]
    cz = whole.shape[2]
    gx = lax.axis_index("gx")
    for k in range(5):
        for r in range(pairs):
            if other is None:
                whole[k, r] = own[k, r]
            else:
                mine = truth(jnp.where(gx == r // (pairs // 2), 1, 0), (cz, LANES))
                n = r % (pairs // 2)
                whole[k, r] = jnp.where(mine, own[k, n], other[k, n])
    row = iota((8, LANES), 0) // 2
    for m, out in enumerate((z_a, z_b)):
        right = high_side("gz", m)
        start = pl.multiple_of(right * (cz - 8), 8)
        for r in range(pairs):
            for k in range(2):
                parts = [
                    (whole[k + 2 * h, r, pl.ds(0, 8)], whole[k + 2 * h, r, pl.ds(cz - 8, 8)])
                    + (4 * h, 4)
                    for h in range(2)
                ]
                out[k * pairs + r] = z_strip(parts, right)
            out[2 * pairs + r] = whole[4, r, pl.ds(start, 8)]
        toward = truth(right, (8, LANES))
        for q in range(nx):
            total = jnp.zeros((8, LANES), F32)
            for k in range(4):
                low = roll(fields[k, q + 3, pl.ds(0, 8)], 2 * k, 0)
                high = roll(fields[k, q + 3, pl.ds(nz - 8, 8)], 2 * k - 6, 0)
                total = jnp.where(row == k, jnp.where(toward, high, low), total)
            out[3 * pairs + q] = total


def fold_rows(x):
    own = x.shape[0] - 16
    row = iota((8, LANES), 0)
    halo = jnp.where(row < 4, x[own : own + 8], x[own + 8 :])
    return jnp.concatenate([x[:own], halo], axis=0)


def deep_edges(pairs):
    per = LANES // 16
    columns = []
    for n, x in enumerate(pairs):
        for g in range(2):
            t = (2 * n + g) % per
            x_t = roll(x, 16 * t + 8 - 64 * g, 1)
            if t == 0:
                columns.append(x_t)
            else:
                slot = iota(x.shape, 1) // 16
                columns[-1] = jnp.where(slot == t, x_t, columns[-1])
    return columns


def fifth_pack(whole, z_a, z_b, edges, full, full_e, z_halo, y_a, y_b):
    pairs, cz = whole.shape[1:3]
    nx = z_halo.shape[1]
    nz = edges.shape[1]
    _, has_left, has_right = place("gz")
    to_left = truth(has_left, (8, LANES))
    to_right = truth(has_right, (8, LANES))
    deep = []
    for k in range(5):
        for r in range(pairs):
            if k < 4:
                n = k % 2 * pairs + r
                tile = z_tile(z_a[n], z_b[n], k // 2 * 4, 4)
                x = jnp.concatenate([whole[k, r], tile], axis=0)
                full[k, r] = x
            else:
                left, right = left_right("gz", z_a[2 * pairs + r], z_b[2 * pairs + r])
                right = jnp.where(to_right, right, 0.0)
                left = jnp.where(to_left, left, 0.0)
                x = jnp.concatenate([whole[k, r], right, left], axis=0)
                full_e[r] = x
            deep.append(x)
    row = iota((8, LANES), 0)
    for q in range(nx):
        left, right = left_right("gz", z_a[3 * pairs + q], z_b[3 * pairs + q])
        for k in range(4):
            x = jnp.where(row < 2 * has_right, roll(right, -2 * k, 0), 0.0)
            z_halo[k, q] = jnp.where(row >= 8 - 2 * has_left, roll(left, 6 - 2 * k, 0), x)
    columns = deep_edges(deep[: 4 * pairs])
    half = len(columns) // 2
    columns_e = deep_edges(deep[4 * pairs :])
    behind = pair_edges(lambda i: [z_halo[i, q] for q in range(nx)], 4, 8)
    for m, out in enumerate((y_a, y_b)):
        toward = high_side("gy", m)
        parts = [
            strip(columns[j], columns[j + half], toward, 8) for j in range(half)
        ] + columns_e
        for i in range(nz // 8):
            parts.append(y_strip(edges[0, pl.ds(8 * i, 8)], edges[1, pl.ds(8 * i, 8)], toward))
        parts.append(y_strip(behind[0], behind[1], toward))
        n = 0
        for x in parts:
            for i in range(x.shape[0] // 8):
                out[n] = x[8 * i : 8 * i + 8]
                n += 1


def sixth_pack(y_a, y_b, z_halo, halo_full, x_rim):
    tiles = halo_full.shape[1] // 8
    first = y_a.shape[0] - tiles
    for i in range(tiles):
        for j, x in enumerate(merge_y(y_a[first + i], y_b[first + i])):
            halo_full[j, pl.ds(8 * i, 8)] = x
    nx = z_halo.shape[1]

    def rim(plane):
        return [rows_of([(z_halo[k, plane(1)], 2 * k, 2 * k - 1, 2) for k in range(4)])]

    pack_rim(x_rim, rim, lambda j: halo_full[j], 4, 1, nx)


def coarse_solve(full, full_e, y_a, y_b, main, halo, ca, cb, force, e, w0, w1, w2, w3, w4, w5, deep_e, grown):
    pairs, rows = full.shape[1:3]
    deep = full_e.shape[1]
    planes = 2 * pairs
    own = main.shape[1] - 2
    cz = rows - 8
    half = LANES // 2
    _, zl, zr = place("gz")
    _, yl, yr = place("gy")
    gx = lax.axis_index("gx")

    def inside(rows, width):
        lane = iota((rows, LANES), 1)
        row = iota((rows, LANES), 0)
        kept = (row < cz + width * zr) | (row >= rows - width * zl)
        return kept & ((lane < half + SLOT * yr) | (lane >= LANES - SLOT * yl))

    zero = jnp.zeros((rows, LANES), F32)
    w = (w0, w1, w2, w3, w4, w5)
    for k in range(4):
        for p in (0, planes + 1):
            ca[k, p] = zero
            cb[k, p] = zero
    e[0] = zero
    e[planes + 1] = zero
    deep_e[0] = jnp.zeros((deep, LANES), F32)
    deep_e[planes + 1] = jnp.zeros((deep, LANES), F32)

    tiles, deep_tiles = rows // 8, deep // 8
    count = pairs // 2
    columns = []

    def taken(ref, n, tiles):
        return jnp.concatenate([ref[n + i] for i in range(tiles)], axis=0)

    seconds = []
    for j in range(count):
        left, right = left_right("gy", taken(y_a, j * tiles, tiles), taken(y_b, j * tiles, tiles))
        spot = iota(left.shape, 1) % 16
        columns.append(jnp.where(spot < 8, left, roll(right, 8, 1)))
        seconds.append(jnp.where(spot < 8, roll(left, -8, 1), right))
    columns += seconds
    columns_e = []
    for j in range(-(-pairs // 4)):
        n = count * tiles + j * deep_tiles
        left, right = left_right("gy", taken(y_a, n, deep_tiles), taken(y_b, n, deep_tiles))
        spot = iota(left.shape, 1) % 16
        columns_e.append(jnp.where(spot < 8, left, right))

    def whole_plane(pair, columns, n, s):
        lane = iota(pair.shape, 1)
        last, first = 2 * n + 1 - s, 2 * n + s
        low = roll(columns[first // 8], half - 16 * (first % 8) - 8, 1)
        high = roll(columns[last // 8], LANES - 8 - 16 * (last % 8), 1)
        x = jnp.where(lane < half, roll(pair, -s * half, 1), low)
        return jnp.where(lane < LANES - 8, x, high)

    near, far = inside(rows, 4), inside(deep, 8)
    for r in range(pairs):
        for s in range(2):
            p = 2 * r + s
            x = jnp.where(far, whole_plane(full_e[r], columns_e, r, s), 0.0)
            deep_e[p + 1] = x
            e[p + 1] = fold_rows(x)
            for k in range(4):
                x = whole_plane(full[k, r], columns, k * pairs + r, s)
                force[k, p] = jnp.where(near, x, 0.0)

    def shifts(x):
        return (
            roll(x, LANES - 1, 1),
            roll(x, 1, 1),
            roll(x, x.shape[0] - 1, 0),
            roll(x, 1, 0),
        )

    def two_by_two(width, body):
        lo = jnp.maximum(gx * own - width, 0)
        hi = jnp.minimum(gx * own + own + width, planes)
        steps = (hi - lo + 1) // 2
        lo = jnp.minimum(lo, planes - 2 * steps)

        def step(i, carry):
            body(lo + 2 * i + 1)
            body(lo + 2 * i + 2)
            return carry

        lax.fori_loop(0, steps, step, 0)

    def start(p):
        x = deep_e[p]
        up, down = x + deep_e[p + 1], x + deep_e[p - 1]
        w0[p] = fold_rows(up)
        total = up + down
        for n, y in enumerate(shifts(x)):
            total += x + y
            w[1 + n][p] = fold_rows(x + y)
        factor = jnp.where(near, fold_rows(relax_weight / total), 0.0)
        w5[p] = factor
        for k in range(3):
            ca[k, p] = factor * force[k, p - 1]
        ca[3, p] = e[p] * force[3, p - 1]

    w0[0] = e[0] + e[1]
    two_by_two(planes, start)

    def sweep(src, dst, width):
        def body(p):
            wxp, wxm = w0[p], w0[p - 1]
            wyp, wym, wzp, wzm = w1[p], w2[p], w3[p], w4[p]
            x = src[3, p]
            around = shifts(x)
            up, down = src[3, p + 1], src[3, p - 1]
            spread = 0.0
            for k in range(3):
                u = src[k, p]
                yp, ym, zp, zm = shifts(u)
                xp, xm = src[k, p + 1], src[k, p - 1]
                total = force[k, p - 1] - 2.0 * terms(k, up, down, *around)
                total += wxp * xp + wxm * xm
                total += wyp * yp + wym * ym
                total += wzp * zp + wzm * zm
                spread += terms(k, xp, xm, yp, ym, zp, zm)
                dst[k, p] = jnp.where(near, 0.4 * u + w5[p] * total, 0.0)
            dst[3, p] = jnp.where(near, x + e[p] * (force[3, p - 1] - 0.125 * spread), 0.0)

        two_by_two(width, body)

    sweep(ca, cb, 3)
    sweep(cb, ca, 2)
    sweep(ca, cb, 1)

    lane = iota((LANES, 2 * LANES), 1)
    cell = iota((LANES, 2 * LANES), 0)
    spot = lane % SLOT
    wanted = jnp.where(spot < 4, LANES - 2, half - 2) + spot // 2
    slot = (lane - LANES) // SLOT
    column = jnp.zeros((4 * rows, LANES), F32)
    first = gx * own

    def grow(ref, index, x):
        ref[index + (pl.ds(0, cz, stride=2),)] = x[:cz]
        ref[index + (pl.ds(1, cz, stride=2),)] = x[:cz]
        grown[pl.ds(0, 8, stride=2)] = x[cz:]
        grown[pl.ds(1, 8, stride=2)] = x[cz:]
        r = iota((8, LANES), 0)
        tail = jnp.where(r < 4, grown[pl.ds(0, 8)], grown[pl.ds(8, 8)])
        ref[index + (pl.ds(2 * cz, 8),)] = tail

    for i in range(own + 2):
        x = jnp.concatenate([cb[k, first + i] for k in range(4)], axis=0)
        here = (lane >= LANES) & ((slot + 1) // 2 - 1 == i) & (cell == wanted)
        chosen = (here | ((lane < LANES) & (lane // 2 == cell))).astype(F32)
        wide = jnp.dot(x, chosen, precision=lax.Precision.HIGHEST, preferred_element_type=F32)
        for k in range(4):
            grow(main, (k, i), wide[k * rows : (k + 1) * rows, :LANES])
        column += wide[:, LANES:]
    for k in range(4):
        grow(halo, (k,), column[k * rows : (k + 1) * rows])


def post_smooth(
    e, halo_e, force, halo_f, w0, w1, w2, w3, w4, w5, hw,
    fields, z_halo, halo_full, x_fine, x_rim, main, column, v_out, p_out,
    ua, ub, ha, hb, ca, beside,
):
    nx, nz, _ = p_out.shape
    slots = nx + 6
    w = (w0, w1, w2, w3, w4, w5)
    zero = jnp.zeros((nz + 8, LANES), F32)
    for k in range(4):
        for p in (1, 2, nx + 3, nx + 4):
            ua[k, p] = zero
            ub[k, p] = zero
        for q in range(nx):
            i = q // 2 + 1
            ua[k, q + 3, pl.ds(0, nz)] = fields[k, q + 3, pl.ds(0, nz)] + main[k, i, pl.ds(0, nz)]
            ua[k, q + 3, pl.ds(nz, 8)] = z_halo[k, q] + main[k, i, pl.ds(nz, 8)]
        ha[k] = own_slots(halo_full[k % 2], nx, k // 2)
    for m in range(x_fine.shape[0]):
        right, valid = x_side(m)
        there = truth(valid, (nz, LANES))
        there8 = truth(valid, (8, LANES))
        tiles = (nz + 8) // 8
        side = jnp.concatenate([x_rim[m, 1 + r] for r in range(tiles)], axis=0)
        i = right * (nx // 2 + 1)
        for k in range(4):
            for j in range(2):
                at = 1 + right * (nx + 2) + j
                x = x_fine[m, 2 * k + j] + main[k, i, pl.ds(0, nz)]
                ua[k, at, pl.ds(0, nz)] = jnp.where(there, x, 0.0)
            x = roll(x_rim[m, 0], -2 * k, 0) + main[k, i, pl.ds(nz, 8)]
            ua[k, 2 + right * (nx + 1), pl.ds(nz, 8)] = jnp.where(there8, x, 0.0)
            x, kept = rim_halo(side, k, SLOT, 1, right, valid, nx)
            ha[k] = jnp.where(kept, x, ha[k])
    masks = fine_masks(nz + 8, slots)
    for k in range(4):
        ha[k] = jnp.where(masks[1], ha[k] + column[k], 0.0)
    fill_edges(ca, ua, range(1, slots - 1))
    main_sweep(ua, ha, ub, w, e, force, 1, masks[0], beside)
    halo_sweep(ha, ca, hb, hw, halo_e, halo_f, masks[1])

    spread_halo(hb, beside, slots, 0, full=False)

    def last(p):
        new = main_operator(ub, beside, w, force, p, nz)
        new = relaxed(*new, w5[p, pl.ds(0, nz)], e[p, pl.ds(0, nz)])
        for k in range(3):
            v_out[k, p - 3] = new[k]
        p_out[p - 3] = new[3]

    over_planes(slots, 0, last)


def local(velocity, pressure, viscosity, body_force):
    nx, nz, ny = pressure.shape
    if ny != LANES or nx * SLOT * 2 != LANES or nz % 16:
        raise ValueError("unsupported block")
    sides = x_messages()
    rows, slots = nz + 8, nx + 6
    inputs = [velocity, pressure, viscosity, body_force]
    block = (nz, LANES)

    z_shape = (3 * nx, 8, LANES)
    half = (nx // 2,) + block
    *staged, y_a, y_b = call(
        first_pack, [half] * 16 + [(2,) + block] * 2, inputs, outside=4, copies=16
    )
    x_main, z_a, z_b = call(side_pack, [(sides, 21) + block, z_shape, z_shape], staged)
    y_a, y_b = swap(y_a, "gy", 0), swap(y_b, "gy", 1)
    x_main = swap_x(x_main)
    halo, z_b = call(second_pack, [(4,) + block, z_shape], [z_b, y_a, y_b])
    (z_a,) = call(second_pack_near, [z_shape], [z_a, halo])
    z_a, z_b = swap(z_a, "gz", 0), swap(z_b, "gz", 1)
    tiles = rows // 8
    z_first, halo_first, x_first = call(
        third_pack,
        [(8, nx, 8, LANES), (4, rows, LANES), (sides, 6 + tiles, 8, LANES)],
        [z_a, z_b, halo],
    )
    x_first = swap_x(x_first)

    spread, column = (4, slots, rows, LANES), (4, rows, LANES)
    started = [(slots, rows, LANES), (rows, LANES), (3, slots, rows, LANES), (3, rows, LANES)]
    started += [(slots, rows, LANES)] * 6 + [spread, spread] + [column] * 3 + [(rows, LANES)]
    started += [(5, nx // 2, nz, LANES)]
    state = call(
        pre_start,
        started,
        [*staged, z_first, halo_first, x_main],
        [(7, rows, LANES), column, column, spread],
        cost=4,
    )
    *operator, fields, _, _, _, _, _, _, factors, own = call(
        pre_smooth,
        started + [(7, rows, LANES), (5, nx // 4, nz // 2, LANES)],
        [x_first, *state],
        [column, spread],
        cost=8,
        aliases={i + 1: i for i in range(len(started))},
    )
    operator.append(factors)
    edges, x_fine = call(smooth_pack, [(2,) + block, (sides, 8) + block], [fields])
    if lax.axis_size("gx") == 2:
        parts = [own, swap(own, "gx", 0)]
        gather = fourth_pack
    else:
        parts = [lax.all_gather(own, "gx", axis=1, tiled=True)]

        def gather(a, *refs):
            fourth_pack(a, None, *refs)

    x_fine = swap_x(x_fine)
    pairs = lax.axis_size("gx") * (nx // 4)
    z_shape = (3 * pairs + nx, 8, LANES)
    whole, z_a, z_b = call(
        gather, [(5, pairs, nz // 2, LANES), z_shape, z_shape], parts + [fields]
    )
    z_a, z_b = swap(z_a, "gz", 0), swap(z_b, "gz", 1)
    deep = nz // 2 + 16
    shallow = deep - 8
    y_shape = (pairs // 2 * (shallow // 8) + -(-pairs // 4) * (deep // 8) + tiles, 8, LANES)
    full, full_e, z_halo, y_a, y_b = call(
        fifth_pack,
        [(4, pairs, shallow, LANES), (pairs, deep, LANES), (4, nx, 8, LANES), y_shape, y_shape],
        [whole, z_a, z_b, edges],
    )
    y_a, y_b = swap(y_a, "gy", 0), swap(y_b, "gy", 1)
    halo_full, x_rim = call(
        sixth_pack,
        [(2, rows, LANES), (sides, 1 + tiles, 8, LANES)],
        [y_a, y_b, z_halo],
    )
    x_rim = swap_x(x_rim)
    planes = 2 * pairs
    plane = (shallow, LANES)
    grown, beside = call(
        coarse_solve,
        [(4, nx // 2 + 2, rows, LANES), (4, rows, LANES)],
        [full, full_e, y_a, y_b],
        [(4, planes + 2) + plane] * 2
        + [(4, planes) + plane]
        + [(planes + 2,) + plane] * 7
        + [(planes + 2, deep, LANES), (16, LANES)],
        cost=4,
    )
    v_out, p_out = call(
        post_smooth,
        [(3, nx) + block, (nx,) + block],
        operator + [fields, z_halo, halo_full, x_fine, x_rim, grown, beside],
        [spread] * 2 + [column] * 3 + [spread],
        cost=8,
    )
    return v_out, p_out


def swap_x(array):
    if array.shape[0] == 1:
        return swap(array, "gx", 0)
    parts = [swap(array[m], "gx", m) for m in range(2)]
    return jnp.stack(parts)


def solution(mesh):
    return jax.shard_map(
        local,
        mesh=mesh,
        in_specs=(
            P(None, "gx", "gz", "gy"),
            P("gx", "gz", "gy"),
            P("gx", "gz", "gy"),
            P(None, "gx", "gz", "gy"),
        ),
        out_specs=(P(None, "gx", "gz", "gy"), P("gx", "gz", "gy")),
        check_vma=False,
    )
```

```python
import jax
import jax.numpy as jnp
from jax import lax
from jax.experimental import pallas as pl
from jax.experimental.pallas import tpu as pltpu
from jax.sharding import PartitionSpec as P

LANES = 128
SLOT = 8
F32 = jnp.float32
relax_weight = 0.6
HELD = 846 * 2**16
Z_PLACES = (
    ((0, 0, 3), (1, 3, 3), (5, 6, 2)),
    ((2, 0, 3), (3, 3, 3), (6, 6, 2)),
    ((4, 0, 3), (7, 3, 2)),
)


def call(body, outs, args, scratch=(), cost=1, outside=0, copies=0, aliases=None):
    return pl.pallas_call(
        body,
        out_shape=[jax.ShapeDtypeStruct(shape, F32) for shape in outs],
        in_specs=[pl.BlockSpec(memory_space=pltpu.HBM)] * outside
        + [pl.BlockSpec(memory_space=pltpu.VMEM)] * (len(args) - outside),
        out_specs=[pl.BlockSpec(memory_space=pltpu.VMEM)] * len(outs),
        scratch_shapes=[pltpu.VMEM(shape, F32) for shape in scratch]
        + [pltpu.SemaphoreType.DMA((copies,))] * (copies > 0),
        input_output_aliases=aliases or {},
        compiler_params=pltpu.CompilerParams(vmem_limit_bytes=HELD if outside else 40 * 2**20),
        cost_estimate=pl.CostEstimate(
            flops=cost * 10**6, bytes_accessed=cost * 10**6, transcendentals=0
        ),
    )(*args)


def swap(array, axis, which):
    count = lax.axis_size(axis)
    if axis != "gx" and which == 1:
        ys, zs = lax.axis_size("gy"), lax.axis_size("gz")
        pairs = []
        for y in range(ys):
            for z in range(zs):
                i = y if axis == "gy" else z
                j = i + 1 if i % 2 else i - 1
                if axis == "gy":
                    to = (j, z) if 0 <= j < count else (y, z ^ 1)
                else:
                    to = (y, j) if 0 <= j < count else (y ^ 1, z)
                pairs.append((y * zs + z, to[0] * zs + to[1]))
        return lax.ppermute(array, ("gy", "gz"), pairs)
    pairs = []
    for i in range(which, count, 2):
        j = (i + 1) % count
        pairs += [(i, j), (j, i)]
    return lax.ppermute(array, axis, pairs)


FIXED = []


def by_sides(body):
    def kernel(*refs):
        count = lax.axis_size("gx")
        _, xl, xr = place("gx")
        for sides in [(0, 1), (1, 0), (1, 1)][: 2 if count == 2 else 3]:

            def branch(sides=sides):
                FIXED.append(sides)
                body(*refs)
                FIXED.pop()

            pl.when((xl == sides[0]) & (xr == sides[1]))(branch)

    return kernel


def place(axis):
    if axis == "gx" and FIXED:
        return (None,) + FIXED[-1]
    i = lax.axis_index(axis)
    last = lax.axis_size(axis) - 1
    return i, jnp.where(i > 0, 1, 0), jnp.where(i < last, 1, 0)


def iota(shape, dim):
    return lax.broadcasted_iota(jnp.int32, shape, dim)


def truth(flag, shape):
    return jnp.full(shape, flag, jnp.int32) > 0


def roll(x, shift, dim):
    if isinstance(shift, int):
        shift %= x.shape[dim]
        return x if shift == 0 else pltpu.roll(x, shift, dim)
    return pltpu.roll(x, lax.rem(shift + 2 * x.shape[dim], x.shape[dim]), dim)


def high_side(axis, message):
    return jnp.where(lax.axis_index(axis) % 2 == message, 1, 0)


def left_right(axis, a, b):
    odd = truth(lax.axis_index(axis) % 2, a.shape)
    return jnp.where(odd, a, b), jnp.where(odd, b, a)


def x_messages():
    return 1 if lax.axis_size("gx") == 2 else 2


def pair_edges(planes, fields, rows):
    lane = iota((rows, LANES), 1) // SLOT
    half = fields // 2
    out = []
    for j in range(half):
        total = jnp.zeros((rows, LANES), F32)
        for part in range(2):
            for q, x in enumerate(planes(j + part * half)):
                slot = q + part * (LANES // SLOT // 2)
                total = jnp.where(lane == slot, roll(x, slot * SLOT + 4, 1), total)
        out.append(total)
    return out


def merge_y(a, b):
    _, has_left, has_right = place("gy")
    left, right = left_right("gy", a, b)
    spot = iota(a.shape, 1) % SLOT
    kept = (spot < 4 * has_left) | (spot >= SLOT - 4 * has_right)
    first = jnp.where(spot < 4, left, roll(right, 4, 1))
    second = jnp.where(spot < 4, roll(left, -4, 1), right)
    return jnp.where(kept, first, 0.0), jnp.where(kept, second, 0.0)


class Staged:
    def __init__(self, refs):
        self.refs = refs
        self.half, self.nz = refs[0].shape[:2]
        self.nx = 2 * self.half

    def __getitem__(self, index):
        i, q = index[:2]
        return self.refs[2 * i + q // self.half][(q % self.half,) + index[2:]]


def first_pack(v_in, p_in, e_in, f_in, *refs):
    staged = Staged(refs[:16])
    y_a, y_b, arrived = refs[16:]
    nx, nz = staged.nx, staged.nz
    loads = []
    for n in range(16):
        i, planes = n // 2, pl.ds(n % 2 * staged.half, staged.half)
        if i < 3:
            part = v_in.at[i, planes]
        elif i < 5:
            part = (p_in, e_in)[i - 3].at[planes]
        else:
            part = f_in.at[i - 5, planes]
        loads.append(pltpu.make_async_copy(part, refs[n], arrived.at[n]))
    for load in loads:
        load.start()
    for load in loads:
        load.wait()
    edges = pair_edges(lambda i: [staged[i, q] for q in range(nx)], 8, nz)
    for m, out in enumerate((y_a, y_b)):
        for j in range(2):
            out[j] = y_strip(edges[j], edges[j + 2], high_side("gy", m))


def side_pack(*refs):
    staged = Staged(refs[:16])
    x_main, z_a, z_b = refs[16:]
    nx, nz = staged.nx, staged.nz
    for m in range(x_main.shape[0]):
        top = truth(high_side("gx", m), (nz, LANES))
        n = 0
        for i in range(8):
            width = 3 if i < 5 else 2
            for j in range(width):
                x_main[m, n] = jnp.where(top, staged[i, nx - width + j], staged[i, j])
                n += 1
    low, high = pl.ds(0, 8), pl.ds(nz - 8, 8)
    for q in range(nx):
        for n, fields in enumerate(Z_PLACES):
            for m, out in enumerate((z_a, z_b)):
                out[3 * q + n] = z_strip(
                    [(staged[i, q, low], staged[i, q, high], at, rows) for i, at, rows in fields],
                    high_side("gz", m),
                )


def strip(first, second, toward_right, width):
    right = truth(toward_right, first.shape)
    spot = iota(first.shape, 1) % (2 * width)
    first = jnp.where(right, first, roll(first, -width, 1))
    second = jnp.where(right, roll(second, width, 1), second)
    return jnp.where(spot < width, first, second)


def y_strip(first, second, toward_right):
    return strip(first, second, toward_right, SLOT // 2)


def z_strip(parts, toward_right):
    right = truth(toward_right, (8, LANES))
    return rows_of(
        [
            (jnp.where(right, roll(high, at + rows, 0), roll(low, at, 0)), 0, at, rows)
            for low, high, at, rows in parts
        ]
    )


def z_tail(halo, first, out, message):
    nz = halo.shape[1]
    row = iota((8, LANES), 0)
    for n in range(first.shape[0]):
        out[n] = first[n]
    for j in range(4):
        tiles = halo[j, pl.ds(0, 8)], halo[j, pl.ds(nz - 8, 8)]
        x = z_strip([tiles + (5, 3)], high_side("gz", message))
        out[3 * j + 2] = jnp.where(row < 5, first[3 * j + 2], x)


def second_pack(z_first, y_a, y_b, halo, z_b):
    for j in range(2):
        halo[j], halo[j + 2] = merge_y(y_a[j], y_b[j])
    z_tail(halo, z_first, z_b, 1)


def second_pack_near(z_first, halo, z_a):
    z_tail(halo, z_first, z_a, 0)


def z_tile(a, b, at, rows):
    _, has_left, has_right = place("gz")
    left, right = left_right("gz", a, b)
    row = iota(a.shape, 0)
    x = jnp.where(row < rows * has_right, roll(right, -at, 0), 0.0)
    return jnp.where(row >= 8 - rows * has_left, roll(left, 8 - at - rows, 0), x)


def third_pack(z_a, z_b, halo, z_halo, halo_full, x_rim):
    nx = z_halo.shape[1]
    nz = halo.shape[1]
    for q in range(nx):
        for n, fields in enumerate(Z_PLACES):
            for i, at, rows in fields:
                z_halo[i, q] = z_tile(z_a[3 * q + n], z_b[3 * q + n], at, rows)
    for j in range(4):
        halo_full[j, pl.ds(0, nz)] = halo[j]
        halo_full[j, pl.ds(nz, 8)] = z_tile(z_a[3 * j + 2], z_b[3 * j + 2], 5, 3)

    def tiles(plane):
        out = [
            rows_of([(z_halo[i, plane(1)], 0, 6, 4), (z_halo[i, plane(2)], 3, 2, 2)])
            for i in range(5)
        ]
        force = zip((0, 3, 5), (7, 2, 4))
        out.append(
            rows_of([(z_halo[5 + k, plane(1)], at, row, 2) for k, (at, row) in enumerate(force)])
        )
        return out

    pack_rim(x_rim, tiles, lambda j: halo_full[j], 8, 2, nx)


def rows_of(parts):
    row = iota((8, LANES), 0)
    total = jnp.zeros((8, LANES), F32)
    for x, shift, first, count in parts:
        total = jnp.where((row - first) % 8 < count, roll(x, shift, 0), total)
    return total


def pack_rim(x_rim, tiles, halo_pair, fields, planes, nx):
    half = fields // 2
    stride = LANES // 8 if fields == 8 else SLOT
    for m in range(x_rim.shape[0]):
        high = high_side("gx", m)
        done = tiles(lambda d, high=high: high * (nx - 2 * d + 1) + d - 1)
        for n, x in enumerate(done):
            x_rim[m, n] = x
        pairs = [halo_pair(j) for j in range(half)]
        rows = pairs[0].shape[0]
        column = iota((rows, LANES), 1) // stride
        first = high * (nx - planes) * SLOT
        total = jnp.zeros((rows, LANES), F32)
        for i in range(fields):
            at = i * stride - first - (i // half) * (LANES // 2)
            total = jnp.where(column == i, roll(pairs[i % half], at + LANES, 1), total)
        for r in range(rows // 8):
            x_rim[m, len(done) + r] = total[8 * r : 8 * r + 8]


def main_shifts(x, beside, kept):
    rows = x.shape[0]
    y, beside = x[:kept], beside[:kept]
    lane = iota(y.shape, 1)
    return (
        roll(jnp.where(lane == 0, beside, y), LANES - 1, 1),
        roll(jnp.where(lane == LANES - 1, beside, y), 1, 1),
        roll(x, rows - 1, 0)[:kept],
        roll(x, 1, 0)[:kept],
    )


def halo_shifts(x, edge):
    spot = iota(x.shape, 1) % SLOT
    rows = x.shape[0]
    return (
        roll(x, LANES - SLOT, 1),
        roll(x, SLOT, 1),
        roll(jnp.where(spot == 4, edge, x), LANES - 1, 1),
        roll(jnp.where(spot == 3, edge, x), 1, 1),
        roll(x, rows - 1, 0),
        roll(x, 1, 0),
    )


def main_weights(e, halo_e, w, width, chosen, faces):
    slots = e.shape[0]
    for p in faces:
        w[0][p] = e[p] + e[p + 1]

    def body(p):
        x = e[p]
        total = w[0][p] + w[0][p - 1]
        for n, y in enumerate(main_shifts(x, roll(halo_e[...], LANES - SLOT * p - 4, 1), x.shape[0])):
            total += x + y
            w[1 + n][p] = x + y
        w[5][p] = relax_weight / total

    over_planes(slots, width, body, chosen)


def halo_weights(e, edge_e, w):
    x = e[...]
    total = jnp.zeros_like(x)
    for n, y in enumerate(halo_shifts(x, edge_e[...])):
        total += x + y
        w[n] = x + y
    w[6] = relax_weight / total


def terms(k, up, down, yp, ym, zp, zm):
    return (up - down, zp - zm, yp - ym)[k]


def spread_halo(halo, beside, slots, width, chosen=None, full=True):
    kept = beside.shape[2] - (0 if full else 8)

    def body(p):
        for k in range(4):
            beside[k, p, pl.ds(0, kept)] = roll(halo[k][:kept], LANES - SLOT * p - 4, 1)

    over_planes(slots, width, body, chosen)


def main_operator(src, beside, w, force, p, kept):
    def at(ref, *index):
        return ref[index + (pl.ds(0, kept),)]

    wxp, wxm, wyp, wym, wzp, wzm = (
        at(ref, q) for ref, q in zip((w[0],) + w[:5], (p, p - 1, p, p, p, p))
    )
    around = main_shifts(src[3, p], at(beside, 3, p), kept)
    up, down = at(src, 3, p + 1), at(src, 3, p - 1)
    olds, sums, spread = [], [], 0.0
    for k in range(3):
        yp, ym, zp, zm = main_shifts(src[k, p], at(beside, k, p), kept)
        xp, xm = at(src, k, p + 1), at(src, k, p - 1)
        total = at(force, k, p) - terms(k, up, down, *around)
        total += wxp * xp + wxm * xm
        total += wyp * yp + wym * ym
        total += wzp * zp + wzm * zm
        spread += terms(k, xp, xm, yp, ym, zp, zm)
        olds.append(at(src, k, p))
        sums.append(total)
    olds.append(at(src, 3, p))
    return olds, sums, spread


def halo_operator(halo, edge, w, force):
    x = halo[3]
    px = halo_shifts(x, edge[3])
    olds, sums, spread = [], [], 0.0
    for k in range(3):
        u = halo[k]
        around = halo_shifts(u, edge[k])
        total = force[k] - terms(k, *px)
        for n in range(6):
            total += w[n] * around[n]
        spread += terms(k, *around)
        olds.append(u)
        sums.append(total)
    olds.append(x)
    return olds, sums, spread


def relaxed(olds, sums, spread, factor, e):
    new = [0.4 * olds[k] + factor * sums[k] for k in range(3)]
    return new + [olds[3] - 0.25 * e * spread]


def edges_of(plane, slots, total=None):
    shape = plane(slots[0]).shape
    slot = iota(shape, 1) // SLOT
    total = jnp.zeros(shape, F32) if total is None else total
    for p in slots:
        total = jnp.where(slot == p, roll(plane(p), p * SLOT + 4, 1), total)
    return total


def fill_edges(edge, src, slots, fresh=True):
    for k in range(4):
        edge[k] = edges_of(lambda p: src[k, p], slots, None if fresh else edge[k])


def fine_masks(rows, slots):
    nz = rows - 8
    _, zl, zr = place("gz")
    _, yl, yr = place("gy")
    _, xl, xr = place("gx")
    r = iota((8, LANES), 0)
    tile = (r < 4 * zr) | (r >= 8 - 4 * zl)
    r = iota((rows, LANES), 0)
    lane = iota((rows, LANES), 1)
    spot, slot = lane % SLOT, lane // SLOT
    column = (r < nz + 4 * zr) | (r >= rows - 4 * zl)
    column &= (spot < 4 * yl) | (spot >= SLOT - 4 * yr)
    column &= (slot >= 3 - 3 * xl) & (slot < slots - 3 + 3 * xr)
    return tile, column


def main_sweep(src, halo, dst, w, e, force, width, tile, beside, chosen=None):
    nz = src.shape[2] - 8
    slots = src.shape[1]

    def body(p):
        new = relaxed(*main_operator(src, beside, w, force, p, nz + 8), w[5][p], e[p])
        for k in range(4):
            x = new[k]
            dst[k, p, pl.ds(0, nz)] = x[:nz]
            dst[k, p, pl.ds(nz, 8)] = jnp.where(tile, x[nz:], 0.0)

    spread_halo(halo, beside, slots, width, chosen)
    over_planes(slots, width, body, chosen)


def halo_sweep(halo, edge, halo_dst, hw, halo_e, halo_f, column):
    new = relaxed(*halo_operator(halo, edge, hw, halo_f), hw[6], halo_e[...])
    for k in range(4):
        halo_dst[k] = jnp.where(column, new[k], 0.0)


def over_planes(slots, width, body, chosen=None):
    _, xl, xr = place("gx")
    for p in range(3 - width, slots - 3 + width):
        wanted = True if chosen is None else chosen(p)
        if wanted and (p >= 3 or xl) and (p < slots - 3 or xr):
            body(p)


def own_slots(x, nx, part):
    lane = iota(x.shape, 1)
    x = roll(x, 3 * SLOT - part * (LANES // 2), 1)
    return jnp.where((lane >= 3 * SLOT) & (lane < (3 + nx) * SLOT), x, 0.0)


def x_side(m):
    _, has_left, has_right = place("gx")
    if lax.axis_size("gx") == 2:
        return has_right, 1
    right = high_side("gx", m)
    return right, jnp.where(right > 0, has_right, has_left)


def rim_halo(x, t, stride, planes, right, valid, nx):
    base = right * (nx + 3) + (1 - right) * (3 - planes)
    lane = iota(x.shape, 1)
    x = roll(x, base * SLOT - t * stride + LANES, 1)
    kept = (lane >= base * SLOT) & (lane < (base + planes * valid) * SLOT)
    return jnp.where(kept, x, 0.0), kept


def viscosity_force(staged, z_halo, halo_full, x_main, e, halo_e, force, halo_f):
    nx, nz = staged.nx, staged.nz
    slots = nx + 6
    zero = jnp.zeros((nz + 8, LANES), F32)
    for p in list(range(3)) + list(range(nx + 3, slots)):
        e[p] = zero
        for k in range(3):
            force[k, p] = zero
    for q in range(nx):
        e[q + 3, pl.ds(0, nz)] = staged[4, q]
        e[q + 3, pl.ds(nz, 8)] = z_halo[4, q]
        for k in range(3):
            force[k, q + 3, pl.ds(0, nz)] = 2.0 * staged[5 + k, q]
            force[k, q + 3, pl.ds(nz, 8)] = 2.0 * z_halo[5 + k, q]
    halo_e[...] = own_slots(halo_full[0], nx, 1)
    for k in range(3):
        halo_f[k] = 2.0 * own_slots(halo_full[k + 1], nx, 1)
    for m in range(x_main.shape[0]):
        right, valid = x_side(m)
        there = truth(valid, (nz, LANES))
        for j in range(3):
            e[right * (nx + 3) + j, pl.ds(0, nz)] = jnp.where(there, x_main[m, 12 + j], 0.0)
        for j in range(2):
            at = right * (nx + 2) + 1 + j
            for k in range(3):
                force[k, at, pl.ds(0, nz)] = jnp.where(there, 2.0 * x_main[m, 15 + 2 * k + j], 0.0)


def first_fields(staged, z_halo, halo_full, x_main, u, other, halo):
    nx, nz = staged.nx, staged.nz
    slots = nx + 6
    zero = jnp.zeros((nz + 8, LANES), F32)
    for k in range(4):
        for p in list(range(3)) + list(range(nx + 3, slots)):
            u[k, p] = zero
            other[k, p] = zero
        for q in range(nx):
            u[k, q + 3, pl.ds(0, nz)] = staged[k, q]
            u[k, q + 3, pl.ds(nz, 8)] = z_halo[k, q]
        halo[k] = own_slots(halo_full[k], nx, 0)
    for m in range(x_main.shape[0]):
        right, valid = x_side(m)
        there = truth(valid, (nz, LANES))
        for k in range(4):
            for j in range(3):
                x = jnp.where(there, x_main[m, 3 * k + j], 0.0)
                u[k, right * (nx + 3) + j, pl.ds(0, nz)] = x


def add_rims(x_rim, nx, u, halo, e, halo_e, force, halo_f, edge, edge_e):
    nz = e.shape[1] - 8
    tiles = (nz + 8) // 8
    tail = pl.ds(nz, 8)
    slot = iota((8, LANES), 1) // SLOT
    for m in range(x_rim.shape[0]):
        right, valid = x_side(m)
        there = truth(valid, (8, LANES))
        column = jnp.concatenate([x_rim[m, 6 + r] for r in range(tiles)], axis=0)
        near = right * (nx + 1) + 2
        far = near + 2 * right - 1
        for k in range(5):
            x = jnp.where(there, x_rim[m, k], 0.0)
            for p, y in ((near, x), (far, roll(x, -3, 0))):
                moved = roll(y, p * SLOT + 4, 1)
                if k < 4:
                    u[k, p, tail] = y
                    edge[k, tail] = jnp.where(slot == p, moved, edge[k, tail])
                else:
                    e[p, tail] = y
                    edge_e[tail] = jnp.where(slot == p, moved, edge_e[tail])
            x, kept = rim_halo(column, k, LANES // 8, 2, right, valid, nx)
            if k < 4:
                halo[k] = jnp.where(kept, x, halo[k])
            else:
                halo_e[...] = jnp.where(kept, x, halo_e[...])
        x = jnp.where(there, 2.0 * x_rim[m, 5], 0.0)
        for k, at in enumerate((0, 3, 5)):
            force[k, near, tail] = roll(x, -at, 0)
            x_k, kept = rim_halo(column, 5 + k, LANES // 8, 2, right, valid, nx)
            halo_f[k] = jnp.where(kept, 2.0 * x_k, halo_f[k])


def early(nx, sweep):
    _, xl, xr = place("gx")

    def chosen(p):
        if 3 + sweep <= p < nx + 3 - sweep:
            return True
        if 3 <= p < nx + 3:
            return xl == 0 if p < 3 + sweep else xr == 0
        return False

    return chosen


def early_block(nx):
    _, xl, xr = place("gx")
    return lambda q: xl == 0 if 2 * q + 5 <= nx else xr == 0 if 2 * q + 2 >= 5 else False


def late(chosen):
    return lambda p: not chosen(p)


def inside_slots(slots, width, chosen=None):
    _, xl, xr = place("gx")
    inside = range(3 - width * xl, slots - 3 + width * xr)
    return [p for p in inside if chosen is None or chosen(p)]


def residuals(u, halo, beside, w, force, e, summed, chosen):
    _, blocks, nz, _ = summed.shape
    slots = u.shape[1]
    spread_halo(halo, beside, slots, 0, lambda p: chosen((p - 3) // 2), False)

    def body(q):
        totals = [0.0] * 5
        for j in range(2):
            p = 2 * q + 3 + j
            olds, sums, spread = main_operator(u, beside, w, force, p, nz)
            diagonal = (w[0][p] + w[0][p - 1] + w[1][p] + w[2][p] + w[3][p] + w[4][p])[:nz]
            for k in range(3):
                totals[k] += sums[k] - diagonal * olds[k]
            totals[3] += spread
            totals[4] += e[p, pl.ds(0, nz)]
        for k in range(5):
            summed[k, q] = totals[k]

    for q in range(blocks):
        if chosen(q):
            body(q)


def pre_start(*refs):
    pre_start_on(Staged(refs[:16]), *refs[16:])


def pre_start_on(
    staged, z_halo, halo_full, x_main,
    e, halo_e, force, halo_f, w0, w1, w2, w3, w4, w5, ua, ub, ha, ca, cb, edge_e, summed,
    hw, hb, hc, beside,
):
    nx, nz = staged.nx, staged.nz
    slots = nx + 6
    w = (w0, w1, w2, w3, w4, w5)
    viscosity_force(staged, z_halo, halo_full, x_main, e, halo_e, force, halo_f)
    first_fields(staged, z_halo, halo_full, x_main, ua, ub, ha)
    tile, column = fine_masks(nz + 8, slots)
    fill_edges(ca, ua, inside_slots(slots, 3))
    edge_e[...] = edges_of(lambda p: e[p], inside_slots(slots, 3))
    main_weights(e, halo_e, w, 0, early(nx, 1), range(2, nx + 3))
    main_sweep(ua, ha, ub, w, e, force, 0, tile, beside, early(nx, 1))
    halo_weights(halo_e, edge_e, hw)
    halo_sweep(ha, ca, hb, hw, halo_e, halo_f, column)
    fill_edges(cb, ub, inside_slots(slots, 0, early(nx, 1)))
    main_sweep(ub, hb, ua, w, e, force, 0, tile, beside, early(nx, 2))
    halo_sweep(hb, cb, hc, hw, halo_e, halo_f, column)
    residuals(ua, hc, beside, w, force, e, summed, early_block(nx))


def pre_smooth(
    x_rim, _e, _halo_e, _force, _halo_f, _w0, _w1, _w2, _w3, _w4, _w5, _ua, _ub, _ha, _ca, _cb,
    _edge_e, _summed, e, halo_e, force, halo_f, w0, w1, w2, w3, w4, w5, ua, ub, ha, ca, cb, edge_e,
    summed, hw, coarse, hb, beside,
):
    slots = e.shape[0]
    nx, nz = slots - 6, e.shape[1] - 8
    w = (w0, w1, w2, w3, w4, w5)
    add_rims(x_rim, nx, ua, ha, e, halo_e, force, halo_f, ca, edge_e)
    tile, column = fine_masks(nz + 8, slots)
    faces = [p for p in range(slots - 1) if not 3 <= p < nx + 2]
    main_weights(e, halo_e, w, 2, late(early(nx, 1)), faces)
    halo_weights(halo_e, edge_e, hw)
    main_sweep(ua, ha, ub, w, e, force, 2, tile, beside, late(early(nx, 1)))
    halo_sweep(ha, ca, hb, hw, halo_e, halo_f, column)
    fill_edges(cb, ub, inside_slots(slots, 2, late(early(nx, 1))), False)
    main_sweep(ub, hb, ua, w, e, force, 1, tile, beside, late(early(nx, 2)))
    halo_sweep(hb, cb, ha, hw, halo_e, halo_f, column)
    residuals(ua, ha, beside, w, force, e, summed, late(early_block(nx)))
    scale = (0.5, 0.5, 0.5, -1.0 / 32.0, 0.125)
    cz = nz // 2
    left = []
    for k in range(5):
        for r in range(nx // 4):
            halves = []
            for s in range(2):
                q = 2 * r + s
                even = summed[k, q, pl.ds(0, cz, stride=2)]
                halves.append((even + summed[k, q, pl.ds(1, cz, stride=2)]) * scale[k])
            left.append(jnp.concatenate(halves, axis=1))
    left = jnp.concatenate(left, axis=0)
    pick = iota((2 * LANES, LANES), 0) // 2 == iota((2 * LANES, LANES), 1)
    out = jnp.dot(
        left, pick.astype(F32), precision=lax.Precision.HIGHEST, preferred_element_type=F32
    )
    for k in range(5):
        for r in range(nx // 4):
            at = (k * (nx // 4) + r) * cz
            coarse[k, r] = out[at : at + cz]


def smooth_pack(fields, edges, x_fine):
    nx, nz = fields.shape[1] - 6, fields.shape[2] - 8
    for m in range(x_fine.shape[0]):
        high = high_side("gx", m)
        for k in range(4):
            for j in range(2):
                x_fine[m, 2 * k + j] = fields[k, 3 + high * (nx - 2) + j, pl.ds(0, nz)]

    def planes(k):
        return [fields[k, q + 3, pl.ds(0, nz)] for q in range(nx)]

    for j, x in enumerate(pair_edges(planes, 4, nz)):
        edges[j] = x


def fourth_pack(own, other, fields, whole, z_a, z_b):
    nx, nz = fields.shape[1] - 6, fields.shape[2] - 8
    pairs = whole.shape[1]
    cz = whole.shape[2]
    gx = lax.axis_index("gx")
    for k in range(5):
        for r in range(pairs):
            if other is None:
                whole[k, r] = own[k, r]
            else:
                mine = truth(jnp.where(gx == r // (pairs // 2), 1, 0), (cz, LANES))
                n = r % (pairs // 2)
                whole[k, r] = jnp.where(mine, own[k, n], other[k, n])
    row = iota((8, LANES), 0) // 2
    for m, out in enumerate((z_a, z_b)):
        right = high_side("gz", m)
        start = pl.multiple_of(right * (cz - 8), 8)
        for r in range(pairs):
            for k in range(2):
                parts = [
                    (whole[k + 2 * h, r, pl.ds(0, 8)], whole[k + 2 * h, r, pl.ds(cz - 8, 8)])
                    + (4 * h, 4)
                    for h in range(2)
                ]
                out[k * pairs + r] = z_strip(parts, right)
            out[2 * pairs + r] = whole[4, r, pl.ds(start, 8)]
        toward = truth(right, (8, LANES))
        for q in range(nx):
            total = jnp.zeros((8, LANES), F32)
            for k in range(4):
                low = roll(fields[k, q + 3, pl.ds(0, 8)], 2 * k, 0)
                high = roll(fields[k, q + 3, pl.ds(nz - 8, 8)], 2 * k - 6, 0)
                total = jnp.where(row == k, jnp.where(toward, high, low), total)
            out[3 * pairs + q] = total


def fold_rows(x):
    own = x.shape[0] - 16
    row = iota((8, LANES), 0)
    halo = jnp.where(row < 4, x[own : own + 8], x[own + 8 :])
    return jnp.concatenate([x[:own], halo], axis=0)


def deep_edges(pairs):
    per = LANES // 16
    columns = []
    for n, x in enumerate(pairs):
        for g in range(2):
            t = (2 * n + g) % per
            x_t = roll(x, 16 * t + 8 - 64 * g, 1)
            if t == 0:
                columns.append(x_t)
            else:
                slot = iota(x.shape, 1) // 16
                columns[-1] = jnp.where(slot == t, x_t, columns[-1])
    return columns


def fifth_pack(whole, z_a, z_b, edges, full, full_e, z_halo, y_a, y_b):
    pairs, cz = whole.shape[1:3]
    nx = z_halo.shape[1]
    nz = edges.shape[1]
    _, has_left, has_right = place("gz")
    to_left = truth(has_left, (8, LANES))
    to_right = truth(has_right, (8, LANES))
    deep = []
    for k in range(5):
        for r in range(pairs):
            if k < 4:
                n = k % 2 * pairs + r
                tile = z_tile(z_a[n], z_b[n], k // 2 * 4, 4)
                x = jnp.concatenate([whole[k, r], tile], axis=0)
                full[k, r] = x
            else:
                left, right = left_right("gz", z_a[2 * pairs + r], z_b[2 * pairs + r])
                right = jnp.where(to_right, right, 0.0)
                left = jnp.where(to_left, left, 0.0)
                x = jnp.concatenate([whole[k, r], right, left], axis=0)
                full_e[r] = x
            deep.append(x)
    row = iota((8, LANES), 0)
    for q in range(nx):
        left, right = left_right("gz", z_a[3 * pairs + q], z_b[3 * pairs + q])
        for k in range(4):
            x = jnp.where(row < 2 * has_right, roll(right, -2 * k, 0), 0.0)
            z_halo[k, q] = jnp.where(row >= 8 - 2 * has_left, roll(left, 6 - 2 * k, 0), x)
    columns = deep_edges(deep[: 4 * pairs])
    half = len(columns) // 2
    columns_e = deep_edges(deep[4 * pairs :])
    behind = pair_edges(lambda i: [z_halo[i, q] for q in range(nx)], 4, 8)
    for m, out in enumerate((y_a, y_b)):
        toward = high_side("gy", m)
        parts = [
            strip(columns[j], columns[j + half], toward, 8) for j in range(half)
        ] + columns_e
        for i in range(nz // 8):
            parts.append(y_strip(edges[0, pl.ds(8 * i, 8)], edges[1, pl.ds(8 * i, 8)], toward))
        parts.append(y_strip(behind[0], behind[1], toward))
        n = 0
        for x in parts:
            for i in range(x.shape[0] // 8):
                out[n] = x[8 * i : 8 * i + 8]
                n += 1


def sixth_pack(y_a, y_b, z_halo, halo_full, x_rim):
    tiles = halo_full.shape[1] // 8
    first = y_a.shape[0] - tiles
    for i in range(tiles):
        for j, x in enumerate(merge_y(y_a[first + i], y_b[first + i])):
            halo_full[j, pl.ds(8 * i, 8)] = x
    nx = z_halo.shape[1]

    def rim(plane):
        return [rows_of([(z_halo[k, plane(1)], 2 * k, 2 * k - 1, 2) for k in range(4)])]

    pack_rim(x_rim, rim, lambda j: halo_full[j], 4, 1, nx)


def coarse_solve(full, full_e, y_a, y_b, main, halo, ca, cb, force, e, w0, w1, w2, w3, w4, w5, deep_e, grown):
    pairs, rows = full.shape[1:3]
    deep = full_e.shape[1]
    planes = 2 * pairs
    own = main.shape[1] - 2
    cz = rows - 8
    half = LANES // 2
    _, zl, zr = place("gz")
    _, yl, yr = place("gy")
    two = lax.axis_size("gx") == 2
    gx = FIXED[-1][0] if two else lax.axis_index("gx")

    def inside(rows, width):
        lane = iota((rows, LANES), 1)
        row = iota((rows, LANES), 0)
        kept = (row < cz + width * zr) | (row >= rows - width * zl)
        return kept & ((lane < half + SLOT * yr) | (lane >= LANES - SLOT * yl))

    zero = jnp.zeros((rows, LANES), F32)
    w = (w0, w1, w2, w3, w4, w5)
    for k in range(4):
        for p in (0, planes + 1):
            ca[k, p] = zero
            cb[k, p] = zero
    e[0] = zero
    e[planes + 1] = zero
    deep_e[0] = jnp.zeros((deep, LANES), F32)
    deep_e[planes + 1] = jnp.zeros((deep, LANES), F32)

    tiles, deep_tiles = rows // 8, deep // 8
    count = pairs // 2
    columns = []

    def taken(ref, n, tiles):
        return jnp.concatenate([ref[n + i] for i in range(tiles)], axis=0)

    seconds = []
    for j in range(count):
        left, right = left_right("gy", taken(y_a, j * tiles, tiles), taken(y_b, j * tiles, tiles))
        spot = iota(left.shape, 1) % 16
        columns.append(jnp.where(spot < 8, left, roll(right, 8, 1)))
        seconds.append(jnp.where(spot < 8, roll(left, -8, 1), right))
    columns += seconds
    columns_e = []
    for j in range(-(-pairs // 4)):
        n = count * tiles + j * deep_tiles
        left, right = left_right("gy", taken(y_a, n, deep_tiles), taken(y_b, n, deep_tiles))
        spot = iota(left.shape, 1) % 16
        columns_e.append(jnp.where(spot < 8, left, right))

    def whole_plane(pair, columns, n, s):
        lane = iota(pair.shape, 1)
        last, first = 2 * n + 1 - s, 2 * n + s
        low = roll(columns[first // 8], half - 16 * (first % 8) - 8, 1)
        high = roll(columns[last // 8], LANES - 8 - 16 * (last % 8), 1)
        x = jnp.where(lane < half, roll(pair, -s * half, 1), low)
        return jnp.where(lane < LANES - 8, x, high)

    near, far = inside(rows, 4), inside(deep, 8)
    for r in range(pairs):
        for s in range(2):
            p = 2 * r + s
            x = jnp.where(far, whole_plane(full_e[r], columns_e, r, s), 0.0)
            deep_e[p + 1] = x
            e[p + 1] = fold_rows(x)
            for k in range(4):
                x = whole_plane(full[k, r], columns, k * pairs + r, s)
                force[k, p] = jnp.where(near, x, 0.0)

    def shifts(x):
        return (
            roll(x, LANES - 1, 1),
            roll(x, 1, 1),
            roll(x, x.shape[0] - 1, 0),
            roll(x, 1, 0),
        )

    def two_by_two(width, body):
        if two:
            for p in range(max(gx * own - width, 0), min(gx * own + own + width, planes)):
                body(p + 1)
            return
        lo = jnp.maximum(gx * own - width, 0)
        hi = jnp.minimum(gx * own + own + width, planes)
        steps = (hi - lo + 1) // 2
        lo = jnp.minimum(lo, planes - 2 * steps)

        def step(i, carry):
            body(lo + 2 * i + 1)
            body(lo + 2 * i + 2)
            return carry

        lax.fori_loop(0, steps, step, 0)

    def start(p):
        x = deep_e[p]
        up, down = x + deep_e[p + 1], x + deep_e[p - 1]
        w0[p] = fold_rows(up)
        total = up + down
        for n, y in enumerate(shifts(x)):
            total += x + y
            w[1 + n][p] = fold_rows(x + y)
        factor = jnp.where(near, fold_rows(relax_weight / total), 0.0)
        w5[p] = factor
        for k in range(3):
            ca[k, p] = factor * force[k, p - 1]
        ca[3, p] = e[p] * force[3, p - 1]

    w0[0] = e[0] + e[1]
    two_by_two(planes, start)

    def sweep(src, dst, width):
        def body(p):
            wxp, wxm = w0[p], w0[p - 1]
            wyp, wym, wzp, wzm = w1[p], w2[p], w3[p], w4[p]
            x = src[3, p]
            around = shifts(x)
            up, down = src[3, p + 1], src[3, p - 1]
            spread = 0.0
            for k in range(3):
                u = src[k, p]
                yp, ym, zp, zm = shifts(u)
                xp, xm = src[k, p + 1], src[k, p - 1]
                total = force[k, p - 1] - 2.0 * terms(k, up, down, *around)
                total += wxp * xp + wxm * xm
                total += wyp * yp + wym * ym
                total += wzp * zp + wzm * zm
                spread += terms(k, xp, xm, yp, ym, zp, zm)
                dst[k, p] = jnp.where(near, 0.4 * u + w5[p] * total, 0.0)
            dst[3, p] = jnp.where(near, x + e[p] * (force[3, p - 1] - 0.125 * spread), 0.0)

        two_by_two(width, body)

    sweep(ca, cb, 3)
    sweep(cb, ca, 2)
    sweep(ca, cb, 1)

    lane = iota((LANES, 2 * LANES), 1)
    cell = iota((LANES, 2 * LANES), 0)
    spot = lane % SLOT
    wanted = jnp.where(spot < 4, LANES - 2, half - 2) + spot // 2
    slot = (lane - LANES) // SLOT
    column = jnp.zeros((4 * rows, LANES), F32)
    first = gx * own

    def grow(ref, index, x):
        ref[index + (pl.ds(0, cz, stride=2),)] = x[:cz]
        ref[index + (pl.ds(1, cz, stride=2),)] = x[:cz]
        grown[pl.ds(0, 8, stride=2)] = x[cz:]
        grown[pl.ds(1, 8, stride=2)] = x[cz:]
        r = iota((8, LANES), 0)
        tail = jnp.where(r < 4, grown[pl.ds(0, 8)], grown[pl.ds(8, 8)])
        ref[index + (pl.ds(2 * cz, 8),)] = tail

    for i in range(own + 2):
        x = jnp.concatenate([cb[k, first + i] for k in range(4)], axis=0)
        here = (lane >= LANES) & ((slot + 1) // 2 - 1 == i) & (cell == wanted)
        chosen = (here | ((lane < LANES) & (lane // 2 == cell))).astype(F32)
        wide = jnp.dot(x, chosen, precision=lax.Precision.HIGHEST, preferred_element_type=F32)
        for k in range(4):
            grow(main, (k, i), wide[k * rows : (k + 1) * rows, :LANES])
        column += wide[:, LANES:]
    for k in range(4):
        grow(halo, (k,), column[k * rows : (k + 1) * rows])


def post_smooth(
    e, halo_e, force, halo_f, w0, w1, w2, w3, w4, w5, hw,
    fields, z_halo, halo_full, x_fine, x_rim, main, column, v_out, p_out,
    ua, ub, ha, hb, ca, beside,
):
    nx, nz, _ = p_out.shape
    slots = nx + 6
    w = (w0, w1, w2, w3, w4, w5)
    zero = jnp.zeros((nz + 8, LANES), F32)
    for k in range(4):
        for p in (1, 2, nx + 3, nx + 4):
            ua[k, p] = zero
            ub[k, p] = zero
        for q in range(nx):
            i = q // 2 + 1
            ua[k, q + 3, pl.ds(0, nz)] = fields[k, q + 3, pl.ds(0, nz)] + main[k, i, pl.ds(0, nz)]
            ua[k, q + 3, pl.ds(nz, 8)] = z_halo[k, q] + main[k, i, pl.ds(nz, 8)]
        ha[k] = own_slots(halo_full[k % 2], nx, k // 2)
    for m in range(x_fine.shape[0]):
        right, valid = x_side(m)
        there = truth(valid, (nz, LANES))
        there8 = truth(valid, (8, LANES))
        tiles = (nz + 8) // 8
        side = jnp.concatenate([x_rim[m, 1 + r] for r in range(tiles)], axis=0)
        i = right * (nx // 2 + 1)
        for k in range(4):
            for j in range(2):
                at = 1 + right * (nx + 2) + j
                x = x_fine[m, 2 * k + j] + main[k, i, pl.ds(0, nz)]
                ua[k, at, pl.ds(0, nz)] = jnp.where(there, x, 0.0)
            x = roll(x_rim[m, 0], -2 * k, 0) + main[k, i, pl.ds(nz, 8)]
            ua[k, 2 + right * (nx + 1), pl.ds(nz, 8)] = jnp.where(there8, x, 0.0)
            x, kept = rim_halo(side, k, SLOT, 1, right, valid, nx)
            ha[k] = jnp.where(kept, x, ha[k])
    masks = fine_masks(nz + 8, slots)
    for k in range(4):
        ha[k] = jnp.where(masks[1], ha[k] + column[k], 0.0)
    fill_edges(ca, ua, inside_slots(slots, 2))
    main_sweep(ua, ha, ub, w, e, force, 1, masks[0], beside)
    halo_sweep(ha, ca, hb, hw, halo_e, halo_f, masks[1])

    spread_halo(hb, beside, slots, 0, full=False)

    def last(p):
        new = main_operator(ub, beside, w, force, p, nz)
        new = relaxed(*new, w5[p, pl.ds(0, nz)], e[p, pl.ds(0, nz)])
        for k in range(3):
            v_out[k, p - 3] = new[k]
        p_out[p - 3] = new[3]

    over_planes(slots, 0, last)


def local(velocity, pressure, viscosity, body_force):
    nx, nz, ny = pressure.shape
    if ny != LANES or nx * SLOT * 2 != LANES or nz % 16:
        raise ValueError("unsupported block")
    sides = x_messages()
    rows, slots = nz + 8, nx + 6
    inputs = [velocity, pressure, viscosity, body_force]
    block = (nz, LANES)

    z_shape = (3 * nx, 8, LANES)
    half = (nx // 2,) + block
    *staged, y_a, y_b = call(
        first_pack, [half] * 16 + [(2,) + block] * 2, inputs, outside=4, copies=16
    )
    x_main, z_a, z_b = call(side_pack, [(sides, 21) + block, z_shape, z_shape], staged)
    y_a, y_b = swap(y_a, "gy", 0), swap(y_b, "gy", 1)
    x_main = swap_x(x_main)
    halo, z_b = call(second_pack, [(4,) + block, z_shape], [z_b, y_a, y_b])
    (z_a,) = call(second_pack_near, [z_shape], [z_a, halo])
    z_a, z_b = swap(z_a, "gz", 0), swap(z_b, "gz", 1)
    tiles = rows // 8
    z_first, halo_first, x_first = call(
        third_pack,
        [(8, nx, 8, LANES), (4, rows, LANES), (sides, 6 + tiles, 8, LANES)],
        [z_a, z_b, halo],
    )
    x_first = swap_x(x_first)

    spread, column = (4, slots, rows, LANES), (4, rows, LANES)
    started = [(slots, rows, LANES), (rows, LANES), (3, slots, rows, LANES), (3, rows, LANES)]
    started += [(slots, rows, LANES)] * 6 + [spread, spread] + [column] * 3 + [(rows, LANES)]
    started += [(5, nx // 2, nz, LANES)]
    state = call(
        by_sides(pre_start),
        started,
        [*staged, z_first, halo_first, x_main],
        [(7, rows, LANES), column, column, spread],
        cost=4,
    )
    *operator, fields, _, _, _, _, _, _, factors, own = call(
        by_sides(pre_smooth),
        started + [(7, rows, LANES), (5, nx // 4, nz // 2, LANES)],
        [x_first, *state],
        [column, spread],
        cost=8,
        aliases={i + 1: i for i in range(len(started))},
    )
    operator.append(factors)
    edges, x_fine = call(smooth_pack, [(2,) + block, (sides, 8) + block], [fields])
    if lax.axis_size("gx") == 2:
        parts = [own, swap(own, "gx", 0)]
        gather = fourth_pack
    else:
        parts = [lax.all_gather(own, "gx", axis=1, tiled=True)]

        def gather(a, *refs):
            fourth_pack(a, None, *refs)

    x_fine = swap_x(x_fine)
    pairs = lax.axis_size("gx") * (nx // 4)
    z_shape = (3 * pairs + nx, 8, LANES)
    whole, z_a, z_b = call(
        gather, [(5, pairs, nz // 2, LANES), z_shape, z_shape], parts + [fields]
    )
    z_a, z_b = swap(z_a, "gz", 0), swap(z_b, "gz", 1)
    deep = nz // 2 + 16
    shallow = deep - 8
    y_shape = (pairs // 2 * (shallow // 8) + -(-pairs // 4) * (deep // 8) + tiles, 8, LANES)
    full, full_e, z_halo, y_a, y_b = call(
        fifth_pack,
        [(4, pairs, shallow, LANES), (pairs, deep, LANES), (4, nx, 8, LANES), y_shape, y_shape],
        [whole, z_a, z_b, edges],
    )
    y_a, y_b = swap(y_a, "gy", 0), swap(y_b, "gy", 1)
    halo_full, x_rim = call(
        sixth_pack,
        [(2, rows, LANES), (sides, 1 + tiles, 8, LANES)],
        [y_a, y_b, z_halo],
    )
    x_rim = swap_x(x_rim)
    planes = 2 * pairs
    plane = (shallow, LANES)
    grown, beside = call(
        by_sides(coarse_solve),
        [(4, nx // 2 + 2, rows, LANES), (4, rows, LANES)],
        [full, full_e, y_a, y_b],
        [(4, planes + 2) + plane] * 2
        + [(4, planes) + plane]
        + [(planes + 2,) + plane] * 7
        + [(planes + 2, deep, LANES), (16, LANES)],
        cost=4,
    )
    v_out, p_out = call(
        by_sides(post_smooth),
        [(3, nx) + block, (nx,) + block],
        operator + [fields, z_halo, halo_full, x_fine, x_rim, grown, beside],
        [spread] * 2 + [column] * 3 + [spread],
        cost=8,
    )
    return v_out, p_out


def swap_x(array):
    if array.shape[0] == 1:
        return swap(array, "gx", 0)
    parts = [swap(array[m], "gx", m) for m in range(2)]
    return jnp.stack(parts)


def solution(mesh):
    return jax.shard_map(
        local,
        mesh=mesh,
        in_specs=(
            P(None, "gx", "gz", "gy"),
            P("gx", "gz", "gy"),
            P("gx", "gz", "gy"),
            P(None, "gx", "gz", "gy"),
        ),
        out_specs=(P(None, "gx", "gz", "gy"), P("gx", "gz", "gy")),
        check_vma=False,
    )
```

```python
import jax
import jax.numpy as jnp
from jax import lax
from jax.experimental import pallas as pl
from jax.experimental.pallas import tpu as pltpu
from jax.sharding import PartitionSpec as P

LANES = 128
SLOT = 8
F32 = jnp.float32
relax_weight = 0.6
HELD = 846 * 2**16
Z_PLACES = (
    ((0, 0, 3), (1, 3, 3), (5, 6, 2)),
    ((2, 0, 3), (3, 3, 3), (6, 6, 2)),
    ((4, 0, 3), (7, 3, 2)),
)


def call(body, outs, args, scratch=(), cost=1, outside=0, copies=0, aliases=None):
    return pl.pallas_call(
        body,
        out_shape=[jax.ShapeDtypeStruct(shape, F32) for shape in outs],
        in_specs=[pl.BlockSpec(memory_space=pltpu.HBM)] * outside
        + [pl.BlockSpec(memory_space=pltpu.VMEM)] * (len(args) - outside),
        out_specs=[pl.BlockSpec(memory_space=pltpu.VMEM)] * len(outs),
        scratch_shapes=[pltpu.VMEM(shape, F32) for shape in scratch]
        + [pltpu.SemaphoreType.DMA((copies,))] * (copies > 0),
        input_output_aliases=aliases or {},
        compiler_params=pltpu.CompilerParams(vmem_limit_bytes=HELD if outside else 40 * 2**20),
        cost_estimate=pl.CostEstimate(
            flops=cost * 10**6, bytes_accessed=cost * 10**6, transcendentals=0
        ),
    )(*args)


def swap(array, axis, which):
    count = lax.axis_size(axis)
    if axis != "gx" and which == 1:
        ys, zs = lax.axis_size("gy"), lax.axis_size("gz")
        pairs = []
        for y in range(ys):
            for z in range(zs):
                i = y if axis == "gy" else z
                j = i + 1 if i % 2 else i - 1
                if axis == "gy":
                    to = (j, z) if 0 <= j < count else (y, z ^ 1)
                else:
                    to = (y, j) if 0 <= j < count else (y ^ 1, z)
                pairs.append((y * zs + z, to[0] * zs + to[1]))
        return lax.ppermute(array, ("gy", "gz"), pairs)
    pairs = []
    for i in range(which, count, 2):
        j = (i + 1) % count
        pairs += [(i, j), (j, i)]
    return lax.ppermute(array, axis, pairs)


FIXED = []


def by_sides(body):
    def kernel(*refs):
        count = lax.axis_size("gx")
        _, xl, xr = place("gx")
        for sides in [(0, 1), (1, 0), (1, 1)][: 2 if count == 2 else 3]:

            def branch(sides=sides):
                FIXED.append(sides)
                body(*refs)
                FIXED.pop()

            pl.when((xl == sides[0]) & (xr == sides[1]))(branch)

    return kernel


def place(axis):
    if axis == "gx" and FIXED:
        return (None,) + FIXED[-1]
    i = lax.axis_index(axis)
    last = lax.axis_size(axis) - 1
    return i, jnp.where(i > 0, 1, 0), jnp.where(i < last, 1, 0)


def iota(shape, dim):
    return lax.broadcasted_iota(jnp.int32, shape, dim)


def truth(flag, shape):
    return jnp.full(shape, flag, jnp.int32) > 0


def roll(x, shift, dim):
    if isinstance(shift, int):
        shift %= x.shape[dim]
        return x if shift == 0 else pltpu.roll(x, shift, dim)
    return pltpu.roll(x, lax.rem(shift + 2 * x.shape[dim], x.shape[dim]), dim)


def high_side(axis, message):
    return jnp.where(lax.axis_index(axis) % 2 == message, 1, 0)


def left_right(axis, a, b):
    odd = truth(lax.axis_index(axis) % 2, a.shape)
    return jnp.where(odd, a, b), jnp.where(odd, b, a)


def x_messages():
    return 1 if lax.axis_size("gx") == 2 else 2


def pair_edges(planes, fields, rows):
    lane = iota((rows, LANES), 1) // SLOT
    half = fields // 2
    out = []
    for j in range(half):
        total = jnp.zeros((rows, LANES), F32)
        for part in range(2):
            for q, x in enumerate(planes(j + part * half)):
                slot = q + part * (LANES // SLOT // 2)
                total = jnp.where(lane == slot, roll(x, slot * SLOT + 4, 1), total)
        out.append(total)
    return out


def merge_y(a, b):
    _, has_left, has_right = place("gy")
    left, right = left_right("gy", a, b)
    spot = iota(a.shape, 1) % SLOT
    kept = (spot < 4 * has_left) | (spot >= SLOT - 4 * has_right)
    first = jnp.where(spot < 4, left, roll(right, 4, 1))
    second = jnp.where(spot < 4, roll(left, -4, 1), right)
    return jnp.where(kept, first, 0.0), jnp.where(kept, second, 0.0)


class Staged:
    def __init__(self, refs):
        self.refs = refs
        self.half, self.nz = refs[0].shape[:2]
        self.nx = 2 * self.half

    def __getitem__(self, index):
        i, q = index[:2]
        return self.refs[2 * i + q // self.half][(q % self.half,) + index[2:]]


def first_pack(v_in, p_in, e_in, f_in, *refs):
    staged = Staged(refs[:16])
    y_a, y_b, arrived = refs[16:]
    nx, nz = staged.nx, staged.nz
    loads = []
    for n in range(16):
        i, planes = n // 2, pl.ds(n % 2 * staged.half, staged.half)
        if i < 3:
            part = v_in.at[i, planes]
        elif i < 5:
            part = (p_in, e_in)[i - 3].at[planes]
        else:
            part = f_in.at[i - 5, planes]
        loads.append(pltpu.make_async_copy(part, refs[n], arrived.at[n]))
    for load in loads:
        load.start()
    for load in loads:
        load.wait()
    edges = pair_edges(lambda i: [staged[i, q] for q in range(nx)], 8, nz)
    for m, out in enumerate((y_a, y_b)):
        for j in range(2):
            out[j] = y_strip(edges[j], edges[j + 2], high_side("gy", m))


def side_pack(*refs):
    staged = Staged(refs[:16])
    x_main, z_a, z_b = refs[16:]
    nx, nz = staged.nx, staged.nz
    for m in range(x_main.shape[0]):
        top = truth(high_side("gx", m), (nz, LANES))
        n = 0
        for i in range(8):
            width = 3 if i < 5 else 2
            for j in range(width):
                x_main[m, n] = jnp.where(top, staged[i, nx - width + j], staged[i, j])
                n += 1
    low, high = pl.ds(0, 8), pl.ds(nz - 8, 8)
    for q in range(nx):
        for n, fields in enumerate(Z_PLACES):
            for m, out in enumerate((z_a, z_b)):
                out[3 * q + n] = z_strip(
                    [(staged[i, q, low], staged[i, q, high], at, rows) for i, at, rows in fields],
                    high_side("gz", m),
                )


def strip(first, second, toward_right, width):
    right = truth(toward_right, first.shape)
    spot = iota(first.shape, 1) % (2 * width)
    first = jnp.where(right, first, roll(first, -width, 1))
    second = jnp.where(right, roll(second, width, 1), second)
    return jnp.where(spot < width, first, second)


def y_strip(first, second, toward_right):
    return strip(first, second, toward_right, SLOT // 2)


def z_strip(parts, toward_right):
    right = truth(toward_right, (8, LANES))
    return rows_of(
        [
            (jnp.where(right, roll(high, at + rows, 0), roll(low, at, 0)), 0, at, rows)
            for low, high, at, rows in parts
        ]
    )


def z_tail(halo, first, out, message):
    nz = halo.shape[1]
    row = iota((8, LANES), 0)
    for n in range(first.shape[0]):
        out[n] = first[n]
    for j in range(4):
        tiles = halo[j, pl.ds(0, 8)], halo[j, pl.ds(nz - 8, 8)]
        x = z_strip([tiles + (5, 3)], high_side("gz", message))
        out[3 * j + 2] = jnp.where(row < 5, first[3 * j + 2], x)


def second_pack(z_first, y_a, y_b, halo, z_b):
    for j in range(2):
        halo[j], halo[j + 2] = merge_y(y_a[j], y_b[j])
    z_tail(halo, z_first, z_b, 1)


def second_pack_near(z_first, halo, z_a):
    z_tail(halo, z_first, z_a, 0)


def z_tile(a, b, at, rows):
    _, has_left, has_right = place("gz")
    left, right = left_right("gz", a, b)
    row = iota(a.shape, 0)
    x = jnp.where(row < rows * has_right, roll(right, -at, 0), 0.0)
    return jnp.where(row >= 8 - rows * has_left, roll(left, 8 - at - rows, 0), x)


def third_pack(z_a, z_b, halo, z_halo, halo_full, x_rim):
    nx = z_halo.shape[1]
    nz = halo.shape[1]
    for q in range(nx):
        for n, fields in enumerate(Z_PLACES):
            for i, at, rows in fields:
                z_halo[i, q] = z_tile(z_a[3 * q + n], z_b[3 * q + n], at, rows)
    for j in range(4):
        halo_full[j, pl.ds(0, nz)] = halo[j]
        halo_full[j, pl.ds(nz, 8)] = z_tile(z_a[3 * j + 2], z_b[3 * j + 2], 5, 3)

    def tiles(plane):
        out = [
            rows_of([(z_halo[i, plane(1)], 0, 6, 4), (z_halo[i, plane(2)], 3, 2, 2)])
            for i in range(5)
        ]
        force = zip((0, 3, 5), (7, 2, 4))
        out.append(
            rows_of([(z_halo[5 + k, plane(1)], at, row, 2) for k, (at, row) in enumerate(force)])
        )
        return out

    pack_rim(x_rim, tiles, lambda j: halo_full[j], 8, 2, nx)


def rows_of(parts):
    row = iota((8, LANES), 0)
    total = jnp.zeros((8, LANES), F32)
    for x, shift, first, count in parts:
        total = jnp.where((row - first) % 8 < count, roll(x, shift, 0), total)
    return total


def pack_rim(x_rim, tiles, halo_pair, fields, planes, nx):
    half = fields // 2
    stride = LANES // 8 if fields == 8 else SLOT
    for m in range(x_rim.shape[0]):
        high = high_side("gx", m)
        done = tiles(lambda d, high=high: high * (nx - 2 * d + 1) + d - 1)
        for n, x in enumerate(done):
            x_rim[m, n] = x
        pairs = [halo_pair(j) for j in range(half)]
        rows = pairs[0].shape[0]
        column = iota((rows, LANES), 1) // stride
        first = high * (nx - planes) * SLOT
        total = jnp.zeros((rows, LANES), F32)
        for i in range(fields):
            at = i * stride - first - (i // half) * (LANES // 2)
            total = jnp.where(column == i, roll(pairs[i % half], at + LANES, 1), total)
        for r in range(rows // 8):
            x_rim[m, len(done) + r] = total[8 * r : 8 * r + 8]


def main_shifts(x, beside, kept):
    rows = x.shape[0]
    y, beside = x[:kept], beside[:kept]
    lane = iota(y.shape, 1)
    return (
        roll(jnp.where(lane == 0, beside, y), LANES - 1, 1),
        roll(jnp.where(lane == LANES - 1, beside, y), 1, 1),
        roll(x, rows - 1, 0)[:kept],
        roll(x, 1, 0)[:kept],
    )


def halo_shifts(x, edge):
    spot = iota(x.shape, 1) % SLOT
    rows = x.shape[0]
    return (
        roll(x, LANES - SLOT, 1),
        roll(x, SLOT, 1),
        roll(jnp.where(spot == 4, edge, x), LANES - 1, 1),
        roll(jnp.where(spot == 3, edge, x), 1, 1),
        roll(x, rows - 1, 0),
        roll(x, 1, 0),
    )


def main_weights(e, halo_e, w, width, chosen, faces):
    slots = e.shape[0]
    for p in faces:
        w[0][p] = e[p] + e[p + 1]

    def body(p):
        x = e[p]
        total = w[0][p] + w[0][p - 1]
        for n, y in enumerate(main_shifts(x, roll(halo_e[...], LANES - SLOT * p - 4, 1), x.shape[0])):
            total += x + y
            w[1 + n][p] = x + y
        w[5][p] = relax_weight / total

    over_planes(slots, width, body, chosen)


def halo_weights(e, edge_e, w):
    x = e[...]
    total = jnp.zeros_like(x)
    for n, y in enumerate(halo_shifts(x, edge_e[...])):
        total += x + y
        w[n] = x + y
    w[6] = relax_weight / total


def terms(k, up, down, yp, ym, zp, zm):
    return (up - down, zp - zm, yp - ym)[k]


def spread_halo(halo, beside, slots, width, chosen=None, full=True):
    kept = beside.shape[2] - (0 if full else 8)

    def body(p):
        for k in range(4):
            beside[k, p, pl.ds(0, kept)] = roll(halo[k][:kept], LANES - SLOT * p - 4, 1)

    over_planes(slots, width, body, chosen)


def main_operator(src, beside, w, force, p, kept):
    def at(ref, *index):
        return ref[index + (pl.ds(0, kept),)]

    wxp, wxm, wyp, wym, wzp, wzm = (
        at(ref, q) for ref, q in zip((w[0],) + w[:5], (p, p - 1, p, p, p, p))
    )
    around = main_shifts(src[3, p], at(beside, 3, p), kept)
    up, down = at(src, 3, p + 1), at(src, 3, p - 1)
    olds, sums, spread = [], [], 0.0
    for k in range(3):
        yp, ym, zp, zm = main_shifts(src[k, p], at(beside, k, p), kept)
        xp, xm = at(src, k, p + 1), at(src, k, p - 1)
        total = at(force, k, p) - terms(k, up, down, *around)
        total += wxp * xp + wxm * xm
        total += wyp * yp + wym * ym
        total += wzp * zp + wzm * zm
        spread += terms(k, xp, xm, yp, ym, zp, zm)
        olds.append(at(src, k, p))
        sums.append(total)
    olds.append(at(src, 3, p))
    return olds, sums, spread


def halo_operator(halo, edge, w, force):
    x = halo[3]
    px = halo_shifts(x, edge[3])
    olds, sums, spread = [], [], 0.0
    for k in range(3):
        u = halo[k]
        around = halo_shifts(u, edge[k])
        total = force[k] - terms(k, *px)
        for n in range(6):
            total += w[n] * around[n]
        spread += terms(k, *around)
        olds.append(u)
        sums.append(total)
    olds.append(x)
    return olds, sums, spread


def relaxed(olds, sums, spread, factor, e):
    new = [0.4 * olds[k] + factor * sums[k] for k in range(3)]
    return new + [olds[3] - 0.25 * e * spread]


def edges_of(plane, slots, total=None):
    shape = plane(slots[0]).shape
    slot = iota(shape, 1) // SLOT
    total = jnp.zeros(shape, F32) if total is None else total
    for p in slots:
        total = jnp.where(slot == p, roll(plane(p), p * SLOT + 4, 1), total)
    return total


def fill_edges(edge, src, slots, fresh=True):
    for k in range(4):
        edge[k] = edges_of(lambda p: src[k, p], slots, None if fresh else edge[k])


def fine_masks(rows, slots):
    nz = rows - 8
    _, zl, zr = place("gz")
    _, yl, yr = place("gy")
    _, xl, xr = place("gx")
    r = iota((8, LANES), 0)
    tile = (r < 4 * zr) | (r >= 8 - 4 * zl)
    r = iota((rows, LANES), 0)
    lane = iota((rows, LANES), 1)
    spot, slot = lane % SLOT, lane // SLOT
    column = (r < nz + 4 * zr) | (r >= rows - 4 * zl)
    column &= (spot < 4 * yl) | (spot >= SLOT - 4 * yr)
    column &= (slot >= 3 - 3 * xl) & (slot < slots - 3 + 3 * xr)
    return tile, column


def main_sweep(src, halo, dst, w, e, force, width, tile, beside, chosen=None):
    nz = src.shape[2] - 8
    slots = src.shape[1]

    def body(p):
        new = relaxed(*main_operator(src, beside, w, force, p, nz + 8), w[5][p], e[p])
        for k in range(4):
            x = new[k]
            dst[k, p, pl.ds(0, nz)] = x[:nz]
            dst[k, p, pl.ds(nz, 8)] = jnp.where(tile, x[nz:], 0.0)

    spread_halo(halo, beside, slots, width, chosen)
    over_planes(slots, width, body, chosen)


def halo_sweep(halo, edge, halo_dst, hw, halo_e, halo_f, column):
    new = relaxed(*halo_operator(halo, edge, hw, halo_f), hw[6], halo_e[...])
    for k in range(4):
        halo_dst[k] = jnp.where(column, new[k], 0.0)


def over_planes(slots, width, body, chosen=None):
    _, xl, xr = place("gx")
    for p in range(3 - width, slots - 3 + width):
        wanted = True if chosen is None else chosen(p)
        if wanted and (p >= 3 or xl) and (p < slots - 3 or xr):
            body(p)


def own_slots(x, nx, part):
    lane = iota(x.shape, 1)
    x = roll(x, 3 * SLOT - part * (LANES // 2), 1)
    return jnp.where((lane >= 3 * SLOT) & (lane < (3 + nx) * SLOT), x, 0.0)


def x_side(m):
    _, has_left, has_right = place("gx")
    if lax.axis_size("gx") == 2:
        return has_right, 1
    right = high_side("gx", m)
    return right, jnp.where(right > 0, has_right, has_left)


def rim_halo(x, t, stride, planes, right, valid, nx):
    base = right * (nx + 3) + (1 - right) * (3 - planes)
    lane = iota(x.shape, 1)
    x = roll(x, base * SLOT - t * stride + LANES, 1)
    kept = (lane >= base * SLOT) & (lane < (base + planes * valid) * SLOT)
    return jnp.where(kept, x, 0.0), kept


def viscosity_force(staged, z_halo, halo_full, x_main, e, halo_e, force, halo_f):
    nx, nz = staged.nx, staged.nz
    slots = nx + 6
    zero = jnp.zeros((nz + 8, LANES), F32)
    for p in list(range(3)) + list(range(nx + 3, slots)):
        e[p] = zero
        for k in range(3):
            force[k, p] = zero
    for q in range(nx):
        e[q + 3, pl.ds(0, nz)] = staged[4, q]
        e[q + 3, pl.ds(nz, 8)] = z_halo[4, q]
        for k in range(3):
            force[k, q + 3, pl.ds(0, nz)] = 2.0 * staged[5 + k, q]
            force[k, q + 3, pl.ds(nz, 8)] = 2.0 * z_halo[5 + k, q]
    halo_e[...] = own_slots(halo_full[0], nx, 1)
    for k in range(3):
        halo_f[k] = 2.0 * own_slots(halo_full[k + 1], nx, 1)
    for m in range(x_main.shape[0]):
        right, valid = x_side(m)
        there = truth(valid, (nz, LANES))
        for j in range(3):
            e[right * (nx + 3) + j, pl.ds(0, nz)] = jnp.where(there, x_main[m, 12 + j], 0.0)
        for j in range(2):
            at = right * (nx + 2) + 1 + j
            for k in range(3):
                force[k, at, pl.ds(0, nz)] = jnp.where(there, 2.0 * x_main[m, 15 + 2 * k + j], 0.0)


def first_fields(staged, z_halo, halo_full, x_main, u, other, halo):
    nx, nz = staged.nx, staged.nz
    slots = nx + 6
    zero = jnp.zeros((nz + 8, LANES), F32)
    for k in range(4):
        for p in list(range(3)) + list(range(nx + 3, slots)):
            u[k, p] = zero
            other[k, p] = zero
        for q in range(nx):
            u[k, q + 3, pl.ds(0, nz)] = staged[k, q]
            u[k, q + 3, pl.ds(nz, 8)] = z_halo[k, q]
        halo[k] = own_slots(halo_full[k], nx, 0)
    for m in range(x_main.shape[0]):
        right, valid = x_side(m)
        there = truth(valid, (nz, LANES))
        for k in range(4):
            for j in range(3):
                x = jnp.where(there, x_main[m, 3 * k + j], 0.0)
                u[k, right * (nx + 3) + j, pl.ds(0, nz)] = x


def add_rims(x_rim, nx, u, halo, e, halo_e, force, halo_f, edge, edge_e):
    nz = e.shape[1] - 8
    tiles = (nz + 8) // 8
    tail = pl.ds(nz, 8)
    slot = iota((8, LANES), 1) // SLOT
    for m in range(x_rim.shape[0]):
        right, valid = x_side(m)
        there = truth(valid, (8, LANES))
        column = jnp.concatenate([x_rim[m, 6 + r] for r in range(tiles)], axis=0)
        near = right * (nx + 1) + 2
        far = near + 2 * right - 1
        for k in range(5):
            x = jnp.where(there, x_rim[m, k], 0.0)
            for p, y in ((near, x), (far, roll(x, -3, 0))):
                moved = roll(y, p * SLOT + 4, 1)
                if k < 4:
                    u[k, p, tail] = y
                    edge[k, tail] = jnp.where(slot == p, moved, edge[k, tail])
                else:
                    e[p, tail] = y
                    edge_e[tail] = jnp.where(slot == p, moved, edge_e[tail])
            x, kept = rim_halo(column, k, LANES // 8, 2, right, valid, nx)
            if k < 4:
                halo[k] = jnp.where(kept, x, halo[k])
            else:
                halo_e[...] = jnp.where(kept, x, halo_e[...])
        x = jnp.where(there, 2.0 * x_rim[m, 5], 0.0)
        for k, at in enumerate((0, 3, 5)):
            force[k, near, tail] = roll(x, -at, 0)
            x_k, kept = rim_halo(column, 5 + k, LANES // 8, 2, right, valid, nx)
            halo_f[k] = jnp.where(kept, 2.0 * x_k, halo_f[k])


def early(nx, sweep):
    _, xl, xr = place("gx")

    def chosen(p):
        if 3 + sweep <= p < nx + 3 - sweep:
            return True
        if 3 <= p < nx + 3:
            return xl == 0 if p < 3 + sweep else xr == 0
        return False

    return chosen


def early_block(nx):
    _, xl, xr = place("gx")
    return lambda q: xl == 0 if 2 * q + 5 <= nx else xr == 0 if 2 * q + 2 >= 5 else False


def late(chosen):
    return lambda p: not chosen(p)


def inside_slots(slots, width, chosen=None):
    _, xl, xr = place("gx")
    inside = range(3 - width * xl, slots - 3 + width * xr)
    return [p for p in inside if chosen is None or chosen(p)]


def residuals(u, halo, beside, w, force, e, summed, chosen):
    _, blocks, nz, _ = summed.shape
    slots = u.shape[1]
    spread_halo(halo, beside, slots, 0, lambda p: chosen((p - 3) // 2), False)

    def body(q):
        totals = [0.0] * 5
        for j in range(2):
            p = 2 * q + 3 + j
            olds, sums, spread = main_operator(u, beside, w, force, p, nz)
            diagonal = (w[0][p] + w[0][p - 1] + w[1][p] + w[2][p] + w[3][p] + w[4][p])[:nz]
            for k in range(3):
                totals[k] += sums[k] - diagonal * olds[k]
            totals[3] += spread
            totals[4] += e[p, pl.ds(0, nz)]
        for k in range(5):
            summed[k, q] = totals[k]

    for q in range(blocks):
        if chosen(q):
            body(q)


def pre_start(*refs):
    pre_start_on(Staged(refs[:16]), *refs[16:])


def pre_start_on(
    staged, z_halo, halo_full, x_main,
    e, halo_e, force, halo_f, w0, w1, w2, w3, w4, w5, ua, ub, ha, ca, cb, edge_e, summed,
    hw, hb, hc, beside,
):
    nx, nz = staged.nx, staged.nz
    slots = nx + 6
    w = (w0, w1, w2, w3, w4, w5)
    viscosity_force(staged, z_halo, halo_full, x_main, e, halo_e, force, halo_f)
    first_fields(staged, z_halo, halo_full, x_main, ua, ub, ha)
    tile, column = fine_masks(nz + 8, slots)
    fill_edges(ca, ua, inside_slots(slots, 3))
    edge_e[...] = edges_of(lambda p: e[p], inside_slots(slots, 3))
    main_weights(e, halo_e, w, 0, early(nx, 1), range(2, nx + 3))
    main_sweep(ua, ha, ub, w, e, force, 0, tile, beside, early(nx, 1))
    halo_weights(halo_e, edge_e, hw)
    halo_sweep(ha, ca, hb, hw, halo_e, halo_f, column)
    fill_edges(cb, ub, inside_slots(slots, 0, early(nx, 1)))
    main_sweep(ub, hb, ua, w, e, force, 0, tile, beside, early(nx, 2))
    halo_sweep(hb, cb, hc, hw, halo_e, halo_f, column)
    residuals(ua, hc, beside, w, force, e, summed, early_block(nx))


def pre_smooth(
    x_rim, _e, _halo_e, _force, _halo_f, _w0, _w1, _w2, _w3, _w4, _w5, _ua, _ub, _ha, _ca, _cb,
    _edge_e, _summed, e, halo_e, force, halo_f, w0, w1, w2, w3, w4, w5, ua, ub, ha, ca, cb, edge_e,
    summed, hw, coarse, hb, beside,
):
    slots = e.shape[0]
    nx, nz = slots - 6, e.shape[1] - 8
    w = (w0, w1, w2, w3, w4, w5)
    add_rims(x_rim, nx, ua, ha, e, halo_e, force, halo_f, ca, edge_e)
    tile, column = fine_masks(nz + 8, slots)
    faces = [p for p in range(slots - 1) if not 3 <= p < nx + 2]
    main_weights(e, halo_e, w, 2, late(early(nx, 1)), faces)
    halo_weights(halo_e, edge_e, hw)
    main_sweep(ua, ha, ub, w, e, force, 2, tile, beside, late(early(nx, 1)))
    halo_sweep(ha, ca, hb, hw, halo_e, halo_f, column)
    fill_edges(cb, ub, inside_slots(slots, 2, late(early(nx, 1))), False)
    main_sweep(ub, hb, ua, w, e, force, 1, tile, beside, late(early(nx, 2)))
    halo_sweep(hb, cb, ha, hw, halo_e, halo_f, column)
    residuals(ua, ha, beside, w, force, e, summed, late(early_block(nx)))
    scale = (0.5, 0.5, 0.5, -1.0 / 32.0, 0.125)
    cz = nz // 2
    left = []
    for k in range(5):
        for r in range(nx // 4):
            halves = []
            for s in range(2):
                q = 2 * r + s
                even = summed[k, q, pl.ds(0, cz, stride=2)]
                halves.append((even + summed[k, q, pl.ds(1, cz, stride=2)]) * scale[k])
            left.append(jnp.concatenate(halves, axis=1))
    left = jnp.concatenate(left, axis=0)
    pick = iota((2 * LANES, LANES), 0) // 2 == iota((2 * LANES, LANES), 1)
    out = jnp.dot(
        left, pick.astype(F32), precision=lax.Precision.HIGHEST, preferred_element_type=F32
    )
    for k in range(5):
        for r in range(nx // 4):
            at = (k * (nx // 4) + r) * cz
            coarse[k, r] = out[at : at + cz]


def smooth_pack(fields, edges, x_fine):
    nx, nz = fields.shape[1] - 6, fields.shape[2] - 8
    for m in range(x_fine.shape[0]):
        high = high_side("gx", m)
        for k in range(4):
            for j in range(2):
                x_fine[m, 2 * k + j] = fields[k, 3 + high * (nx - 2) + j, pl.ds(0, nz)]

    def planes(k):
        return [fields[k, q + 3, pl.ds(0, nz)] for q in range(nx)]

    for j, x in enumerate(pair_edges(planes, 4, nz)):
        edges[j] = x


def fourth_pack(own, other, fields, whole, z_a, z_b):
    nx, nz = fields.shape[1] - 6, fields.shape[2] - 8
    pairs = whole.shape[1]
    cz = whole.shape[2]
    gx = lax.axis_index("gx")
    for k in range(5):
        for r in range(pairs):
            if other is None:
                whole[k, r] = own[k, r]
            else:
                mine = truth(jnp.where(gx == r // (pairs // 2), 1, 0), (cz, LANES))
                n = r % (pairs // 2)
                whole[k, r] = jnp.where(mine, own[k, n], other[k, n])
    row = iota((8, LANES), 0) // 2
    for m, out in enumerate((z_a, z_b)):
        right = high_side("gz", m)
        start = pl.multiple_of(right * (cz - 8), 8)
        for r in range(pairs):
            for k in range(2):
                parts = [
                    (whole[k + 2 * h, r, pl.ds(0, 8)], whole[k + 2 * h, r, pl.ds(cz - 8, 8)])
                    + (4 * h, 4)
                    for h in range(2)
                ]
                out[k * pairs + r] = z_strip(parts, right)
            out[2 * pairs + r] = whole[4, r, pl.ds(start, 8)]
        toward = truth(right, (8, LANES))
        for q in range(nx):
            total = jnp.zeros((8, LANES), F32)
            for k in range(4):
                low = roll(fields[k, q + 3, pl.ds(0, 8)], 2 * k, 0)
                high = roll(fields[k, q + 3, pl.ds(nz - 8, 8)], 2 * k - 6, 0)
                total = jnp.where(row == k, jnp.where(toward, high, low), total)
            out[3 * pairs + q] = total


def fold_rows(x):
    own = x.shape[0] - 16
    row = iota((8, LANES), 0)
    halo = jnp.where(row < 4, x[own : own + 8], x[own + 8 :])
    return jnp.concatenate([x[:own], halo], axis=0)


def deep_edges(pairs, width):
    per = LANES // (2 * width)
    columns = []
    for n, x in enumerate(pairs):
        for g in range(2):
            t = (2 * n + g) % per
            x_t = roll(x, 2 * width * t + width - 64 * g, 1)
            if t == 0:
                columns.append(x_t)
            else:
                slot = iota(x.shape, 1) // (2 * width)
                columns[-1] = jnp.where(slot == t, x_t, columns[-1])
    return columns


def unfold(left, right, width):
    spot = iota(left.shape, 1) % (2 * width)
    first = jnp.where(spot < width, left, roll(right, width, 1))
    second = jnp.where(spot < width, roll(left, -width, 1), right)
    return first, second


def fifth_pack(whole, z_a, z_b, edges, full, full_e, z_halo, y_a, y_b):
    pairs, cz = whole.shape[1:3]
    nx = z_halo.shape[1]
    nz = edges.shape[1]
    _, has_left, has_right = place("gz")
    to_left = truth(has_left, (8, LANES))
    to_right = truth(has_right, (8, LANES))
    deep = []
    for k in range(5):
        for r in range(pairs):
            if k < 4:
                n = k % 2 * pairs + r
                tile = z_tile(z_a[n], z_b[n], k // 2 * 4, 4)
                x = jnp.concatenate([whole[k, r], tile], axis=0)
                full[k, r] = x
            else:
                left, right = left_right("gz", z_a[2 * pairs + r], z_b[2 * pairs + r])
                right = jnp.where(to_right, right, 0.0)
                left = jnp.where(to_left, left, 0.0)
                x = jnp.concatenate([whole[k, r], right, left], axis=0)
                full_e[r] = x
            deep.append(x)
    row = iota((8, LANES), 0)
    for q in range(nx):
        left, right = left_right("gz", z_a[3 * pairs + q], z_b[3 * pairs + q])
        for k in range(4):
            x = jnp.where(row < 2 * has_right, roll(right, -2 * k, 0), 0.0)
            z_halo[k, q] = jnp.where(row >= 8 - 2 * has_left, roll(left, 6 - 2 * k, 0), x)
    columns = deep_edges(deep[: 4 * pairs], 4)
    half = len(columns) // 2
    columns_e = deep_edges(deep[4 * pairs :], 8)
    upper = (cz + 16) // 2
    behind = pair_edges(lambda i: [z_halo[i, q] for q in range(nx)], 4, 8)
    for m, out in enumerate((y_a, y_b)):
        toward = high_side("gy", m)
        parts = [
            strip(columns[j], columns[j + half], toward, 4) for j in range(half)
        ] + [strip(x[:upper], x[upper:], toward, 8) for x in columns_e]
        for i in range(nz // 8):
            parts.append(y_strip(edges[0, pl.ds(8 * i, 8)], edges[1, pl.ds(8 * i, 8)], toward))
        parts.append(y_strip(behind[0], behind[1], toward))
        n = 0
        for x in parts:
            for i in range(x.shape[0] // 8):
                out[n] = x[8 * i : 8 * i + 8]
                n += 1


def sixth_pack(y_a, y_b, z_halo, halo_full, x_rim):
    tiles = halo_full.shape[1] // 8
    first = y_a.shape[0] - tiles
    for i in range(tiles):
        for j, x in enumerate(merge_y(y_a[first + i], y_b[first + i])):
            halo_full[j, pl.ds(8 * i, 8)] = x
    nx = z_halo.shape[1]

    def rim(plane):
        return [rows_of([(z_halo[k, plane(1)], 2 * k, 2 * k - 1, 2) for k in range(4)])]

    pack_rim(x_rim, rim, lambda j: halo_full[j], 4, 1, nx)


def coarse_solve(full, full_e, y_a, y_b, main, halo, ca, cb, force, e, w0, w1, w2, w3, w4, w5, deep_e, grown):
    pairs, rows = full.shape[1:3]
    deep = full_e.shape[1]
    planes = 2 * pairs
    own = main.shape[1] - 2
    cz = rows - 8
    half = LANES // 2
    _, zl, zr = place("gz")
    _, yl, yr = place("gy")
    two = lax.axis_size("gx") == 2
    gx = FIXED[-1][0] if two else lax.axis_index("gx")

    def inside(rows, width):
        lane = iota((rows, LANES), 1)
        row = iota((rows, LANES), 0)
        kept = (row < cz + width * zr) | (row >= rows - width * zl)
        return kept & ((lane < half + width * yr) | (lane >= LANES - width * yl))

    zero = jnp.zeros((rows, LANES), F32)
    w = (w0, w1, w2, w3, w4, w5)
    for k in range(4):
        for p in (0, planes + 1):
            ca[k, p] = zero
            cb[k, p] = zero
    e[0] = zero
    e[planes + 1] = zero
    deep_e[0] = jnp.zeros((deep, LANES), F32)
    deep_e[planes + 1] = jnp.zeros((deep, LANES), F32)

    tiles, deep_tiles = rows // 8, deep // 16
    count = pairs // 4
    columns = []

    def taken(n, tiles):
        a, b = (jnp.concatenate([ref[n + i] for i in range(tiles)], axis=0) for ref in (y_a, y_b))
        return left_right("gy", a, b)

    unfolded = [unfold(*taken(j * tiles, tiles), 4) for j in range(count)]
    columns = [x for x, _ in unfolded] + [x for _, x in unfolded]
    columns_e = []
    for j in range(-(-pairs // 4)):
        x = unfold(*taken(count * tiles + j * deep_tiles, deep_tiles), 8)
        columns_e.append(jnp.concatenate(x, axis=0))

    def whole_plane(pair, columns, n, s, width):
        lane = iota(pair.shape, 1)
        per = LANES // (2 * width)
        last, first = 2 * n + 1 - s, 2 * n + s
        low = roll(columns[first // per], half - 2 * width * (first % per) - width, 1)
        high = roll(columns[last // per], LANES - width - 2 * width * (last % per), 1)
        x = jnp.where(lane < half, roll(pair, -s * half, 1), low)
        return jnp.where(lane < LANES - width, x, high)

    near, far = inside(rows, 4), inside(deep, 8)
    for r in range(pairs):
        for s in range(2):
            p = 2 * r + s
            x = jnp.where(far, whole_plane(full_e[r], columns_e, r, s, 8), 0.0)
            deep_e[p + 1] = x
            e[p + 1] = fold_rows(x)
            for k in range(4):
                x = whole_plane(full[k, r], columns, k * pairs + r, s, 4)
                force[k, p] = jnp.where(near, x, 0.0)

    def shifts(x):
        return (
            roll(x, LANES - 1, 1),
            roll(x, 1, 1),
            roll(x, x.shape[0] - 1, 0),
            roll(x, 1, 0),
        )

    def two_by_two(width, body):
        if two:
            for p in range(max(gx * own - width, 0), min(gx * own + own + width, planes)):
                body(p + 1)
            return
        lo = jnp.maximum(gx * own - width, 0)
        hi = jnp.minimum(gx * own + own + width, planes)
        steps = (hi - lo + 1) // 2
        lo = jnp.minimum(lo, planes - 2 * steps)

        def step(i, carry):
            body(lo + 2 * i + 1)
            body(lo + 2 * i + 2)
            return carry

        lax.fori_loop(0, steps, step, 0)

    def start(p):
        x = deep_e[p]
        up, down = x + deep_e[p + 1], x + deep_e[p - 1]
        w0[p] = fold_rows(up)
        total = up + down
        for n, y in enumerate(shifts(x)):
            total += x + y
            w[1 + n][p] = fold_rows(x + y)
        factor = jnp.where(near, fold_rows(relax_weight / total), 0.0)
        w5[p] = factor
        for k in range(3):
            ca[k, p] = factor * force[k, p - 1]
        ca[3, p] = e[p] * force[3, p - 1]

    w0[0] = e[0] + e[1]
    two_by_two(planes, start)

    def sweep(src, dst, width):
        def body(p):
            wxp, wxm = w0[p], w0[p - 1]
            wyp, wym, wzp, wzm = w1[p], w2[p], w3[p], w4[p]
            x = src[3, p]
            around = shifts(x)
            up, down = src[3, p + 1], src[3, p - 1]
            spread = 0.0
            for k in range(3):
                u = src[k, p]
                yp, ym, zp, zm = shifts(u)
                xp, xm = src[k, p + 1], src[k, p - 1]
                total = force[k, p - 1] - 2.0 * terms(k, up, down, *around)
                total += wxp * xp + wxm * xm
                total += wyp * yp + wym * ym
                total += wzp * zp + wzm * zm
                spread += terms(k, xp, xm, yp, ym, zp, zm)
                dst[k, p] = jnp.where(near, 0.4 * u + w5[p] * total, 0.0)
            dst[3, p] = jnp.where(near, x + e[p] * (force[3, p - 1] - 0.125 * spread), 0.0)

        two_by_two(width, body)

    sweep(ca, cb, 3)
    sweep(cb, ca, 2)
    sweep(ca, cb, 1)

    lane = iota((LANES, 2 * LANES), 1)
    cell = iota((LANES, 2 * LANES), 0)
    spot = lane % SLOT
    wanted = jnp.where(spot < 4, LANES - 2, half - 2) + spot // 2
    slot = (lane - LANES) // SLOT
    column = jnp.zeros((4 * rows, LANES), F32)
    first = gx * own

    def grow(ref, index, x):
        ref[index + (pl.ds(0, cz, stride=2),)] = x[:cz]
        ref[index + (pl.ds(1, cz, stride=2),)] = x[:cz]
        grown[pl.ds(0, 8, stride=2)] = x[cz:]
        grown[pl.ds(1, 8, stride=2)] = x[cz:]
        r = iota((8, LANES), 0)
        tail = jnp.where(r < 4, grown[pl.ds(0, 8)], grown[pl.ds(8, 8)])
        ref[index + (pl.ds(2 * cz, 8),)] = tail

    for i in range(own + 2):
        x = jnp.concatenate([cb[k, first + i] for k in range(4)], axis=0)
        here = (lane >= LANES) & ((slot + 1) // 2 - 1 == i) & (cell == wanted)
        chosen = (here | ((lane < LANES) & (lane // 2 == cell))).astype(F32)
        wide = jnp.dot(x, chosen, precision=lax.Precision.HIGHEST, preferred_element_type=F32)
        for k in range(4):
            grow(main, (k, i), wide[k * rows : (k + 1) * rows, :LANES])
        column += wide[:, LANES:]
    for k in range(4):
        grow(halo, (k,), column[k * rows : (k + 1) * rows])


def post_start(
    e, halo_e, force, halo_f, w0, w1, w2, w3, w4, w5, hw,
    fields, z_halo, halo_full, x_fine, main, column, ua, ub, ha, ca, part,
    hb, beside,
):
    _, nx, nz, _ = part.shape
    slots = nx + 6
    w = (w0, w1, w2, w3, w4, w5)
    zero = jnp.zeros((nz + 8, LANES), F32)
    tile, inside = fine_masks(nz + 8, slots)
    for k in range(4):
        for p in (1, 2, nx + 3, nx + 4):
            ua[k, p] = zero
            ub[k, p] = zero
        for q in range(nx):
            i = q // 2 + 1
            ua[k, q + 3, pl.ds(0, nz)] = fields[k, q + 3, pl.ds(0, nz)] + main[k, i, pl.ds(0, nz)]
            ua[k, q + 3, pl.ds(nz, 8)] = z_halo[k, q] + main[k, i, pl.ds(nz, 8)]
        x = own_slots(halo_full[k % 2], nx, k // 2) + column[k]
        ha[k] = jnp.where(inside, x, 0.0)
    for m in range(x_fine.shape[0]):
        right, valid = x_side(m)
        there = truth(valid, (nz, LANES))
        there8 = truth(valid, (8, LANES))
        i = right * (nx // 2 + 1)
        for k in range(4):
            for j in range(2):
                at = 1 + right * (nx + 2) + j
                x = x_fine[m, 2 * k + j] + main[k, i, pl.ds(0, nz)]
                ua[k, at, pl.ds(0, nz)] = jnp.where(there, x, 0.0)
            x = jnp.where(there8, main[k, i, pl.ds(nz, 8)], 0.0)
            ua[k, 2 + right * (nx + 1), pl.ds(nz, 8)] = x
    fill_edges(ca, ua, inside_slots(slots, 2))
    main_sweep(ua, ha, ub, w, e, force, 0, tile, beside, early(nx, 1))
    halo_sweep(ha, ca, hb, hw, halo_e, halo_f, inside)

    def store(p, k, x):
        part[k, p - 3] = x

    last_sweep(ub, hb, beside, w, e, force, early(nx, 2), store)


def last_sweep(src, halo, beside, w, e, force, chosen, store):
    slots, nz = src.shape[1], src.shape[2] - 8
    spread_halo(halo, beside, slots, 0, chosen, False)

    def body(p):
        new = main_operator(src, beside, w, force, p, nz)
        new = relaxed(*new, w[5][p, pl.ds(0, nz)], e[p, pl.ds(0, nz)])
        for k in range(4):
            store(p, k, new[k])

    over_planes(slots, 0, body, chosen)


def post_smooth(
    x_rim, part, e, halo_e, force, halo_f, w0, w1, w2, w3, w4, w5, hw,
    _ua, _ub, _ha, _ca, v_out, p_out, ua, ub, ha, ca,
    hb, beside,
):
    nx, nz, _ = p_out.shape
    slots = nx + 6
    w = (w0, w1, w2, w3, w4, w5)
    tile, inside = fine_masks(nz + 8, slots)
    tail = pl.ds(nz, 8)
    slot = iota((8, LANES), 1) // SLOT
    for m in range(x_rim.shape[0]):
        right, valid = x_side(m)
        there = truth(valid, (8, LANES))
        tiles = (nz + 8) // 8
        side = jnp.concatenate([x_rim[m, 1 + r] for r in range(tiles)], axis=0)
        near = 2 + right * (nx + 1)
        for k in range(4):
            x = ua[k, near, tail] + jnp.where(there, roll(x_rim[m, 0], -2 * k, 0), 0.0)
            ua[k, near, tail] = x
            ca[k, tail] = jnp.where(slot == near, roll(x, near * SLOT + 4, 1), ca[k, tail])
            x, _ = rim_halo(side, k, SLOT, 1, right, valid, nx)
            ha[k] = ha[k] + x
    main_sweep(ua, ha, ub, w, e, force, 1, tile, beside, late(early(nx, 1)))
    halo_sweep(ha, ca, hb, hw, halo_e, halo_f, inside)

    def store(p, k, x):
        if k < 3:
            v_out[k, p - 3] = x
        else:
            p_out[p - 3] = x

    last_sweep(ub, hb, beside, w, e, force, late(early(nx, 2)), store)
    for q in range(nx):
        if early(nx, 2)(q + 3):
            for k in range(4):
                store(q + 3, k, part[k, q])


def local(velocity, pressure, viscosity, body_force):
    nx, nz, ny = pressure.shape
    if ny != LANES or nx * SLOT * 2 != LANES or nz % 16:
        raise ValueError("unsupported block")
    sides = x_messages()
    rows, slots = nz + 8, nx + 6
    inputs = [velocity, pressure, viscosity, body_force]
    block = (nz, LANES)

    z_shape = (3 * nx, 8, LANES)
    half = (nx // 2,) + block
    *staged, y_a, y_b = call(
        first_pack, [half] * 16 + [(2,) + block] * 2, inputs, outside=4, copies=16
    )
    x_main, z_a, z_b = call(side_pack, [(sides, 21) + block, z_shape, z_shape], staged)
    y_a, y_b = swap(y_a, "gy", 0), swap(y_b, "gy", 1)
    x_main = swap_x(x_main)
    halo, z_b = call(second_pack, [(4,) + block, z_shape], [z_b, y_a, y_b])
    (z_a,) = call(second_pack_near, [z_shape], [z_a, halo])
    z_a, z_b = swap(z_a, "gz", 0), swap(z_b, "gz", 1)
    tiles = rows // 8
    z_first, halo_first, x_first = call(
        third_pack,
        [(8, nx, 8, LANES), (4, rows, LANES), (sides, 6 + tiles, 8, LANES)],
        [z_a, z_b, halo],
    )
    x_first = swap_x(x_first)

    spread, column = (4, slots, rows, LANES), (4, rows, LANES)
    started = [(slots, rows, LANES), (rows, LANES), (3, slots, rows, LANES), (3, rows, LANES)]
    started += [(slots, rows, LANES)] * 6 + [spread, spread] + [column] * 3 + [(rows, LANES)]
    started += [(5, nx // 2, nz, LANES)]
    state = call(
        by_sides(pre_start),
        started,
        [*staged, z_first, halo_first, x_main],
        [(7, rows, LANES), column, column, spread],
        cost=4,
    )
    *operator, fields, _, _, _, _, _, _, factors, own = call(
        by_sides(pre_smooth),
        started + [(7, rows, LANES), (5, nx // 4, nz // 2, LANES)],
        [x_first, *state],
        [column, spread],
        cost=8,
        aliases={i + 1: i for i in range(len(started))},
    )
    operator.append(factors)
    edges, x_fine = call(smooth_pack, [(2,) + block, (sides, 8) + block], [fields])
    if lax.axis_size("gx") == 2:
        parts = [own, swap(own, "gx", 0)]
        gather = fourth_pack
    else:
        parts = [lax.all_gather(own, "gx", axis=1, tiled=True)]

        def gather(a, *refs):
            fourth_pack(a, None, *refs)

    x_fine = swap_x(x_fine)
    pairs = lax.axis_size("gx") * (nx // 4)
    z_shape = (3 * pairs + nx, 8, LANES)
    whole, z_a, z_b = call(
        gather, [(5, pairs, nz // 2, LANES), z_shape, z_shape], parts + [fields]
    )
    z_a, z_b = swap(z_a, "gz", 0), swap(z_b, "gz", 1)
    deep = nz // 2 + 16
    shallow = deep - 8
    y_shape = (pairs // 4 * (shallow // 8) + -(-pairs // 4) * (deep // 16) + tiles, 8, LANES)
    full, full_e, z_halo, y_a, y_b = call(
        fifth_pack,
        [(4, pairs, shallow, LANES), (pairs, deep, LANES), (4, nx, 8, LANES), y_shape, y_shape],
        [whole, z_a, z_b, edges],
    )
    y_a, y_b = swap(y_a, "gy", 0), swap(y_b, "gy", 1)
    halo_full, x_rim = call(
        sixth_pack,
        [(2, rows, LANES), (sides, 1 + tiles, 8, LANES)],
        [y_a, y_b, z_halo],
    )
    x_rim = swap_x(x_rim)
    planes = 2 * pairs
    plane = (shallow, LANES)
    grown, beside = call(
        by_sides(coarse_solve),
        [(4, nx // 2 + 2, rows, LANES), (4, rows, LANES)],
        [full, full_e, y_a, y_b],
        [(4, planes + 2) + plane] * 2
        + [(4, planes) + plane]
        + [(planes + 2,) + plane] * 7
        + [(planes + 2, deep, LANES), (16, LANES)],
        cost=4,
    )
    *state, part = call(
        by_sides(post_start),
        [spread, spread, column, column, (4, nx) + block],
        operator + [fields, z_halo, halo_full, x_fine, grown, beside],
        [column, spread],
        cost=4,
    )
    first = 2 + len(operator)
    v_out, p_out, *_ = call(
        by_sides(post_smooth),
        [(3, nx) + block, (nx,) + block, spread, spread, column, column],
        [x_rim, part] + operator + state,
        [column, spread],
        cost=8,
        aliases={first + i: 2 + i for i in range(4)},
    )
    return v_out, p_out


def swap_x(array):
    if array.shape[0] == 1:
        return swap(array, "gx", 0)
    parts = [swap(array[m], "gx", m) for m in range(2)]
    return jnp.stack(parts)


def solution(mesh):
    return jax.shard_map(
        local,
        mesh=mesh,
        in_specs=(
            P(None, "gx", "gz", "gy"),
            P("gx", "gz", "gy"),
            P("gx", "gz", "gy"),
            P(None, "gx", "gz", "gy"),
        ),
        out_specs=(P(None, "gx", "gz", "gy"), P("gx", "gz", "gy")),
        check_vma=False,
    )
```

```python
import jax
import jax.numpy as jnp
from jax import lax
from jax.experimental import pallas as pl
from jax.experimental.pallas import tpu as pltpu
from jax.sharding import PartitionSpec as P

LANES = 128
SLOT = 8
F32 = jnp.float32
relax_weight = 0.6
HELD = 846 * 2**16
Z_PLACES = (
    ((0, 0, 3), (1, 3, 3), (5, 6, 2)),
    ((2, 0, 3), (3, 3, 3), (6, 6, 2)),
    ((4, 0, 3), (7, 3, 2)),
)


def call(body, outs, args, scratch=(), cost=1, outside=0, copies=0, aliases=None):
    return pl.pallas_call(
        body,
        out_shape=[jax.ShapeDtypeStruct(shape, F32) for shape in outs],
        in_specs=[pl.BlockSpec(memory_space=pltpu.HBM)] * outside
        + [pl.BlockSpec(memory_space=pltpu.VMEM)] * (len(args) - outside),
        out_specs=[pl.BlockSpec(memory_space=pltpu.VMEM)] * len(outs),
        scratch_shapes=[pltpu.VMEM(shape, F32) for shape in scratch]
        + [pltpu.SemaphoreType.DMA((copies,))] * (copies > 0),
        input_output_aliases=aliases or {},
        compiler_params=pltpu.CompilerParams(vmem_limit_bytes=HELD if outside else 40 * 2**20),
        cost_estimate=pl.CostEstimate(
            flops=cost * 10**6, bytes_accessed=cost * 10**6, transcendentals=0
        ),
    )(*args)


def swap(array, axis, which):
    count = lax.axis_size(axis)
    if axis != "gx" and which == 1:
        ys, zs = lax.axis_size("gy"), lax.axis_size("gz")
        pairs = []
        for y in range(ys):
            for z in range(zs):
                i = y if axis == "gy" else z
                j = i + 1 if i % 2 else i - 1
                if axis == "gy":
                    to = (j, z) if 0 <= j < count else (y, z ^ 1)
                else:
                    to = (y, j) if 0 <= j < count else (y ^ 1, z)
                pairs.append((y * zs + z, to[0] * zs + to[1]))
        return lax.ppermute(array, ("gy", "gz"), pairs)
    pairs = []
    for i in range(which, count, 2):
        j = (i + 1) % count
        pairs += [(i, j), (j, i)]
    return lax.ppermute(array, axis, pairs)


FIXED = []


def by_sides(body):
    def kernel(*refs):
        count = lax.axis_size("gx")
        _, xl, xr = place("gx")
        for sides in [(0, 1), (1, 0), (1, 1)][: 2 if count == 2 else 3]:

            def branch(sides=sides):
                FIXED.append(sides)
                body(*refs)
                FIXED.pop()

            pl.when((xl == sides[0]) & (xr == sides[1]))(branch)

    return kernel


def place(axis):
    if axis == "gx" and FIXED:
        return (None,) + FIXED[-1]
    i = lax.axis_index(axis)
    last = lax.axis_size(axis) - 1
    return i, jnp.where(i > 0, 1, 0), jnp.where(i < last, 1, 0)


def iota(shape, dim):
    return lax.broadcasted_iota(jnp.int32, shape, dim)


def truth(flag, shape):
    return jnp.full(shape, flag, jnp.int32) > 0


def roll(x, shift, dim):
    if isinstance(shift, int):
        shift %= x.shape[dim]
        return x if shift == 0 else pltpu.roll(x, shift, dim)
    return pltpu.roll(x, lax.rem(shift + 2 * x.shape[dim], x.shape[dim]), dim)


def high_side(axis, message):
    return jnp.where(lax.axis_index(axis) % 2 == message, 1, 0)


def left_right(axis, a, b):
    odd = truth(lax.axis_index(axis) % 2, a.shape)
    return jnp.where(odd, a, b), jnp.where(odd, b, a)


def x_messages():
    return 1 if lax.axis_size("gx") == 2 else 2


def pair_edges(planes, fields, rows):
    lane = iota((rows, LANES), 1) // SLOT
    half = fields // 2
    out = []
    for j in range(half):
        total = jnp.zeros((rows, LANES), F32)
        for part in range(2):
            for q, x in enumerate(planes(j + part * half)):
                slot = q + part * (LANES // SLOT // 2)
                total = jnp.where(lane == slot, roll(x, slot * SLOT + 4, 1), total)
        out.append(total)
    return out


def merge_y(a, b):
    _, has_left, has_right = place("gy")
    left, right = left_right("gy", a, b)
    spot = iota(a.shape, 1) % SLOT
    kept = (spot < 4 * has_left) | (spot >= SLOT - 4 * has_right)
    first = jnp.where(spot < 4, left, roll(right, 4, 1))
    second = jnp.where(spot < 4, roll(left, -4, 1), right)
    return jnp.where(kept, first, 0.0), jnp.where(kept, second, 0.0)


class Staged:
    def __init__(self, refs):
        self.refs = refs
        self.half, self.nz = refs[0].shape[:2]
        self.nx = 2 * self.half

    def __getitem__(self, index):
        i, q = index[:2]
        return self.refs[2 * i + q // self.half][(q % self.half,) + index[2:]]


def first_pack(v_in, p_in, e_in, f_in, *refs):
    staged = Staged(refs[:16])
    y_a, y_b, arrived = refs[16:]
    nx, nz = staged.nx, staged.nz
    loads = []
    for n in range(16):
        i, planes = n // 2, pl.ds(n % 2 * staged.half, staged.half)
        if i < 3:
            part = v_in.at[i, planes]
        elif i < 5:
            part = (p_in, e_in)[i - 3].at[planes]
        else:
            part = f_in.at[i - 5, planes]
        loads.append(pltpu.make_async_copy(part, refs[n], arrived.at[n]))
    for load in loads:
        load.start()
    for load in loads:
        load.wait()
    edges = pair_edges(lambda i: [staged[i, q] for q in range(nx)], 8, nz)
    for m, out in enumerate((y_a, y_b)):
        for j in range(2):
            out[j] = y_strip(edges[j], edges[j + 2], high_side("gy", m))


def side_pack(*refs):
    staged = Staged(refs[:16])
    x_main, z_a, z_b = refs[16:]
    nx, nz = staged.nx, staged.nz
    for m in range(x_main.shape[0]):
        top = truth(high_side("gx", m), (nz, LANES))
        n = 0
        for i in range(8):
            width = 3 if i < 5 else 2
            for j in range(width):
                x_main[m, n] = jnp.where(top, staged[i, nx - width + j], staged[i, j])
                n += 1
    low, high = pl.ds(0, 8), pl.ds(nz - 8, 8)
    for q in range(nx):
        for n, fields in enumerate(Z_PLACES):
            for m, out in enumerate((z_a, z_b)):
                out[3 * q + n] = z_strip(
                    [(staged[i, q, low], staged[i, q, high], at, rows) for i, at, rows in fields],
                    high_side("gz", m),
                )


def strip(first, second, toward_right, width):
    right = truth(toward_right, first.shape)
    spot = iota(first.shape, 1) % (2 * width)
    first = jnp.where(right, first, roll(first, -width, 1))
    second = jnp.where(right, roll(second, width, 1), second)
    return jnp.where(spot < width, first, second)


def y_strip(first, second, toward_right):
    return strip(first, second, toward_right, SLOT // 2)


def z_strip(parts, toward_right):
    right = truth(toward_right, (8, LANES))
    return rows_of(
        [
            (jnp.where(right, roll(high, at + rows, 0), roll(low, at, 0)), 0, at, rows)
            for low, high, at, rows in parts
        ]
    )


def z_tail(halo, first, out, message):
    nz = halo.shape[1]
    row = iota((8, LANES), 0)
    for n in range(first.shape[0]):
        out[n] = first[n]
    for j in range(4):
        tiles = halo[j, pl.ds(0, 8)], halo[j, pl.ds(nz - 8, 8)]
        x = z_strip([tiles + (5, 3)], high_side("gz", message))
        out[3 * j + 2] = jnp.where(row < 5, first[3 * j + 2], x)


def second_pack(z_first, y_a, y_b, halo, z_b):
    for j in range(2):
        halo[j], halo[j + 2] = merge_y(y_a[j], y_b[j])
    z_tail(halo, z_first, z_b, 1)


def second_pack_near(z_first, halo, z_a):
    z_tail(halo, z_first, z_a, 0)


def z_tile(a, b, at, rows):
    _, has_left, has_right = place("gz")
    left, right = left_right("gz", a, b)
    row = iota(a.shape, 0)
    x = jnp.where(row < rows * has_right, roll(right, -at, 0), 0.0)
    return jnp.where(row >= 8 - rows * has_left, roll(left, 8 - at - rows, 0), x)


def third_pack(z_a, z_b, halo, z_halo, halo_full, x_rim):
    nx = z_halo.shape[1]
    nz = halo.shape[1]
    for q in range(nx):
        for n, fields in enumerate(Z_PLACES):
            for i, at, rows in fields:
                z_halo[i, q] = z_tile(z_a[3 * q + n], z_b[3 * q + n], at, rows)
    for j in range(4):
        halo_full[j, pl.ds(0, nz)] = halo[j]
        halo_full[j, pl.ds(nz, 8)] = z_tile(z_a[3 * j + 2], z_b[3 * j + 2], 5, 3)

    def tiles(plane):
        out = [
            rows_of([(z_halo[i, plane(1)], 0, 6, 4), (z_halo[i, plane(2)], 3, 2, 2)])
            for i in range(5)
        ]
        force = zip((0, 3, 5), (7, 2, 4))
        out.append(
            rows_of([(z_halo[5 + k, plane(1)], at, row, 2) for k, (at, row) in enumerate(force)])
        )
        return out

    pack_rim(x_rim, tiles, lambda j: halo_full[j], 8, 2, nx)


def rows_of(parts):
    row = iota((8, LANES), 0)
    total = jnp.zeros((8, LANES), F32)
    for x, shift, first, count in parts:
        total = jnp.where((row - first) % 8 < count, roll(x, shift, 0), total)
    return total


def pack_rim(x_rim, tiles, halo_pair, fields, planes, nx):
    half = fields // 2
    stride = LANES // 8 if fields == 8 else SLOT
    for m in range(x_rim.shape[0]):
        high = high_side("gx", m)
        done = tiles(lambda d, high=high: high * (nx - 2 * d + 1) + d - 1)
        for n, x in enumerate(done):
            x_rim[m, n] = x
        pairs = [halo_pair(j) for j in range(half)]
        rows = pairs[0].shape[0]
        column = iota((rows, LANES), 1) // stride
        first = high * (nx - planes) * SLOT
        total = jnp.zeros((rows, LANES), F32)
        for i in range(fields):
            at = i * stride - first - (i // half) * (LANES // 2)
            total = jnp.where(column == i, roll(pairs[i % half], at + LANES, 1), total)
        for r in range(rows // 8):
            x_rim[m, len(done) + r] = total[8 * r : 8 * r + 8]


def main_shifts(x, beside, kept):
    rows = x.shape[0]
    y, beside = x[:kept], beside[:kept]
    lane = iota(y.shape, 1)
    return (
        roll(jnp.where(lane == 0, beside, y), LANES - 1, 1),
        roll(jnp.where(lane == LANES - 1, beside, y), 1, 1),
        roll(x, rows - 1, 0)[:kept],
        roll(x, 1, 0)[:kept],
    )


def halo_shifts(x, edge):
    spot = iota(x.shape, 1) % SLOT
    rows = x.shape[0]
    return (
        roll(x, LANES - SLOT, 1),
        roll(x, SLOT, 1),
        roll(jnp.where(spot == 4, edge, x), LANES - 1, 1),
        roll(jnp.where(spot == 3, edge, x), 1, 1),
        roll(x, rows - 1, 0),
        roll(x, 1, 0),
    )


def main_weights(e, halo_e, w, width, chosen, faces):
    slots = e.shape[0]
    for p in faces:
        w[0][p] = e[p] + e[p + 1]

    def body(p):
        x = e[p]
        total = w[0][p] + w[0][p - 1]
        for n, y in enumerate(main_shifts(x, roll(halo_e[...], LANES - SLOT * p - 4, 1), x.shape[0])):
            total += x + y
            w[1 + n][p] = x + y
        w[5][p] = relax_weight / total

    over_planes(slots, width, body, chosen)


def halo_weights(e, edge_e, w):
    x = e[...]
    total = jnp.zeros_like(x)
    for n, y in enumerate(halo_shifts(x, edge_e[...])):
        total += x + y
        w[n] = x + y
    w[6] = relax_weight / total


def terms(k, up, down, yp, ym, zp, zm):
    return (up - down, zp - zm, yp - ym)[k]


def spread_halo(halo, beside, slots, width, chosen=None, full=True):
    kept = beside.shape[2] - (0 if full else 8)

    def body(p):
        for k in range(4):
            beside[k, p, pl.ds(0, kept)] = roll(halo[k][:kept], LANES - SLOT * p - 4, 1)

    over_planes(slots, width, body, chosen)


def main_operator(src, beside, w, force, p, kept):
    def at(ref, *index):
        return ref[index + (pl.ds(0, kept),)]

    wxp, wxm, wyp, wym, wzp, wzm = (
        at(ref, q) for ref, q in zip((w[0],) + w[:5], (p, p - 1, p, p, p, p))
    )
    around = main_shifts(src[3, p], at(beside, 3, p), kept)
    up, down = at(src, 3, p + 1), at(src, 3, p - 1)
    olds, sums, spread = [], [], 0.0
    for k in range(3):
        yp, ym, zp, zm = main_shifts(src[k, p], at(beside, k, p), kept)
        xp, xm = at(src, k, p + 1), at(src, k, p - 1)
        total = at(force, k, p) - terms(k, up, down, *around)
        total += wxp * xp + wxm * xm
        total += wyp * yp + wym * ym
        total += wzp * zp + wzm * zm
        spread += terms(k, xp, xm, yp, ym, zp, zm)
        olds.append(at(src, k, p))
        sums.append(total)
    olds.append(at(src, 3, p))
    return olds, sums, spread


def halo_operator(halo, edge, w, force):
    x = halo[3]
    px = halo_shifts(x, edge[3])
    olds, sums, spread = [], [], 0.0
    for k in range(3):
        u = halo[k]
        around = halo_shifts(u, edge[k])
        total = force[k] - terms(k, *px)
        for n in range(6):
            total += w[n] * around[n]
        spread += terms(k, *around)
        olds.append(u)
        sums.append(total)
    olds.append(x)
    return olds, sums, spread


def relaxed(olds, sums, spread, factor, e):
    new = [0.4 * olds[k] + factor * sums[k] for k in range(3)]
    return new + [olds[3] - 0.25 * e * spread]


def edges_of(plane, slots, total=None):
    shape = plane(slots[0]).shape
    slot = iota(shape, 1) // SLOT
    total = jnp.zeros(shape, F32) if total is None else total
    for p in slots:
        total = jnp.where(slot == p, roll(plane(p), p * SLOT + 4, 1), total)
    return total


def fill_edges(edge, src, slots, fresh=True):
    for k in range(4):
        edge[k] = edges_of(lambda p: src[k, p], slots, None if fresh else edge[k])


def fine_masks(rows, slots):
    nz = rows - 8
    _, zl, zr = place("gz")
    _, yl, yr = place("gy")
    _, xl, xr = place("gx")
    r = iota((8, LANES), 0)
    tile = (r < 4 * zr) | (r >= 8 - 4 * zl)
    r = iota((rows, LANES), 0)
    lane = iota((rows, LANES), 1)
    spot, slot = lane % SLOT, lane // SLOT
    column = (r < nz + 4 * zr) | (r >= rows - 4 * zl)
    column &= (spot < 4 * yl) | (spot >= SLOT - 4 * yr)
    column &= (slot >= 3 - 3 * xl) & (slot < slots - 3 + 3 * xr)
    return tile, column


def main_sweep(src, halo, dst, w, e, force, width, tile, beside, chosen=None):
    nz = src.shape[2] - 8
    slots = src.shape[1]

    def body(p):
        new = relaxed(*main_operator(src, beside, w, force, p, nz + 8), w[5][p], e[p])
        for k in range(4):
            x = new[k]
            dst[k, p, pl.ds(0, nz)] = x[:nz]
            dst[k, p, pl.ds(nz, 8)] = jnp.where(tile, x[nz:], 0.0)

    spread_halo(halo, beside, slots, width, chosen)
    over_planes(slots, width, body, chosen)


def halo_sweep(halo, edge, halo_dst, hw, halo_e, halo_f, column):
    new = relaxed(*halo_operator(halo, edge, hw, halo_f), hw[6], halo_e[...])
    for k in range(4):
        halo_dst[k] = jnp.where(column, new[k], 0.0)


def over_planes(slots, width, body, chosen=None):
    _, xl, xr = place("gx")
    for p in range(3 - width, slots - 3 + width):
        wanted = True if chosen is None else chosen(p)
        if wanted and (p >= 3 or xl) and (p < slots - 3 or xr):
            body(p)


def own_slots(x, nx, part):
    lane = iota(x.shape, 1)
    x = roll(x, 3 * SLOT - part * (LANES // 2), 1)
    return jnp.where((lane >= 3 * SLOT) & (lane < (3 + nx) * SLOT), x, 0.0)


def x_side(m):
    _, has_left, has_right = place("gx")
    if lax.axis_size("gx") == 2:
        return has_right, 1
    right = high_side("gx", m)
    return right, jnp.where(right > 0, has_right, has_left)


def rim_halo(x, t, stride, planes, right, valid, nx):
    base = right * (nx + 3) + (1 - right) * (3 - planes)
    lane = iota(x.shape, 1)
    x = roll(x, base * SLOT - t * stride + LANES, 1)
    kept = (lane >= base * SLOT) & (lane < (base + planes * valid) * SLOT)
    return jnp.where(kept, x, 0.0), kept


def viscosity_force(staged, z_halo, halo_full, x_main, e, halo_e, force, halo_f):
    nx, nz = staged.nx, staged.nz
    slots = nx + 6
    zero = jnp.zeros((nz + 8, LANES), F32)
    for p in list(range(3)) + list(range(nx + 3, slots)):
        e[p] = zero
        for k in range(3):
            force[k, p] = zero
    for q in range(nx):
        e[q + 3, pl.ds(0, nz)] = staged[4, q]
        e[q + 3, pl.ds(nz, 8)] = z_halo[4, q]
        for k in range(3):
            force[k, q + 3, pl.ds(0, nz)] = 2.0 * staged[5 + k, q]
            force[k, q + 3, pl.ds(nz, 8)] = 2.0 * z_halo[5 + k, q]
    halo_e[...] = own_slots(halo_full[0], nx, 1)
    for k in range(3):
        halo_f[k] = 2.0 * own_slots(halo_full[k + 1], nx, 1)
    for m in range(x_main.shape[0]):
        right, valid = x_side(m)
        there = truth(valid, (nz, LANES))
        for j in range(3):
            e[right * (nx + 3) + j, pl.ds(0, nz)] = jnp.where(there, x_main[m, 12 + j], 0.0)
        for j in range(2):
            at = right * (nx + 2) + 1 + j
            for k in range(3):
                force[k, at, pl.ds(0, nz)] = jnp.where(there, 2.0 * x_main[m, 15 + 2 * k + j], 0.0)


def first_fields(staged, z_halo, halo_full, x_main, u, other, halo):
    nx, nz = staged.nx, staged.nz
    slots = nx + 6
    zero = jnp.zeros((nz + 8, LANES), F32)
    for k in range(4):
        for p in list(range(3)) + list(range(nx + 3, slots)):
            u[k, p] = zero
            other[k, p] = zero
        for q in range(nx):
            u[k, q + 3, pl.ds(0, nz)] = staged[k, q]
            u[k, q + 3, pl.ds(nz, 8)] = z_halo[k, q]
        halo[k] = own_slots(halo_full[k], nx, 0)
    for m in range(x_main.shape[0]):
        right, valid = x_side(m)
        there = truth(valid, (nz, LANES))
        for k in range(4):
            for j in range(3):
                x = jnp.where(there, x_main[m, 3 * k + j], 0.0)
                u[k, right * (nx + 3) + j, pl.ds(0, nz)] = x


def add_rims(x_rim, nx, u, halo, e, halo_e, force, halo_f, edge, edge_e):
    nz = e.shape[1] - 8
    tiles = (nz + 8) // 8
    tail = pl.ds(nz, 8)
    slot = iota((8, LANES), 1) // SLOT
    for m in range(x_rim.shape[0]):
        right, valid = x_side(m)
        there = truth(valid, (8, LANES))
        column = jnp.concatenate([x_rim[m, 6 + r] for r in range(tiles)], axis=0)
        near = right * (nx + 1) + 2
        far = near + 2 * right - 1
        for k in range(5):
            x = jnp.where(there, x_rim[m, k], 0.0)
            for p, y in ((near, x), (far, roll(x, -3, 0))):
                moved = roll(y, p * SLOT + 4, 1)
                if k < 4:
                    u[k, p, tail] = y
                    edge[k, tail] = jnp.where(slot == p, moved, edge[k, tail])
                else:
                    e[p, tail] = y
                    edge_e[tail] = jnp.where(slot == p, moved, edge_e[tail])
            x, kept = rim_halo(column, k, LANES // 8, 2, right, valid, nx)
            if k < 4:
                halo[k] = jnp.where(kept, x, halo[k])
            else:
                halo_e[...] = jnp.where(kept, x, halo_e[...])
        x = jnp.where(there, 2.0 * x_rim[m, 5], 0.0)
        for k, at in enumerate((0, 3, 5)):
            force[k, near, tail] = roll(x, -at, 0)
            x_k, kept = rim_halo(column, 5 + k, LANES // 8, 2, right, valid, nx)
            halo_f[k] = jnp.where(kept, 2.0 * x_k, halo_f[k])


def early(nx, sweep):
    _, xl, xr = place("gx")

    def chosen(p):
        if 3 + sweep <= p < nx + 3 - sweep:
            return True
        if 3 <= p < nx + 3:
            return xl == 0 if p < 3 + sweep else xr == 0
        return False

    return chosen


def early_block(nx):
    _, xl, xr = place("gx")
    return lambda q: xl == 0 if 2 * q + 5 <= nx else xr == 0 if 2 * q + 2 >= 5 else False


def late(chosen):
    return lambda p: not chosen(p)


def inside_slots(slots, width, chosen=None):
    _, xl, xr = place("gx")
    inside = range(3 - width * xl, slots - 3 + width * xr)
    return [p for p in inside if chosen is None or chosen(p)]


def residuals(u, halo, beside, w, force, e, summed, chosen):
    _, blocks, nz, _ = summed.shape
    slots = u.shape[1]
    spread_halo(halo, beside, slots, 0, lambda p: chosen((p - 3) // 2), False)

    def body(q):
        totals = [0.0] * 5
        for j in range(2):
            p = 2 * q + 3 + j
            olds, sums, spread = main_operator(u, beside, w, force, p, nz)
            diagonal = (w[0][p] + w[0][p - 1] + w[1][p] + w[2][p] + w[3][p] + w[4][p])[:nz]
            for k in range(3):
                totals[k] += sums[k] - diagonal * olds[k]
            totals[3] += spread
            totals[4] += e[p, pl.ds(0, nz)]
        for k in range(5):
            summed[k, q] = totals[k]

    for q in range(blocks):
        if chosen(q):
            body(q)


def pre_start(*refs):
    pre_start_on(Staged(refs[:16]), *refs[16:])


def pre_start_on(
    staged, z_halo, halo_full, x_main,
    e, halo_e, force, halo_f, w0, w1, w2, w3, w4, w5, ua, ub, ha, ca, cb, edge_e, summed,
    hw, hb, hc, beside,
):
    nx, nz = staged.nx, staged.nz
    slots = nx + 6
    w = (w0, w1, w2, w3, w4, w5)
    viscosity_force(staged, z_halo, halo_full, x_main, e, halo_e, force, halo_f)
    first_fields(staged, z_halo, halo_full, x_main, ua, ub, ha)
    tile, column = fine_masks(nz + 8, slots)
    fill_edges(ca, ua, inside_slots(slots, 3))
    edge_e[...] = edges_of(lambda p: e[p], inside_slots(slots, 3))
    main_weights(e, halo_e, w, 0, early(nx, 1), range(2, nx + 3))
    main_sweep(ua, ha, ub, w, e, force, 0, tile, beside, early(nx, 1))
    halo_weights(halo_e, edge_e, hw)
    halo_sweep(ha, ca, hb, hw, halo_e, halo_f, column)
    fill_edges(cb, ub, inside_slots(slots, 0, early(nx, 1)))
    main_sweep(ub, hb, ua, w, e, force, 0, tile, beside, early(nx, 2))
    halo_sweep(hb, cb, hc, hw, halo_e, halo_f, column)
    residuals(ua, hc, beside, w, force, e, summed, early_block(nx))


def pre_smooth(
    x_rim, _e, _halo_e, _force, _halo_f, _w0, _w1, _w2, _w3, _w4, _w5, _ua, _ub, _ha, _ca, _cb,
    _edge_e, _summed, e, halo_e, force, halo_f, w0, w1, w2, w3, w4, w5, ua, ub, ha, ca, cb, edge_e,
    summed, hw, message, hb, beside,
):
    slots = e.shape[0]
    nx, nz = slots - 6, e.shape[1] - 8
    w = (w0, w1, w2, w3, w4, w5)
    add_rims(x_rim, nx, ua, ha, e, halo_e, force, halo_f, ca, edge_e)
    tile, column = fine_masks(nz + 8, slots)
    faces = [p for p in range(slots - 1) if not 3 <= p < nx + 2]
    main_weights(e, halo_e, w, 2, late(early(nx, 1)), faces)
    halo_weights(halo_e, edge_e, hw)
    main_sweep(ua, ha, ub, w, e, force, 2, tile, beside, late(early(nx, 1)))
    halo_sweep(ha, ca, hb, hw, halo_e, halo_f, column)
    fill_edges(cb, ub, inside_slots(slots, 2, late(early(nx, 1))), False)
    main_sweep(ub, hb, ua, w, e, force, 1, tile, beside, late(early(nx, 2)))
    halo_sweep(hb, cb, ha, hw, halo_e, halo_f, column)
    residuals(ua, ha, beside, w, force, e, summed, late(early_block(nx)))
    scale = (0.5, 0.5, 0.5, -1.0 / 32.0, 0.125)
    cz = nz // 2
    left = []
    for k in range(5):
        for r in range(nx // 4):
            halves = []
            for s in range(2):
                q = 2 * r + s
                even = summed[k, q, pl.ds(0, cz, stride=2)]
                halves.append((even + summed[k, q, pl.ds(1, cz, stride=2)]) * scale[k])
            left.append(jnp.concatenate(halves, axis=1))
    left = jnp.concatenate(left, axis=0)
    pick = iota((2 * LANES, LANES), 0) // 2 == iota((2 * LANES, LANES), 1)
    out = jnp.dot(
        left, pick.astype(F32), precision=lax.Precision.HIGHEST, preferred_element_type=F32
    )
    for k in range(5):
        for r in range(nx // 4):
            at = (k * (nx // 4) + r) * cz
            for i in range(cz // 8):
                message[at // 8 + i] = out[at + 8 * i : at + 8 * i + 8]
    sides = x_messages()
    lane = iota((nz, LANES), 1)
    _, _, xr = place("gx")
    for m in range(sides):
        high = xr if sides == 1 else high_side("gx", m)
        p = 3 + high * (nx - 1)
        parts, total = [], jnp.zeros((nz, LANES), F32)
        for k in range(4):
            x = ua[k, p, pl.ds(0, nz)]
            parts += [(x[:8], 2 * k, 2 * k, 1), (x[nz - 8 :], 2 * k + 2, 2 * k + 1, 1)]
            total = jnp.where(lane // 2 == k, roll(x, 2 * k + 1, 1), total)
        n = message.shape[0] - 2 * (sides - m)
        message[n] = rows_of(parts)
        column = total[:8]
        for t in range(1, nz // 8):
            x = roll(total[8 * t : 8 * t + 8], 8 * t, 1)
            column = jnp.where(lane[:8] // 8 == t, x, column)
        message[n + 1] = column


def smooth_pack(fields, edges, x_fine):
    nx, nz = fields.shape[1] - 6, fields.shape[2] - 8
    for m in range(x_fine.shape[0]):
        high = high_side("gx", m)
        for k in range(4):
            for j in range(2):
                x_fine[m, 2 * k + j] = fields[k, 3 + high * (nx - 2) + j, pl.ds(0, nz)]

    def planes(k):
        return [fields[k, q + 3, pl.ds(0, nz)] for q in range(nx)]

    for j, x in enumerate(pair_edges(planes, 4, nz)):
        edges[j] = x


def frame(ref, m, part):
    return ref[ref.shape[0] - 2 * (x_messages() - m) + part]


def fourth_pack(own, other, fields, whole, z_a, z_b):
    nx, nz = fields.shape[1] - 6, fields.shape[2] - 8
    pairs, cz = whole.shape[1:3]
    gx = lax.axis_index("gx")
    for k in range(5):
        for r in range(pairs):
            if own.ndim == 4:
                whole[k, r] = own[k, r]
                continue
            mine = truth(jnp.where(gx == r // (pairs // 2), 1, 0), (8, LANES))
            for i in range(cz // 8):
                n = (k * (pairs // 2) + r % (pairs // 2)) * (cz // 8) + i
                whole[k, r, pl.ds(8 * i, 8)] = jnp.where(mine, own[n], other[n])
    row = iota((8, LANES), 0) // 2
    for m, out in enumerate((z_a, z_b)):
        right = high_side("gz", m)
        start = pl.multiple_of(right * (cz - 8), 8)
        for r in range(pairs):
            for k in range(2):
                parts = [
                    (whole[k + 2 * h, r, pl.ds(0, 8)], whole[k + 2 * h, r, pl.ds(cz - 8, 8)])
                    + (4 * h, 4)
                    for h in range(2)
                ]
                out[k * pairs + r] = z_strip(parts, right)
            out[2 * pairs + r] = whole[4, r, pl.ds(start, 8)]
        toward = truth(right, (8, LANES))
        for q in range(nx):
            total = jnp.zeros((8, LANES), F32)
            for k in range(4):
                low = roll(fields[k, q + 3, pl.ds(0, 8)], 2 * k, 0)
                high = roll(fields[k, q + 3, pl.ds(nz - 8, 8)], 2 * k - 6, 0)
                total = jnp.where(row == k, jnp.where(toward, high, low), total)
            out[3 * pairs + q] = total
        for m_x in range(x_messages()):
            out[3 * pairs + nx + m_x] = frame(other, m_x, 0)


def fold_rows(x):
    own = x.shape[0] - 16
    row = iota((8, LANES), 0)
    halo = jnp.where(row < 4, x[own : own + 8], x[own + 8 :])
    return jnp.concatenate([x[:own], halo], axis=0)


def deep_edges(pairs, width):
    per = LANES // (2 * width)
    columns = []
    for n, x in enumerate(pairs):
        for g in range(2):
            t = (2 * n + g) % per
            x_t = roll(x, 2 * width * t + width - 64 * g, 1)
            if t == 0:
                columns.append(x_t)
            else:
                slot = iota(x.shape, 1) // (2 * width)
                columns[-1] = jnp.where(slot == t, x_t, columns[-1])
    return columns


def unfold(left, right, width):
    spot = iota(left.shape, 1) % (2 * width)
    first = jnp.where(spot < width, left, roll(right, width, 1))
    second = jnp.where(spot < width, roll(left, -width, 1), right)
    return first, second


def fifth_pack(whole, z_a, z_b, edges, frames, full, full_e, z_halo, z_rim, y_a, y_b):
    pairs, cz = whole.shape[1:3]
    nx = z_halo.shape[1]
    nz = edges.shape[1]
    _, has_left, has_right = place("gz")
    to_left = truth(has_left, (8, LANES))
    to_right = truth(has_right, (8, LANES))
    deep = []
    for k in range(5):
        for r in range(pairs):
            if k < 4:
                n = k % 2 * pairs + r
                tile = z_tile(z_a[n], z_b[n], k // 2 * 4, 4)
                x = jnp.concatenate([whole[k, r], tile], axis=0)
                full[k, r] = x
            else:
                left, right = left_right("gz", z_a[2 * pairs + r], z_b[2 * pairs + r])
                right = jnp.where(to_right, right, 0.0)
                left = jnp.where(to_left, left, 0.0)
                x = jnp.concatenate([whole[k, r], right, left], axis=0)
                full_e[r] = x
            deep.append(x)
    row = iota((8, LANES), 0)
    for q in range(nx):
        left, right = left_right("gz", z_a[3 * pairs + q], z_b[3 * pairs + q])
        for k in range(4):
            x = jnp.where(row < 2 * has_right, roll(right, -2 * k, 0), 0.0)
            z_halo[k, q] = jnp.where(row >= 8 - 2 * has_left, roll(left, 6 - 2 * k, 0), x)
    for m in range(z_rim.shape[0]):
        n = 3 * pairs + nx + m
        left, right = left_right("gz", z_a[n], z_b[n])
        x = jnp.where(to_right & (row % 2 == 0), right, 0.0)
        z_rim[m] = jnp.where(to_left & (row % 2 == 1), left, x)
    columns = deep_edges(deep[: 4 * pairs], 4)
    half = len(columns) // 2
    columns_e = deep_edges(deep[4 * pairs :], 8)
    upper = (cz + 16) // 2
    behind = pair_edges(lambda i: [z_halo[i, q] for q in range(nx)], 4, 8)
    for m, out in enumerate((y_a, y_b)):
        toward = high_side("gy", m)
        parts = [
            strip(columns[j], columns[j + half], toward, 4) for j in range(half)
        ] + [strip(x[:upper], x[upper:], toward, 8) for x in columns_e]
        for i in range(nz // 8):
            parts.append(y_strip(edges[0, pl.ds(8 * i, 8)], edges[1, pl.ds(8 * i, 8)], toward))
        parts.append(y_strip(behind[0], behind[1], toward))
        parts += [frame(frames, m_x, 1) for m_x in range(z_rim.shape[0])]
        n = 0
        for x in parts:
            for i in range(x.shape[0] // 8):
                out[n] = x[8 * i : 8 * i + 8]
                n += 1


def sixth_pack(y_a, y_b, halo_full, y_rim):
    tiles, sides = halo_full.shape[1] // 8, y_rim.shape[0]
    first = y_a.shape[0] - tiles - sides
    for i in range(tiles):
        for j, x in enumerate(merge_y(y_a[first + i], y_b[first + i])):
            halo_full[j, pl.ds(8 * i, 8)] = x
    _, has_left, has_right = place("gy")
    odd = iota((8, LANES), 1) % 2
    for m in range(sides):
        left, right = left_right("gy", y_a[first + tiles + m], y_b[first + tiles + m])
        kept = (odd < has_left) & (odd == 0) | (odd > 1 - has_right)
        y_rim[m] = jnp.where(kept, jnp.where(odd == 0, left, right), 0.0)


def coarse_solve(full, full_e, y_a, y_b, main, halo, ca, cb, force, e, w0, w1, w2, w3, w4, w5, deep_e, grown):
    pairs, rows = full.shape[1:3]
    deep = full_e.shape[1]
    planes = 2 * pairs
    own = main.shape[1] - 2
    cz = rows - 8
    half = LANES // 2
    _, zl, zr = place("gz")
    _, yl, yr = place("gy")
    two = lax.axis_size("gx") == 2
    gx = FIXED[-1][0] if two else lax.axis_index("gx")

    def inside(rows, width):
        lane = iota((rows, LANES), 1)
        row = iota((rows, LANES), 0)
        kept = (row < cz + width * zr) | (row >= rows - width * zl)
        return kept & ((lane < half + width * yr) | (lane >= LANES - width * yl))

    zero = jnp.zeros((rows, LANES), F32)
    w = (w0, w1, w2, w3, w4, w5)
    for k in range(4):
        for p in (0, planes + 1):
            ca[k, p] = zero
            cb[k, p] = zero
    e[0] = zero
    e[planes + 1] = zero
    deep_e[0] = jnp.zeros((deep, LANES), F32)
    deep_e[planes + 1] = jnp.zeros((deep, LANES), F32)

    tiles, deep_tiles = rows // 8, deep // 16
    count = pairs // 4
    columns = []

    def taken(n, tiles):
        a, b = (jnp.concatenate([ref[n + i] for i in range(tiles)], axis=0) for ref in (y_a, y_b))
        return left_right("gy", a, b)

    unfolded = [unfold(*taken(j * tiles, tiles), 4) for j in range(count)]
    columns = [x for x, _ in unfolded] + [x for _, x in unfolded]
    columns_e = []
    for j in range(-(-pairs // 4)):
        x = unfold(*taken(count * tiles + j * deep_tiles, deep_tiles), 8)
        columns_e.append(jnp.concatenate(x, axis=0))

    def whole_plane(pair, columns, n, s, width):
        lane = iota(pair.shape, 1)
        per = LANES // (2 * width)
        last, first = 2 * n + 1 - s, 2 * n + s
        low = roll(columns[first // per], half - 2 * width * (first % per) - width, 1)
        high = roll(columns[last // per], LANES - width - 2 * width * (last % per), 1)
        x = jnp.where(lane < half, roll(pair, -s * half, 1), low)
        return jnp.where(lane < LANES - width, x, high)

    near, far = inside(rows, 4), inside(deep, 8)
    for r in range(pairs):
        for s in range(2):
            p = 2 * r + s
            x = jnp.where(far, whole_plane(full_e[r], columns_e, r, s, 8), 0.0)
            deep_e[p + 1] = x
            e[p + 1] = fold_rows(x)
            for k in range(4):
                x = whole_plane(full[k, r], columns, k * pairs + r, s, 4)
                force[k, p] = jnp.where(near, x, 0.0)

    def shifts(x):
        return (
            roll(x, LANES - 1, 1),
            roll(x, 1, 1),
            roll(x, x.shape[0] - 1, 0),
            roll(x, 1, 0),
        )

    def two_by_two(width, body):
        if two:
            for p in range(max(gx * own - width, 0), min(gx * own + own + width, planes)):
                body(p + 1)
            return
        lo = jnp.maximum(gx * own - width, 0)
        hi = jnp.minimum(gx * own + own + width, planes)
        steps = (hi - lo + 1) // 2
        lo = jnp.minimum(lo, planes - 2 * steps)

        def step(i, carry):
            body(lo + 2 * i + 1)
            body(lo + 2 * i + 2)
            return carry

        lax.fori_loop(0, steps, step, 0)

    def start(p):
        x = deep_e[p]
        up, down = x + deep_e[p + 1], x + deep_e[p - 1]
        w0[p] = fold_rows(up)
        total = up + down
        for n, y in enumerate(shifts(x)):
            total += x + y
            w[1 + n][p] = fold_rows(x + y)
        factor = jnp.where(near, fold_rows(relax_weight / total), 0.0)
        w5[p] = factor
        for k in range(3):
            ca[k, p] = factor * force[k, p - 1]
        ca[3, p] = e[p] * force[3, p - 1]

    w0[0] = e[0] + e[1]
    two_by_two(planes, start)

    def sweep(src, dst, width):
        def body(p):
            wxp, wxm = w0[p], w0[p - 1]
            wyp, wym, wzp, wzm = w1[p], w2[p], w3[p], w4[p]
            x = src[3, p]
            around = shifts(x)
            up, down = src[3, p + 1], src[3, p - 1]
            spread = 0.0
            for k in range(3):
                u = src[k, p]
                yp, ym, zp, zm = shifts(u)
                xp, xm = src[k, p + 1], src[k, p - 1]
                total = force[k, p - 1] - 2.0 * terms(k, up, down, *around)
                total += wxp * xp + wxm * xm
                total += wyp * yp + wym * ym
                total += wzp * zp + wzm * zm
                spread += terms(k, xp, xm, yp, ym, zp, zm)
                dst[k, p] = jnp.where(near, 0.4 * u + w5[p] * total, 0.0)
            dst[3, p] = jnp.where(near, x + e[p] * (force[3, p - 1] - 0.125 * spread), 0.0)

        two_by_two(width, body)

    sweep(ca, cb, 3)
    sweep(cb, ca, 2)
    sweep(ca, cb, 1)

    lane = iota((LANES, 2 * LANES), 1)
    cell = iota((LANES, 2 * LANES), 0)
    spot = lane % SLOT
    wanted = jnp.where(spot < 4, LANES - 2, half - 2) + spot // 2
    slot = (lane - LANES) // SLOT
    column = jnp.zeros((4 * rows, LANES), F32)
    first = gx * own

    def grow(ref, index, x):
        ref[index + (pl.ds(0, cz, stride=2),)] = x[:cz]
        ref[index + (pl.ds(1, cz, stride=2),)] = x[:cz]
        grown[pl.ds(0, 8, stride=2)] = x[cz:]
        grown[pl.ds(1, 8, stride=2)] = x[cz:]
        r = iota((8, LANES), 0)
        tail = jnp.where(r < 4, grown[pl.ds(0, 8)], grown[pl.ds(8, 8)])
        ref[index + (pl.ds(2 * cz, 8),)] = tail

    for i in range(own + 2):
        x = jnp.concatenate([cb[k, first + i] for k in range(4)], axis=0)
        here = (lane >= LANES) & ((slot + 1) // 2 - 1 == i) & (cell == wanted)
        chosen = (here | ((lane < LANES) & (lane // 2 == cell))).astype(F32)
        wide = jnp.dot(x, chosen, precision=lax.Precision.HIGHEST, preferred_element_type=F32)
        for k in range(4):
            grow(main, (k, i), wide[k * rows : (k + 1) * rows, :LANES])
        column += wide[:, LANES:]
    for k in range(4):
        grow(halo, (k,), column[k * rows : (k + 1) * rows])


def last_sweep(src, halo, beside, w, e, force, chosen, store):
    slots, nz = src.shape[1], src.shape[2] - 8
    spread_halo(halo, beside, slots, 0, chosen, False)

    def body(p):
        new = main_operator(src, beside, w, force, p, nz)
        new = relaxed(*new, w[5][p, pl.ds(0, nz)], e[p, pl.ds(0, nz)])
        for k in range(4):
            store(p, k, new[k])

    over_planes(slots, 0, body, chosen)


def post_smooth(
    e, halo_e, force, halo_f, w0, w1, w2, w3, w4, w5, hw,
    fields, z_halo, halo_full, x_fine, z_rim, y_rim, main, column, v_out, p_out,
    ua, ub, ha, hb, ca, beside,
):
    nx, nz, _ = p_out.shape
    slots = nx + 6
    w = (w0, w1, w2, w3, w4, w5)
    zero = jnp.zeros((nz + 8, LANES), F32)
    for k in range(4):
        for p in (1, 2, nx + 3, nx + 4):
            ua[k, p] = zero
            ub[k, p] = zero
        for q in range(nx):
            i = q // 2 + 1
            ua[k, q + 3, pl.ds(0, nz)] = fields[k, q + 3, pl.ds(0, nz)] + main[k, i, pl.ds(0, nz)]
            ua[k, q + 3, pl.ds(nz, 8)] = z_halo[k, q] + main[k, i, pl.ds(nz, 8)]
        ha[k] = own_slots(halo_full[k % 2], nx, k // 2)
    for m in range(x_fine.shape[0]):
        right, valid = x_side(m)
        there = truth(valid, (nz, LANES))
        there8 = truth(valid, (8, LANES))
        near = 2 + right * (nx + 1)
        row = iota((8, LANES), 0)
        lane = iota((nz, LANES), 1)
        kept = (lane == near * SLOT + 3) | (lane == near * SLOT + 4)
        i = right * (nx // 2 + 1)
        for k in range(4):
            for j in range(2):
                at = 1 + right * (nx + 2) + j
                x = x_fine[m, 2 * k + j] + main[k, i, pl.ds(0, nz)]
                ua[k, at, pl.ds(0, nz)] = jnp.where(there, x, 0.0)
            x = jnp.where(row == 0, roll(z_rim[m], -2 * k, 0), 0.0)
            x = jnp.where(row == 7, roll(z_rim[m], 6 - 2 * k, 0), x) + main[k, i, pl.ds(nz, 8)]
            ua[k, near, pl.ds(nz, 8)] = jnp.where(there8, x, 0.0)
            at = near * SLOT + 3 + LANES
            x = [roll(y_rim[m], at - SLOT * t - 2 * k, 1) for t in range(nz // 8)]
            x = jnp.where(kept, jnp.concatenate(x, axis=0), ha[k, pl.ds(0, nz)])
            ha[k, pl.ds(0, nz)] = jnp.where(there, x, ha[k, pl.ds(0, nz)])
    masks = fine_masks(nz + 8, slots)
    for k in range(4):
        ha[k] = jnp.where(masks[1], ha[k] + column[k], 0.0)
    fill_edges(ca, ua, inside_slots(slots, 2))
    main_sweep(ua, ha, ub, w, e, force, 1, masks[0], beside)
    halo_sweep(ha, ca, hb, hw, halo_e, halo_f, masks[1])

    def store(p, k, x):
        if k < 3:
            v_out[k, p - 3] = x
        else:
            p_out[p - 3] = x

    last_sweep(ub, hb, beside, w, e, force, None, store)


def local(velocity, pressure, viscosity, body_force):
    nx, nz, ny = pressure.shape
    if ny != LANES or nx * SLOT * 2 != LANES or nz % 16:
        raise ValueError("unsupported block")
    sides = x_messages()
    rows, slots = nz + 8, nx + 6
    inputs = [velocity, pressure, viscosity, body_force]
    block = (nz, LANES)

    z_shape = (3 * nx, 8, LANES)
    half = (nx // 2,) + block
    *staged, y_a, y_b = call(
        first_pack, [half] * 16 + [(2,) + block] * 2, inputs, outside=4, copies=16
    )
    x_main, z_a, z_b = call(side_pack, [(sides, 21) + block, z_shape, z_shape], staged)
    y_a, y_b = swap(y_a, "gy", 0), swap(y_b, "gy", 1)
    x_main = swap_x(x_main)
    halo, z_b = call(second_pack, [(4,) + block, z_shape], [z_b, y_a, y_b])
    (z_a,) = call(second_pack_near, [z_shape], [z_a, halo])
    z_a, z_b = swap(z_a, "gz", 0), swap(z_b, "gz", 1)
    tiles = rows // 8
    z_first, halo_first, x_first = call(
        third_pack,
        [(8, nx, 8, LANES), (4, rows, LANES), (sides, 6 + tiles, 8, LANES)],
        [z_a, z_b, halo],
    )
    x_first = swap_x(x_first)

    spread, column = (4, slots, rows, LANES), (4, rows, LANES)
    started = [(slots, rows, LANES), (rows, LANES), (3, slots, rows, LANES), (3, rows, LANES)]
    started += [(slots, rows, LANES)] * 6 + [spread, spread] + [column] * 3 + [(rows, LANES)]
    started += [(5, nx // 2, nz, LANES)]
    tiles_c = 5 * (nx // 4) * (nz // 16)
    state = call(
        by_sides(pre_start),
        started,
        [*staged, z_first, halo_first, x_main],
        [(7, rows, LANES), column, column, spread],
        cost=4,
    )
    *operator, fields, _, _, _, _, _, _, factors, own = call(
        by_sides(pre_smooth),
        started + [(7, rows, LANES), (tiles_c + 2 * sides, 8, LANES)],
        [x_first, *state],
        [column, spread],
        cost=8,
        aliases={i + 1: i for i in range(len(started))},
    )
    operator.append(factors)
    edges, x_fine = call(smooth_pack, [(2,) + block, (sides, 8) + block], [fields])
    if lax.axis_size("gx") == 2:
        frames = swap(own, "gx", 0)
    else:
        frames = swap_x(own[tiles_c:].reshape(sides, 2, 8, LANES)).reshape(2 * sides, 8, LANES)
        own = own[:tiles_c].reshape(5, nx // 4, nz // 2, LANES)
        own = lax.all_gather(own, "gx", axis=1, tiled=True)
    x_fine = swap_x(x_fine)
    pairs = lax.axis_size("gx") * (nx // 4)
    z_shape = (3 * pairs + nx + sides, 8, LANES)
    whole, z_a, z_b = call(
        fourth_pack,
        [(5, pairs, nz // 2, LANES), z_shape, z_shape],
        [own, frames, fields],
    )
    z_a, z_b = swap(z_a, "gz", 0), swap(z_b, "gz", 1)
    deep = nz // 2 + 16
    shallow = deep - 8
    y_shape = (pairs // 4 * (shallow // 8) + -(-pairs // 4) * (deep // 16) + tiles, 8, LANES)
    y_shape = (y_shape[0] + sides, 8, LANES)
    rim = (sides, 8, LANES)
    full, full_e, z_halo, z_rim, y_a, y_b = call(
        fifth_pack,
        [(4, pairs, shallow, LANES), (pairs, deep, LANES), (4, nx, 8, LANES), rim, y_shape, y_shape],
        [whole, z_a, z_b, edges, frames],
    )
    y_a, y_b = swap(y_a, "gy", 0), swap(y_b, "gy", 1)
    halo_full, y_rim = call(sixth_pack, [(2, rows, LANES), rim], [y_a, y_b])
    planes = 2 * pairs
    plane = (shallow, LANES)
    grown, beside = call(
        by_sides(coarse_solve),
        [(4, nx // 2 + 2, rows, LANES), (4, rows, LANES)],
        [full, full_e, y_a, y_b],
        [(4, planes + 2) + plane] * 2
        + [(4, planes) + plane]
        + [(planes + 2,) + plane] * 7
        + [(planes + 2, deep, LANES), (16, LANES)],
        cost=4,
    )
    v_out, p_out = call(
        by_sides(post_smooth),
        [(3, nx) + block, (nx,) + block],
        operator + [fields, z_halo, halo_full, x_fine, z_rim, y_rim, grown, beside],
        [spread] * 2 + [column] * 3 + [spread],
        cost=8,
    )
    return v_out, p_out


def swap_x(array):
    if array.shape[0] == 1:
        return swap(array, "gx", 0)
    parts = [swap(array[m], "gx", m) for m in range(2)]
    return jnp.stack(parts)


def solution(mesh):
    return jax.shard_map(
        local,
        mesh=mesh,
        in_specs=(
            P(None, "gx", "gz", "gy"),
            P("gx", "gz", "gy"),
            P("gx", "gz", "gy"),
            P(None, "gx", "gz", "gy"),
        ),
        out_specs=(P(None, "gx", "gz", "gy"), P("gx", "gz", "gy")),
        check_vma=False,
    )
```

```python
import jax
import jax.numpy as jnp
from jax import lax
from jax.experimental import pallas as pl
from jax.experimental.pallas import tpu as pltpu
from jax.sharding import PartitionSpec as P

LANES = 128
SLOT = 8
F32 = jnp.float32
relax_weight = 0.6
HELD = 846 * 2**16
Z_PLACES = (
    ((0, 0, 3), (1, 3, 3), (5, 6, 2)),
    ((2, 0, 3), (3, 3, 3), (6, 6, 2)),
    ((4, 0, 3), (7, 3, 2)),
)


def call(body, outs, args, scratch=(), cost=1, outside=0, copies=0, aliases=None):
    return pl.pallas_call(
        body,
        out_shape=[jax.ShapeDtypeStruct(shape, F32) for shape in outs],
        in_specs=[pl.BlockSpec(memory_space=pltpu.HBM)] * outside
        + [pl.BlockSpec(memory_space=pltpu.VMEM)] * (len(args) - outside),
        out_specs=[pl.BlockSpec(memory_space=pltpu.VMEM)] * len(outs),
        scratch_shapes=[pltpu.VMEM(shape, F32) for shape in scratch]
        + [pltpu.SemaphoreType.DMA((copies,))] * (copies > 0),
        input_output_aliases=aliases or {},
        compiler_params=pltpu.CompilerParams(vmem_limit_bytes=HELD if outside else 40 * 2**20),
        cost_estimate=pl.CostEstimate(
            flops=cost * 10**6, bytes_accessed=cost * 10**6, transcendentals=0
        ),
    )(*args)


def swap(array, axis, which):
    count = lax.axis_size(axis)
    if axis != "gx" and which == 1:
        ys, zs = lax.axis_size("gy"), lax.axis_size("gz")
        pairs = []
        for y in range(ys):
            for z in range(zs):
                i = y if axis == "gy" else z
                j = i + 1 if i % 2 else i - 1
                if axis == "gy":
                    to = (j, z) if 0 <= j < count else (y, z ^ 1)
                else:
                    to = (y, j) if 0 <= j < count else (y ^ 1, z)
                pairs.append((y * zs + z, to[0] * zs + to[1]))
        return lax.ppermute(array, ("gy", "gz"), pairs)
    pairs = []
    for i in range(which, count, 2):
        j = (i + 1) % count
        pairs += [(i, j), (j, i)]
    return lax.ppermute(array, axis, pairs)


FIXED = []


def choose(x, chosen):
    parts = []
    for _ in range(3):
        parts.append(x.astype(jnp.bfloat16))
        x = x - parts[-1].astype(F32)
    chosen = jnp.where(chosen, 1.0, 0.0).astype(jnp.bfloat16)
    return jnp.dot(
        jnp.concatenate(parts, axis=1),
        jnp.concatenate([chosen] * 3, axis=0),
        preferred_element_type=F32,
    )


def by_sides(body):
    def kernel(*refs):
        count = lax.axis_size("gx")
        _, xl, xr = place("gx")
        for sides in [(0, 1), (1, 0), (1, 1)][: 2 if count == 2 else 3]:

            def branch(sides=sides):
                FIXED.append(sides)
                body(*refs)
                FIXED.pop()

            pl.when((xl == sides[0]) & (xr == sides[1]))(branch)

    return kernel


def place(axis):
    if axis == "gx" and FIXED:
        return (None,) + FIXED[-1]
    i = lax.axis_index(axis)
    last = lax.axis_size(axis) - 1
    return i, jnp.where(i > 0, 1, 0), jnp.where(i < last, 1, 0)


def iota(shape, dim):
    return lax.broadcasted_iota(jnp.int32, shape, dim)


def truth(flag, shape):
    return jnp.full(shape, flag, jnp.int32) > 0


def roll(x, shift, dim):
    if isinstance(shift, int):
        shift %= x.shape[dim]
        return x if shift == 0 else pltpu.roll(x, shift, dim)
    return pltpu.roll(x, lax.rem(shift + 2 * x.shape[dim], x.shape[dim]), dim)


def high_side(axis, message):
    return jnp.where(lax.axis_index(axis) % 2 == message, 1, 0)


def left_right(axis, a, b):
    odd = truth(lax.axis_index(axis) % 2, a.shape)
    return jnp.where(odd, a, b), jnp.where(odd, b, a)


def x_messages():
    return 1 if lax.axis_size("gx") == 2 else 2


def pair_edges(planes, fields, rows):
    lane = iota((rows, LANES), 1) // SLOT
    half = fields // 2
    out = []
    for j in range(half):
        total = jnp.zeros((rows, LANES), F32)
        for part in range(2):
            for q, x in enumerate(planes(j + part * half)):
                slot = q + part * (LANES // SLOT // 2)
                total = jnp.where(lane == slot, roll(x, slot * SLOT + 4, 1), total)
        out.append(total)
    return out


def merge_y(a, b):
    _, has_left, has_right = place("gy")
    left, right = left_right("gy", a, b)
    spot = iota(a.shape, 1) % SLOT
    kept = (spot < 4 * has_left) | (spot >= SLOT - 4 * has_right)
    first = jnp.where(spot < 4, left, roll(right, 4, 1))
    second = jnp.where(spot < 4, roll(left, -4, 1), right)
    return jnp.where(kept, first, 0.0), jnp.where(kept, second, 0.0)


class Staged:
    def __init__(self, refs):
        self.refs = refs
        self.half, self.nz = refs[0].shape[:2]
        self.nx = 2 * self.half

    def __getitem__(self, index):
        i, q = index[:2]
        return self.refs[2 * i + q // self.half][(q % self.half,) + index[2:]]


def first_pack(v_in, p_in, e_in, f_in, *refs):
    staged = Staged(refs[:16])
    y_a, y_b, arrived = refs[16:]
    nx, nz = staged.nx, staged.nz
    loads = []
    for n in range(16):
        i, planes = n // 2, pl.ds(n % 2 * staged.half, staged.half)
        if i < 3:
            part = v_in.at[i, planes]
        elif i < 5:
            part = (p_in, e_in)[i - 3].at[planes]
        else:
            part = f_in.at[i - 5, planes]
        loads.append(pltpu.make_async_copy(part, refs[n], arrived.at[n]))
    for load in loads:
        load.start()
    for load in loads:
        load.wait()
    edges = pair_edges(lambda i: [staged[i, q] for q in range(nx)], 8, nz)
    for m, out in enumerate((y_a, y_b)):
        for j in range(2):
            out[j] = y_strip(edges[j], edges[j + 2], high_side("gy", m))


def side_pack(*refs):
    staged = Staged(refs[:16])
    x_main, z_a, z_b = refs[16:]
    nx, nz = staged.nx, staged.nz
    for m in range(x_main.shape[0]):
        top = truth(high_side("gx", m), (nz, LANES))
        n = 0
        for i in range(8):
            width = 3 if i < 5 else 2
            for j in range(width):
                x_main[m, n] = jnp.where(top, staged[i, nx - width + j], staged[i, j])
                n += 1
    low, high = pl.ds(0, 8), pl.ds(nz - 8, 8)
    for q in range(nx):
        for n, fields in enumerate(Z_PLACES):
            for m, out in enumerate((z_a, z_b)):
                out[3 * q + n] = z_strip(
                    [(staged[i, q, low], staged[i, q, high], at, rows) for i, at, rows in fields],
                    high_side("gz", m),
                )


def strip(first, second, toward_right, width):
    right = truth(toward_right, first.shape)
    spot = iota(first.shape, 1) % (2 * width)
    first = jnp.where(right, first, roll(first, -width, 1))
    second = jnp.where(right, roll(second, width, 1), second)
    return jnp.where(spot < width, first, second)


def y_strip(first, second, toward_right):
    return strip(first, second, toward_right, SLOT // 2)


def z_strip(parts, toward_right):
    right = truth(toward_right, (8, LANES))
    return rows_of(
        [
            (jnp.where(right, roll(high, at + rows, 0), roll(low, at, 0)), 0, at, rows)
            for low, high, at, rows in parts
        ]
    )


def z_tail(halo, first, out, message):
    nz = halo.shape[1]
    row = iota((8, LANES), 0)
    for n in range(first.shape[0]):
        out[n] = first[n]
    for j in range(4):
        tiles = halo[j, pl.ds(0, 8)], halo[j, pl.ds(nz - 8, 8)]
        x = z_strip([tiles + (5, 3)], high_side("gz", message))
        out[3 * j + 2] = jnp.where(row < 5, first[3 * j + 2], x)


def second_pack(z_first, y_a, y_b, halo, z_b):
    for j in range(2):
        halo[j], halo[j + 2] = merge_y(y_a[j], y_b[j])
    z_tail(halo, z_first, z_b, 1)


def second_pack_near(z_first, halo, z_a):
    z_tail(halo, z_first, z_a, 0)


def z_tile(a, b, at, rows):
    _, has_left, has_right = place("gz")
    left, right = left_right("gz", a, b)
    row = iota(a.shape, 0)
    x = jnp.where(row < rows * has_right, roll(right, -at, 0), 0.0)
    return jnp.where(row >= 8 - rows * has_left, roll(left, 8 - at - rows, 0), x)


def third_pack(z_a, z_b, halo, z_halo, halo_full, x_rim):
    nx = z_halo.shape[1]
    nz = halo.shape[1]
    for q in range(nx):
        for n, fields in enumerate(Z_PLACES):
            for i, at, rows in fields:
                z_halo[i, q] = z_tile(z_a[3 * q + n], z_b[3 * q + n], at, rows)
    for j in range(4):
        halo_full[j, pl.ds(0, nz)] = halo[j]
        halo_full[j, pl.ds(nz, 8)] = z_tile(z_a[3 * j + 2], z_b[3 * j + 2], 5, 3)

    def tiles(plane):
        out = [
            rows_of([(z_halo[i, plane(1)], 0, 6, 4), (z_halo[i, plane(2)], 3, 2, 2)])
            for i in range(5)
        ]
        force = zip((0, 3, 5), (7, 2, 4))
        out.append(
            rows_of([(z_halo[5 + k, plane(1)], at, row, 2) for k, (at, row) in enumerate(force)])
        )
        return out

    pack_rim(x_rim, tiles, lambda j: halo_full[j], 8, 2, nx)


def rows_of(parts):
    row = iota((8, LANES), 0)
    total = jnp.zeros((8, LANES), F32)
    for x, shift, first, count in parts:
        total = jnp.where((row - first) % 8 < count, roll(x, shift, 0), total)
    return total


def pack_rim(x_rim, tiles, halo_pair, fields, planes, nx):
    half = fields // 2
    stride = LANES // 8 if fields == 8 else SLOT
    for m in range(x_rim.shape[0]):
        high = high_side("gx", m)
        done = tiles(lambda d, high=high: high * (nx - 2 * d + 1) + d - 1)
        for n, x in enumerate(done):
            x_rim[m, n] = x
        pairs = [halo_pair(j) for j in range(half)]
        rows = pairs[0].shape[0]
        column = iota((rows, LANES), 1) // stride
        first = high * (nx - planes) * SLOT
        total = jnp.zeros((rows, LANES), F32)
        for i in range(fields):
            at = i * stride - first - (i // half) * (LANES // 2)
            total = jnp.where(column == i, roll(pairs[i % half], at + LANES, 1), total)
        for r in range(rows // 8):
            x_rim[m, len(done) + r] = total[8 * r : 8 * r + 8]


def main_shifts(x, beside, kept):
    rows = x.shape[0]
    y, beside = x[:kept], beside[:kept]
    lane = iota(y.shape, 1)
    return (
        roll(jnp.where(lane == 0, beside, y), LANES - 1, 1),
        roll(jnp.where(lane == LANES - 1, beside, y), 1, 1),
        roll(x, rows - 1, 0)[:kept],
        roll(x, 1, 0)[:kept],
    )


def halo_shifts(x, edge):
    spot = iota(x.shape, 1) % SLOT
    rows = x.shape[0]
    return (
        roll(x, LANES - SLOT, 1),
        roll(x, SLOT, 1),
        roll(jnp.where(spot == 4, edge, x), LANES - 1, 1),
        roll(jnp.where(spot == 3, edge, x), 1, 1),
        roll(x, rows - 1, 0),
        roll(x, 1, 0),
    )


def main_weights(e, halo_e, w, width, chosen, faces):
    slots = e.shape[0]
    for p in faces:
        w[0][p] = e[p] + e[p + 1]

    def body(p):
        x = e[p]
        total = w[0][p] + w[0][p - 1]
        for n, y in enumerate(main_shifts(x, roll(halo_e[...], LANES - SLOT * p - 4, 1), x.shape[0])):
            total += x + y
            w[1 + n][p] = x + y
        w[5][p] = relax_weight / total

    over_planes(slots, width, body, chosen)


def halo_weights(e, edge_e, w):
    x = e[...]
    total = jnp.zeros_like(x)
    for n, y in enumerate(halo_shifts(x, edge_e[...])):
        total += x + y
        w[n] = x + y
    w[6] = relax_weight / total


def terms(k, up, down, yp, ym, zp, zm):
    return (up - down, zp - zm, yp - ym)[k]


def spread_halo(halo, beside, slots, width, chosen=None, full=True):
    kept = beside.shape[2] - (0 if full else 8)

    def body(p):
        for k in range(4):
            beside[k, p, pl.ds(0, kept)] = roll(halo[k][:kept], LANES - SLOT * p - 4, 1)

    over_planes(slots, width, body, chosen)


def main_operator(src, beside, w, force, p, kept):
    def at(ref, *index):
        return ref[index + (pl.ds(0, kept),)]

    wxp, wxm, wyp, wym, wzp, wzm = (
        at(ref, q) for ref, q in zip((w[0],) + w[:5], (p, p - 1, p, p, p, p))
    )
    around = main_shifts(src[3, p], at(beside, 3, p), kept)
    up, down = at(src, 3, p + 1), at(src, 3, p - 1)
    olds, sums, spread = [], [], 0.0
    for k in range(3):
        yp, ym, zp, zm = main_shifts(src[k, p], at(beside, k, p), kept)
        xp, xm = at(src, k, p + 1), at(src, k, p - 1)
        total = at(force, k, p) - terms(k, up, down, *around)
        total += wxp * xp + wxm * xm
        total += wyp * yp + wym * ym
        total += wzp * zp + wzm * zm
        spread += terms(k, xp, xm, yp, ym, zp, zm)
        olds.append(at(src, k, p))
        sums.append(total)
    olds.append(at(src, 3, p))
    return olds, sums, spread


def halo_operator(halo, edge, w, force):
    x = halo[3]
    px = halo_shifts(x, edge[3])
    olds, sums, spread = [], [], 0.0
    for k in range(3):
        u = halo[k]
        around = halo_shifts(u, edge[k])
        total = force[k] - terms(k, *px)
        for n in range(6):
            total += w[n] * around[n]
        spread += terms(k, *around)
        olds.append(u)
        sums.append(total)
    olds.append(x)
    return olds, sums, spread


def relaxed(olds, sums, spread, factor, e):
    new = [0.4 * olds[k] + factor * sums[k] for k in range(3)]
    return new + [olds[3] - 0.25 * e * spread]


def edges_of(plane, slots, total=None):
    shape = plane(slots[0]).shape
    slot = iota(shape, 1) // SLOT
    total = jnp.zeros(shape, F32) if total is None else total
    for p in slots:
        total = jnp.where(slot == p, roll(plane(p), p * SLOT + 4, 1), total)
    return total


def fill_edges(edge, src, slots, fresh=True):
    for k in range(4):
        edge[k] = edges_of(lambda p: src[k, p], slots, None if fresh else edge[k])


def fine_masks(rows, slots):
    nz = rows - 8
    _, zl, zr = place("gz")
    _, yl, yr = place("gy")
    _, xl, xr = place("gx")
    r = iota((8, LANES), 0)
    tile = (r < 4 * zr) | (r >= 8 - 4 * zl)
    r = iota((rows, LANES), 0)
    lane = iota((rows, LANES), 1)
    spot, slot = lane % SLOT, lane // SLOT
    column = (r < nz + 4 * zr) | (r >= rows - 4 * zl)
    column &= (spot < 4 * yl) | (spot >= SLOT - 4 * yr)
    column &= (slot >= 3 - 3 * xl) & (slot < slots - 3 + 3 * xr)
    return tile, column


def main_sweep(src, halo, dst, w, e, force, width, tile, beside, chosen=None):
    nz = src.shape[2] - 8
    slots = src.shape[1]

    def body(p):
        new = relaxed(*main_operator(src, beside, w, force, p, nz + 8), w[5][p], e[p])
        for k in range(4):
            x = new[k]
            dst[k, p, pl.ds(0, nz)] = x[:nz]
            dst[k, p, pl.ds(nz, 8)] = jnp.where(tile, x[nz:], 0.0)

    spread_halo(halo, beside, slots, width, chosen)
    over_planes(slots, width, body, chosen)


def halo_sweep(halo, edge, halo_dst, hw, halo_e, halo_f, column):
    new = relaxed(*halo_operator(halo, edge, hw, halo_f), hw[6], halo_e[...])
    for k in range(4):
        halo_dst[k] = jnp.where(column, new[k], 0.0)


def over_planes(slots, width, body, chosen=None):
    _, xl, xr = place("gx")
    for p in range(3 - width, slots - 3 + width):
        wanted = True if chosen is None else chosen(p)
        if wanted and (p >= 3 or xl) and (p < slots - 3 or xr):
            body(p)


def own_slots(x, nx, part):
    lane = iota(x.shape, 1)
    x = roll(x, 3 * SLOT - part * (LANES // 2), 1)
    return jnp.where((lane >= 3 * SLOT) & (lane < (3 + nx) * SLOT), x, 0.0)


def x_side(m):
    _, has_left, has_right = place("gx")
    if lax.axis_size("gx") == 2:
        return has_right, 1
    right = high_side("gx", m)
    return right, jnp.where(right > 0, has_right, has_left)


def rim_halo(x, t, stride, planes, right, valid, nx):
    base = right * (nx + 3) + (1 - right) * (3 - planes)
    lane = iota(x.shape, 1)
    x = roll(x, base * SLOT - t * stride + LANES, 1)
    kept = (lane >= base * SLOT) & (lane < (base + planes * valid) * SLOT)
    return jnp.where(kept, x, 0.0), kept


def viscosity_force(staged, z_halo, halo_full, x_main, e, halo_e, force, halo_f):
    nx, nz = staged.nx, staged.nz
    slots = nx + 6
    zero = jnp.zeros((nz + 8, LANES), F32)
    for p in list(range(3)) + list(range(nx + 3, slots)):
        e[p] = zero
        for k in range(3):
            force[k, p] = zero
    for q in range(nx):
        e[q + 3, pl.ds(0, nz)] = staged[4, q]
        e[q + 3, pl.ds(nz, 8)] = z_halo[4, q]
        for k in range(3):
            force[k, q + 3, pl.ds(0, nz)] = 2.0 * staged[5 + k, q]
            force[k, q + 3, pl.ds(nz, 8)] = 2.0 * z_halo[5 + k, q]
    halo_e[...] = own_slots(halo_full[0], nx, 1)
    for k in range(3):
        halo_f[k] = 2.0 * own_slots(halo_full[k + 1], nx, 1)
    for m in range(x_main.shape[0]):
        right, valid = x_side(m)
        there = truth(valid, (nz, LANES))
        for j in range(3):
            e[right * (nx + 3) + j, pl.ds(0, nz)] = jnp.where(there, x_main[m, 12 + j], 0.0)
        for j in range(2):
            at = right * (nx + 2) + 1 + j
            for k in range(3):
                force[k, at, pl.ds(0, nz)] = jnp.where(there, 2.0 * x_main[m, 15 + 2 * k + j], 0.0)


def first_fields(staged, z_halo, halo_full, x_main, u, other, halo):
    nx, nz = staged.nx, staged.nz
    slots = nx + 6
    zero = jnp.zeros((nz + 8, LANES), F32)
    for k in range(4):
        for p in list(range(3)) + list(range(nx + 3, slots)):
            u[k, p] = zero
            other[k, p] = zero
        for q in range(nx):
            u[k, q + 3, pl.ds(0, nz)] = staged[k, q]
            u[k, q + 3, pl.ds(nz, 8)] = z_halo[k, q]
        halo[k] = own_slots(halo_full[k], nx, 0)
    for m in range(x_main.shape[0]):
        right, valid = x_side(m)
        there = truth(valid, (nz, LANES))
        for k in range(4):
            for j in range(3):
                x = jnp.where(there, x_main[m, 3 * k + j], 0.0)
                u[k, right * (nx + 3) + j, pl.ds(0, nz)] = x


def add_rims(x_rim, nx, u, halo, e, halo_e, force, halo_f, edge, edge_e):
    nz = e.shape[1] - 8
    tiles = (nz + 8) // 8
    tail = pl.ds(nz, 8)
    slot = iota((8, LANES), 1) // SLOT
    for m in range(x_rim.shape[0]):
        right, valid = x_side(m)
        there = truth(valid, (8, LANES))
        column = jnp.concatenate([x_rim[m, 6 + r] for r in range(tiles)], axis=0)
        near = right * (nx + 1) + 2
        far = near + 2 * right - 1
        for k in range(5):
            x = jnp.where(there, x_rim[m, k], 0.0)
            for p, y in ((near, x), (far, roll(x, -3, 0))):
                moved = roll(y, p * SLOT + 4, 1)
                if k < 4:
                    u[k, p, tail] = y
                    edge[k, tail] = jnp.where(slot == p, moved, edge[k, tail])
                else:
                    e[p, tail] = y
                    edge_e[tail] = jnp.where(slot == p, moved, edge_e[tail])
            x, kept = rim_halo(column, k, LANES // 8, 2, right, valid, nx)
            if k < 4:
                halo[k] = jnp.where(kept, x, halo[k])
            else:
                halo_e[...] = jnp.where(kept, x, halo_e[...])
        x = jnp.where(there, 2.0 * x_rim[m, 5], 0.0)
        for k, at in enumerate((0, 3, 5)):
            force[k, near, tail] = roll(x, -at, 0)
            x_k, kept = rim_halo(column, 5 + k, LANES // 8, 2, right, valid, nx)
            halo_f[k] = jnp.where(kept, 2.0 * x_k, halo_f[k])


def early(nx, sweep):
    _, xl, xr = place("gx")

    def chosen(p):
        if 3 + sweep <= p < nx + 3 - sweep:
            return True
        if 3 <= p < nx + 3:
            return xl == 0 if p < 3 + sweep else xr == 0
        return False

    return chosen


def early_block(nx):
    _, xl, xr = place("gx")
    return lambda q: xl == 0 if 2 * q + 5 <= nx else xr == 0 if 2 * q + 2 >= 5 else False


def late(chosen):
    return lambda p: not chosen(p)


def inside_slots(slots, width, chosen=None):
    _, xl, xr = place("gx")
    inside = range(3 - width * xl, slots - 3 + width * xr)
    return [p for p in inside if chosen is None or chosen(p)]


def residuals(u, halo, beside, w, force, e, summed, chosen):
    _, blocks, nz, _ = summed.shape
    slots = u.shape[1]
    spread_halo(halo, beside, slots, 0, lambda p: chosen((p - 3) // 2), False)

    def body(q):
        totals = [0.0] * 5
        for j in range(2):
            p = 2 * q + 3 + j
            olds, sums, spread = main_operator(u, beside, w, force, p, nz)
            diagonal = (w[0][p] + w[0][p - 1] + w[1][p] + w[2][p] + w[3][p] + w[4][p])[:nz]
            for k in range(3):
                totals[k] += sums[k] - diagonal * olds[k]
            totals[3] += spread
            totals[4] += e[p, pl.ds(0, nz)]
        for k in range(5):
            summed[k, q] = totals[k]

    for q in range(blocks):
        if chosen(q):
            body(q)


def pre_start(*refs):
    pre_start_on(Staged(refs[:16]), *refs[16:])


def pre_start_on(
    staged, z_halo, halo_full, x_main,
    e, halo_e, force, halo_f, w0, w1, w2, w3, w4, w5, ua, ub, ha, ca, cb, edge_e, summed,
    hw, hb, hc, beside,
):
    nx, nz = staged.nx, staged.nz
    slots = nx + 6
    w = (w0, w1, w2, w3, w4, w5)
    viscosity_force(staged, z_halo, halo_full, x_main, e, halo_e, force, halo_f)
    first_fields(staged, z_halo, halo_full, x_main, ua, ub, ha)
    tile, column = fine_masks(nz + 8, slots)
    fill_edges(ca, ua, inside_slots(slots, 3))
    edge_e[...] = edges_of(lambda p: e[p], inside_slots(slots, 3))
    main_weights(e, halo_e, w, 0, early(nx, 1), range(2, nx + 3))
    main_sweep(ua, ha, ub, w, e, force, 0, tile, beside, early(nx, 1))
    halo_weights(halo_e, edge_e, hw)
    halo_sweep(ha, ca, hb, hw, halo_e, halo_f, column)
    fill_edges(cb, ub, inside_slots(slots, 0, early(nx, 1)))
    main_sweep(ub, hb, ua, w, e, force, 0, tile, beside, early(nx, 2))
    halo_sweep(hb, cb, hc, hw, halo_e, halo_f, column)
    residuals(ua, hc, beside, w, force, e, summed, early_block(nx))


def pre_smooth(
    x_rim, _e, _halo_e, _force, _halo_f, _w0, _w1, _w2, _w3, _w4, _w5, _ua, _ub, _ha, _ca, _cb,
    _edge_e, _summed, e, halo_e, force, halo_f, w0, w1, w2, w3, w4, w5, ua, ub, ha, ca, cb, edge_e,
    summed, hw, message, hb, beside,
):
    slots = e.shape[0]
    nx, nz = slots - 6, e.shape[1] - 8
    w = (w0, w1, w2, w3, w4, w5)
    add_rims(x_rim, nx, ua, ha, e, halo_e, force, halo_f, ca, edge_e)
    tile, column = fine_masks(nz + 8, slots)
    faces = [p for p in range(slots - 1) if not 3 <= p < nx + 2]
    main_weights(e, halo_e, w, 2, late(early(nx, 1)), faces)
    halo_weights(halo_e, edge_e, hw)
    main_sweep(ua, ha, ub, w, e, force, 2, tile, beside, late(early(nx, 1)))
    halo_sweep(ha, ca, hb, hw, halo_e, halo_f, column)
    fill_edges(cb, ub, inside_slots(slots, 2, late(early(nx, 1))), False)
    main_sweep(ub, hb, ua, w, e, force, 1, tile, beside, late(early(nx, 2)))
    halo_sweep(hb, cb, ha, hw, halo_e, halo_f, column)
    residuals(ua, ha, beside, w, force, e, summed, late(early_block(nx)))
    scale = (0.5, 0.5, 0.5, -1.0 / 32.0, 0.125)
    cz = nz // 2
    left = []
    for k in range(5):
        for r in range(nx // 4):
            halves = []
            for s in range(2):
                q = 2 * r + s
                even = summed[k, q, pl.ds(0, cz, stride=2)]
                halves.append((even + summed[k, q, pl.ds(1, cz, stride=2)]) * scale[k])
            left.append(jnp.concatenate(halves, axis=1))
    left = jnp.concatenate(left, axis=0)
    pick = iota((2 * LANES, LANES), 0) // 2 == iota((2 * LANES, LANES), 1)
    out = choose(left, pick)
    for k in range(5):
        for r in range(nx // 4):
            at = (k * (nx // 4) + r) * cz
            for i in range(cz // 8):
                message[at // 8 + i] = out[at + 8 * i : at + 8 * i + 8]
    sides = x_messages()
    lane = iota((nz, LANES), 1)
    _, _, xr = place("gx")
    for m in range(sides):
        high = xr if sides == 1 else high_side("gx", m)
        p = 3 + high * (nx - 1)
        parts, total = [], jnp.zeros((nz, LANES), F32)
        for k in range(4):
            x = ua[k, p, pl.ds(0, nz)]
            parts += [(x[:8], 2 * k, 2 * k, 1), (x[nz - 8 :], 2 * k + 2, 2 * k + 1, 1)]
            total = jnp.where(lane // 2 == k, roll(x, 2 * k + 1, 1), total)
        n = message.shape[0] - 2 * (sides - m)
        message[n] = rows_of(parts)
        column = total[:8]
        for t in range(1, nz // 8):
            x = roll(total[8 * t : 8 * t + 8], 8 * t, 1)
            column = jnp.where(lane[:8] // 8 == t, x, column)
        message[n + 1] = column


def smooth_pack(fields, edges, x_fine):
    nx, nz = fields.shape[1] - 6, fields.shape[2] - 8
    for m in range(x_fine.shape[0]):
        high = high_side("gx", m)
        for k in range(4):
            for j in range(2):
                x_fine[m, 2 * k + j] = fields[k, 3 + high * (nx - 2) + j, pl.ds(0, nz)]

    def planes(k):
        return [fields[k, q + 3, pl.ds(0, nz)] for q in range(nx)]

    for j, x in enumerate(pair_edges(planes, 4, nz)):
        edges[j] = x


def frame(ref, m, part):
    return ref[ref.shape[0] - 2 * (x_messages() - m) + part]


def fourth_pack(own, other, fields, whole, z_a, z_b):
    nx, nz = fields.shape[1] - 6, fields.shape[2] - 8
    pairs, cz = whole.shape[1:3]
    gx = lax.axis_index("gx")
    for k in range(5):
        for r in range(pairs):
            if own.ndim == 4:
                whole[k, r] = own[k, r]
                continue
            mine = truth(jnp.where(gx == r // (pairs // 2), 1, 0), (8, LANES))
            for i in range(cz // 8):
                n = (k * (pairs // 2) + r % (pairs // 2)) * (cz // 8) + i
                whole[k, r, pl.ds(8 * i, 8)] = jnp.where(mine, own[n], other[n])
    row = iota((8, LANES), 0) // 2
    for m, out in enumerate((z_a, z_b)):
        right = high_side("gz", m)
        start = pl.multiple_of(right * (cz - 8), 8)
        for r in range(pairs):
            for k in range(2):
                parts = [
                    (whole[k + 2 * h, r, pl.ds(0, 8)], whole[k + 2 * h, r, pl.ds(cz - 8, 8)])
                    + (4 * h, 4)
                    for h in range(2)
                ]
                out[k * pairs + r] = z_strip(parts, right)
            out[2 * pairs + r] = whole[4, r, pl.ds(start, 8)]
        toward = truth(right, (8, LANES))
        for q in range(nx):
            total = jnp.zeros((8, LANES), F32)
            for k in range(4):
                low = roll(fields[k, q + 3, pl.ds(0, 8)], 2 * k, 0)
                high = roll(fields[k, q + 3, pl.ds(nz - 8, 8)], 2 * k - 6, 0)
                total = jnp.where(row == k, jnp.where(toward, high, low), total)
            out[3 * pairs + q] = total
        for m_x in range(x_messages()):
            out[3 * pairs + nx + m_x] = frame(other, m_x, 0)


def fold_rows(x):
    own = x.shape[0] - 16
    row = iota((8, LANES), 0)
    halo = jnp.where(row < 4, x[own : own + 8], x[own + 8 :])
    return jnp.concatenate([x[:own], halo], axis=0)


def deep_edges(pairs, width):
    per = LANES // (2 * width)
    columns = []
    for n, x in enumerate(pairs):
        for g in range(2):
            t = (2 * n + g) % per
            x_t = roll(x, 2 * width * t + width - 64 * g, 1)
            if t == 0:
                columns.append(x_t)
            else:
                slot = iota(x.shape, 1) // (2 * width)
                columns[-1] = jnp.where(slot == t, x_t, columns[-1])
    return columns


def unfold(left, right, width):
    spot = iota(left.shape, 1) % (2 * width)
    first = jnp.where(spot < width, left, roll(right, width, 1))
    second = jnp.where(spot < width, roll(left, -width, 1), right)
    return first, second


def fifth_pack(whole, z_a, z_b, edges, frames, full, full_e, z_halo, z_rim, y_a, y_b):
    pairs, cz = whole.shape[1:3]
    nx = z_halo.shape[1]
    nz = edges.shape[1]
    _, has_left, has_right = place("gz")
    to_left = truth(has_left, (8, LANES))
    to_right = truth(has_right, (8, LANES))
    deep = []
    for k in range(5):
        for r in range(pairs):
            if k < 4:
                n = k % 2 * pairs + r
                tile = z_tile(z_a[n], z_b[n], k // 2 * 4, 4)
                x = jnp.concatenate([whole[k, r], tile], axis=0)
                full[k, r] = x
            else:
                left, right = left_right("gz", z_a[2 * pairs + r], z_b[2 * pairs + r])
                right = jnp.where(to_right, right, 0.0)
                left = jnp.where(to_left, left, 0.0)
                x = jnp.concatenate([whole[k, r], right, left], axis=0)
                full_e[r] = x
            deep.append(x)
    row = iota((8, LANES), 0)
    for q in range(nx):
        left, right = left_right("gz", z_a[3 * pairs + q], z_b[3 * pairs + q])
        for k in range(4):
            x = jnp.where(row < 2 * has_right, roll(right, -2 * k, 0), 0.0)
            z_halo[k, q] = jnp.where(row >= 8 - 2 * has_left, roll(left, 6 - 2 * k, 0), x)
    for m in range(z_rim.shape[0]):
        n = 3 * pairs + nx + m
        left, right = left_right("gz", z_a[n], z_b[n])
        x = jnp.where(to_right & (row % 2 == 0), right, 0.0)
        z_rim[m] = jnp.where(to_left & (row % 2 == 1), left, x)
    columns = deep_edges(deep[: 4 * pairs], 4)
    half = len(columns) // 2
    columns_e = deep_edges(deep[4 * pairs :], 8)
    upper = (cz + 16) // 2
    behind = pair_edges(lambda i: [z_halo[i, q] for q in range(nx)], 4, 8)
    for m, out in enumerate((y_a, y_b)):
        toward = high_side("gy", m)
        parts = [
            strip(columns[j], columns[j + half], toward, 4) for j in range(half)
        ] + [strip(x[:upper], x[upper:], toward, 8) for x in columns_e]
        for i in range(nz // 8):
            parts.append(y_strip(edges[0, pl.ds(8 * i, 8)], edges[1, pl.ds(8 * i, 8)], toward))
        parts.append(y_strip(behind[0], behind[1], toward))
        parts += [frame(frames, m_x, 1) for m_x in range(z_rim.shape[0])]
        n = 0
        for x in parts:
            for i in range(x.shape[0] // 8):
                out[n] = x[8 * i : 8 * i + 8]
                n += 1


def sixth_pack(y_a, y_b, halo_full, y_rim):
    tiles, sides = halo_full.shape[1] // 8, y_rim.shape[0]
    first = y_a.shape[0] - tiles - sides
    for i in range(tiles):
        for j, x in enumerate(merge_y(y_a[first + i], y_b[first + i])):
            halo_full[j, pl.ds(8 * i, 8)] = x
    _, has_left, has_right = place("gy")
    odd = iota((8, LANES), 1) % 2
    for m in range(sides):
        left, right = left_right("gy", y_a[first + tiles + m], y_b[first + tiles + m])
        kept = (odd < has_left) & (odd == 0) | (odd > 1 - has_right)
        y_rim[m] = jnp.where(kept, jnp.where(odd == 0, left, right), 0.0)


def coarse_solve(full, full_e, y_a, y_b, main, halo, ca, cb, force, e, w0, w1, w2, w3, w4, w5, deep_e, grown):
    pairs, rows = full.shape[1:3]
    deep = full_e.shape[1]
    planes = 2 * pairs
    own = main.shape[1] - 2
    cz = rows - 8
    half = LANES // 2
    _, zl, zr = place("gz")
    _, yl, yr = place("gy")
    two = lax.axis_size("gx") == 2
    gx = FIXED[-1][0] if two else lax.axis_index("gx")

    def inside(rows, width):
        lane = iota((rows, LANES), 1)
        row = iota((rows, LANES), 0)
        kept = (row < cz + width * zr) | (row >= rows - width * zl)
        return kept & ((lane < half + width * yr) | (lane >= LANES - width * yl))

    zero = jnp.zeros((rows, LANES), F32)
    w = (w0, w1, w2, w3, w4, w5)
    for k in range(4):
        for p in (0, planes + 1):
            ca[k, p] = zero
            cb[k, p] = zero
    e[0] = zero
    e[planes + 1] = zero
    deep_e[0] = jnp.zeros((deep, LANES), F32)
    deep_e[planes + 1] = jnp.zeros((deep, LANES), F32)

    tiles, deep_tiles = rows // 8, deep // 16
    count = pairs // 4
    columns = []

    def taken(n, tiles):
        a, b = (jnp.concatenate([ref[n + i] for i in range(tiles)], axis=0) for ref in (y_a, y_b))
        return left_right("gy", a, b)

    unfolded = [unfold(*taken(j * tiles, tiles), 4) for j in range(count)]
    columns = [x for x, _ in unfolded] + [x for _, x in unfolded]
    columns_e = []
    for j in range(-(-pairs // 4)):
        x = unfold(*taken(count * tiles + j * deep_tiles, deep_tiles), 8)
        columns_e.append(jnp.concatenate(x, axis=0))

    def whole_plane(pair, columns, n, s, width):
        lane = iota(pair.shape, 1)
        per = LANES // (2 * width)
        last, first = 2 * n + 1 - s, 2 * n + s
        low = roll(columns[first // per], half - 2 * width * (first % per) - width, 1)
        high = roll(columns[last // per], LANES - width - 2 * width * (last % per), 1)
        x = jnp.where(lane < half, roll(pair, -s * half, 1), low)
        return jnp.where(lane < LANES - width, x, high)

    near, far = inside(rows, 4), inside(deep, 8)
    for r in range(pairs):
        for s in range(2):
            p = 2 * r + s
            x = jnp.where(far, whole_plane(full_e[r], columns_e, r, s, 8), 0.0)
            deep_e[p + 1] = x
            e[p + 1] = fold_rows(x)
            for k in range(4):
                x = whole_plane(full[k, r], columns, k * pairs + r, s, 4)
                force[k, p] = jnp.where(near, x, 0.0)

    def shifts(x):
        return (
            roll(x, LANES - 1, 1),
            roll(x, 1, 1),
            roll(x, x.shape[0] - 1, 0),
            roll(x, 1, 0),
        )

    def two_by_two(width, body):
        if two:
            for p in range(max(gx * own - width, 0), min(gx * own + own + width, planes)):
                body(p + 1)
            return
        lo = jnp.maximum(gx * own - width, 0)
        hi = jnp.minimum(gx * own + own + width, planes)
        steps = (hi - lo + 1) // 2
        lo = jnp.minimum(lo, planes - 2 * steps)

        def step(i, carry):
            body(lo + 2 * i + 1)
            body(lo + 2 * i + 2)
            return carry

        lax.fori_loop(0, steps, step, 0)

    def start(p):
        x = deep_e[p]
        up, down = x + deep_e[p + 1], x + deep_e[p - 1]
        w0[p] = fold_rows(up)
        total = up + down
        for n, y in enumerate(shifts(x)):
            total += x + y
            w[1 + n][p] = fold_rows(x + y)
        factor = jnp.where(near, fold_rows(relax_weight / total), 0.0)
        w5[p] = factor
        for k in range(3):
            ca[k, p] = factor * force[k, p - 1]
        ca[3, p] = e[p] * force[3, p - 1]

    w0[0] = e[0] + e[1]
    two_by_two(planes, start)

    def sweep(src, dst, width):
        def body(p):
            wxp, wxm = w0[p], w0[p - 1]
            wyp, wym, wzp, wzm = w1[p], w2[p], w3[p], w4[p]
            x = src[3, p]
            around = shifts(x)
            up, down = src[3, p + 1], src[3, p - 1]
            spread = 0.0
            for k in range(3):
                u = src[k, p]
                yp, ym, zp, zm = shifts(u)
                xp, xm = src[k, p + 1], src[k, p - 1]
                total = force[k, p - 1] - 2.0 * terms(k, up, down, *around)
                total += wxp * xp + wxm * xm
                total += wyp * yp + wym * ym
                total += wzp * zp + wzm * zm
                spread += terms(k, xp, xm, yp, ym, zp, zm)
                dst[k, p] = jnp.where(near, 0.4 * u + w5[p] * total, 0.0)
            dst[3, p] = jnp.where(near, x + e[p] * (force[3, p - 1] - 0.125 * spread), 0.0)

        two_by_two(width, body)

    sweep(ca, cb, 3)
    sweep(cb, ca, 2)
    sweep(ca, cb, 1)

    lane = iota((LANES, 2 * LANES), 1)
    cell = iota((LANES, 2 * LANES), 0)
    spot = lane % SLOT
    wanted = jnp.where(spot < 4, LANES - 2, half - 2) + spot // 2
    slot = (lane - LANES) // SLOT
    column = jnp.zeros((4 * rows, LANES), F32)
    first = gx * own

    def grow(ref, index, x):
        ref[index + (pl.ds(0, cz, stride=2),)] = x[:cz]
        ref[index + (pl.ds(1, cz, stride=2),)] = x[:cz]
        grown[pl.ds(0, 8, stride=2)] = x[cz:]
        grown[pl.ds(1, 8, stride=2)] = x[cz:]
        r = iota((8, LANES), 0)
        tail = jnp.where(r < 4, grown[pl.ds(0, 8)], grown[pl.ds(8, 8)])
        ref[index + (pl.ds(2 * cz, 8),)] = tail

    for i in range(own + 2):
        x = jnp.concatenate([cb[k, first + i] for k in range(4)], axis=0)
        here = (lane >= LANES) & ((slot + 1) // 2 - 1 == i) & (cell == wanted)
        wide = choose(x, here | ((lane < LANES) & (lane // 2 == cell)))
        for k in range(4):
            grow(main, (k, i), wide[k * rows : (k + 1) * rows, :LANES])
        column += wide[:, LANES:]
    for k in range(4):
        grow(halo, (k,), column[k * rows : (k + 1) * rows])


def last_sweep(src, halo, beside, w, e, force, chosen, store):
    slots, nz = src.shape[1], src.shape[2] - 8
    spread_halo(halo, beside, slots, 0, chosen, False)

    def body(p):
        new = main_operator(src, beside, w, force, p, nz)
        new = relaxed(*new, w[5][p, pl.ds(0, nz)], e[p, pl.ds(0, nz)])
        for k in range(4):
            store(p, k, new[k])

    over_planes(slots, 0, body, chosen)


def post_smooth(
    e, halo_e, force, halo_f, w0, w1, w2, w3, w4, w5, hw,
    fields, z_halo, halo_full, x_fine, z_rim, y_rim, main, column, v_out, p_out,
    ua, ub, ha, hb, ca, beside,
):
    nx, nz, _ = p_out.shape
    slots = nx + 6
    w = (w0, w1, w2, w3, w4, w5)
    zero = jnp.zeros((nz + 8, LANES), F32)
    for k in range(4):
        for p in (1, 2, nx + 3, nx + 4):
            ua[k, p] = zero
            ub[k, p] = zero
        for q in range(nx):
            i = q // 2 + 1
            ua[k, q + 3, pl.ds(0, nz)] = fields[k, q + 3, pl.ds(0, nz)] + main[k, i, pl.ds(0, nz)]
            ua[k, q + 3, pl.ds(nz, 8)] = z_halo[k, q] + main[k, i, pl.ds(nz, 8)]
        ha[k] = own_slots(halo_full[k % 2], nx, k // 2)
    for m in range(x_fine.shape[0]):
        right, valid = x_side(m)
        there = truth(valid, (nz, LANES))
        there8 = truth(valid, (8, LANES))
        near = 2 + right * (nx + 1)
        row = iota((8, LANES), 0)
        lane = iota((nz, LANES), 1)
        kept = (lane == near * SLOT + 3) | (lane == near * SLOT + 4)
        i = right * (nx // 2 + 1)
        for k in range(4):
            for j in range(2):
                at = 1 + right * (nx + 2) + j
                x = x_fine[m, 2 * k + j] + main[k, i, pl.ds(0, nz)]
                ua[k, at, pl.ds(0, nz)] = jnp.where(there, x, 0.0)
            x = jnp.where(row == 0, roll(z_rim[m], -2 * k, 0), 0.0)
            x = jnp.where(row == 7, roll(z_rim[m], 6 - 2 * k, 0), x) + main[k, i, pl.ds(nz, 8)]
            ua[k, near, pl.ds(nz, 8)] = jnp.where(there8, x, 0.0)
            at = near * SLOT + 3 + LANES
            x = [roll(y_rim[m], at - SLOT * t - 2 * k, 1) for t in range(nz // 8)]
            x = jnp.where(kept, jnp.concatenate(x, axis=0), ha[k, pl.ds(0, nz)])
            ha[k, pl.ds(0, nz)] = jnp.where(there, x, ha[k, pl.ds(0, nz)])
    masks = fine_masks(nz + 8, slots)
    for k in range(4):
        ha[k] = jnp.where(masks[1], ha[k] + column[k], 0.0)
    fill_edges(ca, ua, inside_slots(slots, 2))
    main_sweep(ua, ha, ub, w, e, force, 1, masks[0], beside)
    halo_sweep(ha, ca, hb, hw, halo_e, halo_f, masks[1])

    def store(p, k, x):
        if k < 3:
            v_out[k, p - 3] = x
        else:
            p_out[p - 3] = x

    last_sweep(ub, hb, beside, w, e, force, None, store)


def finish(*refs):
    coarse, operator, rest = refs[:4], refs[4:15], refs[15:]
    fields, z_halo, x_fine, z_rim, v_out, p_out, halo_full, y_rim, main, column = rest[:10]
    sixth_pack(*coarse[2:], halo_full, y_rim)
    coarse_solve(*coarse, main, column, *rest[10:22])
    post_smooth(
        *operator, fields, z_halo, halo_full, x_fine, z_rim, y_rim, main, column, v_out, p_out,
        *rest[22:],
    )


def local(velocity, pressure, viscosity, body_force):
    nx, nz, ny = pressure.shape
    if ny != LANES or nx * SLOT * 2 != LANES or nz % 16:
        raise ValueError("unsupported block")
    sides = x_messages()
    rows, slots = nz + 8, nx + 6
    inputs = [velocity, pressure, viscosity, body_force]
    block = (nz, LANES)

    z_shape = (3 * nx, 8, LANES)
    half = (nx // 2,) + block
    *staged, y_a, y_b = call(
        first_pack, [half] * 16 + [(2,) + block] * 2, inputs, outside=4, copies=16
    )
    x_main, z_a, z_b = call(side_pack, [(sides, 21) + block, z_shape, z_shape], staged)
    y_a, y_b = swap(y_a, "gy", 0), swap(y_b, "gy", 1)
    x_main = swap_x(x_main)
    halo, z_b = call(second_pack, [(4,) + block, z_shape], [z_b, y_a, y_b])
    (z_a,) = call(second_pack_near, [z_shape], [z_a, halo])
    z_a, z_b = swap(z_a, "gz", 0), swap(z_b, "gz", 1)
    tiles = rows // 8
    z_first, halo_first, x_first = call(
        third_pack,
        [(8, nx, 8, LANES), (4, rows, LANES), (sides, 6 + tiles, 8, LANES)],
        [z_a, z_b, halo],
    )
    x_first = swap_x(x_first)

    spread, column = (4, slots, rows, LANES), (4, rows, LANES)
    started = [(slots, rows, LANES), (rows, LANES), (3, slots, rows, LANES), (3, rows, LANES)]
    started += [(slots, rows, LANES)] * 6 + [spread, spread] + [column] * 3 + [(rows, LANES)]
    started += [(5, nx // 2, nz, LANES)]
    tiles_c = 5 * (nx // 4) * (nz // 16)
    state = call(
        by_sides(pre_start),
        started,
        [*staged, z_first, halo_first, x_main],
        [(7, rows, LANES), column, column, spread],
        cost=4,
    )
    *operator, fields, _, _, _, _, _, _, factors, own = call(
        by_sides(pre_smooth),
        started + [(7, rows, LANES), (tiles_c + 2 * sides, 8, LANES)],
        [x_first, *state],
        [column, spread],
        cost=8,
        aliases={i + 1: i for i in range(len(started))},
    )
    operator.append(factors)
    edges, x_fine = call(smooth_pack, [(2,) + block, (sides, 8) + block], [fields])
    if lax.axis_size("gx") == 2:
        frames = swap(own, "gx", 0)
    else:
        frames = swap_x(own[tiles_c:].reshape(sides, 2, 8, LANES)).reshape(2 * sides, 8, LANES)
        own = own[:tiles_c].reshape(5, nx // 4, nz // 2, LANES)
        own = lax.all_gather(own, "gx", axis=1, tiled=True)
    x_fine = swap_x(x_fine)
    pairs = lax.axis_size("gx") * (nx // 4)
    z_shape = (3 * pairs + nx + sides, 8, LANES)
    whole, z_a, z_b = call(
        fourth_pack,
        [(5, pairs, nz // 2, LANES), z_shape, z_shape],
        [own, frames, fields],
    )
    z_a, z_b = swap(z_a, "gz", 0), swap(z_b, "gz", 1)
    deep = nz // 2 + 16
    shallow = deep - 8
    y_shape = (pairs // 4 * (shallow // 8) + -(-pairs // 4) * (deep // 16) + tiles, 8, LANES)
    y_shape = (y_shape[0] + sides, 8, LANES)
    rim = (sides, 8, LANES)
    full, full_e, z_halo, z_rim, y_a, y_b = call(
        fifth_pack,
        [(4, pairs, shallow, LANES), (pairs, deep, LANES), (4, nx, 8, LANES), rim, y_shape, y_shape],
        [whole, z_a, z_b, edges, frames],
    )
    y_a, y_b = swap(y_a, "gy", 0), swap(y_b, "gy", 1)
    planes = 2 * pairs
    plane = (shallow, LANES)
    coarse_scratch = [(4, nx // 2 + 2, rows, LANES), (4, rows, LANES)]
    coarse_scratch += [(4, planes + 2) + plane] * 2 + [(4, planes) + plane]
    coarse_scratch += [(planes + 2,) + plane] * 7 + [(planes + 2, deep, LANES), (16, LANES)]
    v_out, p_out = call(
        by_sides(finish),
        [(3, nx) + block, (nx,) + block],
        [full, full_e, y_a, y_b] + operator + [fields, z_halo, x_fine, z_rim],
        [(2, rows, LANES), rim] + coarse_scratch + [spread] * 2 + [column] * 3 + [spread],
        cost=8,
    )
    return v_out, p_out


def swap_x(array):
    if array.shape[0] == 1:
        return swap(array, "gx", 0)
    parts = [swap(array[m], "gx", m) for m in range(2)]
    return jnp.stack(parts)


def solution(mesh):
    return jax.shard_map(
        local,
        mesh=mesh,
        in_specs=(
            P(None, "gx", "gz", "gy"),
            P("gx", "gz", "gy"),
            P("gx", "gz", "gy"),
            P(None, "gx", "gz", "gy"),
        ),
        out_specs=(P(None, "gx", "gz", "gy"), P("gx", "gz", "gy")),
        check_vma=False,
    )
```

```python
import jax
import jax.numpy as jnp
from jax import lax
from jax.experimental import pallas as pl
from jax.experimental.pallas import tpu as pltpu
from jax.sharding import PartitionSpec as P

LANES = 128
SLOT = 8
F32 = jnp.float32
relax_weight = 0.6
HELD = 846 * 2**16
Z_PLACES = (
    ((0, 0, 3), (1, 3, 3), (5, 6, 2)),
    ((2, 0, 3), (3, 3, 3), (6, 6, 2)),
    ((4, 0, 3), (7, 3, 2)),
)


def call(body, outs, args, scratch=(), cost=1, outside=0, copies=0, aliases=None):
    return pl.pallas_call(
        body,
        out_shape=[jax.ShapeDtypeStruct(shape, F32) for shape in outs],
        in_specs=[pl.BlockSpec(memory_space=pltpu.HBM)] * outside
        + [pl.BlockSpec(memory_space=pltpu.VMEM)] * (len(args) - outside),
        out_specs=[pl.BlockSpec(memory_space=pltpu.VMEM)] * len(outs),
        scratch_shapes=[pltpu.VMEM(shape, F32) for shape in scratch]
        + [pltpu.SemaphoreType.DMA((copies,))] * (copies > 0),
        input_output_aliases=aliases or {},
        compiler_params=pltpu.CompilerParams(vmem_limit_bytes=HELD if outside else 40 * 2**20),
        cost_estimate=pl.CostEstimate(
            flops=cost * 10**6, bytes_accessed=cost * 10**6, transcendentals=0
        ),
    )(*args)


def swap(array, axis, which):
    count = lax.axis_size(axis)
    if axis != "gx" and which == 1:
        ys, zs = lax.axis_size("gy"), lax.axis_size("gz")
        pairs = []
        for y in range(ys):
            for z in range(zs):
                i = y if axis == "gy" else z
                j = i + 1 if i % 2 else i - 1
                if axis == "gy":
                    to = (j, z) if 0 <= j < count else (y, z ^ 1)
                else:
                    to = (y, j) if 0 <= j < count else (y ^ 1, z)
                pairs.append((y * zs + z, to[0] * zs + to[1]))
        return lax.ppermute(array, ("gy", "gz"), pairs)
    pairs = []
    for i in range(which, count, 2):
        j = (i + 1) % count
        pairs += [(i, j), (j, i)]
    return lax.ppermute(array, axis, pairs)


FIXED = []


def choose(x, chosen):
    parts = []
    for _ in range(3):
        parts.append(x.astype(jnp.bfloat16))
        x = x - parts[-1].astype(F32)
    chosen = jnp.where(chosen, 1.0, 0.0).astype(jnp.bfloat16)
    return jnp.dot(
        jnp.concatenate(parts, axis=1),
        jnp.concatenate([chosen] * 3, axis=0),
        preferred_element_type=F32,
    )


def by_sides(body):
    def kernel(*refs):
        count = lax.axis_size("gx")
        _, xl, xr = place("gx")
        for sides in [(0, 1), (1, 0), (1, 1)][: 2 if count == 2 else 3]:

            def branch(sides=sides):
                FIXED.append(sides)
                body(*refs)
                FIXED.pop()

            pl.when((xl == sides[0]) & (xr == sides[1]))(branch)

    return kernel


def place(axis):
    if axis == "gx" and FIXED:
        return (None,) + FIXED[-1]
    i = lax.axis_index(axis)
    last = lax.axis_size(axis) - 1
    return i, jnp.where(i > 0, 1, 0), jnp.where(i < last, 1, 0)


def iota(shape, dim):
    return lax.broadcasted_iota(jnp.int32, shape, dim)


def truth(flag, shape):
    return jnp.full(shape, flag, jnp.int32) > 0


def roll(x, shift, dim):
    if isinstance(shift, int):
        shift %= x.shape[dim]
        return x if shift == 0 else pltpu.roll(x, shift, dim)
    return pltpu.roll(x, lax.rem(shift + 2 * x.shape[dim], x.shape[dim]), dim)


def high_side(axis, message):
    return jnp.where(lax.axis_index(axis) % 2 == message, 1, 0)


def left_right(axis, a, b):
    odd = truth(lax.axis_index(axis) % 2, a.shape)
    return jnp.where(odd, a, b), jnp.where(odd, b, a)


def x_messages():
    return 1 if lax.axis_size("gx") == 2 else 2


def pair_edges(planes, fields, rows):
    lane = iota((rows, LANES), 1) // SLOT
    half = fields // 2
    out = []
    for j in range(half):
        total = jnp.zeros((rows, LANES), F32)
        for part in range(2):
            for q, x in enumerate(planes(j + part * half)):
                slot = q + part * (LANES // SLOT // 2)
                total = jnp.where(lane == slot, roll(x, slot * SLOT + 4, 1), total)
        out.append(total)
    return out


def merge_y(a, b):
    _, has_left, has_right = place("gy")
    left, right = left_right("gy", a, b)
    spot = iota(a.shape, 1) % SLOT
    kept = (spot < 4 * has_left) | (spot >= SLOT - 4 * has_right)
    first = jnp.where(spot < 4, left, roll(right, 4, 1))
    second = jnp.where(spot < 4, roll(left, -4, 1), right)
    return jnp.where(kept, first, 0.0), jnp.where(kept, second, 0.0)


class Staged:
    def __init__(self, refs):
        self.refs = refs
        self.half, self.nz = refs[0].shape[:2]
        self.nx = 2 * self.half

    def __getitem__(self, index):
        i, q = index[:2]
        return self.refs[2 * i + q // self.half][(q % self.half,) + index[2:]]


def first_pack(v_in, p_in, e_in, f_in, *refs):
    staged = Staged(refs[:16])
    y_a, y_b, arrived = refs[16:]
    nx, nz = staged.nx, staged.nz
    loads = []
    for n in range(16):
        i, planes = n // 2, pl.ds(n % 2 * staged.half, staged.half)
        if i < 3:
            part = v_in.at[i, planes]
        elif i < 5:
            part = (p_in, e_in)[i - 3].at[planes]
        else:
            part = f_in.at[i - 5, planes]
        loads.append(pltpu.make_async_copy(part, refs[n], arrived.at[n]))
    for load in loads:
        load.start()
    for load in loads:
        load.wait()
    edges = pair_edges(lambda i: [staged[i, q] for q in range(nx)], 8, nz)
    for m, out in enumerate((y_a, y_b)):
        for j in range(2):
            out[j] = y_strip(edges[j], edges[j + 2], high_side("gy", m))


def side_pack(*refs):
    staged = Staged(refs[:16])
    x_main, z_a, z_b = refs[16:]
    nx, nz = staged.nx, staged.nz
    for m in range(x_main.shape[0]):
        top = truth(high_side("gx", m), (nz, LANES))
        n = 0
        for i in range(8):
            width = 3 if i < 5 else 2
            for j in range(width):
                x_main[m, n] = jnp.where(top, staged[i, nx - width + j], staged[i, j])
                n += 1
    low, high = pl.ds(0, 8), pl.ds(nz - 8, 8)
    for q in range(nx):
        for n, fields in enumerate(Z_PLACES):
            for m, out in enumerate((z_a, z_b)):
                out[3 * q + n] = z_strip(
                    [(staged[i, q, low], staged[i, q, high], at, rows) for i, at, rows in fields],
                    high_side("gz", m),
                )


def strip(first, second, toward_right, width):
    right = truth(toward_right, first.shape)
    spot = iota(first.shape, 1) % (2 * width)
    first = jnp.where(right, first, roll(first, -width, 1))
    second = jnp.where(right, roll(second, width, 1), second)
    return jnp.where(spot < width, first, second)


def y_strip(first, second, toward_right):
    return strip(first, second, toward_right, SLOT // 2)


def z_strip(parts, toward_right):
    right = truth(toward_right, (8, LANES))
    return rows_of(
        [
            (jnp.where(right, roll(high, at + rows, 0), roll(low, at, 0)), 0, at, rows)
            for low, high, at, rows in parts
        ]
    )


def z_tail(halo, first, out, message):
    nz = halo.shape[1]
    row = iota((8, LANES), 0)
    for n in range(first.shape[0]):
        out[n] = first[n]
    for j in range(4):
        tiles = halo[j, pl.ds(0, 8)], halo[j, pl.ds(nz - 8, 8)]
        x = z_strip([tiles + (5, 3)], high_side("gz", message))
        out[3 * j + 2] = jnp.where(row < 5, first[3 * j + 2], x)


def second_pack(z_first_a, z_first_b, y_a, y_b, halo, z_a, z_b):
    for j in range(2):
        halo[j], halo[j + 2] = merge_y(y_a[j], y_b[j])
    z_tail(halo, z_first_a, z_a, 0)
    z_tail(halo, z_first_b, z_b, 1)


def z_tile(a, b, at, rows):
    _, has_left, has_right = place("gz")
    left, right = left_right("gz", a, b)
    row = iota(a.shape, 0)
    x = jnp.where(row < rows * has_right, roll(right, -at, 0), 0.0)
    return jnp.where(row >= 8 - rows * has_left, roll(left, 8 - at - rows, 0), x)


def third_pack(z_a, z_b, halo, z_halo, halo_full, x_rim):
    nx = z_halo.shape[1]
    nz = halo.shape[1]
    for q in range(nx):
        for n, fields in enumerate(Z_PLACES):
            for i, at, rows in fields:
                z_halo[i, q] = z_tile(z_a[3 * q + n], z_b[3 * q + n], at, rows)
    for j in range(4):
        halo_full[j, pl.ds(0, nz)] = halo[j]
        halo_full[j, pl.ds(nz, 8)] = z_tile(z_a[3 * j + 2], z_b[3 * j + 2], 5, 3)

    def tiles(plane):
        out = [
            rows_of([(z_halo[i, plane(1)], 0, 6, 4), (z_halo[i, plane(2)], 3, 2, 2)])
            for i in range(5)
        ]
        force = zip((0, 3, 5), (7, 2, 4))
        out.append(
            rows_of([(z_halo[5 + k, plane(1)], at, row, 2) for k, (at, row) in enumerate(force)])
        )
        return out

    pack_rim(x_rim, tiles, lambda j: halo_full[j], 8, 2, nx)


def rows_of(parts):
    row = iota((8, LANES), 0)
    total = jnp.zeros((8, LANES), F32)
    for x, shift, first, count in parts:
        total = jnp.where((row - first) % 8 < count, roll(x, shift, 0), total)
    return total


def pack_rim(x_rim, tiles, halo_pair, fields, planes, nx):
    half = fields // 2
    stride = LANES // 8 if fields == 8 else SLOT
    for m in range(x_rim.shape[0]):
        high = high_side("gx", m)
        done = tiles(lambda d, high=high: high * (nx - 2 * d + 1) + d - 1)
        for n, x in enumerate(done):
            x_rim[m, n] = x
        pairs = [halo_pair(j) for j in range(half)]
        rows = pairs[0].shape[0]
        column = iota((rows, LANES), 1) // stride
        first = high * (nx - planes) * SLOT
        total = jnp.zeros((rows, LANES), F32)
        for i in range(fields):
            at = i * stride - first - (i // half) * (LANES // 2)
            total = jnp.where(column == i, roll(pairs[i % half], at + LANES, 1), total)
        for r in range(rows // 8):
            x_rim[m, len(done) + r] = total[8 * r : 8 * r + 8]


def main_shifts(x, beside, kept):
    rows = x.shape[0]
    y, beside = x[:kept], beside[:kept]
    lane = iota(y.shape, 1)
    return (
        roll(jnp.where(lane == 0, beside, y), LANES - 1, 1),
        roll(jnp.where(lane == LANES - 1, beside, y), 1, 1),
        roll(x, rows - 1, 0)[:kept],
        roll(x, 1, 0)[:kept],
    )


def halo_shifts(x, edge):
    spot = iota(x.shape, 1) % SLOT
    rows = x.shape[0]
    return (
        roll(x, LANES - SLOT, 1),
        roll(x, SLOT, 1),
        roll(jnp.where(spot == 4, edge, x), LANES - 1, 1),
        roll(jnp.where(spot == 3, edge, x), 1, 1),
        roll(x, rows - 1, 0),
        roll(x, 1, 0),
    )


def main_weights(e, halo_e, w, width, chosen, faces):
    slots = e.shape[0]
    for p in faces:
        w[0][p] = e[p] + e[p + 1]

    def body(p):
        x = e[p]
        total = w[0][p] + w[0][p - 1]
        for n, y in enumerate(main_shifts(x, roll(halo_e[...], LANES - SLOT * p - 4, 1), x.shape[0])):
            total += x + y
            w[1 + n][p] = x + y
        w[5][p] = relax_weight / total

    over_planes(slots, width, body, chosen)


def halo_weights(e, edge_e, w):
    x = e[...]
    total = jnp.zeros_like(x)
    for n, y in enumerate(halo_shifts(x, edge_e[...])):
        total += x + y
        w[n] = x + y
    w[6] = relax_weight / total


def terms(k, up, down, yp, ym, zp, zm):
    return (up - down, zp - zm, yp - ym)[k]


def spread_halo(halo, beside, slots, width, chosen=None, full=True):
    kept = beside.shape[2] - (0 if full else 8)

    def body(p):
        for k in range(4):
            beside[k, p, pl.ds(0, kept)] = roll(halo[k][:kept], LANES - SLOT * p - 4, 1)

    over_planes(slots, width, body, chosen)


def main_operator(src, beside, w, force, p, kept):
    def at(ref, *index):
        return ref[index + (pl.ds(0, kept),)]

    wxp, wxm, wyp, wym, wzp, wzm = (
        at(ref, q) for ref, q in zip((w[0],) + w[:5], (p, p - 1, p, p, p, p))
    )
    around = main_shifts(src[3, p], at(beside, 3, p), kept)
    up, down = at(src, 3, p + 1), at(src, 3, p - 1)
    olds, sums, spread = [], [], 0.0
    for k in range(3):
        yp, ym, zp, zm = main_shifts(src[k, p], at(beside, k, p), kept)
        xp, xm = at(src, k, p + 1), at(src, k, p - 1)
        total = at(force, k, p) - terms(k, up, down, *around)
        total += wxp * xp + wxm * xm
        total += wyp * yp + wym * ym
        total += wzp * zp + wzm * zm
        spread += terms(k, xp, xm, yp, ym, zp, zm)
        olds.append(at(src, k, p))
        sums.append(total)
    olds.append(at(src, 3, p))
    return olds, sums, spread


def halo_operator(halo, edge, w, force):
    x = halo[3]
    px = halo_shifts(x, edge[3])
    olds, sums, spread = [], [], 0.0
    for k in range(3):
        u = halo[k]
        around = halo_shifts(u, edge[k])
        total = force[k] - terms(k, *px)
        for n in range(6):
            total += w[n] * around[n]
        spread += terms(k, *around)
        olds.append(u)
        sums.append(total)
    olds.append(x)
    return olds, sums, spread


def relaxed(olds, sums, spread, factor, e):
    new = [0.4 * olds[k] + factor * sums[k] for k in range(3)]
    return new + [olds[3] - 0.25 * e * spread]


def edges_of(plane, slots, total=None):
    shape = plane(slots[0]).shape
    slot = iota(shape, 1) // SLOT
    total = jnp.zeros(shape, F32) if total is None else total
    for p in slots:
        total = jnp.where(slot == p, roll(plane(p), p * SLOT + 4, 1), total)
    return total


def fill_edges(edge, src, slots, fresh=True):
    for k in range(4):
        edge[k] = edges_of(lambda p: src[k, p], slots, None if fresh else edge[k])


def fine_masks(rows, slots):
    nz = rows - 8
    _, zl, zr = place("gz")
    _, yl, yr = place("gy")
    _, xl, xr = place("gx")
    r = iota((8, LANES), 0)
    tile = (r < 4 * zr) | (r >= 8 - 4 * zl)
    r = iota((rows, LANES), 0)
    lane = iota((rows, LANES), 1)
    spot, slot = lane % SLOT, lane // SLOT
    column = (r < nz + 4 * zr) | (r >= rows - 4 * zl)
    column &= (spot < 4 * yl) | (spot >= SLOT - 4 * yr)
    column &= (slot >= 3 - 3 * xl) & (slot < slots - 3 + 3 * xr)
    return tile, column


def main_sweep(src, halo, dst, w, e, force, width, tile, beside, chosen=None):
    nz = src.shape[2] - 8
    slots = src.shape[1]

    def body(p):
        new = relaxed(*main_operator(src, beside, w, force, p, nz + 8), w[5][p], e[p])
        for k in range(4):
            x = new[k]
            dst[k, p, pl.ds(0, nz)] = x[:nz]
            dst[k, p, pl.ds(nz, 8)] = jnp.where(tile, x[nz:], 0.0)

    spread_halo(halo, beside, slots, width, chosen)
    over_planes(slots, width, body, chosen)


def halo_sweep(halo, edge, halo_dst, hw, halo_e, halo_f, column):
    new = relaxed(*halo_operator(halo, edge, hw, halo_f), hw[6], halo_e[...])
    for k in range(4):
        halo_dst[k] = jnp.where(column, new[k], 0.0)


def over_planes(slots, width, body, chosen=None):
    _, xl, xr = place("gx")
    for p in range(3 - width, slots - 3 + width):
        wanted = True if chosen is None else chosen(p)
        if wanted and (p >= 3 or xl) and (p < slots - 3 or xr):
            body(p)


def own_slots(x, nx, part):
    lane = iota(x.shape, 1)
    x = roll(x, 3 * SLOT - part * (LANES // 2), 1)
    return jnp.where((lane >= 3 * SLOT) & (lane < (3 + nx) * SLOT), x, 0.0)


def x_side(m):
    _, has_left, has_right = place("gx")
    if lax.axis_size("gx") == 2:
        return has_right, 1
    right = high_side("gx", m)
    return right, jnp.where(right > 0, has_right, has_left)


def rim_halo(x, t, stride, planes, right, valid, nx):
    base = right * (nx + 3) + (1 - right) * (3 - planes)
    lane = iota(x.shape, 1)
    x = roll(x, base * SLOT - t * stride + LANES, 1)
    kept = (lane >= base * SLOT) & (lane < (base + planes * valid) * SLOT)
    return jnp.where(kept, x, 0.0), kept


def viscosity_force(staged, z_halo, halo_full, x_main, e, halo_e, force, halo_f):
    nx, nz = staged.nx, staged.nz
    slots = nx + 6
    zero = jnp.zeros((nz + 8, LANES), F32)
    for p in list(range(3)) + list(range(nx + 3, slots)):
        e[p] = zero
        for k in range(3):
            force[k, p] = zero
    for q in range(nx):
        e[q + 3, pl.ds(0, nz)] = staged[4, q]
        e[q + 3, pl.ds(nz, 8)] = z_halo[4, q]
        for k in range(3):
            force[k, q + 3, pl.ds(0, nz)] = 2.0 * staged[5 + k, q]
            force[k, q + 3, pl.ds(nz, 8)] = 2.0 * z_halo[5 + k, q]
    halo_e[...] = own_slots(halo_full[0], nx, 1)
    for k in range(3):
        halo_f[k] = 2.0 * own_slots(halo_full[k + 1], nx, 1)
    for m in range(x_main.shape[0]):
        right, valid = x_side(m)
        there = truth(valid, (nz, LANES))
        for j in range(3):
            e[right * (nx + 3) + j, pl.ds(0, nz)] = jnp.where(there, x_main[m, 12 + j], 0.0)
        for j in range(2):
            at = right * (nx + 2) + 1 + j
            for k in range(3):
                force[k, at, pl.ds(0, nz)] = jnp.where(there, 2.0 * x_main[m, 15 + 2 * k + j], 0.0)


def first_fields(staged, z_halo, halo_full, x_main, u, other, halo):
    nx, nz = staged.nx, staged.nz
    slots = nx + 6
    zero = jnp.zeros((nz + 8, LANES), F32)
    for k in range(4):
        for p in list(range(3)) + list(range(nx + 3, slots)):
            u[k, p] = zero
            other[k, p] = zero
        for q in range(nx):
            u[k, q + 3, pl.ds(0, nz)] = staged[k, q]
            u[k, q + 3, pl.ds(nz, 8)] = z_halo[k, q]
        halo[k] = own_slots(halo_full[k], nx, 0)
    for m in range(x_main.shape[0]):
        right, valid = x_side(m)
        there = truth(valid, (nz, LANES))
        for k in range(4):
            for j in range(3):
                x = jnp.where(there, x_main[m, 3 * k + j], 0.0)
                u[k, right * (nx + 3) + j, pl.ds(0, nz)] = x


def add_rims(x_rim, nx, u, halo, e, halo_e, force, halo_f, edge, edge_e):
    nz = e.shape[1] - 8
    tiles = (nz + 8) // 8
    tail = pl.ds(nz, 8)
    slot = iota((8, LANES), 1) // SLOT
    for m in range(x_rim.shape[0]):
        right, valid = x_side(m)
        there = truth(valid, (8, LANES))
        column = jnp.concatenate([x_rim[m, 6 + r] for r in range(tiles)], axis=0)
        near = right * (nx + 1) + 2
        far = near + 2 * right - 1
        for k in range(5):
            x = jnp.where(there, x_rim[m, k], 0.0)
            for p, y in ((near, x), (far, roll(x, -3, 0))):
                moved = roll(y, p * SLOT + 4, 1)
                if k < 4:
                    u[k, p, tail] = y
                    edge[k, tail] = jnp.where(slot == p, moved, edge[k, tail])
                else:
                    e[p, tail] = y
                    edge_e[tail] = jnp.where(slot == p, moved, edge_e[tail])
            x, kept = rim_halo(column, k, LANES // 8, 2, right, valid, nx)
            if k < 4:
                halo[k] = jnp.where(kept, x, halo[k])
            else:
                halo_e[...] = jnp.where(kept, x, halo_e[...])
        x = jnp.where(there, 2.0 * x_rim[m, 5], 0.0)
        for k, at in enumerate((0, 3, 5)):
            force[k, near, tail] = roll(x, -at, 0)
            x_k, kept = rim_halo(column, 5 + k, LANES // 8, 2, right, valid, nx)
            halo_f[k] = jnp.where(kept, 2.0 * x_k, halo_f[k])


def early(nx, sweep):
    _, xl, xr = place("gx")

    def chosen(p):
        if 3 + sweep <= p < nx + 3 - sweep:
            return True
        if 3 <= p < nx + 3:
            return xl == 0 if p < 3 + sweep else xr == 0
        return False

    return chosen


def early_block(nx):
    _, xl, xr = place("gx")
    return lambda q: xl == 0 if 2 * q + 5 <= nx else xr == 0 if 2 * q + 2 >= 5 else False


def late(chosen):
    return lambda p: not chosen(p)


def inside_slots(slots, width, chosen=None):
    _, xl, xr = place("gx")
    inside = range(3 - width * xl, slots - 3 + width * xr)
    return [p for p in inside if chosen is None or chosen(p)]


def residuals(u, halo, beside, w, force, e, summed, chosen):
    blocks, nz = summed.shape[1], summed.shape[2] - 8
    slots = u.shape[1]
    spread_halo(halo, beside, slots, 0, lambda p: chosen((p - 3) // 2), False)

    def body(q):
        totals = [0.0] * 5
        for j in range(2):
            p = 2 * q + 3 + j
            olds, sums, spread = main_operator(u, beside, w, force, p, nz)
            diagonal = (w[0][p] + w[0][p - 1] + w[1][p] + w[2][p] + w[3][p] + w[4][p])[:nz]
            for k in range(3):
                totals[k] += sums[k] - diagonal * olds[k]
            totals[3] += spread
            totals[4] += e[p, pl.ds(0, nz)]
        for k in range(5):
            summed[k, q, pl.ds(0, nz)] = totals[k]

    for q in range(blocks):
        if chosen(q):
            body(q)


def pre_start(*refs):
    pre_start_on(Staged(refs[:16]), *refs[16:])


def pre_start_on(
    staged, z_halo, halo_full, x_main,
    e, halo_e, force, halo_f, w0, w1, w2, w3, w4, w5, ua, ub, ha, ca, cb, edge_e, summed,
    hw, hb, hc, beside,
):
    nx, nz = staged.nx, staged.nz
    slots = nx + 6
    w = (w0, w1, w2, w3, w4, w5)
    viscosity_force(staged, z_halo, halo_full, x_main, e, halo_e, force, halo_f)
    first_fields(staged, z_halo, halo_full, x_main, ua, ub, ha)
    tile, column = fine_masks(nz + 8, slots)
    fill_edges(ca, ua, inside_slots(slots, 3))
    edge_e[...] = edges_of(lambda p: e[p], inside_slots(slots, 3))
    main_weights(e, halo_e, w, 0, early(nx, 1), range(2, nx + 3))
    main_sweep(ua, ha, ub, w, e, force, 0, tile, beside, early(nx, 1))
    halo_weights(halo_e, edge_e, hw)
    halo_sweep(ha, ca, hb, hw, halo_e, halo_f, column)
    fill_edges(cb, ub, inside_slots(slots, 0, early(nx, 1)))
    main_sweep(ub, hb, ua, w, e, force, 0, tile, beside, early(nx, 2))
    halo_sweep(hb, cb, hc, hw, halo_e, halo_f, column)
    residuals(ua, hc, beside, w, force, e, summed, early_block(nx))


def pre_smooth(
    x_rim, _e, _halo_e, _force, _halo_f, _w0, _w1, _w2, _w3, _w4, _w5, _ua, _ub, _ha, _ca, _cb,
    _edge_e, _summed, e, halo_e, force, halo_f, w0, w1, w2, w3, w4, w5, ua, ub, ha, ca, cb, edge_e,
    summed, hw, message, hb, beside,
):
    slots = e.shape[0]
    nx, nz = slots - 6, e.shape[1] - 8
    w = (w0, w1, w2, w3, w4, w5)
    add_rims(x_rim, nx, ua, ha, e, halo_e, force, halo_f, ca, edge_e)
    tile, column = fine_masks(nz + 8, slots)
    faces = [p for p in range(slots - 1) if not 3 <= p < nx + 2]
    main_weights(e, halo_e, w, 2, late(early(nx, 1)), faces)
    halo_weights(halo_e, edge_e, hw)
    main_sweep(ua, ha, ub, w, e, force, 2, tile, beside, late(early(nx, 1)))
    halo_sweep(ha, ca, hb, hw, halo_e, halo_f, column)
    fill_edges(cb, ub, inside_slots(slots, 2, late(early(nx, 1))), False)
    main_sweep(ub, hb, ua, w, e, force, 1, tile, beside, late(early(nx, 2)))
    halo_sweep(hb, cb, ha, hw, halo_e, halo_f, column)
    residuals(ua, ha, beside, w, force, e, summed, late(early_block(nx)))
    scale = (0.5, 0.5, 0.5, -1.0 / 32.0, 0.125)
    cz = nz // 2
    left = []
    for k in range(5):
        for r in range(nx // 4):
            halves = []
            for s in range(2):
                q = 2 * r + s
                even = summed[k, q, pl.ds(0, cz, stride=2)]
                halves.append((even + summed[k, q, pl.ds(1, cz, stride=2)]) * scale[k])
            left.append(jnp.concatenate(halves, axis=1))
    left = jnp.concatenate(left, axis=0)
    pick = iota((2 * LANES, LANES), 0) // 2 == iota((2 * LANES, LANES), 1)
    out = choose(left, pick)
    for k in range(5):
        for r in range(nx // 4):
            at = (k * (nx // 4) + r) * cz
            for i in range(cz // 8):
                message[at // 8 + i] = out[at + 8 * i : at + 8 * i + 8]
    sides = x_messages()
    lane = iota((nz, LANES), 1)
    _, _, xr = place("gx")
    for m in range(sides):
        high = xr if sides == 1 else high_side("gx", m)
        p = 3 + high * (nx - 1)
        parts, total = [], jnp.zeros((nz, LANES), F32)
        for k in range(4):
            x = ua[k, p, pl.ds(0, nz)]
            parts += [(x[:8], 2 * k, 2 * k, 1), (x[nz - 8 :], 2 * k + 2, 2 * k + 1, 1)]
            total = jnp.where(lane // 2 == k, roll(x, 2 * k + 1, 1), total)
        n = message.shape[0] - 2 * (sides - m)
        message[n] = rows_of(parts)
        column = total[:8]
        for t in range(1, nz // 8):
            x = roll(total[8 * t : 8 * t + 8], 8 * t, 1)
            column = jnp.where(lane[:8] // 8 == t, x, column)
        message[n + 1] = column


def smooth_pack(fields, edges, x_fine):
    nx, nz = fields.shape[1] - 6, fields.shape[2] - 8
    for m in range(x_fine.shape[0]):
        high = high_side("gx", m)
        for k in range(4):
            for j in range(2):
                x_fine[m, 2 * k + j] = fields[k, 3 + high * (nx - 2) + j, pl.ds(0, nz)]

    def planes(k):
        return [fields[k, q + 3, pl.ds(0, nz)] for q in range(nx)]

    for j, x in enumerate(pair_edges(planes, 4, nz)):
        edges[j] = x


def frame(ref, m, part):
    return ref[ref.shape[0] - 2 * (x_messages() - m) + part]


def fourth_pack(own, other, fields, whole, z_a, z_b):
    nx, nz = fields.shape[1] - 6, fields.shape[2] - 8
    pairs, cz = whole.shape[1:3]
    gx = lax.axis_index("gx")
    for k in range(5):
        for r in range(pairs):
            if own.ndim == 4:
                whole[k, r] = own[k, r]
                continue
            mine = truth(jnp.where(gx == r // (pairs // 2), 1, 0), (8, LANES))
            for i in range(cz // 8):
                n = (k * (pairs // 2) + r % (pairs // 2)) * (cz // 8) + i
                whole[k, r, pl.ds(8 * i, 8)] = jnp.where(mine, own[n], other[n])
    row = iota((8, LANES), 0) // 2
    for m, out in enumerate((z_a, z_b)):
        right = high_side("gz", m)
        start = pl.multiple_of(right * (cz - 8), 8)
        for r in range(pairs):
            for k in range(2):
                parts = [
                    (whole[k + 2 * h, r, pl.ds(0, 8)], whole[k + 2 * h, r, pl.ds(cz - 8, 8)])
                    + (4 * h, 4)
                    for h in range(2)
                ]
                out[k * pairs + r] = z_strip(parts, right)
            out[2 * pairs + r] = whole[4, r, pl.ds(start, 8)]
        toward = truth(right, (8, LANES))
        for q in range(nx):
            total = jnp.zeros((8, LANES), F32)
            for k in range(4):
                low = roll(fields[k, q + 3, pl.ds(0, 8)], 2 * k, 0)
                high = roll(fields[k, q + 3, pl.ds(nz - 8, 8)], 2 * k - 6, 0)
                total = jnp.where(row == k, jnp.where(toward, high, low), total)
            out[3 * pairs + q] = total
        for m_x in range(x_messages()):
            out[3 * pairs + nx + m_x] = frame(other, m_x, 0)


def fold_rows(x):
    own = x.shape[0] - 16
    row = iota((8, LANES), 0)
    halo = jnp.where(row < 4, x[own : own + 8], x[own + 8 :])
    return jnp.concatenate([x[:own], halo], axis=0)


def deep_edges(pairs, width):
    per = LANES // (2 * width)
    columns = []
    for n, x in enumerate(pairs):
        for g in range(2):
            t = (2 * n + g) % per
            x_t = roll(x, 2 * width * t + width - 64 * g, 1)
            if t == 0:
                columns.append(x_t)
            else:
                slot = iota(x.shape, 1) // (2 * width)
                columns[-1] = jnp.where(slot == t, x_t, columns[-1])
    return columns


def unfold(left, right, width):
    spot = iota(left.shape, 1) % (2 * width)
    first = jnp.where(spot < width, left, roll(right, width, 1))
    second = jnp.where(spot < width, roll(left, -width, 1), right)
    return first, second


def fifth_pack(whole, z_a, z_b, edges, frames, full, full_e, z_halo, z_rim, y_a, y_b):
    pairs, cz = whole.shape[1:3]
    nx = z_halo.shape[1]
    nz = edges.shape[1]
    _, has_left, has_right = place("gz")
    to_left = truth(has_left, (8, LANES))
    to_right = truth(has_right, (8, LANES))
    deep = []
    for k in range(5):
        for r in range(pairs):
            if k < 4:
                n = k % 2 * pairs + r
                tile = z_tile(z_a[n], z_b[n], k // 2 * 4, 4)
                x = jnp.concatenate([whole[k, r], tile], axis=0)
                full[k, r] = x
            else:
                left, right = left_right("gz", z_a[2 * pairs + r], z_b[2 * pairs + r])
                right = jnp.where(to_right, right, 0.0)
                left = jnp.where(to_left, left, 0.0)
                x = jnp.concatenate([whole[k, r], right, left], axis=0)
                full_e[r] = x
            deep.append(x)
    row = iota((8, LANES), 0)
    for q in range(nx):
        left, right = left_right("gz", z_a[3 * pairs + q], z_b[3 * pairs + q])
        for k in range(4):
            x = jnp.where(row < 2 * has_right, roll(right, -2 * k, 0), 0.0)
            z_halo[k, q] = jnp.where(row >= 8 - 2 * has_left, roll(left, 6 - 2 * k, 0), x)
    for m in range(z_rim.shape[0]):
        n = 3 * pairs + nx + m
        left, right = left_right("gz", z_a[n], z_b[n])
        x = jnp.where(to_right & (row % 2 == 0), right, 0.0)
        z_rim[m] = jnp.where(to_left & (row % 2 == 1), left, x)
    columns = deep_edges(deep[: 4 * pairs], 4)
    half = len(columns) // 2
    columns_e = deep_edges(deep[4 * pairs :], 8)
    upper = (cz + 16) // 2
    behind = pair_edges(lambda i: [z_halo[i, q] for q in range(nx)], 4, 8)
    for m, out in enumerate((y_a, y_b)):
        toward = high_side("gy", m)
        parts = [
            strip(columns[j], columns[j + half], toward, 4) for j in range(half)
        ] + [strip(x[:upper], x[upper:], toward, 8) for x in columns_e]
        for i in range(nz // 8):
            parts.append(y_strip(edges[0, pl.ds(8 * i, 8)], edges[1, pl.ds(8 * i, 8)], toward))
        parts.append(y_strip(behind[0], behind[1], toward))
        parts += [frame(frames, m_x, 1) for m_x in range(z_rim.shape[0])]
        n = 0
        for x in parts:
            for i in range(x.shape[0] // 8):
                out[n] = x[8 * i : 8 * i + 8]
                n += 1


def sixth_pack(y_a, y_b, halo_full, y_rim):
    tiles, sides = halo_full.shape[1] // 8, y_rim.shape[0]
    first = y_a.shape[0] - tiles - sides
    for i in range(tiles):
        for j, x in enumerate(merge_y(y_a[first + i], y_b[first + i])):
            halo_full[j, pl.ds(8 * i, 8)] = x
    _, has_left, has_right = place("gy")
    odd = iota((8, LANES), 1) % 2
    for m in range(sides):
        left, right = left_right("gy", y_a[first + tiles + m], y_b[first + tiles + m])
        kept = (odd < has_left) & (odd == 0) | (odd > 1 - has_right)
        y_rim[m] = jnp.where(kept, jnp.where(odd == 0, left, right), 0.0)


def coarse_solve(full, full_e, y_a, y_b, main, halo, ca, cb, force, e, w0, w1, w2, w3, w4, w5, deep_e, grown):
    pairs, rows = full.shape[1:3]
    deep = full_e.shape[1]
    planes = 2 * pairs
    own = main.shape[1] - 2
    cz = rows - 8
    half = LANES // 2
    _, zl, zr = place("gz")
    _, yl, yr = place("gy")
    two = lax.axis_size("gx") == 2
    gx = FIXED[-1][0] if two else lax.axis_index("gx")

    def inside(rows, width):
        lane = iota((rows, LANES), 1)
        row = iota((rows, LANES), 0)
        kept = (row < cz + width * zr) | (row >= rows - width * zl)
        return kept & ((lane < half + width * yr) | (lane >= LANES - width * yl))

    zero = jnp.zeros((rows, LANES), F32)
    w = (w0, w1, w2, w3, w4, w5)
    for k in range(4):
        for p in (0, planes + 1):
            ca[k, p] = zero
            cb[k, p] = zero
    e[0] = zero
    e[planes + 1] = zero
    deep_e[0] = jnp.zeros((deep, LANES), F32)
    deep_e[planes + 1] = jnp.zeros((deep, LANES), F32)

    tiles, deep_tiles = rows // 8, deep // 16
    count = pairs // 4
    columns = []

    def taken(n, tiles):
        a, b = (jnp.concatenate([ref[n + i] for i in range(tiles)], axis=0) for ref in (y_a, y_b))
        return left_right("gy", a, b)

    unfolded = [unfold(*taken(j * tiles, tiles), 4) for j in range(count)]
    columns = [x for x, _ in unfolded] + [x for _, x in unfolded]
    columns_e = []
    for j in range(-(-pairs // 4)):
        x = unfold(*taken(count * tiles + j * deep_tiles, deep_tiles), 8)
        columns_e.append(jnp.concatenate(x, axis=0))

    def whole_plane(pair, columns, n, s, width):
        lane = iota(pair.shape, 1)
        per = LANES // (2 * width)
        last, first = 2 * n + 1 - s, 2 * n + s
        low = roll(columns[first // per], half - 2 * width * (first % per) - width, 1)
        high = roll(columns[last // per], LANES - width - 2 * width * (last % per), 1)
        x = jnp.where(lane < half, roll(pair, -s * half, 1), low)
        return jnp.where(lane < LANES - width, x, high)

    near, far = inside(rows, 4), inside(deep, 8)
    for r in range(pairs):
        for s in range(2):
            p = 2 * r + s
            x = jnp.where(far, whole_plane(full_e[r], columns_e, r, s, 8), 0.0)
            deep_e[p + 1] = x
            e[p + 1] = fold_rows(x)
            for k in range(4):
                x = whole_plane(full[k, r], columns, k * pairs + r, s, 4)
                force[k, p] = jnp.where(near, x, 0.0)

    def shifts(x):
        return (
            roll(x, LANES - 1, 1),
            roll(x, 1, 1),
            roll(x, x.shape[0] - 1, 0),
            roll(x, 1, 0),
        )

    def two_by_two(width, body):
        if two:
            for p in range(max(gx * own - width, 0), min(gx * own + own + width, planes)):
                body(p + 1)
            return
        lo = jnp.maximum(gx * own - width, 0)
        hi = jnp.minimum(gx * own + own + width, planes)
        steps = (hi - lo + 1) // 2
        lo = jnp.minimum(lo, planes - 2 * steps)

        def step(i, carry):
            body(lo + 2 * i + 1)
            body(lo + 2 * i + 2)
            return carry

        lax.fori_loop(0, steps, step, 0)

    def start(p):
        x = deep_e[p]
        up, down = x + deep_e[p + 1], x + deep_e[p - 1]
        w0[p] = fold_rows(up)
        total = up + down
        for n, y in enumerate(shifts(x)):
            total += x + y
            w[1 + n][p] = fold_rows(x + y)
        factor = jnp.where(near, fold_rows(relax_weight / total), 0.0)
        w5[p] = factor
        for k in range(3):
            ca[k, p] = factor * force[k, p - 1]
        ca[3, p] = e[p] * force[3, p - 1]

    w0[0] = e[0] + e[1]
    two_by_two(planes, start)

    def sweep(src, dst, width):
        def body(p):
            wxp, wxm = w0[p], w0[p - 1]
            wyp, wym, wzp, wzm = w1[p], w2[p], w3[p], w4[p]
            x = src[3, p]
            around = shifts(x)
            up, down = src[3, p + 1], src[3, p - 1]
            spread = 0.0
            for k in range(3):
                u = src[k, p]
                yp, ym, zp, zm = shifts(u)
                xp, xm = src[k, p + 1], src[k, p - 1]
                total = force[k, p - 1] - 2.0 * terms(k, up, down, *around)
                total += wxp * xp + wxm * xm
                total += wyp * yp + wym * ym
                total += wzp * zp + wzm * zm
                spread += terms(k, xp, xm, yp, ym, zp, zm)
                dst[k, p] = jnp.where(near, 0.4 * u + w5[p] * total, 0.0)
            dst[3, p] = jnp.where(near, x + e[p] * (force[3, p - 1] - 0.125 * spread), 0.0)

        two_by_two(width, body)

    sweep(ca, cb, 3)
    sweep(cb, ca, 2)
    sweep(ca, cb, 1)

    lane = iota((LANES, 2 * LANES), 1)
    cell = iota((LANES, 2 * LANES), 0)
    spot = lane % SLOT
    wanted = jnp.where(spot < 4, LANES - 2, half - 2) + spot // 2
    slot = (lane - LANES) // SLOT
    column = jnp.zeros((4 * rows, LANES), F32)
    first = gx * own

    def grow(ref, index, x):
        ref[index + (pl.ds(0, cz, stride=2),)] = x[:cz]
        ref[index + (pl.ds(1, cz, stride=2),)] = x[:cz]
        grown[pl.ds(0, 8, stride=2)] = x[cz:]
        grown[pl.ds(1, 8, stride=2)] = x[cz:]
        r = iota((8, LANES), 0)
        tail = jnp.where(r < 4, grown[pl.ds(0, 8)], grown[pl.ds(8, 8)])
        ref[index + (pl.ds(2 * cz, 8),)] = tail

    for i in range(own + 2):
        x = jnp.concatenate([cb[k, first + i] for k in range(4)], axis=0)
        here = (lane >= LANES) & ((slot + 1) // 2 - 1 == i) & (cell == wanted)
        wide = choose(x, here | ((lane < LANES) & (lane // 2 == cell)))
        for k in range(4):
            grow(main, (k, i), wide[k * rows : (k + 1) * rows, :LANES])
        column += wide[:, LANES:]
    for k in range(4):
        grow(halo, (k,), column[k * rows : (k + 1) * rows])


def last_sweep(src, halo, beside, w, e, force, chosen, store):
    slots, nz = src.shape[1], src.shape[2] - 8
    spread_halo(halo, beside, slots, 0, chosen, False)

    def body(p):
        new = main_operator(src, beside, w, force, p, nz)
        new = relaxed(*new, w[5][p, pl.ds(0, nz)], e[p, pl.ds(0, nz)])
        for k in range(4):
            store(p, k, new[k])

    over_planes(slots, 0, body, chosen)


def post_smooth(
    e, halo_e, force, halo_f, w0, w1, w2, w3, w4, w5, hw,
    fields, z_halo, halo_full, x_fine, z_rim, y_rim, main, column, v_out, p_out,
    ua, ub, ha, hb, ca, beside,
):
    nx, nz, _ = p_out.shape
    slots = nx + 6
    w = (w0, w1, w2, w3, w4, w5)
    zero = jnp.zeros((nz + 8, LANES), F32)
    for k in range(4):
        for p in (1, 2, nx + 3, nx + 4):
            ua[k, p] = zero
            ub[k, p] = zero
        for q in range(nx):
            i = q // 2 + 1
            ua[k, q + 3, pl.ds(0, nz)] = fields[k, q + 3, pl.ds(0, nz)] + main[k, i, pl.ds(0, nz)]
            ua[k, q + 3, pl.ds(nz, 8)] = z_halo[k, q] + main[k, i, pl.ds(nz, 8)]
        ha[k] = own_slots(halo_full[k % 2], nx, k // 2)
    for m in range(x_fine.shape[0]):
        right, valid = x_side(m)
        there = truth(valid, (nz, LANES))
        there8 = truth(valid, (8, LANES))
        near = 2 + right * (nx + 1)
        row = iota((8, LANES), 0)
        lane = iota((nz, LANES), 1)
        kept = (lane == near * SLOT + 3) | (lane == near * SLOT + 4)
        i = right * (nx // 2 + 1)
        for k in range(4):
            for j in range(2):
                at = 1 + right * (nx + 2) + j
                x = x_fine[m, 2 * k + j] + main[k, i, pl.ds(0, nz)]
                ua[k, at, pl.ds(0, nz)] = jnp.where(there, x, 0.0)
            x = jnp.where(row == 0, roll(z_rim[m], -2 * k, 0), 0.0)
            x = jnp.where(row == 7, roll(z_rim[m], 6 - 2 * k, 0), x) + main[k, i, pl.ds(nz, 8)]
            ua[k, near, pl.ds(nz, 8)] = jnp.where(there8, x, 0.0)
            at = near * SLOT + 3 + LANES
            x = [roll(y_rim[m], at - SLOT * t - 2 * k, 1) for t in range(nz // 8)]
            x = jnp.where(kept, jnp.concatenate(x, axis=0), ha[k, pl.ds(0, nz)])
            ha[k, pl.ds(0, nz)] = jnp.where(there, x, ha[k, pl.ds(0, nz)])
    masks = fine_masks(nz + 8, slots)
    for k in range(4):
        ha[k] = jnp.where(masks[1], ha[k] + column[k], 0.0)
    fill_edges(ca, ua, inside_slots(slots, 2))
    main_sweep(ua, ha, ub, w, e, force, 1, masks[0], beside)
    halo_sweep(ha, ca, hb, hw, halo_e, halo_f, masks[1])

    def store(p, k, x):
        if k < 3:
            v_out[k, p - 3] = x
        else:
            p_out[p - 3] = x

    last_sweep(ub, hb, beside, w, e, force, None, store)


def finish(*refs):
    coarse, operator, rest = refs[:4], refs[4:15], refs[15:]
    fields, z_halo, x_fine, z_rim, v_out, p_out, halo_full, y_rim, main, column = rest[:10]
    sixth_pack(*coarse[2:], halo_full, y_rim)
    coarse_solve(*coarse, main, column, *rest[10:22])
    post_smooth(
        *operator, fields, z_halo, halo_full, x_fine, z_rim, y_rim, main, column, v_out, p_out,
        *rest[22:],
    )


def local(velocity, pressure, viscosity, body_force):
    nx, nz, ny = pressure.shape
    if ny != LANES or nx * SLOT * 2 != LANES or nz % 16:
        raise ValueError("unsupported block")
    sides = x_messages()
    rows, slots = nz + 8, nx + 6
    inputs = [velocity, pressure, viscosity, body_force]
    block = (nz, LANES)

    z_shape = (3 * nx, 8, LANES)
    half = (nx // 2,) + block
    *staged, y_a, y_b = call(
        first_pack, [half] * 16 + [(2,) + block] * 2, inputs, outside=4, copies=16
    )
    x_main, z_a, z_b = call(side_pack, [(sides, 21) + block, z_shape, z_shape], staged)
    y_a, y_b = swap(y_a, "gy", 0), swap(y_b, "gy", 1)
    x_main = swap_x(x_main)
    halo, z_a, z_b = call(
        second_pack, [(4,) + block, z_shape, z_shape], [z_a, z_b, y_a, y_b]
    )
    z_a, z_b = swap(z_a, "gz", 0), swap(z_b, "gz", 1)
    tiles = rows // 8
    z_first, halo_first, x_first = call(
        third_pack,
        [(8, nx, 8, LANES), (4, rows, LANES), (sides, 6 + tiles, 8, LANES)],
        [z_a, z_b, halo],
    )
    x_first = swap_x(x_first)

    spread, column = (4, slots, rows, LANES), (4, rows, LANES)
    started = [(slots, rows, LANES), (rows, LANES), (3, slots, rows, LANES), (3, rows, LANES)]
    started += [(slots, rows, LANES)] * 6 + [spread, spread] + [column] * 3 + [(rows, LANES)]
    started += [(5, nx // 2, rows, LANES)]
    tiles_c = 5 * (nx // 4) * (nz // 16)
    state = call(
        by_sides(pre_start),
        started,
        [*staged, z_first, halo_first, x_main],
        [(7, rows, LANES), column, column, spread],
        cost=4,
    )
    *operator, fields, _, _, _, _, _, _, factors, own = call(
        by_sides(pre_smooth),
        started + [(7, rows, LANES), (tiles_c + 2 * sides, 8, LANES)],
        [x_first, *state],
        [column, spread],
        cost=8,
        aliases={i + 1: i for i in range(len(started))},
    )
    operator.append(factors)
    edges, x_fine = call(smooth_pack, [(2,) + block, (sides, 8) + block], [fields])
    if lax.axis_size("gx") == 2:
        frames = swap(own, "gx", 0)
    else:
        frames = swap_x(own[tiles_c:].reshape(sides, 2, 8, LANES)).reshape(2 * sides, 8, LANES)
        own = own[:tiles_c].reshape(5, nx // 4, nz // 2, LANES)
        own = lax.all_gather(own, "gx", axis=1, tiled=True)
    x_fine = swap_x(x_fine)
    pairs = lax.axis_size("gx") * (nx // 4)
    z_shape = (3 * pairs + nx + sides, 8, LANES)
    whole, z_a, z_b = call(
        fourth_pack,
        [(5, pairs, nz // 2, LANES), z_shape, z_shape],
        [own, frames, fields],
    )
    z_a, z_b = swap(z_a, "gz", 0), swap(z_b, "gz", 1)
    deep = nz // 2 + 16
    shallow = deep - 8
    y_shape = (pairs // 4 * (shallow // 8) + -(-pairs // 4) * (deep // 16) + tiles, 8, LANES)
    y_shape = (y_shape[0] + sides, 8, LANES)
    rim = (sides, 8, LANES)
    full, full_e, z_halo, z_rim, y_a, y_b = call(
        fifth_pack,
        [(4, pairs, shallow, LANES), (pairs, deep, LANES), (4, nx, 8, LANES), rim, y_shape, y_shape],
        [whole, z_a, z_b, edges, frames],
    )
    y_a, y_b = swap(y_a, "gy", 0), swap(y_b, "gy", 1)
    planes = 2 * pairs
    plane = (shallow, LANES)
    coarse_scratch = [(4, nx // 2 + 2, rows, LANES), (4, rows, LANES)]
    coarse_scratch += [(4, planes + 2) + plane] * 2 + [(4, planes) + plane]
    coarse_scratch += [(planes + 2,) + plane] * 7 + [(planes + 2, deep, LANES), (24, LANES)]
    v_out, p_out = call(
        by_sides(finish),
        [(3, nx) + block, (nx,) + block],
        [full, full_e, y_a, y_b] + operator + [fields, z_halo, x_fine, z_rim],
        [(2, rows, LANES), rim] + coarse_scratch + [spread] * 2 + [column] * 3 + [spread],
        cost=8,
    )
    return v_out, p_out


def swap_x(array):
    if array.shape[0] == 1:
        return swap(array, "gx", 0)
    parts = [swap(array[m], "gx", m) for m in range(2)]
    return jnp.stack(parts)


def solution(mesh):
    return jax.shard_map(
        local,
        mesh=mesh,
        in_specs=(
            P(None, "gx", "gz", "gy"),
            P("gx", "gz", "gy"),
            P("gx", "gz", "gy"),
            P(None, "gx", "gz", "gy"),
        ),
        out_specs=(P(None, "gx", "gz", "gy"), P("gx", "gz", "gy")),
        check_vma=False,
    )
```
